32 devices in a mesh: tm: 32 (over z, y, x, core).
Axes of the slice: x: 2, y: 2, z: 4, core: 2. Of those that a mesh axis runs over, the one named last changes fastest.
Arguments:
- inputs: bfloat16 [8, 2048, 75], P(None, 'tm'), may hold values from -12 to 12
- clip_start: int32 [8, 2048], P(None, 'tm'), may hold values from 0 to 1, as said below
- shallow_weight: float32 [75, 2000], replicated, may hold values from -0.75 to 0.75
- shallow_momentum: float32 [75, 2000], replicated, may hold values from -24 to 24
- deep_weight: float32 [4000000], P('tm'), may hold values from -0.125 to 0.125
- deep_momentum: float32 [4000000], P('tm')
- unit_params: float32 [2, 4, 2000], replicated, may hold values from -2 to 12
- unit_first: float32 [2, 4, 2000], replicated
- unit_second: float32 [2, 4, 2000], replicated
- out_grad: bfloat16 [8, 2048, 2000], P(None, 'tm'), may hold values from -12 to 12
Outputs:
- hidden_one: float32 [8, 2048, 2000], P(None, 'tm')
- hidden_two: float32 [8, 2048, 2000], P(None, 'tm')
- input_grad: float32 [8, 2048, 75], P(None, 'tm')
- shallow_grad: float32 [75, 2000], replicated
- shallow_momentum_new: float32 [75, 2000], replicated
- shallow_weight_new: float32 [75, 2000], replicated
- shallow_weight_low: bfloat16 [75, 2000], replicated
- deep_grad: float32 [4000000], P('tm')
- deep_momentum_new: float32 [4000000], P('tm')
- deep_weight_new: float32 [4000000], P('tm')
- deep_weight_low: bfloat16 [4000000], P('tm')
- unit_first_new: float32 [2, 4, 2000], replicated
- unit_second_new: float32 [2, 4, 2000], replicated
- unit_params_new: float32 [2, 4, 2000], replicated
The draws below stay inside these ranges and needn't reach their ends.
Inputs may be any that keep to these rules, and one draw needn't show every extreme that they name: `clip_start`: frame 0 of every row is 1; in every draw at least one row has no other 1.
All inputs are finite; a program needn't handle non-finite values.
Results may differ from the reference program's by a relative error of at most 0.011.
Values may be sent and summed in bfloat16 or wider, within the bound.
No kernel may reach another device: no remote copies, remote signals or barrier semaphores. Data moves between devices by JAX's collectives and lax.ppermute only.
A program may use at most 320 MiB of HBM per device.

```python
import math
import jax
import jax.numpy as jnp
from jax import lax

ROWS = 8
BLOCK_FRAMES = 64
FEATS = 75
H = 2000
NS_STEPS = 2
STEP = 5
FRAMES = 2048


def gradient_scales():
    return jnp.array([0.5, 0.3, 0.3, 0.3], jnp.float32)[None, :, None] * math.sqrt(ROWS * FRAMES)


def draw_inputs(key, part):
    key = jax.random.fold_in(key, 11)
    position = jnp.arange(FRAMES, dtype=jnp.float32)[None, :, None] / FRAMES
    values = jax.random.normal(key, (ROWS, FRAMES, FEATS), jnp.float32) * (1.0 + 2.0 * position)
    return jnp.clip(values, -12.0, 12.0).astype(jnp.bfloat16)


def draw_out_grad(key, part):
    key = jax.random.fold_in(key, 12)
    position = jnp.arange(FRAMES, dtype=jnp.float32)[None, :, None] / FRAMES
    values = jax.random.normal(key, (ROWS, FRAMES, H), jnp.float32) * (1.0 + 2.0 * position)
    return jnp.clip(values, -12.0, 12.0).astype(jnp.bfloat16)


def draw_clip_start(key, part):
    key = jax.random.fold_in(key, 13)
    first_key, second_key = jax.random.split(key)
    starts = (jax.random.randint(first_key, (ROWS, FRAMES), 0, 16 * BLOCK_FRAMES) == 0).astype(jnp.int32)
    whole_row = jax.random.randint(second_key, (), 0, ROWS)
    row_index = jnp.arange(ROWS)[:, None]
    frame_index = jnp.arange(FRAMES)[None, :]
    starts = jnp.where(row_index == whole_row, 0, starts)
    return jnp.where(frame_index == 0, 1, starts).astype(jnp.int32)


def draw_unit_params(key, part):
    key = jax.random.fold_in(key, 14)
    subkeys = jax.random.split(key, 6)
    slow_share = 0.5
    slow_picks = jax.random.uniform(subkeys[0], (2, H), jnp.float32)
    slow_exponent = jax.random.uniform(subkeys[1], (2, H), jnp.float32, math.log(FRAMES / 2.3), math.log(FRAMES / 0.3))
    fast_exponent = -jnp.log(jax.random.uniform(subkeys[2], (2, H), jnp.float32, 0.03, 0.14))
    decays = jnp.where(slow_picks < slow_share, slow_exponent, fast_exponent)
    biases = jnp.clip(0.5 * jax.random.normal(subkeys[3], (2, H), jnp.float32), -2.0, 2.0)
    unit_place = jnp.arange(H, dtype=jnp.float32)[None, :] / H
    gain_values = jax.random.uniform(subkeys[4], (2, H), jnp.float32, 0.6, 1.0) * (0.6 + 1.4 * unit_place)
    shifts = jnp.clip(0.5 * jax.random.normal(subkeys[5], (2, H), jnp.float32), -2.0, 2.0)
    return jnp.stack([decays, biases, gain_values, shifts], axis=1)


def draw_unit_first(key, part):
    key = jax.random.fold_in(key, 15)
    values = jax.random.normal(key, (2, 4, H), jnp.float32)
    return values * (0.111 * gradient_scales())


def draw_unit_second(key, part):
    key = jax.random.fold_in(key, 16)
    factors = jnp.exp(jax.random.uniform(key, (2, 4, H), jnp.float32, 0.0, math.log(4.0)))
    scales = gradient_scales()
    return factors * (0.0526 * scales * scales)


def draw_deep_momentum(key, part):
    key = jax.random.fold_in(key, 17)
    row_place = (jnp.arange(H * H) // H).astype(jnp.float32) / H
    values = jax.random.normal(key, (H * H,), jnp.float32) * (1.0 + 4.0 * row_place)
    return values * (0.04 * math.sqrt(ROWS * FRAMES))


def block_levels(own_key, shape, cuts, low, high):
    loudness, own = 1.0, jax.random.fold_in(own_key, 6)
    for dim, parts in cuts:
        heights = jnp.exp(jax.random.uniform(jax.random.fold_in(own, dim), (parts,), jnp.float32, low / len(cuts), high / len(cuts)))
        loudness = loudness * jnp.repeat(heights, shape[dim] // parts).reshape([-1 if axis == dim else 1 for axis in range(len(shape))])
    return loudness


def noise(stream_key, dims, width, limit, pieces=(), held_as=jnp.bfloat16):
    factor_of = block_levels(stream_key, dims, pieces, -0.22, 0.18) if pieces else 1.0
    values = jax.random.normal(stream_key, dims, jnp.float32) * width * factor_of
    return jnp.minimum(jnp.maximum(values, -limit), limit).astype(held_as)


def setup_inputs(seed: int = 0) -> dict:
    key_of = jax.random.split(jax.random.key(seed), 11)
    inputs = draw_inputs(jax.random.fold_in(key_of[10], 71), 0)
    clip_start = draw_clip_start(jax.random.fold_in(key_of[10], 71), 0)
    shallow_weight = noise(key_of[2], (FEATS, H), FEATS ** -0.5, 0.75, (), jnp.float32)
    shallow_momentum = noise(key_of[3], (FEATS, H), (0.03 * (ROWS * FRAMES) ** 0.5), 24.0, (), jnp.float32)
    deep_weight = noise(key_of[4], (H * H,), H ** -0.5, 0.125, ((0, 32),), jnp.float32)
    deep_momentum = draw_deep_momentum(jax.random.fold_in(key_of[10], 71), 0)
    unit_params = draw_unit_params(jax.random.fold_in(key_of[10], 71), 0)
    unit_first = draw_unit_first(jax.random.fold_in(key_of[10], 71), 0)
    unit_second = draw_unit_second(jax.random.fold_in(key_of[10], 71), 0)
    out_grad = draw_out_grad(jax.random.fold_in(key_of[10], 71), 0)
    return {"inputs": inputs, "clip_start": clip_start, "shallow_weight": shallow_weight, "shallow_momentum": shallow_momentum, "deep_weight": deep_weight, "deep_momentum": deep_momentum, "unit_params": unit_params, "unit_first": unit_first, "unit_second": unit_second, "out_grad": out_grad}


NORM_EPSILON = 1e-05
MUON_EPSILON = 1e-07
COEFF_A = 3.4445
COEFF_B = -4.775
COEFF_C = 2.0315
MUON_BETA = 0.5
MUON_RATE = 4.0
MUON_KEEP = 0.999
FIRST_DECAY = 0.9
SECOND_DECAY = 0.95
ADAM_RATE = 0.5
ADAM_EPSILON = 1e-08
DECAY_FLOOR = 0.9

@jax.custom_vjp
def low(v):
    return lax.optimization_barrier(v.astype(jnp.bfloat16)).astype(jnp.float32)

@jax.custom_vjp
def low_back(v):
    return v

def low_keep(v):
    return (low(v), None)

def low_pass(kept, grad):
    return (grad,)

def back_keep(v):
    return (v, None)

def back_low(kept, grad):
    return (low(grad),)
low.defvjp(low_keep, low_pass)
low_back.defvjp(back_keep, back_low)

def recurrent_layer(layer_input, weight, params, keep_mask):
    row_count, frame_count, width_in = layer_input.shape
    flat_rows = low(layer_input.reshape(row_count * frame_count, width_in))
    projected = low_back(jnp.dot(flat_rows, low(weight), precision=lax.Precision.HIGHEST))
    centre = lax.optimization_barrier(jnp.mean(projected, axis=0))
    spread = lax.optimization_barrier(jnp.mean(jnp.square(projected - centre), axis=0))
    normed = (projected - centre) * lax.rsqrt(spread + NORM_EPSILON)
    gate_in = normed * params[2] + params[3] + params[1]
    decay_rate = jnp.maximum(1.0 - jnp.exp(-params[0]), DECAY_FLOOR)
    driven = ((1.0 - decay_rate) * jax.nn.softplus(gate_in)).reshape(row_count, frame_count, -1)
    keep_rate = decay_rate * keep_mask[:, :, None]

    def advance(carried, frame_pair):
        carried = frame_pair[0] * carried + frame_pair[1]
        return (carried, carried)
    initial = jnp.zeros((row_count, driven.shape[2]), jnp.float32)
    _, states = lax.scan(advance, initial, (jnp.swapaxes(keep_rate, 0, 1), jnp.swapaxes(driven, 0, 1)))
    return jnp.swapaxes(states, 0, 1)

def orthogonal(matrix):
    current = (matrix / (jnp.sqrt(jnp.sum(matrix * matrix)) + MUON_EPSILON)).astype(jnp.bfloat16)
    for repeat in range(NS_STEPS):
        gram_matrix = jnp.dot(current, current.T, preferred_element_type=jnp.float32).astype(jnp.bfloat16)
        square = jnp.dot(gram_matrix, gram_matrix, preferred_element_type=jnp.float32)
        mixing = (COEFF_B * gram_matrix.astype(jnp.float32) + COEFF_C * square).astype(jnp.bfloat16)
        current = (COEFF_A * current.astype(jnp.float32) + jnp.dot(mixing, current, preferred_element_type=jnp.float32)).astype(jnp.bfloat16)
    return current.astype(jnp.float32)

def reference(inputs, clip_start, shallow_weight, shallow_momentum, deep_weight, deep_momentum, unit_params, unit_first, unit_second, out_grad):
    keep_mask = (1 - clip_start).astype(jnp.float32)
    deep_matrix = deep_weight.reshape(H, H)

    def forward(layer_input, shallow_matrix, second_matrix, params):
        hidden_one = recurrent_layer(layer_input, shallow_matrix, params[0], keep_mask)
        hidden_two = recurrent_layer(hidden_one, second_matrix, params[1], keep_mask)
        return (hidden_one, hidden_two)
    outputs, pullback = jax.vjp(forward, inputs.astype(jnp.float32), shallow_weight, deep_matrix, unit_params)
    hidden_one, hidden_two = outputs
    input_grad, shallow_grad, deep_grad, unit_grad = pullback((jnp.zeros_like(hidden_one), out_grad.astype(jnp.float32)))
    shallow_next = MUON_BETA * shallow_momentum + shallow_grad
    deep_flat = deep_grad.reshape(-1)
    deep_next = MUON_BETA * deep_momentum + deep_flat
    shallow_new = MUON_KEEP * shallow_weight - MUON_RATE * orthogonal(shallow_next)
    deep_new = MUON_KEEP * deep_weight - MUON_RATE * orthogonal(deep_next.reshape(H, H)).reshape(-1)
    first_fix = 1.0 - FIRST_DECAY ** STEP
    second_fix = 1.0 - SECOND_DECAY ** STEP
    first_new = FIRST_DECAY * unit_first + (1.0 - FIRST_DECAY) * unit_grad
    second_new = SECOND_DECAY * unit_second + (1.0 - SECOND_DECAY) * unit_grad * unit_grad
    params_new = unit_params - ADAM_RATE * (first_new / first_fix) / (jnp.sqrt(second_new / second_fix) + ADAM_EPSILON)
    return (hidden_one, hidden_two, input_grad, shallow_grad, shallow_next, shallow_new, shallow_new.astype(jnp.bfloat16), deep_flat, deep_next, deep_new, deep_new.astype(jnp.bfloat16), first_new, second_new, params_new)
```

```python
import functools

import jax
import jax.numpy as jnp
from jax import lax
from jax.experimental import pallas as pl
from jax.experimental.pallas import tpu as pltpu
from jax.sharding import PartitionSpec as P

NS_STEPS = 2
STEP = 5


NORM_EPSILON = 1e-05
MUON_EPSILON = 1e-07
COEFF_A = 3.4445
COEFF_B = -4.775
COEFF_C = 2.0315
MUON_BETA = 0.5
MUON_RATE = 4.0
MUON_KEEP = 0.999
FIRST_DECAY = 0.9
SECOND_DECAY = 0.95
ADAM_RATE = 0.5
ADAM_EPSILON = 1e-08
DECAY_FLOOR = 0.9
LANE = 128
WIDE = 512


def kernel_call(body, grid, in_specs, out_specs, out_shape, scratch=(), flops=0, traffic=0):
    return pl.pallas_call(
        body,
        grid=grid,
        in_specs=in_specs,
        out_specs=out_specs,
        out_shape=out_shape,
        scratch_shapes=list(scratch),
        compiler_params=pltpu.CompilerParams(vmem_limit_bytes=56 * 1024 * 1024),
        cost_estimate=pl.CostEstimate(flops=flops, bytes_accessed=traffic, transcendentals=0),
    )


def shape_of(shape, dtype=jnp.float32):
    return jax.ShapeDtypeStruct(shape, dtype)


def whole(shape):
    return pl.BlockSpec(shape, lambda i: (0,) * len(shape))


def lanes_of(rows, width=WIDE):
    return pl.BlockSpec((rows, width), lambda i: (0, i))


def rate_of(params):
    return jnp.maximum(1.0 - jnp.exp(-params[0:1]), DECAY_FLOOR)


def wide_keep(keep_ref, t, rows):
    keep = keep_ref[pl.ds(pl.multiple_of(t * rows, rows), rows), :]
    return jnp.concatenate([keep] * (WIDE // LANE), axis=1)


def rows_at(ref, t, rows):
    return ref[pl.ds(pl.multiple_of(t * rows, rows), rows), :]


def store_at(ref, t, rows, value):
    ref[pl.ds(pl.multiple_of(t * rows, rows), rows), :] = value


def valid_lanes(shape, total, step):
    return lax.broadcasted_iota(jnp.int32, shape, 1) + step * WIDE < total


def unit_terms(params_ref, stat_ref, total_devices, frames):
    params = params_ref[...]
    stat = stat_ref[...]
    centre = stat[0:1]
    inverse = lax.rsqrt(stat[1:2] / (total_devices * frames) + NORM_EPSILON)
    return centre, inverse, params[2:3], params[3:4] + params[1:2]


def front_body(rows, frames, width, x_ref, w_ref, xt_ref, proj_ref, stat_ref):
    step = pl.program_id(0)
    count = rows * frames

    @pl.when(step == 0)
    def _():
        i = lax.broadcasted_iota(jnp.int32, (count, count), 0)
        j = lax.broadcasted_iota(jnp.int32, (count, count), 1)
        move = (j == lax.rem(i, rows) * frames + lax.div(i, rows)).astype(jnp.bfloat16)
        xt_ref[...] = jnp.dot(move, x_ref[...], preferred_element_type=jnp.float32).astype(
            jnp.bfloat16
        )

    weight = w_ref[...]
    weight = jnp.where(valid_lanes(weight.shape, width, step), weight, 0.0).astype(jnp.bfloat16)
    proj = jnp.dot(xt_ref[...], weight, preferred_element_type=jnp.float32)
    proj_ref[...] = proj
    mean = jnp.sum(proj, axis=0, keepdims=True) * (1.0 / count)
    off = proj - mean
    stat_ref[0:1, :] = mean
    stat_ref[1:2, :] = jnp.sum(off * off, axis=0, keepdims=True)


def front(x, weight, rows, frames):
    count, feats = x.shape
    width = weight.shape[1]
    padded = -(-width // WIDE) * WIDE
    return kernel_call(
        functools.partial(front_body, rows, frames, width),
        (padded // WIDE,),
        [whole((count, feats)), lanes_of(feats)],
        [whole((count, feats)), lanes_of(count), lanes_of(2)],
        [shape_of((count, feats), jnp.bfloat16), shape_of((count, padded)), shape_of((2, padded))],
        flops=2 * count * feats * padded,
        traffic=4 * count * padded,
    )(x, weight)


def delta_two_body(rows, frames, width, grad_ref, keep_ref, params_ref, delta_ref, end_ref, held):
    step = pl.program_id(0)
    pieces = WIDE // LANE
    mask = valid_lanes((rows * frames, WIDE), width, step)
    grad = jnp.where(mask, grad_ref[...].astype(jnp.float32), 0.0)
    for g in range(pieces):
        held[g] = grad[:, g * LANE : (g + 1) * LANE]
    rate = rate_of(params_ref[...])

    def body(k, carried):
        t = frames - 1 - k
        own = jnp.concatenate(
            [held[g, pl.ds(t, rows, stride=frames), :] for g in range(pieces)], axis=1
        )
        delta = own + carried
        store_at(delta_ref, t, rows, delta)
        return rate * wide_keep(keep_ref, t, rows) * delta

    end_ref[...] = lax.fori_loop(
        0, frames, body, jnp.zeros((rows, WIDE), jnp.float32), unroll=8
    )


def delta_two(out_grad, keep, params, rows, frames, padded):
    count, width = out_grad.shape
    return kernel_call(
        functools.partial(delta_two_body, rows, frames, width),
        (padded // WIDE,),
        [lanes_of(count), whole((count, LANE)), lanes_of(4)],
        [lanes_of(count), lanes_of(rows)],
        [shape_of((count, padded)), shape_of((rows, padded))],
        [pltpu.VMEM((WIDE // LANE, count, LANE), jnp.float32)],
        traffic=6 * count * padded,
    )(out_grad, keep, params)


def states_body(
    rows, frames, devices, proj_ref, keep_ref, params_ref, stat_ref, state_ref, end_ref
):
    centre, inverse, gain, offset = unit_terms(params_ref, stat_ref, devices, rows * frames)
    rate = rate_of(params_ref[...])
    share = 1.0 - rate

    def body(t, carried):
        gate = (rows_at(proj_ref, t, rows) - centre) * inverse * gain + offset
        soft = jnp.maximum(gate, 0.0) + jnp.log1p(jnp.exp(-jnp.abs(gate)))
        carried = rate * wide_keep(keep_ref, t, rows) * carried + share * soft
        store_at(state_ref, t, rows, carried)
        return carried

    end_ref[...] = lax.fori_loop(
        0, frames, body, jnp.zeros((rows, WIDE), jnp.float32), unroll=8
    )


def local_states(proj, keep, params, stat, rows, frames, devices):
    count, padded = proj.shape
    return kernel_call(
        functools.partial(states_body, rows, frames, devices),
        (padded // WIDE,),
        [lanes_of(count), whole((count, LANE)), lanes_of(4), lanes_of(2)],
        [lanes_of(count), lanes_of(rows)],
        [shape_of((count, padded)), shape_of((rows, padded))],
        traffic=8 * count * padded,
    )(proj, keep, params, stat)


def to_slots(value, group):
    pieces = value.shape[1] // LANE
    lane = lax.broadcasted_iota(jnp.int32, (value.shape[0], LANE), 1)
    parts = [value[:, g * LANE : (g + 1) * LANE] for g in range(pieces)]
    out = []
    for g in range(pieces):
        moved = (LANE - group) * g
        if moved == 0:
            new = parts[g]
        else:
            new = jnp.where(
                lane < moved, pltpu.roll(parts[g - 1], moved, 1), pltpu.roll(parts[g], moved, 1)
            )
        out.append(jnp.where(lane < group, new, 0.0))
    return jnp.concatenate(out, axis=1)


def from_slots(value, group, width):
    pieces = value.shape[1] // LANE
    lane = lax.broadcasted_iota(jnp.int32, (value.shape[0], LANE), 1)
    parts = [value[:, g * LANE : (g + 1) * LANE] for g in range(pieces)]
    out = []
    for j in range(pieces):
        moved = (LANE - group) * j
        new = parts[j] if moved == 0 else pltpu.roll(parts[j], LANE - moved, 1)
        if j + 1 < pieces:
            new = jnp.where(lane < group - moved, new, pltpu.roll(parts[j + 1], group - moved, 1))
        left = width - j * LANE
        out.append(new if left >= LANE else jnp.where(lane < left, new, 0.0))
    return jnp.concatenate(out, axis=1)


def second_body(
    rows,
    frames,
    width,
    group,
    state_ref,
    start_ref,
    keep_ref,
    params_ref,
    weight_ref,
    hidden_ref,
    low_ref,
    proj_ref,
    stat_ref,
    held,
):
    step = pl.program_id(0)
    count = rows * frames
    padded = state_ref.shape[1]
    pieces = padded // LANE

    @pl.when(step == 0)
    def _():
        rate = rate_of(params_ref[...])

        def advance(t, carried):
            keep = rows_at(keep_ref, t, rows)
            carried = rate * jnp.concatenate([keep] * pieces, axis=1) * carried
            return carried, rows_at(state_ref, t, rows) + carried

        def body(k, carried):
            t = 2 * k
            carried, first = advance(t, carried)
            carried, second = advance(t + 1, carried)
            pair = jnp.concatenate([first, second], axis=0)
            for g in range(pieces):
                held[g, pl.ds(pl.multiple_of(t * rows, 2 * rows), 2 * rows), :] = pair[
                    :, g * LANE : (g + 1) * LANE
                ]
            low_ref[pl.ds(pl.multiple_of(t * rows, 2 * rows), 2 * rows), :] = to_slots(
                pair, group
            ).astype(jnp.bfloat16)
            return carried

        lax.fori_loop(0, frames // 2, body, start_ref[...])
        for r in range(rows):
            for g in range(pieces):
                left = min(LANE, width - g * LANE)
                part = held[g, pl.ds(r, frames, stride=rows), :]
                hidden_ref[r * frames : (r + 1) * frames, g * LANE : g * LANE + left] = part[
                    :, :left
                ]

    proj = jnp.dot(low_ref[...], weight_ref[...], preferred_element_type=jnp.float32)
    proj_ref[...] = proj
    mean = jnp.sum(proj, axis=0, keepdims=True) * (1.0 / count)
    off = proj - mean
    stat_ref[0:1, :] = mean
    stat_ref[1:2, :] = jnp.sum(off * off, axis=0, keepdims=True)


def second_forward(states, start, keep, params, weight, rows, frames, width, group):
    count, padded = states.shape
    return kernel_call(
        functools.partial(second_body, rows, frames, width, group),
        (padded // WIDE,),
        [
            whole((count, padded)),
            whole((rows, padded)),
            whole((count, LANE)),
            whole((4, padded)),
            lanes_of(padded),
        ],
        [whole((count, width)), whole((count, padded)), lanes_of(count), lanes_of(2)],
        [
            shape_of((count, width)),
            shape_of((count, padded), jnp.bfloat16),
            shape_of((count, padded)),
            shape_of((2, padded)),
        ],
        [pltpu.VMEM((padded // LANE, count, LANE), jnp.float32)],
        flops=2 * count * padded * padded,
        traffic=14 * count * padded + 2 * padded * padded,
    )(states, start, keep, params, weight)


def gate_two_body(
    rows, frames, devices, proj_ref, delta_ref, start_ref, keep_ref, params_ref, stat_ref, gate_ref, sums_ref
):
    centre, inverse, gain, offset = unit_terms(params_ref, stat_ref, devices, rows * frames)
    rate = rate_of(params_ref[...])
    share = 1.0 - rate
    none = jnp.zeros((rows, WIDE), jnp.float32)

    def body(k, carried):
        carry, bias_sum, gain_sum = carried
        t = frames - 1 - k
        delta = rows_at(delta_ref, t, rows) + carry
        normed = (rows_at(proj_ref, t, rows) - centre) * inverse
        gate = share * delta * jax.nn.sigmoid(normed * gain + offset)
        store_at(gate_ref, t, rows, gate)
        carry = rate * wide_keep(keep_ref, t, rows) * carry
        return carry, bias_sum + gate, gain_sum + gate * normed

    _, bias_sum, gain_sum = lax.fori_loop(
        0, frames, body, (start_ref[...], none, none), unroll=8
    )
    sums_ref[0:1, :] = jnp.sum(bias_sum, axis=0, keepdims=True)
    sums_ref[1:2, :] = jnp.sum(gain_sum, axis=0, keepdims=True)


def gate_two(proj, delta, start, keep, params, stat, rows, frames, devices):
    count, padded = proj.shape
    return kernel_call(
        functools.partial(gate_two_body, rows, frames, devices),
        (padded // WIDE,),
        [lanes_of(count), lanes_of(count), lanes_of(rows), whole((count, LANE)), lanes_of(4), lanes_of(2)],
        [lanes_of(count), lanes_of(2)],
        [shape_of((count, padded)), shape_of((2, padded))],
        traffic=12 * count * padded,
    )(proj, delta, start, keep, params, stat)


def deep_term_body(rows, frames, devices, gate_ref, proj_ref, params_ref, stat_ref, sums_ref, low_ref, grad_ref, term_ref):
    total = devices * rows * frames
    centre, inverse, gain, _ = unit_terms(params_ref, stat_ref, devices, rows * frames)
    sums = sums_ref[...] * (1.0 / total)
    normed = (proj_ref[...] - centre) * inverse
    grad = (gain * inverse * (gate_ref[...] - sums[0:1] - normed * sums[1:2])).astype(jnp.bfloat16)
    grad_ref[...] = grad
    term_ref[...] = lax.dot_general(
        low_ref[...], grad, (((0,), (0,)), ((), ())), preferred_element_type=jnp.float32
    ).astype(term_ref.dtype)


def deep_term(gate, proj, params, stat, sums, low, rows, frames, devices, dtype):
    count, padded = proj.shape
    return kernel_call(
        functools.partial(deep_term_body, rows, frames, devices),
        (padded // WIDE,),
        [lanes_of(count), lanes_of(count), lanes_of(4), lanes_of(2), lanes_of(2), whole((count, padded))],
        [lanes_of(count), lanes_of(padded)],
        [shape_of((count, padded), jnp.bfloat16), shape_of((padded, padded), dtype)],
        flops=2 * count * padded * padded,
        traffic=10 * count * padded + 4 * padded * padded,
    )(gate, proj, params, stat, sums, low)


def back_body(grad_ref, weight_ref, back_ref):
    back_ref[...] = lax.dot_general(
        grad_ref[...], weight_ref[...], (((1,), (1,)), ((), ())), preferred_element_type=jnp.float32
    )


def back_one(grad, weight):
    count, padded = grad.shape
    return kernel_call(
        back_body,
        (padded // WIDE,),
        [whole((count, padded)), pl.BlockSpec((WIDE, padded), lambda i: (i, 0))],
        lanes_of(count),
        shape_of((count, padded)),
        flops=2 * count * padded * padded,
        traffic=6 * count * padded + 2 * padded * padded,
    )(grad, weight)


def delta_one_body(rows, frames, width, group, back_ref, keep_ref, params_ref, delta_ref, end_ref):
    pieces = back_ref.shape[1] // LANE
    rate = rate_of(params_ref[...])

    def body(k, carried):
        t = frames - 1 - k
        delta = from_slots(rows_at(back_ref, t, rows), group, width) + carried
        store_at(delta_ref, t, rows, delta)
        keep = rows_at(keep_ref, t, rows)
        return rate * jnp.concatenate([keep] * pieces, axis=1) * delta

    end_ref[...] = lax.fori_loop(
        0, frames, body, jnp.zeros((rows, back_ref.shape[1]), jnp.float32), unroll=2
    )


def delta_one(back, keep, params, rows, frames, width, group):
    count, padded = back.shape
    return kernel_call(
        functools.partial(delta_one_body, rows, frames, width, group),
        (1,),
        [whole((count, padded)), whole((count, LANE)), whole((4, padded))],
        [whole((count, padded)), whole((rows, padded))],
        [shape_of((count, padded)), shape_of((rows, padded))],
        traffic=8 * count * padded,
    )(back, keep, params)


def gate_one_body(
    rows,
    frames,
    devices,
    proj_ref,
    state_ref,
    first_ref,
    delta_ref,
    start_ref,
    keep_ref,
    params_ref,
    stat_ref,
    gate_ref,
    sums_ref,
    held,
):
    centre, inverse, gain, offset = unit_terms(params_ref, stat_ref, devices, rows * frames)
    rate = rate_of(params_ref[...])
    share = 1.0 - rate
    none = jnp.zeros((rows, WIDE), jnp.float32)

    def backward(k, carry):
        t = frames - 1 - k
        store_at(held, t, rows, rows_at(delta_ref, t, rows) + carry)
        return rate * wide_keep(keep_ref, t, rows) * carry

    lax.fori_loop(0, frames, backward, start_ref[...], unroll=8)

    def forward(t, carried):
        carry, before, bias_sum, gain_sum, decay_sum = carried
        keep = wide_keep(keep_ref, t, rows)
        delta = rows_at(held, t, rows)
        normed = (rows_at(proj_ref, t, rows) - centre) * inverse
        value = normed * gain + offset
        small = jnp.exp(-jnp.abs(value))
        soft = jnp.maximum(value, 0.0) + jnp.log1p(small)
        gate = share * delta * jax.nn.sigmoid(value)
        store_at(gate_ref, t, rows, gate)
        decay_sum = decay_sum + delta * (keep * before - soft)
        carry = rate * keep * carry
        before = rows_at(state_ref, t, rows) + carry
        return carry, before, bias_sum + gate, gain_sum + gate * normed, decay_sum

    first = first_ref[...]
    _, _, bias_sum, gain_sum, decay_sum = lax.fori_loop(
        0, frames, forward, (first, first, none, none, none), unroll=4
    )
    sums_ref[0:1, :] = jnp.sum(bias_sum, axis=0, keepdims=True)
    sums_ref[1:2, :] = jnp.sum(gain_sum, axis=0, keepdims=True)
    sums_ref[2:3, :] = jnp.sum(decay_sum, axis=0, keepdims=True)
    sums_ref[3:4, :] = jnp.zeros((1, WIDE), jnp.float32)


def gate_one(proj, states, first, delta, start, keep, params, stat, rows, frames, devices):
    count, padded = proj.shape
    return kernel_call(
        functools.partial(gate_one_body, rows, frames, devices),
        (padded // WIDE,),
        [
            lanes_of(count),
            lanes_of(count),
            lanes_of(rows),
            lanes_of(count),
            lanes_of(rows),
            whole((count, LANE)),
            lanes_of(4),
            lanes_of(2),
        ],
        [lanes_of(count), lanes_of(4)],
        [shape_of((count, padded)), shape_of((4, padded))],
        [pltpu.VMEM((count, WIDE), jnp.float32)],
        traffic=16 * count * padded,
    )(proj, states, first, delta, start, keep, params, stat)


def hidden_two_body(
    rows,
    frames,
    width,
    devices,
    proj_ref,
    state_ref,
    first_ref,
    delta_ref,
    start_ref,
    keep_ref,
    params_ref,
    stat_ref,
    hidden_ref,
    sums_ref,
    held,
    moved,
):
    pieces = WIDE // LANE
    centre, inverse, gain, offset = unit_terms(params_ref, stat_ref, devices, rows * frames)
    rate = rate_of(params_ref[...])

    def backward(k, carry):
        t = frames - 1 - k
        store_at(held, t, rows, rows_at(delta_ref, t, rows) + carry)
        return rate * wide_keep(keep_ref, t, rows) * carry

    lax.fori_loop(0, frames, backward, start_ref[...], unroll=8)

    def forward(t, carried):
        carry, before, decay_sum = carried
        keep = wide_keep(keep_ref, t, rows)
        delta = rows_at(held, t, rows)
        value = (rows_at(proj_ref, t, rows) - centre) * inverse * gain + offset
        soft = jnp.maximum(value, 0.0) + jnp.log1p(jnp.exp(-jnp.abs(value)))
        decay_sum = decay_sum + delta * (keep * before - soft)
        carry = rate * keep * carry
        before = rows_at(state_ref, t, rows) + carry
        for g in range(pieces):
            moved[g, pl.ds(pl.multiple_of(t * rows, rows), rows), :] = before[
                :, g * LANE : (g + 1) * LANE
            ]
        return carry, before, decay_sum

    first = first_ref[...]
    none = jnp.zeros((rows, WIDE), jnp.float32)
    _, _, decay_sum = lax.fori_loop(0, frames, forward, (first, first, none), unroll=4)
    sums_ref[...] = jnp.sum(decay_sum, axis=0, keepdims=True)
    for r in range(rows):
        for g in range(pieces):
            hidden_ref[r * frames : (r + 1) * frames, g * LANE : (g + 1) * LANE] = moved[
                g, pl.ds(r, frames, stride=rows), :
            ]


def hidden_two_of(proj, states, first, delta, start, keep, params, stat, rows, frames, width, devices):
    count, padded = proj.shape
    return kernel_call(
        functools.partial(hidden_two_body, rows, frames, width, devices),
        (padded // WIDE,),
        [
            lanes_of(count),
            lanes_of(count),
            lanes_of(rows),
            lanes_of(count),
            lanes_of(rows),
            whole((count, LANE)),
            lanes_of(4),
            lanes_of(2),
        ],
        [lanes_of(count), lanes_of(1)],
        [shape_of((count, width)), shape_of((1, padded))],
        [pltpu.VMEM((count, WIDE), jnp.float32), pltpu.VMEM((WIDE // LANE, count, LANE), jnp.float32)],
        traffic=16 * count * padded,
    )(proj, states, first, delta, start, keep, params, stat)


def shallow_body(
    rows, frames, devices, width, gate_ref, proj_ref, params_ref, stat_ref, sums_ref, x_ref, w_ref, term_ref, back_ref
):
    step = pl.program_id(0)
    feats = x_ref.shape[1]
    total = devices * rows * frames
    centre, inverse, gain, _ = unit_terms(params_ref, stat_ref, devices, rows * frames)
    sums = sums_ref[...] * (1.0 / total)
    normed = (proj_ref[...] - centre) * inverse
    grad = (gain * inverse * (gate_ref[...] - sums[0:1] - normed * sums[1:2])).astype(jnp.bfloat16)
    term_ref[0:feats, :] = lax.dot_general(
        x_ref[...], grad, (((0,), (0,)), ((), ())), preferred_element_type=jnp.float32
    )
    term_ref[feats:, :] = jnp.zeros((term_ref.shape[0] - feats, WIDE), jnp.float32)
    weight = w_ref[...]
    weight = jnp.where(valid_lanes(weight.shape, width, step), weight, 0.0).astype(jnp.bfloat16)
    part = lax.dot_general(
        grad, weight, (((1,), (1,)), ((), ())), preferred_element_type=jnp.float32
    )

    @pl.when(step == 0)
    def _():
        back_ref[...] = part

    @pl.when(step > 0)
    def _():
        back_ref[...] += part


def shallow_terms(gate, proj, params, stat, sums, x, weight, rows, frames, devices):
    count, padded = proj.shape
    feats, width = weight.shape
    held = -(-feats // 16) * 16
    return kernel_call(
        functools.partial(shallow_body, rows, frames, devices, width),
        (padded // WIDE,),
        [
            lanes_of(count),
            lanes_of(count),
            lanes_of(4),
            lanes_of(2),
            lanes_of(4),
            whole((count, feats)),
            lanes_of(feats),
        ],
        [lanes_of(held), whole((count, feats))],
        [shape_of((held, padded)), shape_of((count, feats))],
        flops=4 * count * feats * padded,
        traffic=8 * count * padded,
    )(gate, proj, params, stat, sums, x, weight)


def dot_nt(a, b):
    return lax.dot_general(a, b, (((1,), (1,)), ((), ())), preferred_element_type=jnp.float32)


def shallow_newton_body(m_ref, out_ref):
    m = m_ref[...]
    current = (m / (jnp.sqrt(jnp.sum(m * m)) + MUON_EPSILON)).astype(jnp.bfloat16)
    for repeat in range(NS_STEPS):
        gram = dot_nt(current, current).astype(jnp.bfloat16)
        square = jnp.dot(gram, gram, preferred_element_type=jnp.float32)
        mixing = (COEFF_B * gram.astype(jnp.float32) + COEFF_C * square).astype(jnp.bfloat16)
        current = (
            COEFF_A * current.astype(jnp.float32)
            + jnp.dot(mixing, current, preferred_element_type=jnp.float32)
        ).astype(jnp.bfloat16)
    out_ref[...] = current.astype(jnp.float32)


def shallow_newton(m):
    return kernel_call(
        shallow_newton_body, (1,), [whole(m.shape)], whole(m.shape), shape_of(m.shape),
        flops=12 * m.shape[0] * m.shape[0] * m.shape[1], traffic=8 * m.shape[0] * m.shape[1],
    )(m)


def newton_body(window, tile, scale_ref, place_ref, m_ref, out_ref, gram, mixing, following):
    size = m_ref.shape[0]
    blocks = size // tile
    scale = scale_ref[0]
    square_scale = scale * scale
    for i in range(blocks):
        left = m_ref[i * tile : (i + 1) * tile, :]
        for j in range(i, blocks):
            part = dot_nt(left, m_ref[j * tile : (j + 1) * tile, :]) * square_scale
            gram[i * tile : (i + 1) * tile, j * tile : (j + 1) * tile] = part.astype(jnp.bfloat16)
            if i != j:
                gram[j * tile : (j + 1) * tile, i * tile : (i + 1) * tile] = part.T.astype(
                    jnp.bfloat16
                )
    for i in range(blocks):
        left = gram[i * tile : (i + 1) * tile, :]
        for j in range(i, blocks):
            part = dot_nt(left, gram[j * tile : (j + 1) * tile, :])
            own = gram[i * tile : (i + 1) * tile, j * tile : (j + 1) * tile].astype(jnp.float32)
            part = COEFF_B * own + COEFF_C * part
            mixing[i * tile : (i + 1) * tile, j * tile : (j + 1) * tile] = part.astype(jnp.bfloat16)
            if i != j:
                mixing[j * tile : (j + 1) * tile, i * tile : (i + 1) * tile] = part.T.astype(
                    jnp.bfloat16
                )
    for i in range(blocks):
        left = mixing[i * tile : (i + 1) * tile, :]
        for j in range(blocks):
            own = m_ref[i * tile : (i + 1) * tile, j * tile : (j + 1) * tile].astype(jnp.float32)
            part = jnp.dot(left, m_ref[:, j * tile : (j + 1) * tile], preferred_element_type=jnp.float32)
            following[i * tile : (i + 1) * tile, j * tile : (j + 1) * tile] = (
                scale * (COEFF_A * own + part)
            ).astype(jnp.bfloat16)
    own = following[pl.ds(pl.multiple_of(place_ref[0] * 16, 16), window), :]
    every = following[...]
    gram_own = dot_nt(own, every).astype(jnp.bfloat16)
    turned = jnp.dot(gram_own, every, preferred_element_type=jnp.float32).astype(jnp.bfloat16)
    square = dot_nt(turned, every)
    mixed = (COEFF_B * gram_own.astype(jnp.float32) + COEFF_C * square).astype(jnp.bfloat16)
    result = COEFF_A * own.astype(jnp.float32) + jnp.dot(
        mixed, every, preferred_element_type=jnp.float32
    )
    out_ref[...] = result.astype(jnp.bfloat16)


def newton_rows(m, scale, place, window):
    size = m.shape[0]
    return kernel_call(
        functools.partial(newton_body, window, 256),
        (1,),
        [
            pl.BlockSpec(memory_space=pltpu.SMEM),
            pl.BlockSpec(memory_space=pltpu.SMEM),
            pl.BlockSpec(memory_space=pltpu.VMEM),
        ],
        whole((window, size)),
        shape_of((window, size), jnp.bfloat16),
        [pltpu.VMEM((size, size), jnp.bfloat16)] * 3,
        flops=5 * size * size * size,
        traffic=2 * size * size,
    )(scale, place, m)


def swap(value, bit):
    size = lax.axis_size("tm")
    return lax.ppermute(value, "tm", [(i, i ^ bit) for i in range(size)])


def steps_of(size):
    bits = []
    bit = 1
    while bit < size:
        bits.append(bit)
        bit *= 2
    return bits


def sum_all(value):
    for bit in steps_of(lax.axis_size("tm")):
        value = value + swap(value, bit)
    return value


def stat_all(stat, count):
    for bit in steps_of(lax.axis_size("tm")):
        other = swap(stat, bit)
        gap = stat[0:1] - other[0:1]
        mean = 0.5 * (stat[0:1] + other[0:1])
        square = (stat[1:2] + other[1:2]) + gap * gap * (0.5 * count)
        stat = jnp.concatenate([mean, square], axis=0)
        count = 2 * count
    return stat


def carry_all(ends, flags, power, reverse):
    size, mine = lax.axis_size("tm"), lax.axis_index("tm")
    rows, width = ends.shape
    pad = jnp.broadcast_to(flags[:, None], (rows, LANE))
    kept = flags[:, None] * power
    total, total_flags = ends, flags[:, None]
    before = jnp.zeros_like(ends)
    before_keep = jnp.ones_like(ends)
    for bit in steps_of(size):
        sent = jnp.concatenate([total, jnp.broadcast_to(total_flags, (rows, LANE))], axis=1)
        other = swap(sent, bit)
        other_total, other_flags = other[:, :width], other[:, width : width + 1]
        upper = (mine & bit) != 0
        following = jnp.logical_not(upper) if reverse else upper
        keep_mine, keep_other = total_flags * power, other_flags * power
        before = jnp.where(following, before_keep * other_total + before, before)
        before_keep = jnp.where(following, before_keep * keep_other, before_keep)
        total = jnp.where(
            following, keep_mine * other_total + total, keep_other * total + other_total
        )
        total_flags = total_flags * other_flags
        power = power * power
    return before


def pad_lanes(value, padded):
    gap = padded - value.shape[-1]
    return jnp.pad(value, [(0, 0)] * (value.ndim - 1) + [(0, gap)])


def flat_places(shard, width, padded):
    size = lax.axis_size("tm")
    members = size * LANE // padded
    slots = LANE // members
    return members, slots, slots * width - shard


def to_block(flat, width, padded):
    size, mine = lax.axis_size("tm"), lax.axis_index("tm")
    members, slots, excess = flat_places(flat.shape[0], width, padded)
    lacking = excess * (members - 1)
    pairs = [(i + 1, i) for i in range(size - 1) if (i + 1) % members]
    extra = lax.ppermute(flat[:lacking], "tm", pairs)
    tail = jnp.zeros((excess,), flat.dtype)
    held = jnp.concatenate([flat, extra, tail])
    return lax.dynamic_slice_in_dim(held, excess * (mine % members), slots * width).reshape(
        slots, width
    )


def from_block(block, shard, padded):
    width = block.shape[1]
    size, mine = lax.axis_size("tm"), lax.axis_index("tm")
    members, slots, excess = flat_places(shard, width, padded)
    lacking = excess * (members - 1)
    pairs = [(i, i + 1) for i in range(size - 1) if (i + 1) % members]
    flat = block.reshape(-1)
    extra = lax.ppermute(flat[slots * width - lacking :], "tm", pairs)
    held = jnp.concatenate([extra, flat])
    return lax.dynamic_slice_in_dim(held, lacking - excess * (mine % members), shard)


def own_window(shard, width, padded):
    mine = lax.axis_index("tm")
    members, _, _ = flat_places(shard, width, padded)
    window = 16
    for k in range(members):
        first = shard * k // width // 16 * 16
        last = -(-shard * (k + 1) // width)
        window = max(window, -(-(last - first) // 16) * 16)
    member = mine % members
    first = jnp.minimum(shard * member // width // 16 * 16, LANE - window)
    return window, LANE * (mine // members) + first, shard * member - first * width


def per_device(
    inputs,
    clip_start,
    shallow_weight,
    shallow_momentum,
    deep_weight,
    deep_momentum,
    unit_params,
    unit_first,
    unit_second,
    out_grad,
):
    devices = lax.axis_size("tm")
    rows, frames, feats = inputs.shape
    width = shallow_weight.shape[1]
    padded = -(-width // WIDE) * WIDE
    group = width // (padded // LANE)
    count = rows * frames
    keep_mask = (1 - clip_start).astype(jnp.float32)
    flags = jnp.min(keep_mask, axis=1)
    keep = jnp.broadcast_to(keep_mask.T.reshape(count, 1), (count, LANE))
    params = pad_lanes(unit_params, padded)
    rates = jnp.maximum(1.0 - jnp.exp(-params[:, 0:1]), DECAY_FLOOR)
    powers = rates
    for _ in range(frames.bit_length() - 1):
        powers = powers * powers

    deep_low = lax.all_gather(
        pad_lanes(to_block(deep_weight.astype(jnp.bfloat16), width, padded), padded),
        "tm",
        axis=0,
        tiled=True,
    )
    momentum_block = pad_lanes(to_block(deep_momentum, width, padded), padded)

    x, proj_one, stat_one = front(inputs.reshape(count, feats), shallow_weight, rows, frames)
    stat_one = stat_all(stat_one, float(count))
    delta_local, delta_end = delta_two(
        out_grad.reshape(count, width), keep, params[1], rows, frames, padded
    )
    delta_in = carry_all(delta_end, flags, powers[1], True)
    state_local, state_end = local_states(
        proj_one, keep, params[0], stat_one, rows, frames, devices
    )
    state_in = carry_all(state_end, flags, powers[0], False)
    hidden_one, low_one, proj_two, stat_two = second_forward(
        state_local, state_in, keep, params[0], deep_low, rows, frames, width, group
    )
    stat_two = stat_all(stat_two, float(count))
    gate, sums_two = gate_two(
        proj_two, delta_local, delta_in, keep, params[1], stat_two, rows, frames, devices
    )
    sums_two = sum_all(sums_two)
    grad_two, term = deep_term(
        gate, proj_two, params[1], stat_two, sums_two, low_one, rows, frames, devices, jnp.float32
    )
    grad_block = lax.psum_scatter(term, "tm", scatter_dimension=0, tiled=True)
    momentum_new = MUON_BETA * momentum_block + grad_block
    square = sum_all(jnp.sum(momentum_new * momentum_new).reshape(1, 1))
    gathered = lax.all_gather(momentum_new.astype(jnp.bfloat16), "tm", axis=0, tiled=True)

    back = back_one(grad_two, deep_low)
    back_local, back_end = delta_one(back, keep, params[0], rows, frames, width, group)
    back_in = carry_all(back_end, flags, powers[0], True)
    gate_low, sums_one = gate_one(
        proj_one, state_local, state_in, back_local, back_in, keep, params[0], stat_one,
        rows, frames, devices,
    )
    second_local, second_end = local_states(
        proj_two, keep, params[1], stat_two, rows, frames, devices
    )
    second_in = carry_all(second_end, flags, powers[1], False)
    hidden_two, decay_two = hidden_two_of(
        proj_two, second_local, second_in, delta_local, delta_in, keep, params[1], stat_two,
        rows, frames, width, devices,
    )
    sums_one = sum_all(jnp.concatenate([sums_one[0:3], decay_two], axis=0))
    shallow_term, input_back = shallow_terms(
        gate_low, proj_one, params[0], stat_one, sums_one, x, shallow_weight, rows, frames, devices
    )
    input_grad = jnp.swapaxes(input_back.reshape(frames, rows, feats), 0, 1)
    shallow_sum = sum_all(shallow_term)
    shallow_grad = shallow_sum[:feats, :width]
    shallow_next = MUON_BETA * shallow_momentum + shallow_grad
    held = shallow_term.shape[0]
    shallow_ortho = shallow_newton(
        jnp.pad(shallow_next, ((0, held - feats), (0, padded - width)))
    )[:feats, :width]
    shallow_new = MUON_KEEP * shallow_weight - MUON_RATE * shallow_ortho

    shard = deep_weight.shape[0]
    window, first_row, offset = own_window(shard, width, padded)
    scale = 1.0 / (jnp.sqrt(square) + MUON_EPSILON)
    ortho = newton_rows(
        gathered, scale.reshape(1), (first_row // 16).astype(jnp.int32).reshape(1), window
    )
    deep_ortho = lax.dynamic_slice_in_dim(ortho[:, :width].reshape(-1), offset, shard)
    deep_new = MUON_KEEP * deep_weight - MUON_RATE * deep_ortho.astype(jnp.float32)
    deep_grad = from_block(grad_block[:, :width], shard, padded)
    deep_next = MUON_BETA * deep_momentum + deep_grad

    unit_sums = sums_one[:, :width]
    bias_gain_two = sums_two[:, :width]
    slope = jnp.where(
        1.0 - jnp.exp(-unit_params[:, 0]) > DECAY_FLOOR, jnp.exp(-unit_params[:, 0]), 0.0
    )
    unit_grad = jnp.stack(
        [
            jnp.stack([unit_sums[2] * slope[0], unit_sums[0], unit_sums[1], unit_sums[0]]),
            jnp.stack(
                [unit_sums[3] * slope[1], bias_gain_two[0], bias_gain_two[1], bias_gain_two[0]]
            ),
        ]
    )
    first_fix = 1.0 - FIRST_DECAY**STEP
    second_fix = 1.0 - SECOND_DECAY**STEP
    first_new = FIRST_DECAY * unit_first + (1.0 - FIRST_DECAY) * unit_grad
    second_new = SECOND_DECAY * unit_second + (1.0 - SECOND_DECAY) * unit_grad * unit_grad
    params_new = unit_params - ADAM_RATE * (first_new / first_fix) / (
        jnp.sqrt(second_new / second_fix) + ADAM_EPSILON
    )
    return (
        hidden_one.reshape(rows, frames, width),
        hidden_two.reshape(rows, frames, width),
        input_grad,
        shallow_grad,
        shallow_next,
        shallow_new,
        shallow_new.astype(jnp.bfloat16),
        deep_grad,
        deep_next,
        deep_new,
        deep_new.astype(jnp.bfloat16),
        first_new,
        second_new,
        params_new,
    )


def solution(mesh):
    in_specs = (
        P(None, "tm", None),
        P(None, "tm"),
        P(),
        P(),
        P("tm"),
        P("tm"),
        P(),
        P(),
        P(),
        P(None, "tm", None),
    )
    out_specs = (
        P(None, "tm", None),
        P(None, "tm", None),
        P(None, "tm", None),
        P(),
        P(),
        P(),
        P(),
        P("tm"),
        P("tm"),
        P("tm"),
        P("tm"),
        P(),
        P(),
        P(),
    )
    return jax.shard_map(
        per_device, mesh=mesh, in_specs=in_specs, out_specs=out_specs, check_vma=False
    )
```

```python
import functools

import jax
import jax.numpy as jnp
from jax import lax
from jax.experimental import pallas as pl
from jax.experimental.pallas import tpu as pltpu
from jax.sharding import PartitionSpec as P

NS_STEPS = 2
STEP = 5


NORM_EPSILON = 1e-05
MUON_EPSILON = 1e-07
COEFF_A = 3.4445
COEFF_B = -4.775
COEFF_C = 2.0315
MUON_BETA = 0.5
MUON_RATE = 4.0
MUON_KEEP = 0.999
FIRST_DECAY = 0.9
SECOND_DECAY = 0.95
ADAM_RATE = 0.5
ADAM_EPSILON = 1e-08
DECAY_FLOOR = 0.9
LANE = 128
WIDE = 512
PART = 256
SIDE = 80


def kernel_call(body, grid, in_specs, out_specs, out_shape, scratch=(), flops=0, traffic=0):
    return pl.pallas_call(
        body,
        grid=grid,
        in_specs=in_specs,
        out_specs=out_specs,
        out_shape=out_shape,
        scratch_shapes=list(scratch),
        compiler_params=pltpu.CompilerParams(vmem_limit_bytes=56 * 1024 * 1024),
        cost_estimate=pl.CostEstimate(flops=flops, bytes_accessed=traffic, transcendentals=0),
    )


def shape_of(shape, dtype=jnp.float32):
    return jax.ShapeDtypeStruct(shape, dtype)


def whole(shape):
    return pl.BlockSpec(shape, lambda i: (0,) * len(shape))


def lanes_of(rows, width=WIDE):
    return pl.BlockSpec((rows, width), lambda i: (0, i))


def rate_of(params):
    return jnp.maximum(1.0 - jnp.exp(-params[0:1]), DECAY_FLOOR)


def softened(value):
    return jnp.maximum(value, 0.0) + jnp.log(1.0 + jnp.exp(-jnp.abs(value)))


def sigmoid(value):
    return 0.5 * jnp.tanh(0.5 * value) + 0.5


def wide_keep(keep_ref, t, rows):
    keep = keep_ref[pl.ds(pl.multiple_of(t * rows, rows), rows), :]
    return jnp.concatenate([keep] * (WIDE // LANE), axis=1)


def rows_at(ref, t, rows):
    return ref[pl.ds(pl.multiple_of(t * rows, rows), rows), :]


def store_at(ref, t, rows, value):
    ref[pl.ds(pl.multiple_of(t * rows, rows), rows), :] = value


def valid_lanes(shape, total, step):
    return lax.broadcasted_iota(jnp.int32, shape, 1) + step * WIDE < total


def unit_terms(params_ref, stat_ref, total_devices, frames):
    params = params_ref[...]
    stat = stat_ref[...]
    centre = stat[0:1]
    inverse = lax.rsqrt(stat[1:2] / (total_devices * frames) + NORM_EPSILON)
    return centre, inverse, params[2:3], params[3:4] + params[1:2]


def front_body(rows, frames, width, x_ref, w_ref, xt_ref, proj_ref, stat_ref, gram_ref, padded_w):
    step = pl.program_id(0)
    count, feats = x_ref.shape

    @pl.when(step == 0)
    def _():
        i = lax.broadcasted_iota(jnp.int32, (count, count), 0)
        j = lax.broadcasted_iota(jnp.int32, (count, count), 1)
        move = (j == lax.rem(i, rows) * frames + lax.div(i, rows)).astype(jnp.bfloat16)
        moved = jnp.dot(move, x_ref[...], preferred_element_type=jnp.float32).astype(jnp.bfloat16)
        i = lax.broadcasted_iota(jnp.int32, (feats, LANE), 0)
        j = lax.broadcasted_iota(jnp.int32, (feats, LANE), 1)
        wide = jnp.dot(moved, (i == j).astype(jnp.bfloat16), preferred_element_type=jnp.float32)
        lane = lax.broadcasted_iota(jnp.int32, (count, LANE), 1)
        xt = jnp.where(lane == feats, 1.0, wide).astype(jnp.bfloat16)
        xt_ref[...] = xt
        gram_ref[...] = dot_tn(xt, xt)[: gram_ref.shape[0]]
        padded_w[...] = jnp.zeros_like(padded_w)

    weight = w_ref[...]
    padded_w[0:feats, :] = jnp.where(valid_lanes(weight.shape, width, step), weight, 0.0)
    proj = jnp.dot(
        xt_ref[...], padded_w[...].astype(jnp.bfloat16), preferred_element_type=jnp.float32
    )
    proj_ref[...] = proj
    mean = jnp.sum(proj, axis=0, keepdims=True) * (1.0 / count)
    off = proj - mean
    stat_ref[0:1, :] = mean
    stat_ref[1:2, :] = jnp.sum(off * off, axis=0, keepdims=True)


def dot_tn(a, b):
    return lax.dot_general(a, b, (((0,), (0,)), ((), ())), preferred_element_type=jnp.float32)


def front(x, weight, rows, frames):
    count, feats = x.shape
    width = weight.shape[1]
    padded = -(-width // WIDE) * WIDE
    return kernel_call(
        functools.partial(front_body, rows, frames, width),
        (padded // WIDE,),
        [whole((count, feats)), lanes_of(feats)],
        [whole((count, LANE)), lanes_of(count), lanes_of(2), whole((SIDE, LANE))],
        [
            shape_of((count, LANE), jnp.bfloat16),
            shape_of((count, padded)),
            shape_of((2, padded)),
            shape_of((SIDE, LANE)),
        ],
        [pltpu.VMEM((LANE, WIDE), jnp.float32)],
        flops=2 * count * feats * padded,
        traffic=4 * count * padded,
    )(x, weight)


def delta_two_body(rows, frames, width, grad_ref, keep_ref, params_ref, delta_ref, end_ref, held):
    step = pl.program_id(0)
    pieces = WIDE // LANE
    mask = valid_lanes((rows * frames, WIDE), width, step)
    grad = jnp.where(mask, grad_ref[...].astype(jnp.float32), 0.0)
    for g in range(pieces):
        held[g] = grad[:, g * LANE : (g + 1) * LANE]
    rate = rate_of(params_ref[...])

    def body(k, carried):
        t = frames - 1 - k
        own = jnp.concatenate(
            [held[g, pl.ds(t, rows, stride=frames), :] for g in range(pieces)], axis=1
        )
        delta = own + carried
        store_at(delta_ref, t, rows, delta)
        return rate * wide_keep(keep_ref, t, rows) * delta

    end_ref[...] = lax.fori_loop(
        0, frames, body, jnp.zeros((rows, WIDE), jnp.float32), unroll=8
    )


def delta_two(out_grad, keep, params, rows, frames, padded):
    count, width = out_grad.shape
    return kernel_call(
        functools.partial(delta_two_body, rows, frames, width),
        (padded // WIDE,),
        [lanes_of(count), whole((count, LANE)), lanes_of(4)],
        [lanes_of(count), lanes_of(rows)],
        [shape_of((count, padded)), shape_of((rows, padded))],
        [pltpu.VMEM((WIDE // LANE, count, LANE), jnp.float32)],
        traffic=6 * count * padded,
    )(out_grad, keep, params)


def states_body(
    rows, frames, devices, proj_ref, keep_ref, params_ref, stat_ref, state_ref, end_ref
):
    centre, inverse, gain, offset = unit_terms(params_ref, stat_ref, devices, rows * frames)
    rate = rate_of(params_ref[...])
    share = 1.0 - rate

    def body(t, carried):
        gate = (rows_at(proj_ref, t, rows) - centre) * inverse * gain + offset
        soft = softened(gate)
        carried = rate * wide_keep(keep_ref, t, rows) * carried + share * soft
        store_at(state_ref, t, rows, carried)
        return carried

    end_ref[...] = lax.fori_loop(
        0, frames, body, jnp.zeros((rows, WIDE), jnp.float32), unroll=8
    )


def local_states(proj, keep, params, stat, rows, frames, devices):
    count, padded = proj.shape
    return kernel_call(
        functools.partial(states_body, rows, frames, devices),
        (padded // WIDE,),
        [lanes_of(count), whole((count, LANE)), lanes_of(4), lanes_of(2)],
        [lanes_of(count), lanes_of(rows)],
        [shape_of((count, padded)), shape_of((rows, padded))],
        traffic=8 * count * padded,
    )(proj, keep, params, stat)


def to_slots(value, group):
    pieces = value.shape[1] // LANE
    lane = lax.broadcasted_iota(jnp.int32, (value.shape[0], LANE), 1)
    parts = [value[:, g * LANE : (g + 1) * LANE] for g in range(pieces)]
    out = []
    for g in range(pieces):
        moved = (LANE - group) * g
        if moved == 0:
            new = parts[g]
        else:
            new = jnp.where(
                lane < moved, pltpu.roll(parts[g - 1], moved, 1), pltpu.roll(parts[g], moved, 1)
            )
        out.append(jnp.where(lane < group, new, 0.0))
    half = LANE // 2
    low = [
        jnp.where(lane < half, out[g], pltpu.roll(out[g + 1], half, 1)) for g in range(0, pieces, 2)
    ]
    high = [
        jnp.where(lane < half, pltpu.roll(out[g], half, 1), out[g + 1]) for g in range(0, pieces, 2)
    ]
    return jnp.concatenate(low + high, axis=1)


def from_slots(value, group, width):
    pieces = value.shape[1] // LANE
    lane = lax.broadcasted_iota(jnp.int32, (value.shape[0], LANE), 1)
    half = LANE // 2
    parts = []
    for g in range(pieces // 2):
        low = value[:, g * LANE : (g + 1) * LANE]
        high = value[:, (g + pieces // 2) * LANE : (g + pieces // 2 + 1) * LANE]
        parts.append(jnp.where(lane < half, low, pltpu.roll(high, half, 1)))
        parts.append(jnp.where(lane < half, pltpu.roll(low, half, 1), high))
    out = []
    for j in range(pieces):
        moved = (LANE - group) * j
        new = parts[j] if moved == 0 else pltpu.roll(parts[j], LANE - moved, 1)
        if j + 1 < pieces:
            new = jnp.where(lane < group - moved, new, pltpu.roll(parts[j + 1], group - moved, 1))
        left = width - j * LANE
        out.append(new if left >= LANE else jnp.where(lane < left, new, 0.0))
    return jnp.concatenate(out, axis=1)


def hidden_one_body(
    rows, frames, width, group, state_ref, start_ref, keep_ref, params_ref, hidden_ref, low_ref, mean_ref, held
):
    pieces = state_ref.shape[1] // LANE
    rate = rate_of(params_ref[...])

    def advance(t, carried):
        keep = rows_at(keep_ref, t, rows)
        carried = rate * jnp.concatenate([keep] * pieces, axis=1) * carried
        return carried, rows_at(state_ref, t, rows) + carried

    def body(k, both):
        carried, total = both
        t = 2 * k
        carried, first = advance(t, carried)
        carried, second = advance(t + 1, carried)
        pair = jnp.concatenate([first, second], axis=0)
        place = pl.ds(pl.multiple_of(t * rows, 2 * rows), 2 * rows)
        for g in range(pieces):
            held[g, place, :] = pair[:, g * LANE : (g + 1) * LANE]
        slots = to_slots(pair, group)
        low_ref[place, :] = slots.astype(jnp.bfloat16)
        return carried, total + slots[:rows] + slots[rows:]

    start = start_ref[...]
    _, total = lax.fori_loop(0, frames // 2, body, (start, jnp.zeros_like(start)))
    mean_ref[...] = jnp.sum(total, axis=0, keepdims=True) * (1.0 / (rows * frames))
    for r in range(rows):
        for g in range(pieces):
            left = min(LANE, width - g * LANE)
            part = held[g, pl.ds(r, frames, stride=rows), :]
            hidden_ref[r * frames : (r + 1) * frames, g * LANE : g * LANE + left] = part[:, :left]


def hidden_one_of(states, start, keep, params, rows, frames, width, group):
    count, padded = states.shape
    return kernel_call(
        functools.partial(hidden_one_body, rows, frames, width, group),
        (1,),
        [whole((count, padded)), whole((rows, padded)), whole((count, LANE)), whole((4, padded))],
        [whole((count, width)), whole((count, padded)), whole((1, padded))],
        [
            shape_of((count, width)),
            shape_of((count, padded), jnp.bfloat16),
            shape_of((1, padded)),
        ],
        [pltpu.VMEM((padded // LANE, count, LANE), jnp.float32)],
        traffic=10 * count * padded,
    )(states, start, keep, params)


def second_body(parts, half_ref, low_ref, *refs):
    weights, (proj_ref, stat_ref) = refs[: 2 * len(parts)], refs[2 * len(parts) :]
    step = pl.program_id(0)
    half = low_ref.shape[1] // 2
    side = half_ref[0]
    own = low_ref[:, pl.ds(pl.multiple_of(side * half, half), half)]
    other = low_ref[:, pl.ds(pl.multiple_of((1 - side) * half, half), half)]
    for p, (first, lanes) in enumerate(parts):

        @pl.when((step >= first // PART) & (step < (first + lanes) // PART))
        def _():
            proj = jnp.dot(own, weights[p][...], preferred_element_type=jnp.float32)
            proj += jnp.dot(other, weights[len(parts) + p][...], preferred_element_type=jnp.float32)
            proj_ref[...] = proj
            mean = jnp.sum(proj, axis=0, keepdims=True) * (1.0 / proj.shape[0])
            off = proj - mean
            stat_ref[0:1, :] = mean
            stat_ref[1:2, :] = jnp.sum(off * off, axis=0, keepdims=True)


def second_forward(side, low, own, other, parts):
    count, padded = low.shape

    def some(first, lanes):
        def place(i):
            return (0, jnp.clip(i - first // PART, 0, lanes // PART - 1))

        return pl.BlockSpec((padded // 2, PART), place)

    return kernel_call(
        functools.partial(second_body, parts),
        (padded // PART,),
        [pl.BlockSpec(memory_space=pltpu.SMEM), whole((count, padded))]
        + [some(first, lanes) for first, lanes in parts] * 2,
        [lanes_of(count, PART), lanes_of(2, PART)],
        [shape_of((count, padded)), shape_of((2, padded))],
        flops=2 * count * padded * padded,
        traffic=6 * count * padded + 2 * padded * padded,
    )(side, low, *own, *other)


def gate_two_body(
    rows, frames, devices, proj_ref, delta_ref, start_ref, keep_ref, params_ref, stat_ref,
    gate_ref, sums_ref, state_ref, end_ref,
):
    centre, inverse, gain, offset = unit_terms(params_ref, stat_ref, devices, rows * frames)
    rate = rate_of(params_ref[...])
    share = 1.0 - rate
    none = jnp.zeros((rows, WIDE), jnp.float32)

    def body(k, carried):
        carry, bias_sum, gain_sum, state = carried
        t = frames - 1 - k
        delta = rows_at(delta_ref, t, rows) + carry
        normed = (rows_at(proj_ref, t, rows) - centre) * inverse
        gate = share * delta * sigmoid(normed * gain + offset)
        store_at(gate_ref, t, rows, gate)
        carry = rate * wide_keep(keep_ref, t, rows) * carry
        value = (rows_at(proj_ref, k, rows) - centre) * inverse * gain + offset
        state = rate * wide_keep(keep_ref, k, rows) * state + share * softened(value)
        store_at(state_ref, k, rows, state)
        return carry, bias_sum + gate, gain_sum + gate * normed, state

    _, bias_sum, gain_sum, state = lax.fori_loop(
        0, frames, body, (start_ref[...], none, none, none), unroll=4
    )
    sums_ref[0:1, :] = jnp.sum(bias_sum, axis=0, keepdims=True)
    sums_ref[1:2, :] = jnp.sum(gain_sum, axis=0, keepdims=True)
    end_ref[...] = state


def gate_two(proj, delta, start, keep, params, stat, rows, frames, devices):
    count, padded = proj.shape
    return kernel_call(
        functools.partial(gate_two_body, rows, frames, devices),
        (padded // WIDE,),
        [lanes_of(count), lanes_of(count), lanes_of(rows), whole((count, LANE)), lanes_of(4), lanes_of(2)],
        [lanes_of(count), lanes_of(2), lanes_of(count), lanes_of(rows)],
        [
            shape_of((count, padded)),
            shape_of((2, padded)),
            shape_of((count, padded)),
            shape_of((rows, padded)),
        ],
        traffic=16 * count * padded,
    )(proj, delta, start, keep, params, stat)


def deep_term_body(
    rows, frames, devices, core_ref, gate_ref, proj_ref, params_ref, stat_ref, sums_ref, low_ref,
    mean_ref, grad_ref, keep_ref, send_ref, total_ref, centred,
):
    total = devices * rows * frames
    centre, inverse, gain, _ = unit_terms(params_ref, stat_ref, devices, rows * frames)
    sums = sums_ref[...] * (1.0 / total)
    normed = (proj_ref[...] - centre) * inverse
    grad = (gain * inverse * (gate_ref[...] - sums[0:1] - normed * sums[1:2])).astype(jnp.bfloat16)
    grad_ref[...] = grad
    total_ref[...] = jnp.sum(grad.astype(jnp.float32), axis=0, keepdims=True)

    @pl.when(pl.program_id(0) == 0)
    def _():
        centred[...] = (low_ref[...].astype(jnp.float32) - mean_ref[...]).astype(jnp.bfloat16)

    half = keep_ref.shape[0]
    side = core_ref[0]
    keep_ref[...] = dot_tn(centred[:, pl.ds(pl.multiple_of(side * half, half), half)], grad)
    send_ref[...] = dot_tn(
        centred[:, pl.ds(pl.multiple_of((1 - side) * half, half), half)], grad
    ).astype(send_ref.dtype)


def deep_term(first, lanes, core, gate, proj, params, stat, sums, low, mean, rows, frames, devices):
    count, padded = proj.shape
    chunk = PART
    half = padded // 2

    def some(height):
        return pl.BlockSpec((height, chunk), lambda i: (0, first // chunk + i))

    return kernel_call(
        functools.partial(deep_term_body, rows, frames, devices),
        (lanes // chunk,),
        [
            pl.BlockSpec(memory_space=pltpu.SMEM),
            some(count),
            some(count),
            some(4),
            some(2),
            some(2),
            whole((count, padded)),
            whole((1, padded)),
        ],
        [lanes_of(count, chunk), lanes_of(half, chunk), lanes_of(half, chunk), lanes_of(1, chunk)],
        [
            shape_of((count, lanes), jnp.bfloat16),
            shape_of((half, lanes)),
            shape_of((half, lanes), jnp.bfloat16),
            shape_of((1, lanes)),
        ],
        [pltpu.VMEM((count, padded), jnp.bfloat16)],
        flops=2 * count * padded * lanes,
        traffic=10 * count * lanes + 3 * padded * lanes,
    )(core, gate, proj, params, stat, sums, low, mean)


def back_body(parts, *refs):
    grads, weights = refs[: len(parts)], refs[len(parts) : 3 * len(parts)]
    for side, back_ref in enumerate(refs[3 * len(parts) :]):
        total = 0.0
        for p in range(len(parts)):
            total += dot_nt(grads[p][...], weights[side * len(parts) + p][...])
        back_ref[...] = total


def back_one(grads, own, other, parts):
    count, half = grads[0].shape[0], own[0].shape[0]
    padded = 2 * half
    return kernel_call(
        functools.partial(back_body, parts),
        (half // PART,),
        [whole(grad.shape) for grad in grads]
        + [pl.BlockSpec((PART, lanes), lambda i: (i, 0)) for _, lanes in parts] * 2,
        [lanes_of(count, PART)] * 2,
        [shape_of((count, half))] * 2,
        flops=2 * count * padded * padded,
        traffic=6 * count * padded + 2 * padded * padded,
    )(*grads, *own, *other)


def delta_one_body(
    rows, frames, width, group, side_ref, own_ref, other_ref, keep_ref, params_ref, delta_ref, end_ref
):
    padded = delta_ref.shape[1]
    rate = rate_of(params_ref[...])
    straight = side_ref[0] == 0

    def body(k, carried):
        t = frames - 1 - k
        own, other = rows_at(own_ref, t, rows), rows_at(other_ref, t, rows)
        both = jnp.concatenate(
            [jnp.where(straight, own, other), jnp.where(straight, other, own)], axis=1
        )
        delta = from_slots(both, group, width) + carried
        store_at(delta_ref, t, rows, delta)
        keep = rows_at(keep_ref, t, rows)
        return rate * jnp.concatenate([keep] * (padded // LANE), axis=1) * delta

    end_ref[...] = lax.fori_loop(0, frames, body, jnp.zeros((rows, padded), jnp.float32), unroll=2)


def delta_one(side, own, other, keep, params, rows, frames, width, group):
    count, half = own.shape
    padded = 2 * half
    return kernel_call(
        functools.partial(delta_one_body, rows, frames, width, group),
        (1,),
        [
            pl.BlockSpec(memory_space=pltpu.SMEM),
            whole((count, half)),
            whole((count, half)),
            whole((count, LANE)),
            whole((4, padded)),
        ],
        [whole((count, padded)), whole((rows, padded))],
        [shape_of((count, padded)), shape_of((rows, padded))],
        traffic=8 * count * padded,
    )(side, own, other, keep, params)


def gate_one_body(
    rows,
    frames,
    devices,
    feats,
    proj_ref,
    state_ref,
    first_ref,
    delta_ref,
    start_ref,
    keep_ref,
    params_ref,
    stat_ref,
    x_ref,
    gate_ref,
    sums_ref,
    held,
):
    centre, inverse, gain, offset = unit_terms(params_ref, stat_ref, devices, rows * frames)
    rate = rate_of(params_ref[...])
    share = 1.0 - rate
    none = jnp.zeros((rows, WIDE), jnp.float32)

    def backward(k, carry):
        t = frames - 1 - k
        store_at(held, t, rows, rows_at(delta_ref, t, rows) + carry)
        return rate * wide_keep(keep_ref, t, rows) * carry

    lax.fori_loop(0, frames, backward, start_ref[...], unroll=8)

    def forward(t, carried):
        carry, before, bias_sum, gain_sum, decay_sum = carried
        keep = wide_keep(keep_ref, t, rows)
        delta = rows_at(held, t, rows)
        normed = (rows_at(proj_ref, t, rows) - centre) * inverse
        value = normed * gain + offset
        soft = softened(value)
        gate = share * delta * sigmoid(value)
        store_at(gate_ref, t, rows, gate)
        decay_sum = decay_sum + delta * (keep * before - soft)
        carry = rate * keep * carry
        before = rows_at(state_ref, t, rows) + carry
        return carry, before, bias_sum + gate, gain_sum + gate * normed, decay_sum

    first = first_ref[...]
    _, _, bias_sum, gain_sum, decay_sum = lax.fori_loop(
        0, frames, forward, (first, first, none, none, none), unroll=4
    )
    bias = jnp.sum(bias_sum, axis=0, keepdims=True)
    mean = bias * (1.0 / (rows * frames))
    x = x_ref[...]
    ones = jnp.ones((rows * frames, LANE), jnp.bfloat16)
    total = jnp.concatenate([dot_tn(x, ones)] * (WIDE // LANE), axis=1)
    term = dot_tn(x, (gate_ref[...] - mean).astype(jnp.bfloat16)) + total * mean
    sums_ref[...] = term[: sums_ref.shape[0]]
    sums_ref[feats : feats + 1, :] = bias
    sums_ref[feats + 1 : feats + 2, :] = jnp.sum(gain_sum, axis=0, keepdims=True)
    sums_ref[feats + 2 : feats + 3, :] = jnp.sum(decay_sum, axis=0, keepdims=True)


def gate_one(proj, states, first, delta, start, keep, params, stat, x, rows, frames, devices, feats):
    count, padded = proj.shape
    return kernel_call(
        functools.partial(gate_one_body, rows, frames, devices, feats),
        (padded // WIDE,),
        [
            lanes_of(count),
            lanes_of(count),
            lanes_of(rows),
            lanes_of(count),
            lanes_of(rows),
            whole((count, LANE)),
            lanes_of(4),
            lanes_of(2),
            whole((count, LANE)),
        ],
        [lanes_of(count), lanes_of(SIDE)],
        [shape_of((count, padded)), shape_of((SIDE, padded))],
        [pltpu.VMEM((count, WIDE), jnp.float32)],
        traffic=16 * count * padded,
    )(proj, states, first, delta, start, keep, params, stat, x)


def hidden_two_body(
    rows,
    frames,
    width,
    devices,
    proj_ref,
    state_ref,
    first_ref,
    delta_ref,
    start_ref,
    keep_ref,
    params_ref,
    stat_ref,
    hidden_ref,
    sums_ref,
    held,
    moved,
):
    pieces = WIDE // LANE
    centre, inverse, gain, offset = unit_terms(params_ref, stat_ref, devices, rows * frames)
    rate = rate_of(params_ref[...])

    def backward(k, carry):
        t = frames - 1 - k
        store_at(held, t, rows, rows_at(delta_ref, t, rows) + carry)
        return rate * wide_keep(keep_ref, t, rows) * carry

    lax.fori_loop(0, frames, backward, start_ref[...], unroll=8)

    def forward(t, carried):
        carry, before, decay_sum = carried
        keep = wide_keep(keep_ref, t, rows)
        delta = rows_at(held, t, rows)
        value = (rows_at(proj_ref, t, rows) - centre) * inverse * gain + offset
        soft = softened(value)
        decay_sum = decay_sum + delta * (keep * before - soft)
        carry = rate * keep * carry
        before = rows_at(state_ref, t, rows) + carry
        for g in range(pieces):
            moved[g, pl.ds(pl.multiple_of(t * rows, rows), rows), :] = before[
                :, g * LANE : (g + 1) * LANE
            ]
        return carry, before, decay_sum

    first = first_ref[...]
    none = jnp.zeros((rows, WIDE), jnp.float32)
    _, _, decay_sum = lax.fori_loop(0, frames, forward, (first, first, none), unroll=4)
    sums_ref[...] = jnp.sum(decay_sum, axis=0, keepdims=True)
    for r in range(rows):
        for g in range(pieces):
            hidden_ref[r * frames : (r + 1) * frames, g * LANE : (g + 1) * LANE] = moved[
                g, pl.ds(r, frames, stride=rows), :
            ]


def hidden_two_of(proj, states, first, delta, start, keep, params, stat, rows, frames, width, devices):
    count, padded = proj.shape
    return kernel_call(
        functools.partial(hidden_two_body, rows, frames, width, devices),
        (padded // WIDE,),
        [
            lanes_of(count),
            lanes_of(count),
            lanes_of(rows),
            lanes_of(count),
            lanes_of(rows),
            whole((count, LANE)),
            lanes_of(4),
            lanes_of(2),
        ],
        [lanes_of(count), lanes_of(1)],
        [shape_of((count, width)), shape_of((1, padded))],
        [pltpu.VMEM((count, WIDE), jnp.float32), pltpu.VMEM((WIDE // LANE, count, LANE), jnp.float32)],
        traffic=16 * count * padded,
    )(proj, states, first, delta, start, keep, params, stat)


def input_grad_body(
    rows, frames, devices, width, feats, gate_ref, proj_ref, params_ref, stat_ref, sums_ref, w_ref, back_ref
):
    step = pl.program_id(0)
    total = devices * rows * frames
    centre, inverse, gain, _ = unit_terms(params_ref, stat_ref, devices, rows * frames)
    bias = sums_ref[feats : feats + 1, :] * (1.0 / total)
    slope = sums_ref[feats + 1 : feats + 2, :] * (1.0 / total)
    normed = (proj_ref[...] - centre) * inverse
    grad = (gain * inverse * (gate_ref[...] - bias - normed * slope)).astype(jnp.bfloat16)
    weight = w_ref[...]
    weight = jnp.where(valid_lanes(weight.shape, width, step), weight, 0.0).astype(jnp.bfloat16)
    part = dot_nt(grad, weight)

    @pl.when(step == 0)
    def _():
        back_ref[...] = part

    @pl.when(step > 0)
    def _():
        back_ref[...] += part


def input_grad_of(gate, proj, params, stat, sums, weight, rows, frames, devices):
    count, padded = proj.shape
    feats, width = weight.shape
    return kernel_call(
        functools.partial(input_grad_body, rows, frames, devices, width, feats),
        (padded // WIDE,),
        [lanes_of(count), lanes_of(count), lanes_of(4), lanes_of(2), lanes_of(SIDE), lanes_of(feats)],
        whole((count, feats)),
        shape_of((count, feats)),
        flops=2 * count * feats * padded,
        traffic=8 * count * padded,
    )(gate, proj, params, stat, sums, weight)


def dot_nt(a, b):
    return lax.dot_general(a, b, (((1,), (1,)), ((), ())), preferred_element_type=jnp.float32)


def shallow_body(
    total, frames, sums_ref, gram_ref, params_ref, stat_ref, w_ref, m_ref,
    grad_ref, next_ref, new_ref, low_ref, held,
):
    feats, width = w_ref.shape
    centre, inverse, gain, _ = unit_terms(params_ref, stat_ref, total // frames, frames)
    weight = w_ref[...]
    held[...] = jnp.zeros_like(held)
    held[0:feats, 0:width] = weight
    gram = gram_ref[...]
    lane = lax.broadcasted_iota(jnp.int32, gram.shape, 1)
    x_sum = jnp.sum(jnp.where(lane == feats, gram, 0.0), axis=1, keepdims=True)
    raw = jnp.dot(
        gram[:, :SIDE],
        held[...].astype(jnp.bfloat16).astype(jnp.float32),
        precision=lax.Precision.HIGHEST,
        preferred_element_type=jnp.float32,
    )
    normed = (raw - x_sum * centre) * inverse
    bias = sums_ref[feats : feats + 1, :] * (1.0 / total)
    slope = sums_ref[feats + 1 : feats + 2, :] * (1.0 / total)
    grad = gain * inverse * (sums_ref[...] - x_sum * bias - normed * slope)
    grad = grad[:feats, :width]
    grad_ref[...] = grad
    following = MUON_BETA * m_ref[...] + grad
    next_ref[...] = following
    held[0:feats, 0:width] = following
    m = held[...]
    current = (m / (jnp.sqrt(jnp.sum(m * m)) + MUON_EPSILON)).astype(jnp.bfloat16)
    for repeat in range(NS_STEPS):
        gram = dot_nt(current, current).astype(jnp.bfloat16)
        square = jnp.dot(gram, gram, preferred_element_type=jnp.float32)
        mixing = (COEFF_B * gram.astype(jnp.float32) + COEFF_C * square).astype(jnp.bfloat16)
        current = (
            COEFF_A * current.astype(jnp.float32)
            + jnp.dot(mixing, current, preferred_element_type=jnp.float32)
        ).astype(jnp.bfloat16)
    new = MUON_KEEP * weight - MUON_RATE * current[:feats, :width].astype(jnp.float32)
    new_ref[...] = new
    low_ref[...] = new.astype(jnp.bfloat16)


def shallow_step(sums, gram, params, stat, weight, momentum, total, frames):
    padded = sums.shape[1]
    some = shape_of(weight.shape)
    return kernel_call(
        functools.partial(shallow_body, total, frames),
        (1,),
        [whole(value.shape) for value in (sums, gram, params, stat, weight, momentum)],
        [whole(weight.shape)] * 4,
        [some, some, some, shape_of(weight.shape, jnp.bfloat16)],
        [pltpu.VMEM((SIDE, padded), jnp.float32)],
        flops=14 * SIDE * SIDE * padded,
        traffic=24 * SIDE * padded,
    )(sums, gram, params, stat, weight, momentum)


def newton_body(parts, heads, tile, *refs):
    blocks_refs, out_ref = refs[: 2 * len(parts)], refs[2 * len(parts)]
    m_ref, gram, mixing, sems = refs[2 * len(parts) + 1 :]
    size = m_ref.shape[0]
    half = size // 2
    blocks = size // tile
    copies = []
    for side in range(2):
        for p, (first, lanes) in enumerate(parts):
            copies.append(
                pltpu.make_async_copy(
                    blocks_refs[side * len(parts) + p],
                    m_ref.at[side * half : (side + 1) * half, first : first + lanes],
                    sems.at[side * len(parts) + p],
                )
            )
    for copy in copies:
        copy.start()
    for copy in copies:
        copy.wait()

    def place(k):
        return slice(k * tile, (k + 1) * tile)

    squares = jnp.zeros((8, size), jnp.float32)
    for k in range(blocks):
        value = m_ref[place(k), :].astype(jnp.float32)
        squares = squares + jnp.sum((value * value).reshape(tile // 8, 8, size), axis=0)
    scale = 1.0 / (jnp.sqrt(jnp.sum(squares)) + MUON_EPSILON)
    square_scale = scale * scale

    def gram_block(i, j):
        part = dot_nt(m_ref[place(i), :], m_ref[place(j), :]) * square_scale
        gram[place(i), place(j)] = part.astype(jnp.bfloat16)
        if i != j:
            gram[place(j), place(i)] = part.T.astype(jnp.bfloat16)

    for i in range(blocks):
        for j in range(i, blocks):
            gram_block(i, j)
    for i in range(blocks):
        for j in range(i, blocks):
            part = dot_nt(gram[place(i), :], gram[place(j), :])
            part = COEFF_B * gram[place(i), place(j)].astype(jnp.float32) + COEFF_C * part
            mixing[place(i), place(j)] = part.astype(jnp.bfloat16)
            if i != j:
                mixing[place(j), place(i)] = part.T.astype(jnp.bfloat16)

    def taken(ref):
        return jnp.concatenate([ref[first : first + count, :] for first, count in heads], axis=0)

    def times(value, ref):
        return jnp.dot(value.astype(jnp.bfloat16), ref[...], preferred_element_type=jnp.float32)

    def stepped(value):
        return COEFF_A * value + times(value, mixing)

    mixing_own = taken(mixing)
    gram_own = taken(gram).astype(jnp.float32)
    gram_own = stepped(COEFF_A * gram_own + times(mixing_own, gram))
    square_own = stepped(times(stepped(gram_own), gram))
    second_own = COEFF_B * gram_own + COEFF_C * square_own
    weights = COEFF_A * mixing_own.astype(jnp.float32) + stepped(second_own)
    result = COEFF_A * COEFF_A * taken(m_ref).astype(jnp.float32) + times(weights, m_ref)
    out_ref[...] = (scale * result).astype(jnp.bfloat16)


def newton_rows(own, other, parts, heads):
    size = 2 * own[0].shape[0]
    window = sum(count for _, count in heads)
    anywhere = pl.BlockSpec(memory_space=pl.ANY)
    return kernel_call(
        functools.partial(newton_body, parts, heads, 256),
        (1,),
        [anywhere] * (2 * len(parts)),
        whole((window, size)),
        shape_of((window, size), jnp.bfloat16),
        [pltpu.VMEM((size, size), jnp.bfloat16)] * 3 + [pltpu.SemaphoreType.DMA((2 * len(parts),))],
        flops=3 * size * size * size,
        traffic=2 * size * size,
    )(*own, *other)


def swap(value, bit):
    size = lax.axis_size("tm")
    return lax.ppermute(value, "tm", [(i, i ^ bit) for i in range(size)])


def steps_of(size):
    bits = []
    bit = 1
    while bit < size:
        bits.append(bit)
        bit *= 2
    return bits


def sum_all(value):
    for bit in steps_of(lax.axis_size("tm")):
        value = value + swap(value, bit)
    return value


def bit_of(bit):
    return jnp.where((lax.axis_index("tm") & bit) != 0, 1, 0)


class SumSpread:
    def __init__(self, value):
        self.value = value
        self.steps = []
        lanes = value.shape[1]
        cuts = []
        for bit in steps_of(lax.axis_size("tm")):
            if lanes // 2 % LANE == 0:
                lanes //= 2
                self.steps.append((self.halve, bit))
                cuts.append(bit)
            else:
                self.steps.append((self.pair, bit))
        self.steps += [(self.join, bit) for bit in reversed(cuts)]

    def halve(self, bit):
        lanes = self.value.shape[1] // 2
        mine = lax.dynamic_slice_in_dim(self.value, bit_of(bit) * lanes, lanes, 1)
        away = lax.dynamic_slice_in_dim(self.value, (1 - bit_of(bit)) * lanes, lanes, 1)
        self.value = mine + swap(away, bit)

    def pair(self, bit):
        self.value = self.value + swap(self.value, bit)

    def join(self, bit):
        other = swap(self.value, bit)
        upper = bit_of(bit) == 1
        self.value = jnp.concatenate(
            [jnp.where(upper, other, self.value), jnp.where(upper, self.value, other)], axis=1
        )

    def step(self, times=1):
        for _ in range(times):
            if self.steps:
                action, bit = self.steps.pop(0)
                action(bit)


def tie(first, second):
    return lax.optimization_barrier((list(first), list(second)))


def side_bit():
    return lax.axis_size("tm") // 32


def orders_of(size):
    bits = [bit for bit in steps_of(size) if bit != side_bit()]
    return [bits[k * len(bits) // 3 :] + bits[: k * len(bits) // 3] for k in range(3)]


class Scatter:
    def __init__(self, keeps, sends, slots):
        size = lax.axis_size("tm")
        bits = [bit for bit in reversed(steps_of(size)) if bit != side_bit()]
        shape = (2,) * len(bits) + (slots, -1)
        self.orders = orders_of(size)
        self.left = [list(bits) for _ in keeps]
        self.current = [keep.reshape(shape[:-1] + keep.shape[1:]) for keep in keeps]
        self.received = [
            swap(send.reshape(shape[:-1] + send.shape[1:]), side_bit()) for send in sends
        ]

    def step(self):
        for p, left in enumerate(self.left):
            bit = self.orders[p].pop(0)
            axis = left.index(bit)
            left.remove(bit)
            total = self.current[p] + self.received[p].astype(jnp.float32)
            self.current[p] = lax.dynamic_index_in_dim(total, bit_of(bit), axis, False)
            away = lax.dynamic_index_in_dim(total, 1 - bit_of(bit), axis, False)
            self.received[p] = swap(away.astype(jnp.bfloat16), bit)

    def result(self):
        return [a + b.astype(jnp.float32) for a, b in zip(self.current, self.received)]


class Gather:
    def __init__(self, blocks, near):
        self.orders = orders_of(lax.axis_size("tm"))
        self.held = [[] for _ in blocks]
        self.current = list(blocks)
        self.near = near

    def step(self):
        for p, held in enumerate(self.held):
            bit = self.orders[p].pop()
            axis = sum(other > bit for other in held)
            held.append(bit)
            mine, other = self.current[p], swap(self.current[p], bit)
            if not self.near:
                upper = bit_of(bit) == 1
                mine, other = jnp.where(upper, other, mine), jnp.where(upper, mine, other)
            self.current[p] = jnp.stack([mine, other], axis=axis)

    def result(self):
        own = [value.reshape(-1, value.shape[-1]) for value in self.current]
        return own, [swap(value, side_bit()) for value in own]


class Stats:
    def __init__(self, stat, count):
        self.stat = stat
        self.count = float(count)
        self.bits = steps_of(lax.axis_size("tm"))

    def step(self, times=1):
        for _ in range(min(times, len(self.bits))):
            stat = self.stat
            other = swap(stat, self.bits.pop(0))
            gap = stat[0:1] - other[0:1]
            mean = 0.5 * (stat[0:1] + other[0:1])
            square = (stat[1:2] + other[1:2]) + gap * gap * (0.5 * self.count)
            self.stat = jnp.concatenate([mean, square, 0.5 * (stat[2:] + other[2:])], axis=0)
            self.count *= 2


class Exchange:
    def __init__(self, flags, carries, rows, tall=None):
        self.bits = steps_of(lax.axis_size("tm"))
        self.flags = flags[:, None]
        self.totals = [ends for ends, _, _ in carries]
        self.powers = [power for _, power, _ in carries]
        self.reverse = [reverse for _, _, reverse in carries]
        self.before = [jnp.zeros_like(ends) for ends in self.totals]
        self.before_keep = [jnp.ones_like(ends) for ends in self.totals]
        self.sums = rows
        self.tall = tall

    def step(self, times=1):
        for _ in range(min(times, len(self.bits))):
            self.one()

    def one(self):
        bit = self.bits.pop(0)
        high, width = self.totals[0].shape
        sent = [
            jnp.concatenate([total, jnp.broadcast_to(self.flags, (high, LANE))], axis=1)
            for total in self.totals
        ]
        if self.sums is not None:
            sent.append(jnp.pad(self.sums, ((0, 0), (0, LANE))))
        sent = jnp.concatenate(sent, axis=0)
        if self.tall is not None:
            blocks = [self.tall[k : k + len(sent)] for k in range(0, len(self.tall), len(sent))]
            sent = jnp.concatenate([sent] + blocks, axis=1)
        other = swap(sent, bit)
        other_flags = other[:high, width : width + 1]
        upper = bit_of(bit) == 1
        for k, total in enumerate(self.totals):
            other_total = other[k * high : (k + 1) * high, :width]
            power = self.powers[k]
            following = jnp.logical_not(upper) if self.reverse[k] else upper
            keep_other = other_flags * power
            self.before[k] = jnp.where(
                following, self.before_keep[k] * other_total + self.before[k], self.before[k]
            )
            self.before_keep[k] = jnp.where(
                following, self.before_keep[k] * keep_other, self.before_keep[k]
            )
            self.totals[k] = jnp.where(
                following,
                self.flags * power * other_total + total,
                keep_other * total + other_total,
            )
            self.powers[k] = power * power
        self.flags = self.flags * other_flags
        if self.sums is not None:
            self.sums = self.sums + other[len(self.totals) * high :, :width]
        if self.tall is not None:
            first = width + LANE
            blocks = [
                other[:, first + LANE * k : first + LANE * (k + 1)]
                for k in range(len(self.tall) // len(sent))
            ]
            self.tall = self.tall + jnp.concatenate(blocks, axis=0)


def pad_lanes(value, padded):
    gap = padded - value.shape[-1]
    return jnp.pad(value, [(0, 0)] * (value.ndim - 1) + [(0, gap)])


def flat_places(shard, width, padded):
    size = lax.axis_size("tm")
    members = size * LANE // padded
    slots = LANE // members
    return members, slots, slots * width - shard


def to_block(flat, width, padded):
    size, mine = lax.axis_size("tm"), lax.axis_index("tm")
    members, slots, excess = flat_places(flat.shape[0], width, padded)
    lacking = excess * (members - 1)
    pairs = [(i + 1, i) for i in range(size - 1) if (i + 1) % members]
    extra = lax.ppermute(flat[:lacking], "tm", pairs)
    tail = jnp.zeros((excess,), flat.dtype)
    held = jnp.concatenate([flat, extra, tail])
    return lax.dynamic_slice_in_dim(held, excess * (mine % members), slots * width).reshape(
        slots, width
    )


def from_block(block, shard, padded):
    width = block.shape[1]
    size, mine = lax.axis_size("tm"), lax.axis_index("tm")
    members, slots, excess = flat_places(shard, width, padded)
    lacking = excess * (members - 1)
    pairs = [(i, i + 1) for i in range(size - 1) if (i + 1) % members]
    flat = block.reshape(-1)
    extra = lax.ppermute(flat[slots * width - lacking :], "tm", pairs)
    held = jnp.concatenate([extra, flat])
    return lax.dynamic_slice_in_dim(held, lacking - excess * (mine % members), shard)


def own_heads(shard, width, padded):
    members, slots, _ = flat_places(shard, width, padded)
    half = padded // 2
    group = LANE // 2
    if members == 2:
        lacking = slots - shard // width
        kept = -(-(lacking) // 16) * 16
        return [(0, group), (half + group - kept, kept)]
    return [(0, group), (half, group)]


def own_flat(found, shard, width, padded):
    mine = lax.axis_index("tm")
    members, slots, excess = flat_places(shard, width, padded)
    member = mine % members
    if members == 2:
        own, other = found[:slots].reshape(-1), found[slots:].reshape(-1)
        low = own[:shard]
        high = jnp.concatenate([other[other.shape[0] - excess :], own[: shard - excess]])
        return jnp.where(member == 0, low, high)
    near = found.reshape(members, slots * width)
    placed = jnp.take(near, jnp.arange(members) ^ member, axis=0).reshape(-1)
    return lax.dynamic_slice_in_dim(placed, shard * member, shard)


def per_device(
    inputs,
    clip_start,
    shallow_weight,
    shallow_momentum,
    deep_weight,
    deep_momentum,
    unit_params,
    unit_first,
    unit_second,
    out_grad,
):
    devices = lax.axis_size("tm")
    rows, frames, feats = inputs.shape
    width = shallow_weight.shape[1]
    padded = -(-width // WIDE) * WIDE
    group = width // (padded // LANE)
    count = rows * frames
    keep_mask = (1 - clip_start).astype(jnp.float32)
    flags = jnp.min(keep_mask, axis=1)
    keep = jnp.broadcast_to(keep_mask.T.reshape(count, 1), (count, LANE))
    params = pad_lanes(unit_params, padded)
    rates = jnp.maximum(1.0 - jnp.exp(-params[:, 0:1]), DECAY_FLOOR)
    powers = rates
    for _ in range(frames.bit_length() - 1):
        powers = powers * powers

    deep_block = pad_lanes(to_block(deep_weight.astype(jnp.bfloat16), width, padded), padded)
    momentum_block = pad_lanes(to_block(deep_momentum, width, padded), padded)

    shares = [3 * padded // 8, 3 * padded // 8, padded // 4]
    parts = [(sum(shares[:p]), shares[p]) for p in range(3)]
    side = bit_of(side_bit()).astype(jnp.int32).reshape(1)
    gather = Gather([deep_block[:, first : first + lanes] for first, lanes in parts], False)
    gather.step()
    x, proj_one, stat_one, gram = front(
        inputs.reshape(count, feats), shallow_weight, rows, frames
    )
    stats = Stats(stat_one, count)
    gather.current, (stats.stat,) = tie(gather.current, [stats.stat])
    gather.step()
    stats.step(2)
    gather.current, (stats.stat,) = tie(gather.current, [stats.stat])
    gather.step()
    stats.step(len(stats.bits))
    stat_one = stats.stat
    gather.current, (stat_one,) = tie(gather.current, [stat_one])
    while gather.orders[0]:
        gather.step()
    state_local, state_end = local_states(
        proj_one, keep, params[0], stat_one, rows, frames, devices
    )
    delta_local, delta_end = delta_two(
        out_grad.reshape(count, width), keep, params[1], rows, frames, padded
    )
    gather.current, (state_end, delta_end) = tie(gather.current, [state_end, delta_end])
    deep_own, deep_other = gather.result()
    carries = Exchange(
        flags, [(state_end, powers[0], False), (delta_end, powers[1], True)], None, gram
    )
    carries.step(len(carries.bits))
    state_in, delta_in = carries.before
    gram = carries.tall
    hidden_one, low_one, mean_one = hidden_one_of(
        state_local, state_in, keep, params[0], rows, frames, width, group
    )
    proj_two, stat_two = second_forward(side, low_one, deep_own, deep_other, parts)
    stats = Stats(jnp.concatenate([stat_two, mean_one], axis=0), count)
    stats.step(len(stats.bits))
    stat_two, mean_one = stats.stat[:2], stats.stat[2:]
    gate, sums_two, second_local, second_end = gate_two(
        proj_two, delta_local, delta_in, keep, params[1], stat_two, rows, frames, devices
    )
    carries = Exchange(flags, [(second_end, powers[1], False)], sums_two)
    carries.step(len(carries.bits))
    second_in, sums_two = carries.before[0], carries.sums
    grads, keeps, sends, totals = zip(
        *[
            deep_term(
                first, lanes, side, gate, proj_two, params[1], stat_two, sums_two, low_one,
                mean_one, rows, frames, devices,
            )
            for first, lanes in parts
        ]
    )
    slots = padded // devices
    stages = len(steps_of(devices))
    scatter = Scatter(keeps, sends, slots)
    back = back_one(grads, deep_own, deep_other, parts)
    scatter.received, back = tie(scatter.received, back)
    scatter.step()
    back_local, back_end = delta_one(
        side, *back, keep, params[0], rows, frames, width, group
    )
    hidden_two, decay_two = hidden_two_of(
        proj_two, second_local, second_in, delta_local, delta_in, keep, params[1], stat_two,
        rows, frames, width, devices,
    )
    scatter.received, (back_end, decay_two) = tie(scatter.received, [back_end, decay_two])
    carries = Exchange(flags, [(back_end, powers[0], True)], jnp.concatenate(totals, axis=1))
    while len(scatter.orders[0]) > 1:
        scatter.step()
        carries.step(2)
        scatter.received, carries.totals = tie(scatter.received, carries.totals)
    scatter.step()
    carries.step(len(carries.bits))
    back_in, total_two = carries.before[0], carries.sums
    gate_low, sums_one = gate_one(
        proj_one, state_local, state_in, back_local, back_in, keep, params[0], stat_one, x,
        rows, frames, devices, feats,
    )
    sums_one = sums_one + jnp.pad(decay_two, ((feats + 3, SIDE - feats - 4), (0, 0)))
    scatter.received, (sums_one,) = tie(scatter.received, [sums_one])
    mine = lax.axis_index("tm")
    place = mine // (2 * side_bit()) * side_bit() + mine % side_bit()
    place = (side[0] * (devices // 2) + place) * slots
    mean_own = lax.dynamic_slice_in_dim(mean_one[0], place, slots)[:, None]
    grad_parts = [
        part + mean_own * total_two[:, first : first + lanes]
        for (first, lanes), part in zip(parts, scatter.result())
    ]
    gather = Gather(
        [
            (MUON_BETA * momentum_block[:, first : first + lanes] + part).astype(jnp.bfloat16)
            for (first, lanes), part in zip(parts, grad_parts)
        ],
        True,
    )
    spread = SumSpread(sums_one)
    while gather.orders[0]:
        gather.step()
        spread.step(2)
        gather.current, (spread.value,) = tie(gather.current, [spread.value])
    own, other = gather.result()
    spread.step(len(spread.steps))
    sums_one = spread.value
    shallow_grad, shallow_next, shallow_new, shallow_low = shallow_step(
        sums_one, gram, params[0], stat_one, shallow_weight, shallow_momentum,
        count * devices, count,
    )
    input_back = input_grad_of(
        gate_low, proj_one, params[0], stat_one, sums_one, shallow_weight, rows, frames, devices
    )
    input_grad = jnp.swapaxes(input_back.reshape(frames, rows, feats), 0, 1)
    grad_block = jnp.concatenate(grad_parts, axis=1)

    shard = deep_weight.shape[0]
    heads = own_heads(shard, width, padded)
    ortho = newton_rows(own, other, parts, heads)
    deep_ortho = own_flat(ortho[:, :width], shard, width, padded)
    deep_new = MUON_KEEP * deep_weight - MUON_RATE * deep_ortho.astype(jnp.float32)
    deep_grad = from_block(grad_block[:, :width], shard, padded)
    deep_next = MUON_BETA * deep_momentum + deep_grad

    unit_sums = sums_one[feats : feats + 4, :width]
    bias_gain_two = sums_two[:, :width]
    slope = jnp.where(
        1.0 - jnp.exp(-unit_params[:, 0]) > DECAY_FLOOR, jnp.exp(-unit_params[:, 0]), 0.0
    )
    unit_grad = jnp.stack(
        [
            jnp.stack([unit_sums[2] * slope[0], unit_sums[0], unit_sums[1], unit_sums[0]]),
            jnp.stack(
                [unit_sums[3] * slope[1], bias_gain_two[0], bias_gain_two[1], bias_gain_two[0]]
            ),
        ]
    )
    first_fix = 1.0 - FIRST_DECAY**STEP
    second_fix = 1.0 - SECOND_DECAY**STEP
    first_new = FIRST_DECAY * unit_first + (1.0 - FIRST_DECAY) * unit_grad
    second_new = SECOND_DECAY * unit_second + (1.0 - SECOND_DECAY) * unit_grad * unit_grad
    params_new = unit_params - ADAM_RATE * (first_new / first_fix) / (
        jnp.sqrt(second_new / second_fix) + ADAM_EPSILON
    )
    return (
        hidden_one.reshape(rows, frames, width),
        hidden_two.reshape(rows, frames, width),
        input_grad,
        shallow_grad,
        shallow_next,
        shallow_new,
        shallow_low,
        deep_grad,
        deep_next,
        deep_new,
        deep_new.astype(jnp.bfloat16),
        first_new,
        second_new,
        params_new,
    )


def solution(mesh):
    in_specs = (
        P(None, "tm", None),
        P(None, "tm"),
        P(),
        P(),
        P("tm"),
        P("tm"),
        P(),
        P(),
        P(),
        P(None, "tm", None),
    )
    out_specs = (
        P(None, "tm", None),
        P(None, "tm", None),
        P(None, "tm", None),
        P(),
        P(),
        P(),
        P(),
        P("tm"),
        P("tm"),
        P("tm"),
        P("tm"),
        P(),
        P(),
        P(),
    )
    return jax.shard_map(
        per_device, mesh=mesh, in_specs=in_specs, out_specs=out_specs, check_vma=False
    )
```

```python
import functools

import jax
import jax.numpy as jnp
from jax import lax
from jax.experimental import pallas as pl
from jax.experimental.pallas import tpu as pltpu
from jax.sharding import PartitionSpec as P

NS_STEPS = 2
STEP = 5


NORM_EPSILON = 1e-05
MUON_EPSILON = 1e-07
COEFF_A = 3.4445
COEFF_B = -4.775
COEFF_C = 2.0315
MUON_BETA = 0.5
MUON_RATE = 4.0
MUON_KEEP = 0.999
FIRST_DECAY = 0.9
SECOND_DECAY = 0.95
ADAM_RATE = 0.5
ADAM_EPSILON = 1e-08
DECAY_FLOOR = 0.9
LANE = 128
WIDE = 512
PART = 256
SIDE = 80


def kernel_call(body, grid, in_specs, out_specs, out_shape, scratch=(), flops=0, traffic=0):
    return pl.pallas_call(
        body,
        grid=grid,
        in_specs=in_specs,
        out_specs=out_specs,
        out_shape=out_shape,
        scratch_shapes=list(scratch),
        compiler_params=pltpu.CompilerParams(vmem_limit_bytes=56 * 1024 * 1024),
        cost_estimate=pl.CostEstimate(flops=flops, bytes_accessed=traffic, transcendentals=0),
    )


def shape_of(shape, dtype=jnp.float32):
    return jax.ShapeDtypeStruct(shape, dtype)


def whole(shape):
    return pl.BlockSpec(shape, lambda i: (0,) * len(shape))


def lanes_of(rows, width=WIDE):
    return pl.BlockSpec((rows, width), lambda i: (0, i))


def chunk_call(body, place, in_specs, out_specs, out_shape, arrays, previous, scratch=(), traffic=0):
    count = len(in_specs)
    before = list(previous) if previous is not None else []

    def run(*refs):
        body(*refs[:count], *refs[count + len(before) :])

    return pl.pallas_call(
        run,
        grid=(1,),
        in_specs=list(in_specs) + [pl.BlockSpec(memory_space=pl.ANY)] * len(before),
        out_specs=out_specs,
        out_shape=out_shape,
        scratch_shapes=list(scratch),
        input_output_aliases={count + k: k for k in range(len(before))},
        compiler_params=pltpu.CompilerParams(vmem_limit_bytes=56 * 1024 * 1024),
        cost_estimate=pl.CostEstimate(flops=0, bytes_accessed=traffic, transcendentals=0),
    )(*arrays, *before)


def chunk_at(rows, place):
    return pl.BlockSpec((rows, WIDE), lambda i: (0, place))


def rate_of(params):
    return jnp.maximum(1.0 - jnp.exp(-params[0:1]), DECAY_FLOOR)


def softened(value):
    return jnp.maximum(value, 0.0) + jnp.log(1.0 + jnp.exp(-jnp.abs(value)))


def sigmoid(value):
    return 0.5 * jnp.tanh(0.5 * value) + 0.5


def wide_keep(keep_ref, t, rows):
    keep = keep_ref[pl.ds(pl.multiple_of(t * rows, rows), rows), :]
    return jnp.concatenate([keep] * (WIDE // LANE), axis=1)


def rows_at(ref, t, rows):
    return ref[pl.ds(pl.multiple_of(t * rows, rows), rows), :]


def store_at(ref, t, rows, value):
    ref[pl.ds(pl.multiple_of(t * rows, rows), rows), :] = value


def valid_lanes(shape, total, step):
    return lax.broadcasted_iota(jnp.int32, shape, 1) + step * WIDE < total


def unit_terms(params_ref, stat_ref, total_devices, frames):
    params = params_ref[...]
    stat = stat_ref[...]
    centre = stat[0:1]
    inverse = lax.rsqrt(stat[1:2] / (total_devices * frames) + NORM_EPSILON)
    return centre, inverse, params[2:3], params[3:4] + params[1:2]


def front_body(rows, frames, width, x_ref, w_ref, xt_ref, proj_ref, stat_ref, gram_ref, padded_w):
    step = pl.program_id(0)
    count, feats = x_ref.shape

    @pl.when(step == 0)
    def _():
        i = lax.broadcasted_iota(jnp.int32, (count, count), 0)
        j = lax.broadcasted_iota(jnp.int32, (count, count), 1)
        move = (j == lax.rem(i, rows) * frames + lax.div(i, rows)).astype(jnp.bfloat16)
        moved = jnp.dot(move, x_ref[...], preferred_element_type=jnp.float32).astype(jnp.bfloat16)
        i = lax.broadcasted_iota(jnp.int32, (feats, LANE), 0)
        j = lax.broadcasted_iota(jnp.int32, (feats, LANE), 1)
        wide = jnp.dot(moved, (i == j).astype(jnp.bfloat16), preferred_element_type=jnp.float32)
        lane = lax.broadcasted_iota(jnp.int32, (count, LANE), 1)
        xt = jnp.where(lane == feats, 1.0, wide).astype(jnp.bfloat16)
        xt_ref[...] = xt
        gram_ref[...] = dot_tn(xt, xt)[: gram_ref.shape[0]]
        padded_w[...] = jnp.zeros_like(padded_w)

    weight = w_ref[...]
    padded_w[0:feats, :] = jnp.where(valid_lanes(weight.shape, width, step), weight, 0.0)
    proj = jnp.dot(
        xt_ref[...], padded_w[...].astype(jnp.bfloat16), preferred_element_type=jnp.float32
    )
    proj_ref[...] = proj
    mean = jnp.sum(proj, axis=0, keepdims=True) * (1.0 / count)
    off = proj - mean
    stat_ref[0:1, :] = mean
    stat_ref[1:2, :] = jnp.sum(off * off, axis=0, keepdims=True)


def dot_tn(a, b):
    return lax.dot_general(a, b, (((0,), (0,)), ((), ())), preferred_element_type=jnp.float32)


def front(x, weight, rows, frames):
    count, feats = x.shape
    width = weight.shape[1]
    padded = -(-width // WIDE) * WIDE
    return kernel_call(
        functools.partial(front_body, rows, frames, width),
        (padded // WIDE,),
        [whole((count, feats)), lanes_of(feats)],
        [whole((count, LANE)), lanes_of(count), lanes_of(2), whole((SIDE, LANE))],
        [
            shape_of((count, LANE), jnp.bfloat16),
            shape_of((count, padded)),
            shape_of((2, padded)),
            shape_of((SIDE, LANE)),
        ],
        [pltpu.VMEM((LANE, WIDE), jnp.float32)],
        flops=2 * count * feats * padded,
        traffic=4 * count * padded,
    )(x, weight)


def delta_two_body(rows, frames, width, place, grad_ref, keep_ref, params_ref, delta_ref, end_ref, held):
    pieces = WIDE // LANE
    mask = valid_lanes((rows * frames, WIDE), width, place)
    grad = jnp.where(mask, grad_ref[...].astype(jnp.float32), 0.0)
    for g in range(pieces):
        held[g] = grad[:, g * LANE : (g + 1) * LANE]
    rate = rate_of(params_ref[...])

    def body(k, carried):
        t = frames - 1 - k
        own = jnp.concatenate(
            [held[g, pl.ds(t, rows, stride=frames), :] for g in range(pieces)], axis=1
        )
        delta = own + carried
        store_at(delta_ref, t, rows, delta)
        return rate * wide_keep(keep_ref, t, rows) * delta

    end_ref[...] = lax.fori_loop(
        0, frames, body, jnp.zeros((rows, WIDE), jnp.float32), unroll=8
    )


def delta_two(place, previous, out_grad, keep, params, rows, frames, padded):
    count, width = out_grad.shape
    return chunk_call(
        functools.partial(delta_two_body, rows, frames, width, place),
        place,
        [chunk_at(count, place), whole((count, LANE)), chunk_at(4, place)],
        [chunk_at(count, place), chunk_at(rows, place)],
        [shape_of((count, padded)), shape_of((rows, padded))],
        (out_grad, keep, params),
        previous,
        [pltpu.VMEM((WIDE // LANE, count, LANE), jnp.float32)],
        traffic=6 * count * WIDE,
    )


def states_body(
    rows, frames, devices, proj_ref, keep_ref, params_ref, stat_ref, state_ref, end_ref
):
    centre, inverse, gain, offset = unit_terms(params_ref, stat_ref, devices, rows * frames)
    rate = rate_of(params_ref[...])
    share = 1.0 - rate

    def body(t, carried):
        gate = (rows_at(proj_ref, t, rows) - centre) * inverse * gain + offset
        soft = softened(gate)
        carried = rate * wide_keep(keep_ref, t, rows) * carried + share * soft
        store_at(state_ref, t, rows, carried)
        return carried

    end_ref[...] = lax.fori_loop(
        0, frames, body, jnp.zeros((rows, WIDE), jnp.float32), unroll=8
    )


def local_states(proj, keep, params, stat, rows, frames, devices):
    count, padded = proj.shape
    return kernel_call(
        functools.partial(states_body, rows, frames, devices),
        (padded // WIDE,),
        [lanes_of(count), whole((count, LANE)), lanes_of(4), lanes_of(2)],
        [lanes_of(count), lanes_of(rows)],
        [shape_of((count, padded)), shape_of((rows, padded))],
        traffic=8 * count * padded,
    )(proj, keep, params, stat)


def to_slots(value, group):
    pieces = value.shape[1] // LANE
    lane = lax.broadcasted_iota(jnp.int32, (value.shape[0], LANE), 1)
    parts = [value[:, g * LANE : (g + 1) * LANE] for g in range(pieces)]
    out = []
    for g in range(pieces):
        moved = (LANE - group) * g
        if moved == 0:
            new = parts[g]
        else:
            new = jnp.where(
                lane < moved, pltpu.roll(parts[g - 1], moved, 1), pltpu.roll(parts[g], moved, 1)
            )
        out.append(jnp.where(lane < group, new, 0.0))
    half = LANE // 2
    low = [
        jnp.where(lane < half, out[g], pltpu.roll(out[g + 1], half, 1)) for g in range(0, pieces, 2)
    ]
    high = [
        jnp.where(lane < half, pltpu.roll(out[g], half, 1), out[g + 1]) for g in range(0, pieces, 2)
    ]
    return jnp.concatenate(low + high, axis=1)


def from_slots(value, group, width):
    pieces = value.shape[1] // LANE
    lane = lax.broadcasted_iota(jnp.int32, (value.shape[0], LANE), 1)
    half = LANE // 2
    parts = []
    for g in range(pieces // 2):
        low = value[:, g * LANE : (g + 1) * LANE]
        high = value[:, (g + pieces // 2) * LANE : (g + pieces // 2 + 1) * LANE]
        parts.append(jnp.where(lane < half, low, pltpu.roll(high, half, 1)))
        parts.append(jnp.where(lane < half, pltpu.roll(low, half, 1), high))
    out = []
    for j in range(pieces):
        moved = (LANE - group) * j
        new = parts[j] if moved == 0 else pltpu.roll(parts[j], LANE - moved, 1)
        if j + 1 < pieces:
            new = jnp.where(lane < group - moved, new, pltpu.roll(parts[j + 1], group - moved, 1))
        left = width - j * LANE
        out.append(new if left >= LANE else jnp.where(lane < left, new, 0.0))
    return jnp.concatenate(out, axis=1)


def low_one_body(rows, frames, width, group, state_ref, start_ref, keep_ref, params_ref, low_ref, mean_ref):
    pieces = state_ref.shape[1] // LANE
    rate = rate_of(params_ref[...])

    def advance(t, carried):
        keep = rows_at(keep_ref, t, rows)
        carried = rate * jnp.concatenate([keep] * pieces, axis=1) * carried
        return carried, rows_at(state_ref, t, rows) + carried

    def body(k, both):
        carried, total = both
        t = 2 * k
        carried, first = advance(t, carried)
        carried, second = advance(t + 1, carried)
        place = pl.ds(pl.multiple_of(t * rows, 2 * rows), 2 * rows)
        slots = to_slots(jnp.concatenate([first, second], axis=0), group)
        low_ref[place, :] = slots.astype(jnp.bfloat16)
        return carried, total + slots[:rows] + slots[rows:]

    start = start_ref[...]
    _, total = lax.fori_loop(0, frames // 2, body, (start, jnp.zeros_like(start)), unroll=2)
    mean_ref[...] = jnp.sum(total, axis=0, keepdims=True) * (1.0 / (rows * frames))


def low_one_of(states, start, keep, params, rows, frames, width, group):
    count, padded = states.shape
    return kernel_call(
        functools.partial(low_one_body, rows, frames, width, group),
        (1,),
        [whole((count, padded)), whole((rows, padded)), whole((count, LANE)), whole((4, padded))],
        [whole((count, padded)), whole((1, padded))],
        [shape_of((count, padded), jnp.bfloat16), shape_of((1, padded))],
        traffic=6 * count * padded,
    )(states, start, keep, params)


def hidden_body(rows, frames, state_ref, start_ref, keep_ref, params_ref, hidden_ref, held):
    pieces = WIDE // LANE
    rate = rate_of(params_ref[...])

    def body(t, carry):
        carry = rate * wide_keep(keep_ref, t, rows) * carry
        state = rows_at(state_ref, t, rows) + carry
        for g in range(pieces):
            held[g, pl.ds(pl.multiple_of(t * rows, rows), rows), :] = state[
                :, g * LANE : (g + 1) * LANE
            ]
        return carry

    lax.fori_loop(0, frames, body, start_ref[...], unroll=8)
    for r in range(rows):
        for g in range(pieces):
            hidden_ref[r * frames : (r + 1) * frames, g * LANE : (g + 1) * LANE] = held[
                g, pl.ds(r, frames, stride=rows), :
            ]


def hidden_of(place, previous, states, start, keep, params, rows, frames, width):
    count, _ = states.shape
    return chunk_call(
        functools.partial(hidden_body, rows, frames),
        place,
        [chunk_at(count, place), chunk_at(rows, place), whole((count, LANE)), chunk_at(4, place)],
        [chunk_at(count, place)],
        [shape_of((count, width))],
        (states, start, keep, params),
        previous,
        [pltpu.VMEM((WIDE // LANE, count, LANE), jnp.float32)],
        traffic=8 * count * WIDE,
    )


def second_body(parts, half_ref, low_ref, *refs):
    weights, (proj_ref, stat_ref) = refs[: 2 * len(parts)], refs[2 * len(parts) :]
    step = pl.program_id(0)
    half = low_ref.shape[1] // 2
    side = half_ref[0]
    own = low_ref[:, pl.ds(pl.multiple_of(side * half, half), half)]
    other = low_ref[:, pl.ds(pl.multiple_of((1 - side) * half, half), half)]
    for p, (first, lanes) in enumerate(parts):

        @pl.when((step >= first // PART) & (step < (first + lanes) // PART))
        def _():
            proj = jnp.dot(own, weights[p][...], preferred_element_type=jnp.float32)
            proj += jnp.dot(other, weights[len(parts) + p][...], preferred_element_type=jnp.float32)
            proj_ref[...] = proj
            mean = jnp.sum(proj, axis=0, keepdims=True) * (1.0 / proj.shape[0])
            off = proj - mean
            stat_ref[0:1, :] = mean
            stat_ref[1:2, :] = jnp.sum(off * off, axis=0, keepdims=True)


def second_forward(side, low, own, other, parts):
    count, padded = low.shape

    def some(first, lanes):
        def place(i):
            return (0, jnp.clip(i - first // PART, 0, lanes // PART - 1))

        return pl.BlockSpec((padded // 2, PART), place)

    return kernel_call(
        functools.partial(second_body, parts),
        (padded // PART,),
        [pl.BlockSpec(memory_space=pltpu.SMEM), whole((count, padded))]
        + [some(first, lanes) for first, lanes in parts] * 2,
        [lanes_of(count, PART), lanes_of(2, PART)],
        [shape_of((count, padded)), shape_of((2, padded))],
        flops=2 * count * padded * padded,
        traffic=6 * count * padded + 2 * padded * padded,
    )(side, low, *own, *other)


def gate_two_body(
    rows, frames, devices, proj_ref, delta_ref, start_ref, keep_ref, params_ref, stat_ref, gate_ref, sums_ref
):
    centre, inverse, gain, offset = unit_terms(params_ref, stat_ref, devices, rows * frames)
    rate = rate_of(params_ref[...])
    share = 1.0 - rate
    none = jnp.zeros((rows, WIDE), jnp.float32)

    def body(k, carried):
        carry, bias_sum, gain_sum = carried
        t = frames - 1 - k
        delta = rows_at(delta_ref, t, rows) + carry
        normed = (rows_at(proj_ref, t, rows) - centre) * inverse
        gate = share * delta * sigmoid(normed * gain + offset)
        store_at(gate_ref, t, rows, gate)
        carry = rate * wide_keep(keep_ref, t, rows) * carry
        return carry, bias_sum + gate, gain_sum + gate * normed

    _, bias_sum, gain_sum = lax.fori_loop(
        0, frames, body, (start_ref[...], none, none), unroll=8
    )
    sums_ref[0:1, :] = jnp.sum(bias_sum, axis=0, keepdims=True)
    sums_ref[1:2, :] = jnp.sum(gain_sum, axis=0, keepdims=True)


def gate_two(proj, delta, start, keep, params, stat, rows, frames, devices):
    count, padded = proj.shape
    return kernel_call(
        functools.partial(gate_two_body, rows, frames, devices),
        (padded // WIDE,),
        [lanes_of(count), lanes_of(count), lanes_of(rows), whole((count, LANE)), lanes_of(4), lanes_of(2)],
        [lanes_of(count), lanes_of(2)],
        [shape_of((count, padded)), shape_of((2, padded))],
        traffic=12 * count * padded,
    )(proj, delta, start, keep, params, stat)


def states_two_body(
    rows, frames, devices, proj_ref, delta_ref, start_ref, keep_ref, params_ref, stat_ref,
    state_ref, end_ref, decay_ref, held,
):
    centre, inverse, gain, offset = unit_terms(params_ref, stat_ref, devices, rows * frames)
    rate = rate_of(params_ref[...])
    share = 1.0 - rate
    none = jnp.zeros((rows, WIDE), jnp.float32)

    def backward(k, carry):
        t = frames - 1 - k
        store_at(held, t, rows, rows_at(delta_ref, t, rows) + carry)
        return rate * wide_keep(keep_ref, t, rows) * carry

    lax.fori_loop(0, frames, backward, start_ref[...], unroll=8)

    def forward(t, carried):
        state, reach, decay, factor = carried
        keep = wide_keep(keep_ref, t, rows)
        delta = rows_at(held, t, rows)
        value = (rows_at(proj_ref, t, rows) - centre) * inverse * gain + offset
        soft = softened(value)
        decay = decay + delta * (keep * state - soft)
        factor = factor + delta * keep * reach
        state = rate * keep * state + share * soft
        reach = rate * keep * reach
        store_at(state_ref, t, rows, state)
        return state, reach, decay, factor

    state, _, decay, factor = lax.fori_loop(
        0, frames, forward, (none, jnp.ones_like(none), none, none), unroll=4
    )
    end_ref[...] = state
    decay_ref[0:rows, :] = decay
    decay_ref[rows : 2 * rows, :] = factor


def states_two(place, previous, proj, delta, start, keep, params, stat, rows, frames, devices):
    count, padded = proj.shape
    return chunk_call(
        functools.partial(states_two_body, rows, frames, devices),
        place,
        [
            chunk_at(count, place),
            chunk_at(count, place),
            chunk_at(rows, place),
            whole((count, LANE)),
            chunk_at(4, place),
            chunk_at(2, place),
        ],
        [chunk_at(count, place), chunk_at(rows, place), chunk_at(2 * rows, place)],
        [shape_of((count, padded)), shape_of((rows, padded)), shape_of((2 * rows, padded))],
        (proj, delta, start, keep, params, stat),
        previous,
        [pltpu.VMEM((count, WIDE), jnp.float32)],
        traffic=12 * count * WIDE,
    )


def turn_body(low_ref, mean_ref, turned_ref):
    turned_ref[...] = (low_ref[...].astype(jnp.float32) - mean_ref[...]).T.astype(jnp.bfloat16)


def turn(place, previous, low, mean):
    count, padded = low.shape
    return chunk_call(
        turn_body,
        place,
        [chunk_at(count, place), chunk_at(1, place)],
        [pl.BlockSpec((WIDE, count), lambda i: (place, 0))],
        [shape_of((padded, count), jnp.bfloat16)],
        (low, mean),
        previous,
        traffic=4 * count * WIDE,
    )


def deep_term_body(
    rows, frames, devices, core_ref, gate_ref, proj_ref, params_ref, stat_ref, sums_ref, turned_ref,
    grad_ref, keep_ref, send_ref, total_ref,
):
    total = devices * rows * frames
    centre, inverse, gain, _ = unit_terms(params_ref, stat_ref, devices, rows * frames)
    sums = sums_ref[...] * (1.0 / total)
    normed = (proj_ref[...] - centre) * inverse
    grad = (gain * inverse * (gate_ref[...] - sums[0:1] - normed * sums[1:2])).astype(jnp.bfloat16)
    grad_ref[...] = grad
    total_ref[...] = jnp.sum(grad.astype(jnp.float32), axis=0, keepdims=True)

    half = keep_ref.shape[0]
    side = core_ref[0]
    keep_ref[...] = jnp.dot(
        turned_ref[pl.ds(pl.multiple_of(side * half, half), half), :],
        grad,
        preferred_element_type=jnp.float32,
    )
    send_ref[...] = jnp.dot(
        turned_ref[pl.ds(pl.multiple_of((1 - side) * half, half), half), :],
        grad,
        preferred_element_type=jnp.float32,
    ).astype(send_ref.dtype)


def deep_term(first, lanes, core, gate, proj, params, stat, sums, turned, rows, frames, devices):
    count, padded = proj.shape
    chunk = PART
    half = padded // 2

    def some(height):
        return pl.BlockSpec((height, chunk), lambda i: (0, first // chunk + i))

    return kernel_call(
        functools.partial(deep_term_body, rows, frames, devices),
        (lanes // chunk,),
        [
            pl.BlockSpec(memory_space=pltpu.SMEM),
            some(count),
            some(count),
            some(4),
            some(2),
            some(2),
            whole((padded, count)),
        ],
        [lanes_of(count, chunk), lanes_of(half, chunk), lanes_of(half, chunk), lanes_of(1, chunk)],
        [
            shape_of((count, lanes), jnp.bfloat16),
            shape_of((half, lanes)),
            shape_of((half, lanes), jnp.bfloat16),
            shape_of((1, lanes)),
        ],
        flops=2 * count * padded * lanes,
        traffic=10 * count * lanes + 3 * padded * lanes,
    )(core, gate, proj, params, stat, sums, turned)


def back_body(parts, *refs):
    grads, weights = refs[: len(parts)], refs[len(parts) : 3 * len(parts)]
    for side, back_ref in enumerate(refs[3 * len(parts) :]):
        total = 0.0
        for p in range(len(parts)):
            total += dot_nt(grads[p][...], weights[side * len(parts) + p][...])
        back_ref[...] = total


def back_one(grads, own, other, parts):
    count, half = grads[0].shape[0], own[0].shape[0]
    padded = 2 * half
    return kernel_call(
        functools.partial(back_body, parts),
        (half // PART,),
        [whole(grad.shape) for grad in grads]
        + [pl.BlockSpec((PART, lanes), lambda i: (i, 0)) for _, lanes in parts] * 2,
        [lanes_of(count, PART)] * 2,
        [shape_of((count, half))] * 2,
        flops=2 * count * padded * padded,
        traffic=6 * count * padded + 2 * padded * padded,
    )(*grads, *own, *other)


def delta_one_body(
    rows, frames, width, group, side_ref, own_ref, other_ref, keep_ref, params_ref, delta_ref, end_ref
):
    padded = delta_ref.shape[1]
    rate = rate_of(params_ref[...])
    straight = side_ref[0] == 0

    def body(k, carried):
        t = frames - 1 - k
        own, other = rows_at(own_ref, t, rows), rows_at(other_ref, t, rows)
        both = jnp.concatenate(
            [jnp.where(straight, own, other), jnp.where(straight, other, own)], axis=1
        )
        delta = from_slots(both, group, width) + carried
        store_at(delta_ref, t, rows, delta)
        keep = rows_at(keep_ref, t, rows)
        return rate * jnp.concatenate([keep] * (padded // LANE), axis=1) * delta

    end_ref[...] = lax.fori_loop(0, frames, body, jnp.zeros((rows, padded), jnp.float32), unroll=2)


def delta_one(side, own, other, keep, params, rows, frames, width, group):
    count, half = own.shape
    padded = 2 * half
    return kernel_call(
        functools.partial(delta_one_body, rows, frames, width, group),
        (1,),
        [
            pl.BlockSpec(memory_space=pltpu.SMEM),
            whole((count, half)),
            whole((count, half)),
            whole((count, LANE)),
            whole((4, padded)),
        ],
        [whole((count, padded)), whole((rows, padded))],
        [shape_of((count, padded)), shape_of((rows, padded))],
        traffic=8 * count * padded,
    )(side, own, other, keep, params)


def gate_one_body(
    rows,
    frames,
    devices,
    feats,
    proj_ref,
    state_ref,
    first_ref,
    delta_ref,
    start_ref,
    keep_ref,
    params_ref,
    stat_ref,
    x_ref,
    gate_ref,
    sums_ref,
    held,
):
    centre, inverse, gain, offset = unit_terms(params_ref, stat_ref, devices, rows * frames)
    rate = rate_of(params_ref[...])
    share = 1.0 - rate
    none = jnp.zeros((rows, WIDE), jnp.float32)

    def backward(k, carry):
        t = frames - 1 - k
        store_at(held, t, rows, rows_at(delta_ref, t, rows) + carry)
        return rate * wide_keep(keep_ref, t, rows) * carry

    lax.fori_loop(0, frames, backward, start_ref[...], unroll=8)

    def forward(t, carried):
        carry, before, bias_sum, gain_sum, decay_sum = carried
        keep = wide_keep(keep_ref, t, rows)
        delta = rows_at(held, t, rows)
        normed = (rows_at(proj_ref, t, rows) - centre) * inverse
        value = normed * gain + offset
        soft = softened(value)
        gate = share * delta * sigmoid(value)
        store_at(gate_ref, t, rows, gate)
        decay_sum = decay_sum + delta * (keep * before - soft)
        carry = rate * keep * carry
        before = rows_at(state_ref, t, rows) + carry
        return carry, before, bias_sum + gate, gain_sum + gate * normed, decay_sum

    first = first_ref[...]
    _, _, bias_sum, gain_sum, decay_sum = lax.fori_loop(
        0, frames, forward, (first, first, none, none, none), unroll=4
    )
    bias = jnp.sum(bias_sum, axis=0, keepdims=True)
    mean = bias * (1.0 / (rows * frames))
    x = x_ref[...]
    ones = jnp.ones((rows * frames, LANE), jnp.bfloat16)
    total = jnp.concatenate([dot_tn(x, ones)] * (WIDE // LANE), axis=1)
    term = dot_tn(x, (gate_ref[...] - mean).astype(jnp.bfloat16)) + total * mean
    sums_ref[...] = term[: sums_ref.shape[0]]
    sums_ref[feats : feats + 1, :] = bias
    sums_ref[feats + 1 : feats + 2, :] = jnp.sum(gain_sum, axis=0, keepdims=True)
    sums_ref[feats + 2 : feats + 3, :] = jnp.sum(decay_sum, axis=0, keepdims=True)


def gate_one(proj, states, first, delta, start, keep, params, stat, x, rows, frames, devices, feats):
    count, padded = proj.shape
    return kernel_call(
        functools.partial(gate_one_body, rows, frames, devices, feats),
        (padded // WIDE,),
        [
            lanes_of(count),
            lanes_of(count),
            lanes_of(rows),
            lanes_of(count),
            lanes_of(rows),
            whole((count, LANE)),
            lanes_of(4),
            lanes_of(2),
            whole((count, LANE)),
        ],
        [lanes_of(count), lanes_of(SIDE)],
        [shape_of((count, padded)), shape_of((SIDE, padded))],
        [pltpu.VMEM((count, WIDE), jnp.float32)],
        traffic=16 * count * padded,
    )(proj, states, first, delta, start, keep, params, stat, x)


def input_grad_body(
    rows, frames, devices, width, feats, gate_ref, proj_ref, params_ref, stat_ref, sums_ref, w_ref, back_ref
):
    step = pl.program_id(0)
    total = devices * rows * frames
    centre, inverse, gain, _ = unit_terms(params_ref, stat_ref, devices, rows * frames)
    bias = sums_ref[feats : feats + 1, :] * (1.0 / total)
    slope = sums_ref[feats + 1 : feats + 2, :] * (1.0 / total)
    normed = (proj_ref[...] - centre) * inverse
    grad = (gain * inverse * (gate_ref[...] - bias - normed * slope)).astype(jnp.bfloat16)
    weight = w_ref[...]
    weight = jnp.where(valid_lanes(weight.shape, width, step), weight, 0.0).astype(jnp.bfloat16)
    part = dot_nt(grad, weight)

    @pl.when(step == 0)
    def _():
        back_ref[...] = part

    @pl.when(step > 0)
    def _():
        back_ref[...] += part


def input_grad_of(gate, proj, params, stat, sums, weight, rows, frames, devices):
    count, padded = proj.shape
    feats, width = weight.shape
    return kernel_call(
        functools.partial(input_grad_body, rows, frames, devices, width, feats),
        (padded // WIDE,),
        [lanes_of(count), lanes_of(count), lanes_of(4), lanes_of(2), lanes_of(SIDE), lanes_of(feats)],
        whole((count, feats)),
        shape_of((count, feats)),
        flops=2 * count * feats * padded,
        traffic=8 * count * padded,
    )(gate, proj, params, stat, sums, weight)


def dot_nt(a, b):
    return lax.dot_general(a, b, (((1,), (1,)), ((), ())), preferred_element_type=jnp.float32)


def shallow_body(
    total, frames, sums_ref, gram_ref, params_ref, stat_ref, w_ref, m_ref,
    grad_ref, next_ref, new_ref, low_ref, held,
):
    feats, width = w_ref.shape
    centre, inverse, gain, _ = unit_terms(params_ref, stat_ref, total // frames, frames)
    weight = w_ref[...]
    held[...] = jnp.zeros_like(held)
    held[0:feats, 0:width] = weight
    gram = gram_ref[...]
    lane = lax.broadcasted_iota(jnp.int32, gram.shape, 1)
    x_sum = jnp.sum(jnp.where(lane == feats, gram, 0.0), axis=1, keepdims=True)
    raw = jnp.dot(
        gram[:, :SIDE],
        held[...].astype(jnp.bfloat16).astype(jnp.float32),
        precision=lax.Precision.HIGHEST,
        preferred_element_type=jnp.float32,
    )
    normed = (raw - x_sum * centre) * inverse
    bias = sums_ref[feats : feats + 1, :] * (1.0 / total)
    slope = sums_ref[feats + 1 : feats + 2, :] * (1.0 / total)
    grad = gain * inverse * (sums_ref[...] - x_sum * bias - normed * slope)
    grad = grad[:feats, :width]
    grad_ref[...] = grad
    following = MUON_BETA * m_ref[...] + grad
    next_ref[...] = following
    held[0:feats, 0:width] = following
    m = held[...]
    current = (m / (jnp.sqrt(jnp.sum(m * m)) + MUON_EPSILON)).astype(jnp.bfloat16)
    for repeat in range(NS_STEPS):
        gram = dot_nt(current, current).astype(jnp.bfloat16)
        square = jnp.dot(gram, gram, preferred_element_type=jnp.float32)
        mixing = (COEFF_B * gram.astype(jnp.float32) + COEFF_C * square).astype(jnp.bfloat16)
        current = (
            COEFF_A * current.astype(jnp.float32)
            + jnp.dot(mixing, current, preferred_element_type=jnp.float32)
        ).astype(jnp.bfloat16)
    new = MUON_KEEP * weight - MUON_RATE * current[:feats, :width].astype(jnp.float32)
    new_ref[...] = new
    low_ref[...] = new.astype(jnp.bfloat16)


def shallow_step(sums, gram, params, stat, weight, momentum, total, frames):
    padded = sums.shape[1]
    some = shape_of(weight.shape)
    return kernel_call(
        functools.partial(shallow_body, total, frames),
        (1,),
        [whole(value.shape) for value in (sums, gram, params, stat, weight, momentum)],
        [whole(weight.shape)] * 4,
        [some, some, some, shape_of(weight.shape, jnp.bfloat16)],
        [pltpu.VMEM((SIDE, padded), jnp.float32)],
        flops=14 * SIDE * SIDE * padded,
        traffic=24 * SIDE * padded,
    )(sums, gram, params, stat, weight, momentum)


def newton_body(parts, heads, tile, *refs):
    blocks_refs, out_ref = refs[: 2 * len(parts)], refs[2 * len(parts)]
    m_ref, gram, mixing, sems = refs[2 * len(parts) + 1 :]
    size = m_ref.shape[0]
    half = size // 2
    blocks = size // tile
    copies = []
    for side in range(2):
        for p, (first, lanes) in enumerate(parts):
            copies.append(
                pltpu.make_async_copy(
                    blocks_refs[side * len(parts) + p],
                    m_ref.at[side * half : (side + 1) * half, first : first + lanes],
                    sems.at[side * len(parts) + p],
                )
            )
    for copy in copies:
        copy.start()
    for copy in copies:
        copy.wait()

    def place(k):
        return slice(k * tile, (k + 1) * tile)

    squares = jnp.zeros((8, size), jnp.float32)
    for k in range(blocks):
        value = m_ref[place(k), :].astype(jnp.float32)
        squares = squares + jnp.sum((value * value).reshape(tile // 8, 8, size), axis=0)
    scale = 1.0 / (jnp.sqrt(jnp.sum(squares)) + MUON_EPSILON)
    square_scale = scale * scale

    def gram_block(i, j):
        part = dot_nt(m_ref[place(i), :], m_ref[place(j), :]) * square_scale
        gram[place(i), place(j)] = part.astype(jnp.bfloat16)
        if i != j:
            gram[place(j), place(i)] = part.T.astype(jnp.bfloat16)

    for i in range(blocks):
        for j in range(i, blocks):
            gram_block(i, j)
    for i in range(blocks):
        for j in range(i, blocks):
            part = dot_nt(gram[place(i), :], gram[place(j), :])
            part = COEFF_B * gram[place(i), place(j)].astype(jnp.float32) + COEFF_C * part
            mixing[place(i), place(j)] = part.astype(jnp.bfloat16)
            if i != j:
                mixing[place(j), place(i)] = part.T.astype(jnp.bfloat16)

    def taken(ref):
        return jnp.concatenate([ref[first : first + count, :] for first, count in heads], axis=0)

    def times(value, ref):
        return jnp.dot(value.astype(jnp.bfloat16), ref[...], preferred_element_type=jnp.float32)

    def stepped(value):
        return COEFF_A * value + times(value, mixing)

    mixing_own = taken(mixing)
    gram_own = taken(gram).astype(jnp.float32)
    gram_own = stepped(COEFF_A * gram_own + times(mixing_own, gram))
    square_own = stepped(times(stepped(gram_own), gram))
    second_own = COEFF_B * gram_own + COEFF_C * square_own
    weights = COEFF_A * mixing_own.astype(jnp.float32) + stepped(second_own)
    result = COEFF_A * COEFF_A * taken(m_ref).astype(jnp.float32) + times(weights, m_ref)
    out_ref[...] = (scale * result).astype(jnp.bfloat16)


def newton_rows(own, other, parts, heads):
    size = 2 * own[0].shape[0]
    window = sum(count for _, count in heads)
    anywhere = pl.BlockSpec(memory_space=pl.ANY)
    return kernel_call(
        functools.partial(newton_body, parts, heads, 256),
        (1,),
        [anywhere] * (2 * len(parts)),
        whole((window, size)),
        shape_of((window, size), jnp.bfloat16),
        [pltpu.VMEM((size, size), jnp.bfloat16)] * 3 + [pltpu.SemaphoreType.DMA((2 * len(parts),))],
        flops=3 * size * size * size,
        traffic=2 * size * size,
    )(*own, *other)


def swap(value, bit):
    size = lax.axis_size("tm")
    return lax.ppermute(value, "tm", [(i, i ^ bit) for i in range(size)])


def steps_of(size):
    bits = []
    bit = 1
    while bit < size:
        bits.append(bit)
        bit *= 2
    return bits


def bit_of(bit):
    return jnp.where((lax.axis_index("tm") & bit) != 0, 1, 0)


class SumSpread:
    def __init__(self, value):
        self.value = value
        self.steps = []
        lanes = value.shape[1]
        cuts = []
        for bit in steps_of(lax.axis_size("tm")):
            if lanes // 2 % LANE == 0:
                lanes //= 2
                self.steps.append((self.halve, bit))
                cuts.append(bit)
            else:
                self.steps.append((self.pair, bit))
        self.steps += [(self.join, bit) for bit in reversed(cuts)]

    def halve(self, bit):
        lanes = self.value.shape[1] // 2
        mine = lax.dynamic_slice_in_dim(self.value, bit_of(bit) * lanes, lanes, 1)
        away = lax.dynamic_slice_in_dim(self.value, (1 - bit_of(bit)) * lanes, lanes, 1)
        self.value = mine + swap(away, bit)

    def pair(self, bit):
        self.value = self.value + swap(self.value, bit)

    def join(self, bit):
        other = swap(self.value, bit)
        upper = bit_of(bit) == 1
        self.value = jnp.concatenate(
            [jnp.where(upper, other, self.value), jnp.where(upper, self.value, other)], axis=1
        )

    def step(self, times=1):
        for _ in range(times):
            if self.steps:
                action, bit = self.steps.pop(0)
                action(bit)


def tie(first, second):
    return lax.optimization_barrier((list(first), list(second)))


def side_bit():
    return lax.axis_size("tm") // 32


def orders_of(size):
    bits = [bit for bit in steps_of(size) if bit != side_bit()]
    return [bits[k * len(bits) // 3 :] + bits[: k * len(bits) // 3] for k in range(3)]


class Scatter:
    def __init__(self, keeps, sends, slots):
        size = lax.axis_size("tm")
        bits = [bit for bit in reversed(steps_of(size)) if bit != side_bit()]
        shape = (2,) * len(bits) + (slots, -1)
        self.orders = orders_of(size)
        self.left = [list(bits) for _ in keeps]
        self.current = [keep.reshape(shape[:-1] + keep.shape[1:]) for keep in keeps]
        self.received = [
            swap(send.reshape(shape[:-1] + send.shape[1:]), side_bit()) for send in sends
        ]

    def step(self):
        for p, left in enumerate(self.left):
            bit = self.orders[p].pop(0)
            axis = left.index(bit)
            left.remove(bit)
            mine, away = [
                lax.dynamic_index_in_dim(self.current[p], index, axis, False)
                + lax.dynamic_index_in_dim(self.received[p], index, axis, False).astype(jnp.float32)
                for index in (bit_of(bit), 1 - bit_of(bit))
            ]
            self.current[p] = mine
            self.received[p] = swap(away.astype(jnp.bfloat16), bit)

    def result(self):
        return [a + b.astype(jnp.float32) for a, b in zip(self.current, self.received)]


class Gather:
    def __init__(self, blocks, near):
        self.orders = orders_of(lax.axis_size("tm"))
        self.held = [[] for _ in blocks]
        self.current = list(blocks)
        self.near = near

    def step(self):
        for p, held in enumerate(self.held):
            bit = self.orders[p].pop()
            axis = sum(other > bit for other in held)
            held.append(bit)
            mine, other = self.current[p], swap(self.current[p], bit)
            if not self.near:
                upper = bit_of(bit) == 1
                mine, other = jnp.where(upper, other, mine), jnp.where(upper, mine, other)
            self.current[p] = jnp.stack([mine, other], axis=axis)

    def result(self):
        own = [value.reshape(-1, value.shape[-1]) for value in self.current]
        return own, [swap(value, side_bit()) for value in own]


class Stats:
    def __init__(self, stat, count):
        self.stat = stat
        self.count = float(count)
        self.bits = steps_of(lax.axis_size("tm"))

    def step(self, times=1):
        for _ in range(min(times, len(self.bits))):
            stat = self.stat
            other = swap(stat, self.bits.pop(0))
            gap = stat[0:1] - other[0:1]
            mean = 0.5 * (stat[0:1] + other[0:1])
            square = (stat[1:2] + other[1:2]) + gap * gap * (0.5 * self.count)
            self.stat = jnp.concatenate([mean, square, 0.5 * (stat[2:] + other[2:])], axis=0)
            self.count *= 2


class Exchange:
    def __init__(self, flags, carries, sums=()):
        self.bits = steps_of(lax.axis_size("tm"))
        high, self.width = carries[0][0].shape
        rows = high * len(carries)
        flags = jnp.broadcast_to(jnp.tile(flags, len(carries))[:, None], (rows, LANE))
        ends = jnp.concatenate([ends for ends, _, _ in carries], axis=0)
        self.payload = jnp.concatenate([ends, flags, *sums], axis=1)
        self.power = jnp.concatenate(
            [jnp.broadcast_to(power, (high, self.width)) for _, power, _ in carries], axis=0
        )
        self.lane = lax.broadcasted_iota(jnp.int32, self.payload.shape, 1)
        self.high = high
        self.reverse = [reverse for _, _, reverse in carries]
        self.before = jnp.zeros_like(ends)
        self.before_keep = jnp.ones_like(ends)

    def step(self, times=1):
        for _ in range(min(times, len(self.bits))):
            self.one()

    def one(self):
        bit = self.bits.pop(0)
        width = self.width
        mine, other = self.payload, swap(self.payload, bit)
        upper = bit_of(bit)
        row = lax.broadcasted_iota(jnp.int32, (len(mine), 1), 0) // self.high
        turned = sum((row == k) * int(reverse) for k, reverse in enumerate(self.reverse))
        following = turned != upper
        other_total = other[:, :width]
        keep_mine, keep_other = mine[:, width : width + 1], other[:, width : width + 1]
        self.before = jnp.where(
            following, self.before_keep * other_total + self.before, self.before
        )
        self.before_keep = jnp.where(
            following, self.before_keep * keep_other * self.power, self.before_keep
        )
        power = jnp.pad(self.power, ((0, 0), (0, mine.shape[1] - width)))
        carried = jnp.where(
            following, keep_mine * power * other + mine, keep_other * power * mine + other
        )
        self.payload = jnp.where(
            self.lane < width,
            carried,
            jnp.where(self.lane < width + LANE, mine * other, mine + other),
        )
        self.power = self.power * self.power

    def arrived(self, k):
        return self.before[k * self.high : (k + 1) * self.high]

    def sums(self):
        return self.payload[:, self.width + LANE :]


class SumAll:
    def __init__(self, value):
        self.value = value
        self.bits = steps_of(lax.axis_size("tm"))

    def step(self, times=1):
        for _ in range(min(times, len(self.bits))):
            self.value = self.value + swap(self.value, self.bits.pop(0))


def pad_lanes(value, padded):
    gap = padded - value.shape[-1]
    return jnp.pad(value, [(0, 0)] * (value.ndim - 1) + [(0, gap)])


def flat_places(shard, width, padded):
    size = lax.axis_size("tm")
    members = size * LANE // padded
    slots = LANE // members
    return members, slots, slots * width - shard


def to_block(flat, width, padded):
    size, mine = lax.axis_size("tm"), lax.axis_index("tm")
    members, slots, excess = flat_places(flat.shape[0], width, padded)
    lacking = excess * (members - 1)
    pairs = [(i + 1, i) for i in range(size - 1) if (i + 1) % members]
    extra = lax.ppermute(flat[:lacking], "tm", pairs)
    tail = jnp.zeros((excess,), flat.dtype)
    held = jnp.concatenate([flat, extra, tail])
    return lax.dynamic_slice_in_dim(held, excess * (mine % members), slots * width).reshape(
        slots, width
    )


def from_block(block, shard, padded):
    width = block.shape[1]
    size, mine = lax.axis_size("tm"), lax.axis_index("tm")
    members, slots, excess = flat_places(shard, width, padded)
    lacking = excess * (members - 1)
    pairs = [(i, i + 1) for i in range(size - 1) if (i + 1) % members]
    flat = block.reshape(-1)
    extra = lax.ppermute(flat[slots * width - lacking :], "tm", pairs)
    held = jnp.concatenate([extra, flat])
    return lax.dynamic_slice_in_dim(held, lacking - excess * (mine % members), shard)


def own_heads(shard, width, padded):
    members, slots, _ = flat_places(shard, width, padded)
    half = padded // 2
    group = LANE // 2
    if members == 2:
        lacking = slots - shard // width
        kept = -(-(lacking) // 16) * 16
        return [(0, group), (half + group - kept, kept)]
    return [(0, group), (half, group)]


def own_flat(found, shard, width, padded):
    mine = lax.axis_index("tm")
    members, slots, excess = flat_places(shard, width, padded)
    member = mine % members
    if members == 2:
        own, other = found[:slots].reshape(-1), found[slots:].reshape(-1)
        low = own[:shard]
        high = jnp.concatenate([other[other.shape[0] - excess :], own[: shard - excess]])
        return jnp.where(member == 0, low, high)
    near = found.reshape(members, slots * width)
    placed = jnp.take(near, jnp.arange(members) ^ member, axis=0).reshape(-1)
    return lax.dynamic_slice_in_dim(placed, shard * member, shard)


def per_device(
    inputs,
    clip_start,
    shallow_weight,
    shallow_momentum,
    deep_weight,
    deep_momentum,
    unit_params,
    unit_first,
    unit_second,
    out_grad,
):
    devices = lax.axis_size("tm")
    rows, frames, feats = inputs.shape
    width = shallow_weight.shape[1]
    padded = -(-width // WIDE) * WIDE
    group = width // (padded // LANE)
    count = rows * frames
    keep_mask = (1 - clip_start).astype(jnp.float32)
    flags = jnp.min(keep_mask, axis=1)
    keep = jnp.broadcast_to(keep_mask.T.reshape(count, 1), (count, LANE))
    params = pad_lanes(unit_params, padded)
    rates = jnp.maximum(1.0 - jnp.exp(-params[:, 0:1]), DECAY_FLOOR)
    powers = rates
    for _ in range(frames.bit_length() - 1):
        powers = powers * powers

    deep_block = pad_lanes(to_block(deep_weight.astype(jnp.bfloat16), width, padded), padded)
    momentum_block = pad_lanes(to_block(deep_momentum, width, padded), padded)

    shares = [3 * padded // 8, 3 * padded // 8, padded // 4]
    parts = [(sum(shares[:p]), shares[p]) for p in range(3)]
    side = bit_of(side_bit()).astype(jnp.int32).reshape(1)
    gather = Gather([deep_block[:, first : first + lanes] for first, lanes in parts], False)
    chunks = padded // WIDE
    gather.step()
    x, proj_one, stat_one, gram = front(
        inputs.reshape(count, feats), shallow_weight, rows, frames
    )
    stats = Stats(stat_one, count)
    grad_rows = out_grad.reshape(count, width)
    delta = None
    for k in range(chunks):
        stats.step()
        delta = delta_two(k, delta, grad_rows, keep, params[1], rows, frames, padded)
        delta, (stats.stat,) = tie(delta, [stats.stat])
        if k == 1:
            gather.current, (stats.stat,) = tie(gather.current, [stats.stat])
            gather.step()
    delta_local, delta_end = delta
    stats.step(len(stats.bits))
    gather.current, (stat_one,) = tie(gather.current, [stats.stat])
    gather.step()
    state_local, state_end = local_states(
        proj_one, keep, params[0], stat_one, rows, frames, devices
    )
    carries = Exchange(flags, [(state_end, powers[0], False), (delta_end, powers[1], True)])
    carries.step(1)
    gather.current, (carries.payload,) = tie(gather.current, [carries.payload])
    while gather.orders[0]:
        gather.step()
    carries.step(len(carries.bits) - 1)
    gather.current, (carries.payload,) = tie(gather.current, [carries.payload])
    deep_own, deep_other = gather.result()
    carries.step(len(carries.bits))
    state_in, delta_in = carries.arrived(0), carries.arrived(1)
    low_one, mean_one = low_one_of(
        state_local, state_in, keep, params[0], rows, frames, width, group
    )
    proj_two, stat_two = second_forward(side, low_one, deep_own, deep_other, parts)
    stats = Stats(jnp.concatenate([stat_two, mean_one], axis=0), count)
    stats.step(len(stats.bits))
    stat_two, mean_one = stats.stat[:2], stats.stat[2:]
    gate, sums_two = gate_two(
        proj_two, delta_local, delta_in, keep, params[1], stat_two, rows, frames, devices
    )
    sums = SumAll(sums_two)
    second, turned = None, None
    for k in range(chunks):
        sums.step()
        second = states_two(
            k, second, proj_two, delta_local, delta_in, keep, params[1], stat_two,
            rows, frames, devices,
        )
        turned = turn(k, turned, low_one, mean_one)
        (sums.value,), both = tie([sums.value], [*second, *turned])
        second, turned = both[:-1], both[-1:]
    sums.step(len(sums.bits))
    sums_two = sums.value
    second_local, second_end, second_decay = second
    grads, keeps, sends, totals = zip(
        *[
            deep_term(
                first, lanes, side, gate, proj_two, params[1], stat_two, sums_two, turned[0],
                rows, frames, devices,
            )
            for first, lanes in parts
        ]
    )
    slots = padded // devices
    scatter = Scatter(keeps, sends, slots)
    back = back_one(grads, deep_own, deep_other, parts)
    scatter.received, back = tie(scatter.received, back)
    scatter.step()
    back_local, back_end = delta_one(
        side, *back, keep, params[0], rows, frames, width, group
    )
    tall = 2 * rows
    carries = Exchange(
        flags,
        [(back_end, powers[0], True), (second_end, powers[1], False)],
        [jnp.concatenate(totals, axis=1).reshape(tall, -1)]
        + [gram[k : k + tall] for k in range(0, SIDE, tall)],
    )
    carries.step(2)
    scatter.received, (carries.payload,) = tie(scatter.received, [carries.payload])
    while len(scatter.orders[0]) > 2:
        scatter.step()
    carries.step(len(carries.bits))
    scatter.received, (carries.payload, carries.before) = tie(
        scatter.received, [carries.payload, carries.before]
    )
    scatter.step()
    back_in, second_in = carries.arrived(0), carries.arrived(1)
    total_two = carries.sums()[:, : padded // tall].reshape(1, padded)
    gram = carries.sums()[:, padded // tall :]
    gram = jnp.concatenate(
        [gram[:, k * LANE : (k + 1) * LANE] for k in range(SIDE // tall)], axis=0
    )
    gate_low, sums_one = gate_one(
        proj_one, state_local, state_in, back_local, back_in, keep, params[0], stat_one, x,
        rows, frames, devices, feats,
    )
    scatter.received, (sums_one,) = tie(scatter.received, [sums_one])
    scatter.step()
    decay_two = jnp.sum(second_decay[:rows] + second_decay[rows:] * second_in, axis=0, keepdims=True)
    spread = SumSpread(
        sums_one + jnp.pad(decay_two, ((feats + 3, SIDE - feats - 4), (0, 0)))
    )
    hidden = [None, None]
    turns = [(0, k) for k in range(chunks)] + [(1, k) for k in range(chunks)]
    sources = [(state_local, state_in, params[0]), (second_local, second_in, params[1])]

    def next_hidden():
        if turns:
            layer, k = turns.pop()
            states, start, layer_params = sources[layer]
            hidden[layer] = hidden_of(
                k, hidden[layer], states, start, keep, layer_params, rows, frames, width
            )
            hidden[layer], (spread.value,) = tie(hidden[layer], [spread.value])

    for _ in range(2):
        spread.step()
        next_hidden()
    scatter.received, (spread.value,) = tie(scatter.received, [spread.value])
    mine = lax.axis_index("tm")
    place = mine // (2 * side_bit()) * side_bit() + mine % side_bit()
    place = (side[0] * (devices // 2) + place) * slots
    mean_own = lax.dynamic_slice_in_dim(mean_one[0], place, slots)[:, None]
    grad_parts = [
        part + mean_own * total_two[:, first : first + lanes]
        for (first, lanes), part in zip(parts, scatter.result())
    ]
    gather = Gather(
        [
            (MUON_BETA * momentum_block[:, first : first + lanes] + part).astype(jnp.bfloat16)
            for (first, lanes), part in zip(parts, grad_parts)
        ],
        True,
    )
    while gather.orders[0]:
        gather.step()
        for _ in range(2):
            spread.step()
            next_hidden()
        gather.current, (spread.value,) = tie(gather.current, [spread.value])
    own, other = gather.result()
    spread.step(len(spread.steps))
    while turns:
        next_hidden()
    (hidden_one,), (hidden_two,) = hidden
    sums_one = spread.value
    shallow_grad, shallow_next, shallow_new, shallow_low = shallow_step(
        sums_one, gram, params[0], stat_one, shallow_weight, shallow_momentum,
        count * devices, count,
    )
    input_back = input_grad_of(
        gate_low, proj_one, params[0], stat_one, sums_one, shallow_weight, rows, frames, devices
    )
    input_grad = jnp.swapaxes(input_back.reshape(frames, rows, feats), 0, 1)
    grad_block = jnp.concatenate(grad_parts, axis=1)

    shard = deep_weight.shape[0]
    heads = own_heads(shard, width, padded)
    ortho = newton_rows(own, other, parts, heads)
    deep_ortho = own_flat(ortho[:, :width], shard, width, padded)
    deep_new = MUON_KEEP * deep_weight - MUON_RATE * deep_ortho.astype(jnp.float32)
    deep_grad = from_block(grad_block[:, :width], shard, padded)
    deep_next = MUON_BETA * deep_momentum + deep_grad

    unit_sums = sums_one[feats : feats + 4, :width]
    bias_gain_two = sums_two[:, :width]
    slope = jnp.where(
        1.0 - jnp.exp(-unit_params[:, 0]) > DECAY_FLOOR, jnp.exp(-unit_params[:, 0]), 0.0
    )
    unit_grad = jnp.stack(
        [
            jnp.stack([unit_sums[2] * slope[0], unit_sums[0], unit_sums[1], unit_sums[0]]),
            jnp.stack(
                [unit_sums[3] * slope[1], bias_gain_two[0], bias_gain_two[1], bias_gain_two[0]]
            ),
        ]
    )
    first_fix = 1.0 - FIRST_DECAY**STEP
    second_fix = 1.0 - SECOND_DECAY**STEP
    first_new = FIRST_DECAY * unit_first + (1.0 - FIRST_DECAY) * unit_grad
    second_new = SECOND_DECAY * unit_second + (1.0 - SECOND_DECAY) * unit_grad * unit_grad
    params_new = unit_params - ADAM_RATE * (first_new / first_fix) / (
        jnp.sqrt(second_new / second_fix) + ADAM_EPSILON
    )
    return (
        hidden_one.reshape(rows, frames, width),
        hidden_two.reshape(rows, frames, width),
        input_grad,
        shallow_grad,
        shallow_next,
        shallow_new,
        shallow_low,
        deep_grad,
        deep_next,
        deep_new,
        deep_new.astype(jnp.bfloat16),
        first_new,
        second_new,
        params_new,
    )


def solution(mesh):
    in_specs = (
        P(None, "tm", None),
        P(None, "tm"),
        P(),
        P(),
        P("tm"),
        P("tm"),
        P(),
        P(),
        P(),
        P(None, "tm", None),
    )
    out_specs = (
        P(None, "tm", None),
        P(None, "tm", None),
        P(None, "tm", None),
        P(),
        P(),
        P(),
        P(),
        P("tm"),
        P("tm"),
        P("tm"),
        P("tm"),
        P(),
        P(),
        P(),
    )
    return jax.shard_map(
        per_device, mesh=mesh, in_specs=in_specs, out_specs=out_specs, check_vma=False
    )
```

```python
import functools

import jax
import jax.numpy as jnp
from jax import lax
from jax.experimental import pallas as pl
from jax.experimental.pallas import tpu as pltpu
from jax.sharding import PartitionSpec as P

NS_STEPS = 2
STEP = 5


NORM_EPSILON = 1e-05
MUON_EPSILON = 1e-07
COEFF_A = 3.4445
COEFF_B = -4.775
COEFF_C = 2.0315
MUON_BETA = 0.5
MUON_RATE = 4.0
MUON_KEEP = 0.999
FIRST_DECAY = 0.9
SECOND_DECAY = 0.95
ADAM_RATE = 0.5
ADAM_EPSILON = 1e-08
DECAY_FLOOR = 0.9
LANE = 128
WIDE = 512
PART = 256
SIDE = 80


def kernel_call(body, grid, in_specs, out_specs, out_shape, scratch=(), flops=0, traffic=0):
    return pl.pallas_call(
        body,
        grid=grid,
        in_specs=in_specs,
        out_specs=out_specs,
        out_shape=out_shape,
        scratch_shapes=list(scratch),
        compiler_params=pltpu.CompilerParams(vmem_limit_bytes=56 * 1024 * 1024),
        cost_estimate=pl.CostEstimate(flops=flops, bytes_accessed=traffic, transcendentals=0),
    )


def shape_of(shape, dtype=jnp.float32):
    return jax.ShapeDtypeStruct(shape, dtype)


def whole(shape):
    return pl.BlockSpec(shape, lambda i: (0,) * len(shape))


def lanes_of(rows, width=WIDE):
    return pl.BlockSpec((rows, width), lambda i: (0, i))


def chunk_call(body, place, in_specs, out_specs, out_shape, arrays, previous, scratch=(), traffic=0):
    count = len(in_specs)
    before = list(previous) if previous is not None else []

    def run(*refs):
        body(*refs[:count], *refs[count + len(before) :])

    return pl.pallas_call(
        run,
        grid=(1,),
        in_specs=list(in_specs) + [pl.BlockSpec(memory_space=pl.ANY)] * len(before),
        out_specs=out_specs,
        out_shape=out_shape,
        scratch_shapes=list(scratch),
        input_output_aliases={count + k: k for k in range(len(before))},
        compiler_params=pltpu.CompilerParams(vmem_limit_bytes=56 * 1024 * 1024),
        cost_estimate=pl.CostEstimate(flops=0, bytes_accessed=traffic, transcendentals=0),
    )(*arrays, *before)


def chunk_at(rows, place):
    return pl.BlockSpec((rows, WIDE), lambda i: (0, place))


def rate_of(params):
    return jnp.maximum(1.0 - jnp.exp(-params[0:1]), DECAY_FLOOR)


def softened(value):
    return jnp.maximum(value, 0.0) + jnp.log(1.0 + jnp.exp(-jnp.abs(value)))


def sigmoid(value):
    return 0.5 * jnp.tanh(0.5 * value) + 0.5


def wide_keep(keep_ref, t, rows):
    keep = keep_ref[pl.ds(pl.multiple_of(t * rows, rows), rows), :]
    return jnp.concatenate([keep] * (WIDE // LANE), axis=1)


def rows_at(ref, t, rows):
    return ref[pl.ds(pl.multiple_of(t * rows, rows), rows), :]


def store_at(ref, t, rows, value):
    ref[pl.ds(pl.multiple_of(t * rows, rows), rows), :] = value


def valid_lanes(shape, total, step):
    return lax.broadcasted_iota(jnp.int32, shape, 1) + step * WIDE < total


def unit_terms(params_ref, stat_ref, total_devices, frames):
    params = params_ref[...]
    stat = stat_ref[...]
    centre = stat[0:1]
    inverse = lax.rsqrt(stat[1:2] / (total_devices * frames) + NORM_EPSILON)
    return centre, inverse, params[2:3], params[3:4] + params[1:2]


def front_body(rows, frames, width, x_ref, w_ref, xt_ref, proj_ref, stat_ref, gram_ref, padded_w):
    step = pl.program_id(0)
    count, feats = x_ref.shape

    @pl.when(step == 0)
    def _():
        i = lax.broadcasted_iota(jnp.int32, (count, count), 0)
        j = lax.broadcasted_iota(jnp.int32, (count, count), 1)
        move = (j == lax.rem(i, rows) * frames + lax.div(i, rows)).astype(jnp.bfloat16)
        moved = jnp.dot(move, x_ref[...], preferred_element_type=jnp.float32).astype(jnp.bfloat16)
        i = lax.broadcasted_iota(jnp.int32, (feats, LANE), 0)
        j = lax.broadcasted_iota(jnp.int32, (feats, LANE), 1)
        wide = jnp.dot(moved, (i == j).astype(jnp.bfloat16), preferred_element_type=jnp.float32)
        lane = lax.broadcasted_iota(jnp.int32, (count, LANE), 1)
        xt = jnp.where(lane == feats, 1.0, wide).astype(jnp.bfloat16)
        xt_ref[...] = xt
        gram = dot_tn(xt, xt)
        high = gram_ref.shape[0]
        for k in range(SIDE // high):
            gram_ref[:, k * LANE : (k + 1) * LANE] = gram[k * high : (k + 1) * high]
        padded_w[...] = jnp.zeros_like(padded_w)

    weight = w_ref[...]
    padded_w[0:feats, :] = jnp.where(valid_lanes(weight.shape, width, step), weight, 0.0)
    proj = jnp.dot(
        xt_ref[...], padded_w[...].astype(jnp.bfloat16), preferred_element_type=jnp.float32
    )
    proj_ref[...] = proj
    mean = jnp.sum(proj, axis=0, keepdims=True) * (1.0 / count)
    off = proj - mean
    stat_ref[0:1, :] = mean
    stat_ref[1:2, :] = jnp.sum(off * off, axis=0, keepdims=True)


def dot_tn(a, b):
    return lax.dot_general(a, b, (((0,), (0,)), ((), ())), preferred_element_type=jnp.float32)


def front(x, weight, rows, frames):
    count, feats = x.shape
    width = weight.shape[1]
    padded = -(-width // WIDE) * WIDE
    return kernel_call(
        functools.partial(front_body, rows, frames, width),
        (padded // WIDE,),
        [whole((count, feats)), lanes_of(feats)],
        [whole((count, LANE)), lanes_of(count), lanes_of(2), whole((2 * rows, SIDE // (2 * rows) * LANE))],
        [
            shape_of((count, LANE), jnp.bfloat16),
            shape_of((count, padded)),
            shape_of((2, padded)),
            shape_of((2 * rows, SIDE // (2 * rows) * LANE)),
        ],
        [pltpu.VMEM((LANE, WIDE), jnp.float32)],
    )(x, weight)


def delta_two_body(rows, frames, width, place, grad_ref, keep_ref, params_ref, delta_ref, end_ref, held):
    pieces = WIDE // LANE
    mask = valid_lanes((rows * frames, WIDE), width, place)
    grad = jnp.where(mask, grad_ref[...].astype(jnp.float32), 0.0)
    for g in range(pieces):
        held[g] = grad[:, g * LANE : (g + 1) * LANE]
    rate = rate_of(params_ref[...])

    def body(k, carried):
        t = frames - 1 - k
        own = jnp.concatenate(
            [held[g, pl.ds(t, rows, stride=frames), :] for g in range(pieces)], axis=1
        )
        delta = own + carried
        store_at(delta_ref, t, rows, delta)
        return rate * wide_keep(keep_ref, t, rows) * delta

    end_ref[...] = lax.fori_loop(
        0, frames, body, jnp.zeros((rows, WIDE), jnp.float32), unroll=8
    )


def delta_two(place, previous, out_grad, keep, params, rows, frames, padded):
    count, width = out_grad.shape
    return chunk_call(
        functools.partial(delta_two_body, rows, frames, width, place),
        place,
        [chunk_at(count, place), whole((count, LANE)), chunk_at(4, place)],
        [chunk_at(count, place), chunk_at(rows, place)],
        [shape_of((count, padded)), shape_of((rows, padded))],
        (out_grad, keep, params),
        previous,
        [pltpu.VMEM((WIDE // LANE, count, LANE), jnp.float32)],
    )


def states_body(
    rows, frames, devices, proj_ref, keep_ref, params_ref, stat_ref, state_ref, end_ref
):
    centre, inverse, gain, offset = unit_terms(params_ref, stat_ref, devices, rows * frames)
    rate = rate_of(params_ref[...])
    share = 1.0 - rate

    def body(t, carried):
        gate = (rows_at(proj_ref, t, rows) - centre) * inverse * gain + offset
        soft = softened(gate)
        carried = rate * wide_keep(keep_ref, t, rows) * carried + share * soft
        store_at(state_ref, t, rows, carried)
        return carried

    end_ref[...] = lax.fori_loop(
        0, frames, body, jnp.zeros((rows, WIDE), jnp.float32), unroll=8
    )


def local_states(proj, keep, params, stat, rows, frames, devices):
    count, padded = proj.shape
    return kernel_call(
        functools.partial(states_body, rows, frames, devices),
        (padded // WIDE,),
        [lanes_of(count), whole((count, LANE)), lanes_of(4), lanes_of(2)],
        [lanes_of(count), lanes_of(rows)],
        [shape_of((count, padded)), shape_of((rows, padded))],
    )(proj, keep, params, stat)


def to_slots(value, group):
    pieces = value.shape[1] // LANE
    lane = lax.broadcasted_iota(jnp.int32, (value.shape[0], LANE), 1)
    parts = [value[:, g * LANE : (g + 1) * LANE] for g in range(pieces)]
    out = []
    for g in range(pieces):
        moved = (LANE - group) * g
        if moved == 0:
            new = parts[g]
        else:
            new = jnp.where(
                lane < moved, pltpu.roll(parts[g - 1], moved, 1), pltpu.roll(parts[g], moved, 1)
            )
        out.append(jnp.where(lane < group, new, 0.0))
    return jnp.concatenate(out, axis=1)


def from_slots(value, group, width):
    pieces = value.shape[1] // LANE
    lane = lax.broadcasted_iota(jnp.int32, (value.shape[0], LANE), 1)
    parts = [value[:, g * LANE : (g + 1) * LANE] for g in range(pieces)]
    out = []
    for j in range(pieces):
        moved = (LANE - group) * j
        new = parts[j] if moved == 0 else pltpu.roll(parts[j], LANE - moved, 1)
        if j + 1 < pieces:
            new = jnp.where(lane < group - moved, new, pltpu.roll(parts[j + 1], group - moved, 1))
        left = width - j * LANE
        out.append(new if left >= LANE else jnp.where(lane < left, new, 0.0))
    return jnp.concatenate(out, axis=1)


def low_one_body(rows, frames, width, group, state_ref, start_ref, keep_ref, params_ref, low_ref, mean_ref):
    pieces = state_ref.shape[1] // LANE
    rate = rate_of(params_ref[...])

    def advance(t, carried):
        keep = rows_at(keep_ref, t, rows)
        carried = rate * jnp.concatenate([keep] * pieces, axis=1) * carried
        return carried, rows_at(state_ref, t, rows) + carried

    def body(k, both):
        carried, total = both
        t = 2 * k
        carried, first = advance(t, carried)
        carried, second = advance(t + 1, carried)
        place = pl.ds(pl.multiple_of(t * rows, 2 * rows), 2 * rows)
        slots = to_slots(jnp.concatenate([first, second], axis=0), group)
        low_ref[place, :] = slots.astype(jnp.bfloat16)
        return carried, total + slots[:rows] + slots[rows:]

    start = start_ref[...]
    _, total = lax.fori_loop(0, frames // 2, body, (start, jnp.zeros_like(start)), unroll=2)
    mean_ref[...] = jnp.sum(total, axis=0, keepdims=True) * (1.0 / (rows * frames))


def low_one_of(states, start, keep, params, rows, frames, width, group):
    count, padded = states.shape
    return kernel_call(
        functools.partial(low_one_body, rows, frames, width, group),
        (1,),
        [whole((count, padded)), whole((rows, padded)), whole((count, LANE)), whole((4, padded))],
        [whole((count, padded)), whole((1, padded))],
        [shape_of((count, padded), jnp.bfloat16), shape_of((1, padded))],
    )(states, start, keep, params)


def hidden_body(rows, frames, state_ref, start_ref, keep_ref, params_ref, hidden_ref, held):
    pieces = WIDE // LANE
    rate = rate_of(params_ref[...])

    def body(t, carry):
        carry = rate * wide_keep(keep_ref, t, rows) * carry
        state = rows_at(state_ref, t, rows) + carry
        for g in range(pieces):
            held[g, pl.ds(pl.multiple_of(t * rows, rows), rows), :] = state[
                :, g * LANE : (g + 1) * LANE
            ]
        return carry

    lax.fori_loop(0, frames, body, start_ref[...], unroll=8)
    for r in range(rows):
        for g in range(pieces):
            hidden_ref[r * frames : (r + 1) * frames, g * LANE : (g + 1) * LANE] = held[
                g, pl.ds(r, frames, stride=rows), :
            ]


def hidden_of(place, previous, states, start, keep, params, rows, frames, width):
    count, _ = states.shape
    return chunk_call(
        functools.partial(hidden_body, rows, frames),
        place,
        [chunk_at(count, place), chunk_at(rows, place), whole((count, LANE)), chunk_at(4, place)],
        [chunk_at(count, place)],
        [shape_of((count, width))],
        (states, start, keep, params),
        previous,
        [pltpu.VMEM((WIDE // LANE, count, LANE), jnp.float32)],
        traffic=8 * count * WIDE,
    )


def second_body(low_ref, weight_ref, proj_ref, stat_ref):
    proj = jnp.dot(low_ref[...], weight_ref[...], preferred_element_type=jnp.float32)
    proj_ref[...] = proj
    mean = jnp.sum(proj, axis=0, keepdims=True) * (1.0 / proj.shape[0])
    off = proj - mean
    stat_ref[0:1, :] = mean
    stat_ref[1:2, :] = jnp.sum(off * off, axis=0, keepdims=True)


def second_forward(low, weight):
    count, padded = low.shape
    return kernel_call(
        second_body,
        (padded // WIDE,),
        [whole((count, padded)), lanes_of(padded)],
        [lanes_of(count), lanes_of(2)],
        [shape_of((count, padded)), shape_of((2, padded))],
    )(low, weight)


def gate_two_body(
    rows, frames, devices, proj_ref, delta_ref, start_ref, keep_ref, params_ref, stat_ref, gate_ref, sums_ref
):
    centre, inverse, gain, offset = unit_terms(params_ref, stat_ref, devices, rows * frames)
    rate = rate_of(params_ref[...])
    share = 1.0 - rate
    none = jnp.zeros((rows, WIDE), jnp.float32)

    def body(k, carried):
        carry, bias_sum, gain_sum = carried
        t = frames - 1 - k
        delta = rows_at(delta_ref, t, rows) + carry
        normed = (rows_at(proj_ref, t, rows) - centre) * inverse
        gate = share * delta * sigmoid(normed * gain + offset)
        store_at(gate_ref, t, rows, gate)
        carry = rate * wide_keep(keep_ref, t, rows) * carry
        return carry, bias_sum + gate, gain_sum + gate * normed

    _, bias_sum, gain_sum = lax.fori_loop(
        0, frames, body, (start_ref[...], none, none), unroll=8
    )
    sums_ref[0:1, :] = jnp.sum(bias_sum, axis=0, keepdims=True)
    sums_ref[1:2, :] = jnp.sum(gain_sum, axis=0, keepdims=True)


def gate_two(proj, delta, start, keep, params, stat, rows, frames, devices):
    count, padded = proj.shape
    return kernel_call(
        functools.partial(gate_two_body, rows, frames, devices),
        (padded // WIDE,),
        [lanes_of(count), lanes_of(count), lanes_of(rows), whole((count, LANE)), lanes_of(4), lanes_of(2)],
        [lanes_of(count), lanes_of(2)],
        [shape_of((count, padded)), shape_of((2, padded))],
        traffic=12 * count * padded,
    )(proj, delta, start, keep, params, stat)


def states_two_body(
    rows, frames, devices, proj_ref, delta_ref, start_ref, keep_ref, params_ref, stat_ref,
    state_ref, end_ref, decay_ref, held,
):
    centre, inverse, gain, offset = unit_terms(params_ref, stat_ref, devices, rows * frames)
    rate = rate_of(params_ref[...])
    share = 1.0 - rate
    none = jnp.zeros((rows, WIDE), jnp.float32)

    def backward(k, carry):
        t = frames - 1 - k
        store_at(held, t, rows, rows_at(delta_ref, t, rows) + carry)
        return rate * wide_keep(keep_ref, t, rows) * carry

    lax.fori_loop(0, frames, backward, start_ref[...], unroll=8)

    def forward(t, carried):
        state, reach, decay, factor = carried
        keep = wide_keep(keep_ref, t, rows)
        delta = rows_at(held, t, rows)
        value = (rows_at(proj_ref, t, rows) - centre) * inverse * gain + offset
        soft = softened(value)
        decay = decay + delta * (keep * state - soft)
        factor = factor + delta * keep * reach
        state = rate * keep * state + share * soft
        reach = rate * keep * reach
        store_at(state_ref, t, rows, state)
        return state, reach, decay, factor

    state, _, decay, factor = lax.fori_loop(
        0, frames, forward, (none, jnp.ones_like(none), none, none), unroll=4
    )
    end_ref[...] = state
    decay_ref[0:rows, :] = decay
    decay_ref[rows : 2 * rows, :] = factor


def states_two(place, previous, proj, delta, start, keep, params, stat, rows, frames, devices):
    count, padded = proj.shape
    return chunk_call(
        functools.partial(states_two_body, rows, frames, devices),
        place,
        [
            chunk_at(count, place),
            chunk_at(count, place),
            chunk_at(rows, place),
            whole((count, LANE)),
            chunk_at(4, place),
            chunk_at(2, place),
        ],
        [chunk_at(count, place), chunk_at(rows, place), chunk_at(2 * rows, place)],
        [shape_of((count, padded)), shape_of((rows, padded)), shape_of((2 * rows, padded))],
        (proj, delta, start, keep, params, stat),
        previous,
        [pltpu.VMEM((count, WIDE), jnp.float32)],
        traffic=12 * count * WIDE,
    )


def turn_body(low_ref, mean_ref, turned_ref):
    half = LANE // 2
    turned = (low_ref[...].astype(jnp.float32) - mean_ref[...]).T.astype(jnp.bfloat16)
    for g in range(WIDE // LANE):
        for side in range(2):
            turned_ref[side, g * half : (g + 1) * half, :] = turned[
                g * LANE + side * half : g * LANE + (side + 1) * half
            ]


def turn(place, previous, low, mean):
    count, padded = low.shape
    return chunk_call(
        turn_body,
        place,
        [chunk_at(count, place), chunk_at(1, place)],
        [pl.BlockSpec((2, WIDE // 2, count), lambda i: (0, place, 0))],
        [shape_of((2, padded // 2, count), jnp.bfloat16)],
        (low, mean),
        previous,
        traffic=4 * count * WIDE,
    )


def deep_term_body(
    rows, frames, devices, bits, side_ref, gate_ref, proj_ref, params_ref, stat_ref, sums_ref, turned_ref,
    grad_ref, keep_ref, send_ref, total_ref,
):
    step = pl.program_id(0)
    total = devices * rows * frames

    @pl.when(step == 0)
    def _():
        centre, inverse, gain, _ = unit_terms(params_ref, stat_ref, devices, rows * frames)
        sums = sums_ref[...] * (1.0 / total)
        normed = (proj_ref[...] - centre) * inverse
        grad = gain * inverse * (gate_ref[...] - sums[0:1] - normed * sums[1:2])
        grad = grad.astype(jnp.bfloat16)
        grad_ref[...] = grad
        total_ref[...] = jnp.sum(grad.astype(jnp.float32), axis=0, keepdims=True)

    side = side_ref[0]
    half = turned_ref.shape[1]
    slots = half // 2 ** len(bits)
    for which, out_ref in ((side, keep_ref), (1 - side, send_ref)):
        if bits:
            order = [0]
            for bit in bits[1:]:
                order = [k + extra for k in order for extra in (0, bit)]
            left = jnp.concatenate(
                [
                    turned_ref[which, pl.ds(pl.multiple_of((bits[0] * step + k) * slots, slots), slots), :]
                    for k in order
                ],
                axis=0,
            )
        else:
            left = turned_ref[which, pl.ds(pl.multiple_of(step * (half // 2), half // 2), half // 2), :]
        out_ref[...] = jnp.dot(
            left, grad_ref[...], preferred_element_type=jnp.float32
        ).astype(out_ref.dtype)


def deep_term(first, lanes, bits, side, gate, proj, params, stat, sums, turned, rows, frames, devices):
    count, padded = proj.shape
    half = padded // 2

    def some(height):
        return pl.BlockSpec((height, lanes), lambda i: (0, first // lanes))

    steps = pl.BlockSpec((half // 2, lanes), lambda i: (i, 0))
    return kernel_call(
        functools.partial(deep_term_body, rows, frames, devices, bits),
        (2,),
        [
            pl.BlockSpec(memory_space=pltpu.SMEM),
            some(count),
            some(count),
            some(4),
            some(2),
            some(2),
            whole((2, half, count)),
        ],
        [whole((count, lanes)), steps, steps, whole((1, lanes))],
        [
            shape_of((count, lanes), jnp.bfloat16),
            shape_of((half, lanes)),
            shape_of((half, lanes), jnp.bfloat16),
            shape_of((1, lanes)),
        ],
        flops=2 * count * padded * lanes,
        traffic=10 * count * lanes + 3 * padded * lanes,
    )(side, gate, proj, params, stat, sums, turned)


def back_body(parts, *refs):
    grads, weight_ref, back_ref = refs[: len(parts)], refs[-2], refs[-1]
    grad = jnp.concatenate([ref[...] for ref in grads], axis=1)
    back_ref[...] = dot_nt(grad, weight_ref[...])


def back_one(grads, weight, parts):
    count, padded = grads[0].shape[0], weight.shape[0]
    return kernel_call(
        functools.partial(back_body, parts),
        (padded // WIDE,),
        [whole(grad.shape) for grad in grads]
        + [pl.BlockSpec((WIDE, padded), lambda i: (i, 0))],
        lanes_of(count),
        shape_of((count, padded)),
        flops=2 * count * padded * padded,
        traffic=6 * count * padded + 2 * padded * padded,
    )(*grads, weight)


def delta_one_body(rows, frames, width, group, back_ref, keep_ref, params_ref, delta_ref, end_ref):
    pieces = back_ref.shape[1] // LANE
    rate = rate_of(params_ref[...])

    def body(k, carried):
        t = frames - 1 - k
        delta = from_slots(rows_at(back_ref, t, rows), group, width) + carried
        store_at(delta_ref, t, rows, delta)
        keep = rows_at(keep_ref, t, rows)
        return rate * jnp.concatenate([keep] * pieces, axis=1) * delta

    end_ref[...] = lax.fori_loop(
        0, frames, body, jnp.zeros((rows, back_ref.shape[1]), jnp.float32), unroll=2
    )


def delta_one(back, keep, params, rows, frames, width, group):
    count, padded = back.shape
    return kernel_call(
        functools.partial(delta_one_body, rows, frames, width, group),
        (1,),
        [whole((count, padded)), whole((count, LANE)), whole((4, padded))],
        [whole((count, padded)), whole((rows, padded))],
        [shape_of((count, padded)), shape_of((rows, padded))],
        traffic=8 * count * padded,
    )(back, keep, params)


def gate_one_body(
    rows,
    frames,
    devices,
    feats,
    proj_ref,
    state_ref,
    first_ref,
    delta_ref,
    start_ref,
    keep_ref,
    params_ref,
    stat_ref,
    x_ref,
    gate_ref,
    sums_ref,
    held,
):
    centre, inverse, gain, offset = unit_terms(params_ref, stat_ref, devices, rows * frames)
    rate = rate_of(params_ref[...])
    share = 1.0 - rate
    none = jnp.zeros((rows, WIDE), jnp.float32)

    def backward(k, carry):
        t = frames - 1 - k
        store_at(held, t, rows, rows_at(delta_ref, t, rows) + carry)
        return rate * wide_keep(keep_ref, t, rows) * carry

    lax.fori_loop(0, frames, backward, start_ref[...], unroll=8)

    def forward(t, carried):
        carry, before, bias_sum, gain_sum, decay_sum = carried
        keep = wide_keep(keep_ref, t, rows)
        delta = rows_at(held, t, rows)
        normed = (rows_at(proj_ref, t, rows) - centre) * inverse
        value = normed * gain + offset
        soft = softened(value)
        gate = share * delta * sigmoid(value)
        store_at(gate_ref, t, rows, gate)
        decay_sum = decay_sum + delta * (keep * before - soft)
        carry = rate * keep * carry
        before = rows_at(state_ref, t, rows) + carry
        return carry, before, bias_sum + gate, gain_sum + gate * normed, decay_sum

    first = first_ref[...]
    _, _, bias_sum, gain_sum, decay_sum = lax.fori_loop(
        0, frames, forward, (first, first, none, none, none), unroll=4
    )
    bias = jnp.sum(bias_sum, axis=0, keepdims=True)
    mean = bias * (1.0 / (rows * frames))
    x = x_ref[...]
    ones = jnp.ones((rows * frames, LANE), jnp.bfloat16)
    total = jnp.concatenate([dot_tn(x, ones)] * (WIDE // LANE), axis=1)
    term = dot_tn(x, (gate_ref[...] - mean).astype(jnp.bfloat16)) + total * mean
    sums_ref[...] = term[: sums_ref.shape[0]]
    sums_ref[feats : feats + 1, :] = bias
    sums_ref[feats + 1 : feats + 2, :] = jnp.sum(gain_sum, axis=0, keepdims=True)
    sums_ref[feats + 2 : feats + 3, :] = jnp.sum(decay_sum, axis=0, keepdims=True)


def gate_one(proj, states, first, delta, start, keep, params, stat, x, rows, frames, devices, feats):
    count, padded = proj.shape
    return kernel_call(
        functools.partial(gate_one_body, rows, frames, devices, feats),
        (padded // WIDE,),
        [
            lanes_of(count),
            lanes_of(count),
            lanes_of(rows),
            lanes_of(count),
            lanes_of(rows),
            whole((count, LANE)),
            lanes_of(4),
            lanes_of(2),
            whole((count, LANE)),
        ],
        [lanes_of(count), lanes_of(SIDE)],
        [shape_of((count, padded)), shape_of((SIDE, padded))],
        [pltpu.VMEM((count, WIDE), jnp.float32)],
        traffic=16 * count * padded,
    )(proj, states, first, delta, start, keep, params, stat, x)


def input_grad_body(
    rows, frames, devices, width, feats, gate_ref, proj_ref, params_ref, stat_ref, sums_ref, w_ref, back_ref
):
    step = pl.program_id(0)
    total = devices * rows * frames
    centre, inverse, gain, _ = unit_terms(params_ref, stat_ref, devices, rows * frames)
    bias = sums_ref[feats : feats + 1, :] * (1.0 / total)
    slope = sums_ref[feats + 1 : feats + 2, :] * (1.0 / total)
    normed = (proj_ref[...] - centre) * inverse
    grad = (gain * inverse * (gate_ref[...] - bias - normed * slope)).astype(jnp.bfloat16)
    weight = w_ref[...]
    weight = jnp.where(valid_lanes(weight.shape, width, step), weight, 0.0).astype(jnp.bfloat16)
    part = dot_nt(grad, weight)

    @pl.when(step == 0)
    def _():
        back_ref[...] = part

    @pl.when(step > 0)
    def _():
        back_ref[...] += part


def input_grad_of(gate, proj, params, stat, sums, weight, rows, frames, devices):
    count, padded = proj.shape
    feats, width = weight.shape
    return kernel_call(
        functools.partial(input_grad_body, rows, frames, devices, width, feats),
        (padded // WIDE,),
        [lanes_of(count), lanes_of(count), lanes_of(4), lanes_of(2), lanes_of(SIDE), lanes_of(feats)],
        whole((count, feats)),
        shape_of((count, feats)),
        flops=2 * count * feats * padded,
        traffic=8 * count * padded,
    )(gate, proj, params, stat, sums, weight)


def dot_nt(a, b):
    return lax.dot_general(a, b, (((1,), (1,)), ((), ())), preferred_element_type=jnp.float32)


def shallow_body(
    total, frames, sums_ref, gram_ref, params_ref, stat_ref, w_ref, m_ref,
    grad_ref, next_ref, new_ref, low_ref, held,
):
    feats, width = w_ref.shape
    centre, inverse, gain, _ = unit_terms(params_ref, stat_ref, total // frames, frames)
    weight = w_ref[...]
    held[...] = jnp.zeros_like(held)
    held[0:feats, 0:width] = weight
    high = gram_ref.shape[0]
    gram = jnp.concatenate(
        [gram_ref[:, k * LANE : (k + 1) * LANE] for k in range(SIDE // high)], axis=0
    )
    lane = lax.broadcasted_iota(jnp.int32, gram.shape, 1)
    x_sum = jnp.sum(jnp.where(lane == feats, gram, 0.0), axis=1, keepdims=True)
    raw = jnp.dot(
        gram[:, :SIDE],
        held[...].astype(jnp.bfloat16).astype(jnp.float32),
        precision=lax.Precision.HIGHEST,
        preferred_element_type=jnp.float32,
    )
    normed = (raw - x_sum * centre) * inverse
    bias = sums_ref[feats : feats + 1, :] * (1.0 / total)
    slope = sums_ref[feats + 1 : feats + 2, :] * (1.0 / total)
    grad = gain * inverse * (sums_ref[...] - x_sum * bias - normed * slope)
    grad = grad[:feats, :width]
    grad_ref[...] = grad
    following = MUON_BETA * m_ref[...] + grad
    next_ref[...] = following
    held[0:feats, 0:width] = following
    m = held[...]
    current = (m / (jnp.sqrt(jnp.sum(m * m)) + MUON_EPSILON)).astype(jnp.bfloat16)
    for repeat in range(NS_STEPS):
        gram = dot_nt(current, current).astype(jnp.bfloat16)
        square = jnp.dot(gram, gram, preferred_element_type=jnp.float32)
        mixing = (COEFF_B * gram.astype(jnp.float32) + COEFF_C * square).astype(jnp.bfloat16)
        current = (
            COEFF_A * current.astype(jnp.float32)
            + jnp.dot(mixing, current, preferred_element_type=jnp.float32)
        ).astype(jnp.bfloat16)
    new = MUON_KEEP * weight - MUON_RATE * current[:feats, :width].astype(jnp.float32)
    new_ref[...] = new
    low_ref[...] = new.astype(jnp.bfloat16)


def shallow_step(sums, gram, params, stat, weight, momentum, total, frames):
    padded = sums.shape[1]
    some = shape_of(weight.shape)
    return kernel_call(
        functools.partial(shallow_body, total, frames),
        (1,),
        [whole(value.shape) for value in (sums, gram, params, stat, weight, momentum)],
        [whole(weight.shape)] * 4,
        [some, some, some, shape_of(weight.shape, jnp.bfloat16)],
        [pltpu.VMEM((SIDE, padded), jnp.float32)],
        flops=14 * SIDE * SIDE * padded,
        traffic=24 * SIDE * padded,
    )(sums, gram, params, stat, weight, momentum)


def newton_body(parts, heads, tile, *refs):
    blocks_refs, out_ref = refs[: 2 * len(parts)], refs[2 * len(parts)]
    m_ref, gram, mixing, sems = refs[2 * len(parts) + 1 :]
    size = m_ref.shape[0]
    half = size // 2
    blocks = size // tile
    copies = []
    for side in range(2):
        for p, (first, lanes) in enumerate(parts):
            copies.append(
                pltpu.make_async_copy(
                    blocks_refs[side * len(parts) + p],
                    m_ref.at[side * half : (side + 1) * half, first : first + lanes],
                    sems.at[side * len(parts) + p],
                )
            )
    for copy in copies:
        copy.start()
    for copy in copies:
        copy.wait()

    def place(k):
        return slice(k * tile, (k + 1) * tile)

    squares = jnp.zeros((8, size), jnp.float32)
    for k in range(blocks):
        value = m_ref[place(k), :].astype(jnp.float32)
        squares = squares + jnp.sum((value * value).reshape(tile // 8, 8, size), axis=0)
    scale = 1.0 / (jnp.sqrt(jnp.sum(squares)) + MUON_EPSILON)
    square_scale = scale * scale

    def gram_block(i, j):
        part = dot_nt(m_ref[place(i), :], m_ref[place(j), :]) * square_scale
        gram[place(i), place(j)] = part.astype(jnp.bfloat16)
        if i != j:
            gram[place(j), place(i)] = part.T.astype(jnp.bfloat16)

    for i in range(blocks):
        for j in range(i, blocks):
            gram_block(i, j)
    for i in range(blocks):
        for j in range(i, blocks):
            part = dot_nt(gram[place(i), :], gram[place(j), :])
            part = COEFF_B * gram[place(i), place(j)].astype(jnp.float32) + COEFF_C * part
            mixing[place(i), place(j)] = part.astype(jnp.bfloat16)
            if i != j:
                mixing[place(j), place(i)] = part.T.astype(jnp.bfloat16)

    def taken(ref):
        return jnp.concatenate([ref[first : first + count, :] for first, count in heads], axis=0)

    def times(value, ref):
        return jnp.dot(value.astype(jnp.bfloat16), ref[...], preferred_element_type=jnp.float32)

    def stepped(value):
        return COEFF_A * value + times(value, mixing)

    mixing_own = taken(mixing)
    gram_own = taken(gram).astype(jnp.float32)
    gram_own = stepped(COEFF_A * gram_own + times(mixing_own, gram))
    square_own = stepped(times(stepped(gram_own), gram))
    second_own = COEFF_B * gram_own + COEFF_C * square_own
    weights = COEFF_A * mixing_own.astype(jnp.float32) + stepped(second_own)
    result = COEFF_A * COEFF_A * taken(m_ref).astype(jnp.float32) + times(weights, m_ref)
    out_ref[...] = (scale * result).astype(jnp.bfloat16)


def newton_rows(own, other, parts, heads):
    size = 2 * own[0].shape[0]
    window = sum(count for _, count in heads)
    anywhere = pl.BlockSpec(memory_space=pl.ANY)
    return kernel_call(
        functools.partial(newton_body, parts, heads, 256),
        (1,),
        [anywhere] * (2 * len(parts)),
        whole((window, size)),
        shape_of((window, size), jnp.bfloat16),
        [pltpu.VMEM((size, size), jnp.bfloat16)] * 3 + [pltpu.SemaphoreType.DMA((2 * len(parts),))],
        flops=3 * size * size * size,
        traffic=2 * size * size,
    )(*own, *other)


def swap(value, bit):
    size = lax.axis_size("tm")
    return lax.ppermute(value, "tm", [(i, i ^ bit) for i in range(size)])


def steps_of(size):
    bits = []
    bit = 1
    while bit < size:
        bits.append(bit)
        bit *= 2
    return bits


def bit_of(bit):
    return jnp.where((lax.axis_index("tm") & bit) != 0, 1, 0)


class SumSpread:
    def __init__(self, value):
        self.value = value
        self.steps = []
        lanes = value.shape[1]
        cuts = []
        for bit in steps_of(lax.axis_size("tm")):
            if lanes // 2 % LANE == 0:
                lanes //= 2
                self.steps.append((self.halve, bit))
                cuts.append(bit)
            else:
                self.steps.append((self.pair, bit))
        self.steps += [(self.join, bit) for bit in reversed(cuts)]

    def halve(self, bit):
        lanes = self.value.shape[1] // 2
        mine = lax.dynamic_slice_in_dim(self.value, bit_of(bit) * lanes, lanes, 1)
        away = lax.dynamic_slice_in_dim(self.value, (1 - bit_of(bit)) * lanes, lanes, 1)
        self.value = mine + swap(away, bit)

    def pair(self, bit):
        self.value = self.value + swap(self.value, bit)

    def join(self, bit):
        other = swap(self.value, bit)
        upper = bit_of(bit) == 1
        self.value = jnp.concatenate(
            [jnp.where(upper, other, self.value), jnp.where(upper, self.value, other)], axis=1
        )

    def step(self, times=1):
        for _ in range(times):
            if self.steps:
                action, bit = self.steps.pop(0)
                action(bit)


def tie(first, second):
    return lax.optimization_barrier((list(first), list(second)))


def side_bit():
    return lax.axis_size("tm") // 32


def orders_of(size):
    bits = [bit for bit in steps_of(size) if bit != side_bit()]
    return [bits[k * len(bits) // 3 :] + bits[: k * len(bits) // 3] for k in range(3)]


def index_bits(bits):
    return [bit if bit < side_bit() else bit // 2 for bit in bits]


class Scatter:
    def __init__(self, keeps, sends):
        self.orders = orders_of(lax.axis_size("tm"))
        self.current = list(keeps)
        self.received = [swap(send, side_bit()) for send in sends]

    def step(self):
        for p, order in enumerate(self.orders):
            bit = order.pop(0)
            half = self.current[p].shape[0] // 2
            mine, away = [
                lax.dynamic_slice_in_dim(self.current[p], half * index, half)
                + lax.dynamic_slice_in_dim(self.received[p], half * index, half).astype(jnp.float32)
                for index in (bit_of(bit), 1 - bit_of(bit))
            ]
            self.current[p] = mine
            self.received[p] = swap(away.astype(jnp.bfloat16), bit)

    def result(self):
        return [a + b.astype(jnp.float32) for a, b in zip(self.current, self.received)]


class Gather:
    def __init__(self, blocks, near):
        self.orders = orders_of(lax.axis_size("tm"))
        self.held = [[] for _ in blocks]
        self.current = list(blocks)
        self.near = near

    def step(self):
        for p, held in enumerate(self.held):
            bit = self.orders[p].pop()
            axis = sum(other > bit for other in held)
            held.append(bit)
            mine, other = self.current[p], swap(self.current[p], bit)
            if not self.near:
                upper = bit_of(bit) == 1
                mine, other = jnp.where(upper, other, mine), jnp.where(upper, mine, other)
            self.current[p] = jnp.stack([mine, other], axis=axis)

    def result(self):
        own = [value.reshape(-1, value.shape[-1]) for value in self.current]
        return own, [swap(value, side_bit()) for value in own]


class Stats:
    def __init__(self, stat, count):
        self.stat = stat
        self.count = float(count)
        self.bits = steps_of(lax.axis_size("tm"))

    def step(self, times=1):
        for _ in range(min(times, len(self.bits))):
            stat = self.stat
            other = swap(stat, self.bits.pop(0))
            gap = stat[0:1] - other[0:1]
            mean = 0.5 * (stat[0:1] + other[0:1])
            square = (stat[1:2] + other[1:2]) + gap * gap * (0.5 * self.count)
            self.stat = jnp.concatenate([mean, square, 0.5 * (stat[2:] + other[2:])], axis=0)
            self.count *= 2


class Exchange:
    def __init__(self, flags, carries, sums=()):
        self.bits = steps_of(lax.axis_size("tm"))
        high, self.width = carries[0][0].shape
        rows = high * len(carries)
        flags = jnp.broadcast_to(jnp.tile(flags, len(carries))[:, None], (rows, LANE))
        ends = jnp.concatenate([ends for ends, _, _ in carries], axis=0)
        self.payload = jnp.concatenate([ends, flags, *sums], axis=1)
        self.power = jnp.concatenate(
            [jnp.broadcast_to(power, (high, self.width)) for _, power, _ in carries], axis=0
        )
        self.lane = lax.broadcasted_iota(jnp.int32, self.payload.shape, 1)
        self.high = high
        self.reverse = [reverse for _, _, reverse in carries]
        self.before = jnp.zeros_like(ends)
        self.before_keep = jnp.ones_like(ends)

    def step(self, times=1):
        for _ in range(min(times, len(self.bits))):
            self.one()

    def one(self):
        bit = self.bits.pop(0)
        width = self.width
        mine, other = self.payload, swap(self.payload, bit)
        upper = bit_of(bit)
        row = lax.broadcasted_iota(jnp.int32, (len(mine), 1), 0) // self.high
        turned = sum((row == k) * int(reverse) for k, reverse in enumerate(self.reverse))
        following = turned != upper
        other_total = other[:, :width]
        keep_mine, keep_other = mine[:, width : width + 1], other[:, width : width + 1]
        self.before = jnp.where(
            following, self.before_keep * other_total + self.before, self.before
        )
        self.before_keep = jnp.where(
            following, self.before_keep * keep_other * self.power, self.before_keep
        )
        power = jnp.pad(self.power, ((0, 0), (0, mine.shape[1] - width)))
        carried = jnp.where(
            following, keep_mine * power * other + mine, keep_other * power * mine + other
        )
        self.payload = jnp.where(
            self.lane < width,
            carried,
            jnp.where(self.lane < width + LANE, mine * other, mine + other),
        )
        self.power = self.power * self.power

    def arrived(self, k):
        return self.before[k * self.high : (k + 1) * self.high]

    def sums(self):
        return self.payload[:, self.width + LANE :]


class SumAll:
    def __init__(self, value):
        self.value = value
        self.bits = steps_of(lax.axis_size("tm"))

    def step(self, times=1):
        for _ in range(min(times, len(self.bits))):
            self.value = self.value + swap(self.value, self.bits.pop(0))


def in_order(value, bits, slots):
    count = len(bits)
    axes = [count - bit.bit_length() for bit in bits]
    shape = (2,) * count + (slots, value.shape[1])
    return value.reshape(shape).transpose(axes + [count, count + 1]).reshape(value.shape)


def pad_lanes(value, padded):
    gap = padded - value.shape[-1]
    return jnp.pad(value, [(0, 0)] * (value.ndim - 1) + [(0, gap)])


def flat_places(shard, width, padded):
    size = lax.axis_size("tm")
    members = size * LANE // padded
    slots = LANE // members
    return members, slots, slots * width - shard


def to_block(flat, width, padded):
    size, mine = lax.axis_size("tm"), lax.axis_index("tm")
    members, slots, excess = flat_places(flat.shape[0], width, padded)
    lacking = excess * (members - 1)
    pairs = [(i + 1, i) for i in range(size - 1) if (i + 1) % members]
    extra = lax.ppermute(flat[:lacking], "tm", pairs)
    tail = jnp.zeros((excess,), flat.dtype)
    held = jnp.concatenate([flat, extra, tail])
    return lax.dynamic_slice_in_dim(held, excess * (mine % members), slots * width).reshape(
        slots, width
    )


def from_block(block, shard, padded):
    width = block.shape[1]
    size, mine = lax.axis_size("tm"), lax.axis_index("tm")
    members, slots, excess = flat_places(shard, width, padded)
    lacking = excess * (members - 1)
    pairs = [(i, i + 1) for i in range(size - 1) if (i + 1) % members]
    flat = block.reshape(-1)
    extra = lax.ppermute(flat[slots * width - lacking :], "tm", pairs)
    held = jnp.concatenate([extra, flat])
    return lax.dynamic_slice_in_dim(held, lacking - excess * (mine % members), shard)


def own_heads(shard, width, padded):
    members, slots, _ = flat_places(shard, width, padded)
    half = padded // 2
    group = LANE // 2
    if members == 2:
        lacking = slots - shard // width
        kept = -(-(lacking) // 16) * 16
        return [(0, group), (half + group - kept, kept)]
    return [(0, group), (half, group)]


def own_flat(found, shard, width, padded):
    mine = lax.axis_index("tm")
    members, slots, excess = flat_places(shard, width, padded)
    member = mine % members
    if members == 2:
        own, other = found[:slots].reshape(-1), found[slots:].reshape(-1)
        low = own[:shard]
        high = jnp.concatenate([other[other.shape[0] - excess :], own[: shard - excess]])
        return jnp.where(member == 0, low, high)
    near = found.reshape(members, slots * width)
    placed = jnp.take(near, jnp.arange(members) ^ member, axis=0).reshape(-1)
    return lax.dynamic_slice_in_dim(placed, shard * member, shard)


def per_device(
    inputs,
    clip_start,
    shallow_weight,
    shallow_momentum,
    deep_weight,
    deep_momentum,
    unit_params,
    unit_first,
    unit_second,
    out_grad,
):
    devices = lax.axis_size("tm")
    rows, frames, feats = inputs.shape
    width = shallow_weight.shape[1]
    padded = -(-width // WIDE) * WIDE
    group = width // (padded // LANE)
    count = rows * frames
    keep_mask = (1 - clip_start).astype(jnp.float32)
    flags = jnp.min(keep_mask, axis=1)
    keep = jnp.broadcast_to(keep_mask.T.reshape(count, 1), (count, LANE))
    params = pad_lanes(unit_params, padded)
    rates = jnp.maximum(1.0 - jnp.exp(-params[:, 0:1]), DECAY_FLOOR)
    powers = rates
    for _ in range(frames.bit_length() - 1):
        powers = powers * powers

    deep_block = pad_lanes(to_block(deep_weight.astype(jnp.bfloat16), width, padded), padded)
    momentum_block = pad_lanes(to_block(deep_momentum, width, padded), padded)

    shares = [3 * padded // 8, 3 * padded // 8, padded // 4]
    parts = [(sum(shares[:p]), shares[p]) for p in range(3)]
    side = bit_of(side_bit()).astype(jnp.int32).reshape(1)
    chunks = padded // WIDE
    x, proj_one, stat_one, gram = front(
        inputs.reshape(count, feats), shallow_weight, rows, frames
    )
    (deep_block,), (stat_one,) = tie([deep_block], [stat_one])
    deep_low = lax.all_gather(deep_block, "tm", axis=0, tiled=True)
    stats = Stats(stat_one, count)
    grad_rows = out_grad.reshape(count, width)
    delta = None
    for k in range(chunks):
        stats.step()
        delta = delta_two(k, delta, grad_rows, keep, params[1], rows, frames, padded)
        delta, (stats.stat,) = tie(delta, [stats.stat])
    delta_local, delta_end = delta
    stats.step(len(stats.bits))
    (stat_one,), (momentum_block,) = tie([stats.stat], [momentum_block])
    state_local, state_end = local_states(
        proj_one, keep, params[0], stat_one, rows, frames, devices
    )
    carries = Exchange(
        flags, [(state_end, powers[0], False), (delta_end, powers[1], True)], [gram]
    )
    carries.step(len(carries.bits))
    state_in, delta_in, gram = carries.arrived(0), carries.arrived(1), carries.sums()
    low_one, mean_one = low_one_of(
        state_local, state_in, keep, params[0], rows, frames, width, group
    )
    proj_two, stat_two = second_forward(low_one, deep_low)
    stats = Stats(jnp.concatenate([stat_two, mean_one], axis=0), count)
    stats.step(len(stats.bits))
    stat_two, mean_one = stats.stat[:2], stats.stat[2:]
    gate, sums_two = gate_two(
        proj_two, delta_local, delta_in, keep, params[1], stat_two, rows, frames, devices
    )
    sums = SumAll(sums_two)
    second, turned = None, None
    for k in range(chunks):
        sums.step()
        second = states_two(
            k, second, proj_two, delta_local, delta_in, keep, params[1], stat_two,
            rows, frames, devices,
        )
        turned = turn(k, turned, low_one, mean_one)
        (sums.value,), both = tie([sums.value], [*second, *turned])
        second, turned = both[:-1], both[-1:]
    sums.step(len(sums.bits))
    sums_two = sums.value
    second_local, second_end, second_decay = second
    slots = padded // devices
    orders = [index_bits(order) for order in orders_of(devices)]
    aligned = slots % 16 == 0
    grads, keeps, sends, totals = zip(
        *[
            deep_term(
                first, lanes, order if aligned else (), side, gate, proj_two, params[1], stat_two,
                sums_two, turned[0], rows, frames, devices,
            )
            for (first, lanes), order in zip(parts, orders)
        ]
    )
    if not aligned:
        keeps = [in_order(keep, order, slots) for keep, order in zip(keeps, orders)]
        sends = [in_order(send, order, slots) for send, order in zip(sends, orders)]
    scatter = Scatter(keeps, sends)
    hidden = [None, None]
    sources = [(state_local, state_in, params[0]), None]

    def next_hidden(layer, places, waiting):
        states, start, layer_params = sources[layer]
        for k in places:
            hidden[layer] = hidden_of(
                k, hidden[layer], states, start, keep, layer_params, rows, frames, width
            )
        hidden[layer], waiting = tie(hidden[layer], waiting)
        return waiting

    back = back_one(grads, deep_low, parts)
    scatter.received, (back,) = tie(scatter.received, [back])
    scatter.step()
    back_local, back_end = delta_one(back, keep, params[0], rows, frames, width, group)
    tall = 2 * rows
    carries = Exchange(
        flags,
        [(back_end, powers[0], True), (second_end, powers[1], False)],
        [jnp.concatenate(totals, axis=1).reshape(tall, -1)],
    )
    for k in range(2):
        carries.step()
        (carries.payload,) = next_hidden(0, [k], [carries.payload])
    scatter.received, (carries.payload,) = tie(scatter.received, [carries.payload])
    scatter.step()
    for k in range(2, 4):
        carries.step()
        (carries.payload,) = next_hidden(0, [k], [carries.payload])
    carries.step(len(carries.bits))
    scatter.received, (carries.payload, carries.before) = tie(
        scatter.received, [carries.payload, carries.before]
    )
    scatter.step()
    back_in, second_in = carries.arrived(0), carries.arrived(1)
    sources[1] = (second_local, second_in, params[1])
    total_two = carries.sums().reshape(1, padded)
    gate_low, sums_one = gate_one(
        proj_one, state_local, state_in, back_local, back_in, keep, params[0], stat_one, x,
        rows, frames, devices, feats,
    )
    scatter.received, (sums_one,) = tie(scatter.received, [sums_one])
    while scatter.orders[0]:
        scatter.step()
    decay_two = jnp.sum(second_decay[:rows] + second_decay[rows:] * second_in, axis=0, keepdims=True)
    spread = SumSpread(
        sums_one + jnp.pad(decay_two, ((feats + 3, SIDE - feats - 4), (0, 0)))
    )
    spread.step()
    scatter.received, (spread.value,) = tie(scatter.received, [spread.value])
    mine = lax.axis_index("tm")
    place = mine // (2 * side_bit()) * side_bit() + mine % side_bit()
    place = (side[0] * (devices // 2) + place) * slots
    mean_own = lax.dynamic_slice_in_dim(mean_one[0], place, slots)[:, None]
    grad_parts = [
        part + mean_own * total_two[:, first : first + lanes]
        for (first, lanes), part in zip(parts, scatter.result())
    ]
    gather = Gather(
        [
            (MUON_BETA * momentum_block[:, first : first + lanes] + part).astype(jnp.bfloat16)
            for (first, lanes), part in zip(parts, grad_parts)
        ],
        True,
    )
    for count_steps, places in ((1, []), (2, []), (3, [0, 1]), (2, [2, 3])):
        gather.step()
        spread.step(count_steps)
        if places:
            (spread.value,) = next_hidden(1, places, [spread.value])
        gather.current, (spread.value,) = tie(gather.current, [spread.value])
    while gather.orders[0]:
        gather.step()
    own, other = gather.result()
    spread.step(len(spread.steps))
    (hidden_one,), (hidden_two,) = hidden
    sums_one = spread.value
    shallow_grad, shallow_next, shallow_new, shallow_low = shallow_step(
        sums_one, gram, params[0], stat_one, shallow_weight, shallow_momentum,
        count * devices, count,
    )
    input_back = input_grad_of(
        gate_low, proj_one, params[0], stat_one, sums_one, shallow_weight, rows, frames, devices
    )
    input_grad = jnp.swapaxes(input_back.reshape(frames, rows, feats), 0, 1)
    grad_block = jnp.concatenate(grad_parts, axis=1)

    shard = deep_weight.shape[0]
    heads = own_heads(shard, width, padded)
    ortho = newton_rows(own, other, parts, heads)
    deep_ortho = own_flat(ortho[:, :width], shard, width, padded)
    deep_new = MUON_KEEP * deep_weight - MUON_RATE * deep_ortho.astype(jnp.float32)
    deep_grad = from_block(grad_block[:, :width], shard, padded)
    deep_next = MUON_BETA * deep_momentum + deep_grad

    unit_sums = sums_one[feats : feats + 4, :width]
    bias_gain_two = sums_two[:, :width]
    slope = jnp.where(
        1.0 - jnp.exp(-unit_params[:, 0]) > DECAY_FLOOR, jnp.exp(-unit_params[:, 0]), 0.0
    )
    unit_grad = jnp.stack(
        [
            jnp.stack([unit_sums[2] * slope[0], unit_sums[0], unit_sums[1], unit_sums[0]]),
            jnp.stack(
                [unit_sums[3] * slope[1], bias_gain_two[0], bias_gain_two[1], bias_gain_two[0]]
            ),
        ]
    )
    first_fix = 1.0 - FIRST_DECAY**STEP
    second_fix = 1.0 - SECOND_DECAY**STEP
    first_new = FIRST_DECAY * unit_first + (1.0 - FIRST_DECAY) * unit_grad
    second_new = SECOND_DECAY * unit_second + (1.0 - SECOND_DECAY) * unit_grad * unit_grad
    params_new = unit_params - ADAM_RATE * (first_new / first_fix) / (
        jnp.sqrt(second_new / second_fix) + ADAM_EPSILON
    )
    return (
        hidden_one.reshape(rows, frames, width),
        hidden_two.reshape(rows, frames, width),
        input_grad,
        shallow_grad,
        shallow_next,
        shallow_new,
        shallow_low,
        deep_grad,
        deep_next,
        deep_new,
        deep_new.astype(jnp.bfloat16),
        first_new,
        second_new,
        params_new,
    )


def solution(mesh):
    in_specs = (
        P(None, "tm", None),
        P(None, "tm"),
        P(),
        P(),
        P("tm"),
        P("tm"),
        P(),
        P(),
        P(),
        P(None, "tm", None),
    )
    out_specs = (
        P(None, "tm", None),
        P(None, "tm", None),
        P(None, "tm", None),
        P(),
        P(),
        P(),
        P(),
        P("tm"),
        P("tm"),
        P("tm"),
        P("tm"),
        P(),
        P(),
        P(),
    )
    return jax.shard_map(
        per_device, mesh=mesh, in_specs=in_specs, out_specs=out_specs, check_vma=False
    )
```

```python
import functools

import jax
import jax.numpy as jnp
from jax import lax
from jax.experimental import pallas as pl
from jax.experimental.pallas import tpu as pltpu
from jax.sharding import PartitionSpec as P

NS_STEPS = 2
STEP = 5


NORM_EPSILON = 1e-05
MUON_EPSILON = 1e-07
COEFF_A = 3.4445
COEFF_B = -4.775
COEFF_C = 2.0315
MUON_BETA = 0.5
MUON_RATE = 4.0
MUON_KEEP = 0.999
FIRST_DECAY = 0.9
SECOND_DECAY = 0.95
ADAM_RATE = 0.5
ADAM_EPSILON = 1e-08
DECAY_FLOOR = 0.9
LANE = 128
WIDE = 512
PART = 256
SIDE = 80


def kernel_call(body, grid, in_specs, out_specs, out_shape, scratch=(), flops=0, traffic=0):
    return pl.pallas_call(
        body,
        grid=grid,
        in_specs=in_specs,
        out_specs=out_specs,
        out_shape=out_shape,
        scratch_shapes=list(scratch),
        compiler_params=pltpu.CompilerParams(vmem_limit_bytes=56 * 1024 * 1024),
        cost_estimate=pl.CostEstimate(flops=flops, bytes_accessed=traffic, transcendentals=0),
    )


def shape_of(shape, dtype=jnp.float32):
    return jax.ShapeDtypeStruct(shape, dtype)


def whole(shape):
    return pl.BlockSpec(shape, lambda i: (0,) * len(shape))


def lanes_of(rows, width=WIDE):
    return pl.BlockSpec((rows, width), lambda i: (0, i))


def chunk_call(body, place, in_specs, out_specs, out_shape, arrays, previous, scratch=(), traffic=0):
    count = len(in_specs)
    before = list(previous) if previous is not None else []

    def run(*refs):
        body(*refs[:count], *refs[count + len(before) :])

    return pl.pallas_call(
        run,
        grid=(1,),
        in_specs=list(in_specs) + [pl.BlockSpec(memory_space=pl.ANY)] * len(before),
        out_specs=out_specs,
        out_shape=out_shape,
        scratch_shapes=list(scratch),
        input_output_aliases={count + k: k for k in range(len(before))},
        compiler_params=pltpu.CompilerParams(vmem_limit_bytes=56 * 1024 * 1024),
        cost_estimate=pl.CostEstimate(flops=0, bytes_accessed=traffic, transcendentals=0),
    )(*arrays, *before)


def chunk_at(rows, place):
    return pl.BlockSpec((rows, WIDE), lambda i: (0, place))


def rate_of(params):
    return jnp.maximum(1.0 - jnp.exp(-params[0:1]), DECAY_FLOOR)


def softened(value):
    return jnp.maximum(value, 0.0) + jnp.log(1.0 + jnp.exp(-jnp.abs(value)))


def sigmoid(value):
    return 0.5 * jnp.tanh(0.5 * value) + 0.5


def wide_keep(keep_ref, t, rows):
    keep = keep_ref[pl.ds(pl.multiple_of(t * rows, rows), rows), :]
    return jnp.concatenate([keep] * (WIDE // LANE), axis=1)


def rows_at(ref, t, rows):
    return ref[pl.ds(pl.multiple_of(t * rows, rows), rows), :]


def store_at(ref, t, rows, value):
    ref[pl.ds(pl.multiple_of(t * rows, rows), rows), :] = value


def valid_lanes(shape, total, step):
    return lax.broadcasted_iota(jnp.int32, shape, 1) + step * WIDE < total


def unit_terms(params_ref, stat_ref, total_devices, frames):
    params = params_ref[...]
    stat = stat_ref[...]
    centre = stat[0:1]
    inverse = lax.rsqrt(stat[1:2] / (total_devices * frames) + NORM_EPSILON)
    return centre, inverse, params[2:3], params[3:4] + params[1:2]


def front_body(rows, frames, width, x_ref, w_ref, xt_ref, proj_ref, stat_ref, gram_ref, padded_w):
    step = pl.program_id(0)
    count, feats = x_ref.shape

    @pl.when(step == 0)
    def _():
        i = lax.broadcasted_iota(jnp.int32, (count, count), 0)
        j = lax.broadcasted_iota(jnp.int32, (count, count), 1)
        move = (j == lax.rem(i, rows) * frames + lax.div(i, rows)).astype(jnp.bfloat16)
        moved = jnp.dot(move, x_ref[...], preferred_element_type=jnp.float32).astype(jnp.bfloat16)
        i = lax.broadcasted_iota(jnp.int32, (feats, LANE), 0)
        j = lax.broadcasted_iota(jnp.int32, (feats, LANE), 1)
        wide = jnp.dot(moved, (i == j).astype(jnp.bfloat16), preferred_element_type=jnp.float32)
        lane = lax.broadcasted_iota(jnp.int32, (count, LANE), 1)
        xt = jnp.where(lane == feats, 1.0, wide).astype(jnp.bfloat16)
        xt_ref[...] = xt
        gram = dot_tn(xt, xt)
        high = gram_ref.shape[0]
        for k in range(SIDE // high):
            gram_ref[:, k * LANE : (k + 1) * LANE] = gram[k * high : (k + 1) * high]
        padded_w[...] = jnp.zeros_like(padded_w)

    weight = w_ref[...]
    padded_w[0:feats, :] = jnp.where(valid_lanes(weight.shape, width, step), weight, 0.0)
    proj = jnp.dot(
        xt_ref[...], padded_w[...].astype(jnp.bfloat16), preferred_element_type=jnp.float32
    )
    proj_ref[...] = proj
    mean = jnp.sum(proj, axis=0, keepdims=True) * (1.0 / count)
    off = proj - mean
    stat_ref[0:1, :] = mean
    stat_ref[1:2, :] = jnp.sum(off * off, axis=0, keepdims=True)


def dot_tn(a, b):
    return lax.dot_general(a, b, (((0,), (0,)), ((), ())), preferred_element_type=jnp.float32)


def front(x, weight, rows, frames):
    count, feats = x.shape
    width = weight.shape[1]
    padded = -(-width // WIDE) * WIDE
    return kernel_call(
        functools.partial(front_body, rows, frames, width),
        (padded // WIDE,),
        [whole((count, feats)), lanes_of(feats)],
        [whole((count, LANE)), lanes_of(count), lanes_of(2), whole((2 * rows, SIDE // (2 * rows) * LANE))],
        [
            shape_of((count, LANE), jnp.bfloat16),
            shape_of((count, padded)),
            shape_of((2, padded)),
            shape_of((2 * rows, SIDE // (2 * rows) * LANE)),
        ],
        [pltpu.VMEM((LANE, WIDE), jnp.float32)],
    )(x, weight)


def delta_two_body(rows, frames, width, place, grad_ref, keep_ref, params_ref, delta_ref, end_ref, held):
    pieces = WIDE // LANE
    mask = valid_lanes((rows * frames, WIDE), width, place)
    grad = jnp.where(mask, grad_ref[...].astype(jnp.float32), 0.0)
    for g in range(pieces):
        held[g] = grad[:, g * LANE : (g + 1) * LANE]
    rate = rate_of(params_ref[...])

    def body(k, carried):
        t = frames - 1 - k
        own = jnp.concatenate(
            [held[g, pl.ds(t, rows, stride=frames), :] for g in range(pieces)], axis=1
        )
        delta = own + carried
        store_at(delta_ref, t, rows, delta)
        return rate * wide_keep(keep_ref, t, rows) * delta

    end_ref[...] = lax.fori_loop(
        0, frames, body, jnp.zeros((rows, WIDE), jnp.float32), unroll=8
    )


def delta_two(place, previous, out_grad, keep, params, rows, frames, padded):
    count, width = out_grad.shape
    return chunk_call(
        functools.partial(delta_two_body, rows, frames, width, place),
        place,
        [chunk_at(count, place), whole((count, LANE)), chunk_at(4, place)],
        [chunk_at(count, place), chunk_at(rows, place)],
        [shape_of((count, padded)), shape_of((rows, padded))],
        (out_grad, keep, params),
        previous,
        [pltpu.VMEM((WIDE // LANE, count, LANE), jnp.float32)],
    )


def states_body(
    rows, frames, devices, proj_ref, keep_ref, params_ref, stat_ref, state_ref, end_ref
):
    centre, inverse, gain, offset = unit_terms(params_ref, stat_ref, devices, rows * frames)
    rate = rate_of(params_ref[...])
    share = 1.0 - rate

    def body(t, carried):
        gate = (rows_at(proj_ref, t, rows) - centre) * inverse * gain + offset
        soft = softened(gate)
        carried = rate * wide_keep(keep_ref, t, rows) * carried + share * soft
        store_at(state_ref, t, rows, carried)
        return carried

    end_ref[...] = lax.fori_loop(
        0, frames, body, jnp.zeros((rows, WIDE), jnp.float32), unroll=8
    )


def local_states(proj, keep, params, stat, rows, frames, devices):
    count, padded = proj.shape
    return kernel_call(
        functools.partial(states_body, rows, frames, devices),
        (padded // WIDE,),
        [lanes_of(count), whole((count, LANE)), lanes_of(4), lanes_of(2)],
        [lanes_of(count), lanes_of(rows)],
        [shape_of((count, padded)), shape_of((rows, padded))],
    )(proj, keep, params, stat)


def to_slots(value, group):
    pieces = value.shape[1] // LANE
    lane = lax.broadcasted_iota(jnp.int32, (value.shape[0], LANE), 1)
    parts = [value[:, g * LANE : (g + 1) * LANE] for g in range(pieces)]
    out = []
    for g in range(pieces):
        moved = (LANE - group) * g
        if moved == 0:
            new = parts[g]
        else:
            new = jnp.where(
                lane < moved, pltpu.roll(parts[g - 1], moved, 1), pltpu.roll(parts[g], moved, 1)
            )
        out.append(jnp.where(lane < group, new, 0.0))
    half = LANE // 2
    low = [
        jnp.where(lane < half, out[g], pltpu.roll(out[g + 1], half, 1)) for g in range(0, pieces, 2)
    ]
    high = [
        jnp.where(lane < half, pltpu.roll(out[g], half, 1), out[g + 1]) for g in range(0, pieces, 2)
    ]
    return jnp.concatenate(low + high, axis=1)


def from_slots(value, group, width):
    pieces = value.shape[1] // LANE
    lane = lax.broadcasted_iota(jnp.int32, (value.shape[0], LANE), 1)
    half = LANE // 2
    parts = []
    for g in range(pieces // 2):
        low = value[:, g * LANE : (g + 1) * LANE]
        high = value[:, (g + pieces // 2) * LANE : (g + pieces // 2 + 1) * LANE]
        parts.append(jnp.where(lane < half, low, pltpu.roll(high, half, 1)))
        parts.append(jnp.where(lane < half, pltpu.roll(low, half, 1), high))
    out = []
    for j in range(pieces):
        moved = (LANE - group) * j
        new = parts[j] if moved == 0 else pltpu.roll(parts[j], LANE - moved, 1)
        if j + 1 < pieces:
            new = jnp.where(lane < group - moved, new, pltpu.roll(parts[j + 1], group - moved, 1))
        left = width - j * LANE
        out.append(new if left >= LANE else jnp.where(lane < left, new, 0.0))
    return jnp.concatenate(out, axis=1)


def low_one_body(rows, frames, width, group, state_ref, start_ref, keep_ref, params_ref, low_ref, mean_ref):
    pieces = state_ref.shape[1] // LANE
    rate = rate_of(params_ref[...])

    def advance(t, carried):
        keep = rows_at(keep_ref, t, rows)
        carried = rate * jnp.concatenate([keep] * pieces, axis=1) * carried
        return carried, rows_at(state_ref, t, rows) + carried

    def body(k, both):
        carried, total = both
        t = 2 * k
        carried, first = advance(t, carried)
        carried, second = advance(t + 1, carried)
        place = pl.ds(pl.multiple_of(t * rows, 2 * rows), 2 * rows)
        slots = to_slots(jnp.concatenate([first, second], axis=0), group)
        low_ref[place, :] = slots.astype(jnp.bfloat16)
        return carried, total + slots[:rows] + slots[rows:]

    start = start_ref[...]
    _, total = lax.fori_loop(0, frames // 2, body, (start, jnp.zeros_like(start)), unroll=2)
    mean_ref[...] = jnp.sum(total, axis=0, keepdims=True) * (1.0 / (rows * frames))


def low_one_of(states, start, keep, params, rows, frames, width, group):
    count, padded = states.shape
    return kernel_call(
        functools.partial(low_one_body, rows, frames, width, group),
        (1,),
        [whole((count, padded)), whole((rows, padded)), whole((count, LANE)), whole((4, padded))],
        [whole((count, padded)), whole((1, padded))],
        [shape_of((count, padded), jnp.bfloat16), shape_of((1, padded))],
    )(states, start, keep, params)


def hidden_body(rows, frames, state_ref, start_ref, keep_ref, params_ref, hidden_ref, held):
    pieces = WIDE // LANE
    rate = rate_of(params_ref[...])

    def body(t, carry):
        carry = rate * wide_keep(keep_ref, t, rows) * carry
        state = rows_at(state_ref, t, rows) + carry
        for g in range(pieces):
            held[g, pl.ds(pl.multiple_of(t * rows, rows), rows), :] = state[
                :, g * LANE : (g + 1) * LANE
            ]
        return carry

    lax.fori_loop(0, frames, body, start_ref[...], unroll=8)
    for r in range(rows):
        for g in range(pieces):
            hidden_ref[r * frames : (r + 1) * frames, g * LANE : (g + 1) * LANE] = held[
                g, pl.ds(r, frames, stride=rows), :
            ]


def hidden_of(place, previous, states, start, keep, params, rows, frames, width):
    count, _ = states.shape
    return chunk_call(
        functools.partial(hidden_body, rows, frames),
        place,
        [chunk_at(count, place), chunk_at(rows, place), whole((count, LANE)), chunk_at(4, place)],
        [chunk_at(count, place)],
        [shape_of((count, width))],
        (states, start, keep, params),
        previous,
        [pltpu.VMEM((WIDE // LANE, count, LANE), jnp.float32)],
    )


def second_body(parts, last, side_ref, low_ref, *refs):
    weights = refs[: len(parts)]
    held, sems = refs[-2:]
    outs = refs[len(parts) : -2]
    half = held.shape[0]
    copies = [
        pltpu.make_async_copy(weights[p], held.at[:, first : first + lanes], sems.at[p])
        for p, (first, lanes) in enumerate(parts)
    ]
    for copy in copies:
        copy.start()
    side = (1 - side_ref[0]) if last else side_ref[0]
    low = low_ref[:, pl.ds(pl.multiple_of(side * half, half), half)]
    for copy, (first, lanes) in zip(copies, parts):
        copy.wait()
        proj = jnp.dot(
            low, held[:, first : first + lanes], preferred_element_type=jnp.float32
        )
        if not last:
            outs[0][:, first : first + lanes] = proj
            continue
        before_ref, proj_ref, stat_ref = outs
        proj += before_ref[:, first : first + lanes]
        proj_ref[:, first : first + lanes] = proj
        mean = jnp.sum(proj, axis=0, keepdims=True) * (1.0 / proj.shape[0])
        off = proj - mean
        stat_ref[0:1, first : first + lanes] = mean
        stat_ref[1:2, first : first + lanes] = jnp.sum(off * off, axis=0, keepdims=True)


def second_forward(side, low, weights, parts, before=None):
    count, padded = low.shape
    last = before is not None
    some = whole((count, padded))
    return kernel_call(
        functools.partial(second_body, parts, last),
        (1,),
        [pl.BlockSpec(memory_space=pltpu.SMEM), some]
        + [pl.BlockSpec(memory_space=pl.ANY)] * len(parts)
        + [some] * last,
        [some] + [whole((2, padded))] * last,
        [shape_of((count, padded))] + [shape_of((2, padded))] * last,
        [
            pltpu.VMEM((padded // 2, padded), jnp.bfloat16),
            pltpu.SemaphoreType.DMA((len(parts),)),
        ],
    )(side, low, *weights, *([before] if last else []))


def gate_two_body(
    rows, frames, devices, proj_ref, delta_ref, start_ref, keep_ref, params_ref, stat_ref, gate_ref, sums_ref
):
    centre, inverse, gain, offset = unit_terms(params_ref, stat_ref, devices, rows * frames)
    rate = rate_of(params_ref[...])
    share = 1.0 - rate
    none = jnp.zeros((rows, WIDE), jnp.float32)

    def body(k, carried):
        carry, bias_sum, gain_sum = carried
        t = frames - 1 - k
        delta = rows_at(delta_ref, t, rows) + carry
        normed = (rows_at(proj_ref, t, rows) - centre) * inverse
        gate = share * delta * sigmoid(normed * gain + offset)
        store_at(gate_ref, t, rows, gate)
        carry = rate * wide_keep(keep_ref, t, rows) * carry
        return carry, bias_sum + gate, gain_sum + gate * normed

    _, bias_sum, gain_sum = lax.fori_loop(
        0, frames, body, (start_ref[...], none, none), unroll=8
    )
    sums_ref[0:1, :] = jnp.sum(bias_sum, axis=0, keepdims=True)
    sums_ref[1:2, :] = jnp.sum(gain_sum, axis=0, keepdims=True)


def gate_two(proj, delta, start, keep, params, stat, rows, frames, devices):
    count, padded = proj.shape
    return kernel_call(
        functools.partial(gate_two_body, rows, frames, devices),
        (padded // WIDE,),
        [lanes_of(count), lanes_of(count), lanes_of(rows), whole((count, LANE)), lanes_of(4), lanes_of(2)],
        [lanes_of(count), lanes_of(2)],
        [shape_of((count, padded)), shape_of((2, padded))],
    )(proj, delta, start, keep, params, stat)


def states_two_body(
    rows, frames, devices, proj_ref, delta_ref, start_ref, keep_ref, params_ref, stat_ref,
    state_ref, end_ref, decay_ref, held,
):
    centre, inverse, gain, offset = unit_terms(params_ref, stat_ref, devices, rows * frames)
    rate = rate_of(params_ref[...])
    share = 1.0 - rate
    none = jnp.zeros((rows, WIDE), jnp.float32)

    def backward(k, carry):
        t = frames - 1 - k
        store_at(held, t, rows, rows_at(delta_ref, t, rows) + carry)
        return rate * wide_keep(keep_ref, t, rows) * carry

    lax.fori_loop(0, frames, backward, start_ref[...], unroll=8)

    def forward(t, carried):
        state, reach, decay, factor = carried
        keep = wide_keep(keep_ref, t, rows)
        delta = rows_at(held, t, rows)
        value = (rows_at(proj_ref, t, rows) - centre) * inverse * gain + offset
        soft = softened(value)
        decay = decay + delta * (keep * state - soft)
        factor = factor + delta * keep * reach
        state = rate * keep * state + share * soft
        reach = rate * keep * reach
        store_at(state_ref, t, rows, state)
        return state, reach, decay, factor

    state, _, decay, factor = lax.fori_loop(
        0, frames, forward, (none, jnp.ones_like(none), none, none), unroll=4
    )
    end_ref[...] = state
    decay_ref[0:rows, :] = decay
    decay_ref[rows : 2 * rows, :] = factor


def states_two(proj, delta, start, keep, params, stat, rows, frames, devices):
    count, padded = proj.shape
    return kernel_call(
        functools.partial(states_two_body, rows, frames, devices),
        (padded // WIDE,),
        [
            lanes_of(count),
            lanes_of(count),
            lanes_of(rows),
            whole((count, LANE)),
            lanes_of(4),
            lanes_of(2),
        ],
        [lanes_of(count), lanes_of(rows), lanes_of(2 * rows)],
        [shape_of((count, padded)), shape_of((rows, padded)), shape_of((2 * rows, padded))],
        [pltpu.VMEM((count, WIDE), jnp.float32)],
    )(proj, delta, start, keep, params, stat)


def turn_body(low_ref, mean_ref, turned_ref):
    turned_ref[...] = (low_ref[...].astype(jnp.float32) - mean_ref[...]).T.astype(jnp.bfloat16)


def turn(place, previous, low, mean):
    count, padded = low.shape
    return chunk_call(
        turn_body,
        place,
        [chunk_at(count, place), chunk_at(1, place)],
        [pl.BlockSpec((WIDE, count), lambda i: (place, 0))],
        [shape_of((padded, count), jnp.bfloat16)],
        (low, mean),
        previous,
    )


def deep_term_body(
    rows, frames, devices, parts, orders, side_ref, gate_ref, proj_ref, params_ref, stat_ref, sums_ref,
    turned_ref, grad_ref, total_ref, *outs,
):
    step = pl.program_id(0)
    total = devices * rows * frames
    centre, inverse, gain, _ = unit_terms(params_ref, stat_ref, devices, rows * frames)
    sums = sums_ref[...] * (1.0 / total)
    normed = (proj_ref[...] - centre) * inverse
    grad = (gain * inverse * (gate_ref[...] - sums[0:1] - normed * sums[1:2])).astype(jnp.bfloat16)
    grad_ref[...] = grad
    total_ref[...] = jnp.sum(grad.astype(jnp.float32), axis=0, keepdims=True)
    side = side_ref[0]
    half = turned_ref.shape[0] // 2
    tile = 256
    for p, (first, lanes) in enumerate(parts):

        @pl.when((step >= first // PART) & (step < (first + lanes) // PART))
        def _():
            for which, out_ref in ((side, outs[p]), (1 - side, outs[len(parts) + p])):
                for k in range(half // tile):
                    start = pl.multiple_of(which * half + k * tile, tile)
                    part = jnp.dot(
                        turned_ref[pl.ds(start, tile), :],
                        grad_ref[...],
                        preferred_element_type=jnp.float32,
                    ).astype(out_ref.dtype)
                    if orders is None:
                        out_ref[k * tile : (k + 1) * tile, :] = part
                        continue
                    slots = half // 2 ** len(orders[p])
                    for b in range(tile // slots):
                        block = k * (tile // slots) + b
                        place = 0
                        for weight in orders[p]:
                            place = 2 * place + block // weight % 2
                        out_ref[place * slots : (place + 1) * slots, :] = part[
                            b * slots : (b + 1) * slots
                        ]


def deep_term(parts, orders, side, gate, proj, params, stat, sums, turned, rows, frames, devices):
    count, padded = proj.shape
    half = padded // 2

    def some(first, lanes):
        return pl.BlockSpec(
            (half, PART), lambda i: (0, jnp.clip(i - first // PART, 0, lanes // PART - 1))
        )

    found = kernel_call(
        functools.partial(deep_term_body, rows, frames, devices, parts, orders),
        (padded // PART,),
        [
            pl.BlockSpec(memory_space=pltpu.SMEM),
            lanes_of(count, PART),
            lanes_of(count, PART),
            lanes_of(4, PART),
            lanes_of(2, PART),
            lanes_of(2, PART),
            whole((padded, count)),
        ],
        [lanes_of(count, PART), lanes_of(1, PART)] + [some(*part) for part in parts] * 2,
        [shape_of((count, padded), jnp.bfloat16), shape_of((1, padded))]
        + [shape_of((half, lanes)) for _, lanes in parts]
        + [shape_of((half, lanes), jnp.bfloat16) for _, lanes in parts],
    )(side, gate, proj, params, stat, sums, turned)
    return found[0], found[1], found[2 : 2 + len(parts)], found[2 + len(parts) :]


def back_body(parts, grad_ref, *refs):
    for side, back_ref in enumerate(refs[2 * len(parts) :]):
        total = 0.0
        for p, (first, lanes) in enumerate(parts):
            total += dot_nt(grad_ref[:, first : first + lanes], refs[side * len(parts) + p][...])
        back_ref[...] = total


def back_one(grad, own, other, parts):
    count, padded = grad.shape
    half = padded // 2
    return kernel_call(
        functools.partial(back_body, parts),
        (half // PART,),
        [whole(grad.shape)]
        + [pl.BlockSpec((PART, lanes), lambda i: (i, 0)) for _, lanes in parts] * 2,
        [lanes_of(count, PART)] * 2,
        [shape_of((count, half))] * 2,
    )(grad, *own, *other)


def delta_one_body(
    rows, frames, width, group, side_ref, own_ref, other_ref, keep_ref, params_ref, delta_ref, end_ref
):
    padded = delta_ref.shape[1]
    rate = rate_of(params_ref[...])
    straight = side_ref[0] == 0

    def body(k, carried):
        t = frames - 1 - k
        own, other = rows_at(own_ref, t, rows), rows_at(other_ref, t, rows)
        both = jnp.concatenate(
            [jnp.where(straight, own, other), jnp.where(straight, other, own)], axis=1
        )
        delta = from_slots(both, group, width) + carried
        store_at(delta_ref, t, rows, delta)
        keep = rows_at(keep_ref, t, rows)
        return rate * jnp.concatenate([keep] * (padded // LANE), axis=1) * delta

    end_ref[...] = lax.fori_loop(0, frames, body, jnp.zeros((rows, padded), jnp.float32), unroll=2)


def delta_one(side, own, other, keep, params, rows, frames, width, group):
    count, half = own.shape
    padded = 2 * half
    return kernel_call(
        functools.partial(delta_one_body, rows, frames, width, group),
        (1,),
        [
            pl.BlockSpec(memory_space=pltpu.SMEM),
            whole((count, half)),
            whole((count, half)),
            whole((count, LANE)),
            whole((4, padded)),
        ],
        [whole((count, padded)), whole((rows, padded))],
        [shape_of((count, padded)), shape_of((rows, padded))],
    )(side, own, other, keep, params)


def gate_one_body(
    rows,
    frames,
    devices,
    feats,
    proj_ref,
    state_ref,
    first_ref,
    delta_ref,
    start_ref,
    keep_ref,
    params_ref,
    stat_ref,
    x_ref,
    gate_ref,
    sums_ref,
    held,
):
    centre, inverse, gain, offset = unit_terms(params_ref, stat_ref, devices, rows * frames)
    rate = rate_of(params_ref[...])
    share = 1.0 - rate
    none = jnp.zeros((rows, WIDE), jnp.float32)

    def backward(k, carry):
        t = frames - 1 - k
        store_at(held, t, rows, rows_at(delta_ref, t, rows) + carry)
        return rate * wide_keep(keep_ref, t, rows) * carry

    lax.fori_loop(0, frames, backward, start_ref[...], unroll=8)

    def forward(t, carried):
        carry, before, bias_sum, gain_sum, decay_sum = carried
        keep = wide_keep(keep_ref, t, rows)
        delta = rows_at(held, t, rows)
        normed = (rows_at(proj_ref, t, rows) - centre) * inverse
        value = normed * gain + offset
        soft = softened(value)
        gate = share * delta * sigmoid(value)
        store_at(gate_ref, t, rows, gate)
        decay_sum = decay_sum + delta * (keep * before - soft)
        carry = rate * keep * carry
        before = rows_at(state_ref, t, rows) + carry
        return carry, before, bias_sum + gate, gain_sum + gate * normed, decay_sum

    first = first_ref[...]
    _, _, bias_sum, gain_sum, decay_sum = lax.fori_loop(
        0, frames, forward, (first, first, none, none, none), unroll=4
    )
    bias = jnp.sum(bias_sum, axis=0, keepdims=True)
    mean = bias * (1.0 / (rows * frames))
    x = x_ref[...]
    ones = jnp.ones((rows * frames, LANE), jnp.bfloat16)
    total = jnp.concatenate([dot_tn(x, ones)] * (WIDE // LANE), axis=1)
    term = dot_tn(x, (gate_ref[...] - mean).astype(jnp.bfloat16)) + total * mean
    sums_ref[...] = term[: sums_ref.shape[0]]
    sums_ref[feats : feats + 1, :] = bias
    sums_ref[feats + 1 : feats + 2, :] = jnp.sum(gain_sum, axis=0, keepdims=True)
    sums_ref[feats + 2 : feats + 3, :] = jnp.sum(decay_sum, axis=0, keepdims=True)


def gate_one(proj, states, first, delta, start, keep, params, stat, x, rows, frames, devices, feats):
    count, padded = proj.shape
    return kernel_call(
        functools.partial(gate_one_body, rows, frames, devices, feats),
        (padded // WIDE,),
        [
            lanes_of(count),
            lanes_of(count),
            lanes_of(rows),
            lanes_of(count),
            lanes_of(rows),
            whole((count, LANE)),
            lanes_of(4),
            lanes_of(2),
            whole((count, LANE)),
        ],
        [lanes_of(count), lanes_of(SIDE)],
        [shape_of((count, padded)), shape_of((SIDE, padded))],
        [pltpu.VMEM((count, WIDE), jnp.float32)],
    )(proj, states, first, delta, start, keep, params, stat, x)


def input_grad_body(
    rows, frames, devices, width, feats, gate_ref, proj_ref, params_ref, stat_ref, sums_ref, w_ref, back_ref
):
    step = pl.program_id(0)
    total = devices * rows * frames
    centre, inverse, gain, _ = unit_terms(params_ref, stat_ref, devices, rows * frames)
    bias = sums_ref[feats : feats + 1, :] * (1.0 / total)
    slope = sums_ref[feats + 1 : feats + 2, :] * (1.0 / total)
    normed = (proj_ref[...] - centre) * inverse
    grad = (gain * inverse * (gate_ref[...] - bias - normed * slope)).astype(jnp.bfloat16)
    weight = w_ref[...]
    weight = jnp.where(valid_lanes(weight.shape, width, step), weight, 0.0).astype(jnp.bfloat16)
    part = dot_nt(grad, weight)

    @pl.when(step == 0)
    def _():
        back_ref[...] = part

    @pl.when(step > 0)
    def _():
        back_ref[...] += part


def input_grad_of(gate, proj, params, stat, sums, weight, rows, frames, devices):
    count, padded = proj.shape
    feats, width = weight.shape
    return kernel_call(
        functools.partial(input_grad_body, rows, frames, devices, width, feats),
        (padded // WIDE,),
        [lanes_of(count), lanes_of(count), lanes_of(4), lanes_of(2), lanes_of(SIDE), lanes_of(feats)],
        whole((count, feats)),
        shape_of((count, feats)),
    )(gate, proj, params, stat, sums, weight)


def dot_nt(a, b):
    return lax.dot_general(a, b, (((1,), (1,)), ((), ())), preferred_element_type=jnp.float32)


def shallow_body(
    total, frames, sums_ref, gram_ref, params_ref, stat_ref, w_ref, m_ref,
    grad_ref, next_ref, new_ref, low_ref, held,
):
    feats, width = w_ref.shape
    centre, inverse, gain, _ = unit_terms(params_ref, stat_ref, total // frames, frames)
    weight = w_ref[...]
    held[...] = jnp.zeros_like(held)
    held[0:feats, 0:width] = weight
    high = gram_ref.shape[0]
    gram = jnp.concatenate(
        [gram_ref[:, k * LANE : (k + 1) * LANE] for k in range(SIDE // high)], axis=0
    )
    lane = lax.broadcasted_iota(jnp.int32, gram.shape, 1)
    x_sum = jnp.sum(jnp.where(lane == feats, gram, 0.0), axis=1, keepdims=True)
    raw = jnp.dot(
        gram[:, :SIDE],
        held[...].astype(jnp.bfloat16).astype(jnp.float32),
        precision=lax.Precision.HIGHEST,
        preferred_element_type=jnp.float32,
    )
    normed = (raw - x_sum * centre) * inverse
    bias = sums_ref[feats : feats + 1, :] * (1.0 / total)
    slope = sums_ref[feats + 1 : feats + 2, :] * (1.0 / total)
    grad = gain * inverse * (sums_ref[...] - x_sum * bias - normed * slope)
    grad = grad[:feats, :width]
    grad_ref[...] = grad
    following = MUON_BETA * m_ref[...] + grad
    next_ref[...] = following
    held[0:feats, 0:width] = following
    m = held[...]
    current = (m / (jnp.sqrt(jnp.sum(m * m)) + MUON_EPSILON)).astype(jnp.bfloat16)
    for repeat in range(NS_STEPS):
        gram = dot_nt(current, current).astype(jnp.bfloat16)
        square = jnp.dot(gram, gram, preferred_element_type=jnp.float32)
        mixing = (COEFF_B * gram.astype(jnp.float32) + COEFF_C * square).astype(jnp.bfloat16)
        current = (
            COEFF_A * current.astype(jnp.float32)
            + jnp.dot(mixing, current, preferred_element_type=jnp.float32)
        ).astype(jnp.bfloat16)
    new = MUON_KEEP * weight - MUON_RATE * current[:feats, :width].astype(jnp.float32)
    new_ref[...] = new
    low_ref[...] = new.astype(jnp.bfloat16)


def shallow_step(sums, gram, params, stat, weight, momentum, total, frames):
    padded = sums.shape[1]
    some = shape_of(weight.shape)
    return kernel_call(
        functools.partial(shallow_body, total, frames),
        (1,),
        [whole(value.shape) for value in (sums, gram, params, stat, weight, momentum)],
        [whole(weight.shape)] * 4,
        [some, some, some, shape_of(weight.shape, jnp.bfloat16)],
        [pltpu.VMEM((SIDE, padded), jnp.float32)],
    )(sums, gram, params, stat, weight, momentum)


def newton_body(parts, heads, tile, *refs):
    blocks_refs, out_ref = refs[: 2 * len(parts)], refs[2 * len(parts)]
    m_ref, gram, mixing, sems = refs[2 * len(parts) + 1 :]
    size = m_ref.shape[0]
    half = size // 2
    blocks = size // tile
    copies = []
    for side in range(2):
        for p, (first, lanes) in enumerate(parts):
            copies.append(
                pltpu.make_async_copy(
                    blocks_refs[side * len(parts) + p],
                    m_ref.at[side * half : (side + 1) * half, first : first + lanes],
                    sems.at[side * len(parts) + p],
                )
            )
    for copy in copies:
        copy.start()
    for copy in copies:
        copy.wait()

    def place(k):
        return slice(k * tile, (k + 1) * tile)

    squares = jnp.zeros((8, size), jnp.float32)
    for k in range(blocks):
        value = m_ref[place(k), :].astype(jnp.float32)
        squares = squares + jnp.sum((value * value).reshape(tile // 8, 8, size), axis=0)
    scale = 1.0 / (jnp.sqrt(jnp.sum(squares)) + MUON_EPSILON)
    square_scale = scale * scale

    def gram_block(i, j):
        part = dot_nt(m_ref[place(i), :], m_ref[place(j), :]) * square_scale
        gram[place(i), place(j)] = part.astype(jnp.bfloat16)
        if i != j:
            gram[place(j), place(i)] = part.T.astype(jnp.bfloat16)

    for i in range(blocks):
        for j in range(i, blocks):
            gram_block(i, j)
    for i in range(blocks):
        for j in range(i, blocks):
            part = dot_nt(gram[place(i), :], gram[place(j), :])
            part = COEFF_B * gram[place(i), place(j)].astype(jnp.float32) + COEFF_C * part
            mixing[place(i), place(j)] = part.astype(jnp.bfloat16)
            if i != j:
                mixing[place(j), place(i)] = part.T.astype(jnp.bfloat16)

    def taken(ref):
        return jnp.concatenate([ref[first : first + count, :] for first, count in heads], axis=0)

    def times(value, ref):
        return jnp.dot(value.astype(jnp.bfloat16), ref[...], preferred_element_type=jnp.float32)

    def stepped(value):
        return COEFF_A * value + times(value, mixing)

    mixing_own = taken(mixing)
    gram_own = taken(gram).astype(jnp.float32)
    gram_own = stepped(COEFF_A * gram_own + times(mixing_own, gram))
    square_own = stepped(times(stepped(gram_own), gram))
    second_own = COEFF_B * gram_own + COEFF_C * square_own
    weights = COEFF_A * mixing_own.astype(jnp.float32) + stepped(second_own)
    result = COEFF_A * COEFF_A * taken(m_ref).astype(jnp.float32) + times(weights, m_ref)
    out_ref[...] = (scale * result).astype(jnp.bfloat16)


def newton_rows(own, other, parts, heads):
    size = 2 * own[0].shape[0]
    window = sum(count for _, count in heads)
    anywhere = pl.BlockSpec(memory_space=pl.ANY)
    return kernel_call(
        functools.partial(newton_body, parts, heads, 256),
        (1,),
        [anywhere] * (2 * len(parts)),
        whole((window, size)),
        shape_of((window, size), jnp.bfloat16),
        [pltpu.VMEM((size, size), jnp.bfloat16)] * 3 + [pltpu.SemaphoreType.DMA((2 * len(parts),))],
    )(*own, *other)


def swap(value, bit):
    size = lax.axis_size("tm")
    return lax.ppermute(value, "tm", [(i, i ^ bit) for i in range(size)])


def steps_of(size):
    bits = []
    bit = 1
    while bit < size:
        bits.append(bit)
        bit *= 2
    return bits


def bit_of(bit):
    return jnp.where((lax.axis_index("tm") & bit) != 0, 1, 0)


class SumSpread:
    def __init__(self, value):
        self.value = value
        self.steps = []
        lanes = value.shape[1]
        cuts = []
        for bit in steps_of(lax.axis_size("tm")):
            if lanes // 2 % LANE == 0:
                lanes //= 2
                self.steps.append((self.halve, bit))
                cuts.append(bit)
            else:
                self.steps.append((self.pair, bit))
        self.steps += [(self.join, bit) for bit in reversed(cuts)]

    def halve(self, bit):
        lanes = self.value.shape[1] // 2
        mine = lax.dynamic_slice_in_dim(self.value, bit_of(bit) * lanes, lanes, 1)
        away = lax.dynamic_slice_in_dim(self.value, (1 - bit_of(bit)) * lanes, lanes, 1)
        self.value = mine + swap(away, bit)

    def pair(self, bit):
        self.value = self.value + swap(self.value, bit)

    def join(self, bit):
        other = swap(self.value, bit)
        upper = bit_of(bit) == 1
        self.value = jnp.concatenate(
            [jnp.where(upper, other, self.value), jnp.where(upper, self.value, other)], axis=1
        )

    def step(self, times=1):
        for _ in range(times):
            if self.steps:
                action, bit = self.steps.pop(0)
                action(bit)


def tie(first, second):
    return lax.optimization_barrier((list(first), list(second)))


def side_bit():
    return lax.axis_size("tm") // 32


def orders_of(size):
    bits = [bit for bit in steps_of(size) if bit != side_bit()]
    return [bits[k * len(bits) // 3 :] + bits[: k * len(bits) // 3] for k in range(3)]


def index_bits(bits):
    return [bit if bit < side_bit() else bit // 2 for bit in bits]


class Scatter:
    def __init__(self, keeps, sends):
        self.orders = orders_of(lax.axis_size("tm"))
        self.current = list(keeps)
        self.received = [swap(send, side_bit()) for send in sends]

    def step(self, *waiting):
        sends = []
        for p, order in enumerate(self.orders):
            half = self.current[p].shape[0] // 2
            mine, away = [
                lax.dynamic_slice_in_dim(self.current[p], half * index, half)
                + lax.dynamic_slice_in_dim(self.received[p], half * index, half).astype(jnp.float32)
                for index in (bit_of(order[0]), 1 - bit_of(order[0]))
            ]
            self.current[p] = mine
            sends.append(away.astype(jnp.bfloat16))
        sends, waiting = tie(sends, waiting)
        self.received = [swap(send, order.pop(0)) for send, order in zip(sends, self.orders)]
        return waiting

    def join(self, *done):
        self.received, done = tie(self.received, done)
        return done

    def result(self):
        return [a + b.astype(jnp.float32) for a, b in zip(self.current, self.received)]


class Gather:
    def __init__(self, blocks, near):
        self.orders = orders_of(lax.axis_size("tm"))
        self.held = [[] for _ in blocks]
        self.current = list(blocks)
        self.received = None
        self.near = near

    def stack(self):
        if self.received is None:
            return
        for p, other in enumerate(self.received):
            bit, mine = self.held[p][-1], self.current[p]
            axis = sum(before > bit for before in self.held[p])
            if not self.near:
                upper = bit_of(bit) == 1
                mine, other = jnp.where(upper, other, mine), jnp.where(upper, mine, other)
            self.current[p] = jnp.stack([mine, other], axis=axis)

    def step(self, *waiting):
        self.stack()
        self.current, waiting = tie(self.current, waiting)
        self.received = []
        for p, order in enumerate(self.orders):
            bit = order.pop()
            self.held[p].append(bit)
            self.received.append(swap(self.current[p], bit))
        return waiting

    def join(self, *done):
        self.received, done = tie(self.received, done)
        return done

    def finish(self, *waiting):
        self.stack()
        own = [value.reshape(-1, value.shape[-1]) for value in self.current]
        own, waiting = tie(own, waiting)
        return own, [swap(value, side_bit()) for value in own], waiting


class Stats:
    def __init__(self, stat, count):
        self.stat = stat
        self.count = float(count)
        self.bits = steps_of(lax.axis_size("tm"))

    def step(self, times=1):
        for _ in range(min(times, len(self.bits))):
            stat = self.stat
            other = swap(stat, self.bits.pop(0))
            gap = stat[0:1] - other[0:1]
            mean = 0.5 * (stat[0:1] + other[0:1])
            square = (stat[1:2] + other[1:2]) + gap * gap * (0.5 * self.count)
            self.stat = jnp.concatenate([mean, square, 0.5 * (stat[2:] + other[2:])], axis=0)
            self.count *= 2


class Exchange:
    def __init__(self, flags, carries, sums=()):
        self.bits = steps_of(lax.axis_size("tm"))
        high, self.width = carries[0][0].shape
        rows = high * len(carries)
        flags = jnp.broadcast_to(jnp.tile(flags, len(carries))[:, None], (rows, LANE))
        ends = jnp.concatenate([ends for ends, _, _ in carries], axis=0)
        self.payload = jnp.concatenate([ends, flags, *sums], axis=1)
        self.power = jnp.concatenate(
            [jnp.broadcast_to(power, (high, self.width)) for _, power, _ in carries], axis=0
        )
        self.lane = lax.broadcasted_iota(jnp.int32, self.payload.shape, 1)
        self.high = high
        self.reverse = [reverse for _, _, reverse in carries]
        self.before = jnp.zeros_like(ends)
        self.before_keep = jnp.ones_like(ends)

    def step(self, times=1):
        for _ in range(min(times, len(self.bits))):
            self.one()

    def one(self):
        bit = self.bits.pop(0)
        width = self.width
        mine, other = self.payload, swap(self.payload, bit)
        upper = bit_of(bit)
        row = lax.broadcasted_iota(jnp.int32, (len(mine), 1), 0) // self.high
        turned = sum((row == k) * int(reverse) for k, reverse in enumerate(self.reverse))
        following = turned != upper
        other_total = other[:, :width]
        keep_mine, keep_other = mine[:, width : width + 1], other[:, width : width + 1]
        self.before = jnp.where(
            following, self.before_keep * other_total + self.before, self.before
        )
        self.before_keep = jnp.where(
            following, self.before_keep * keep_other * self.power, self.before_keep
        )
        power = jnp.pad(self.power, ((0, 0), (0, mine.shape[1] - width)))
        carried = jnp.where(
            following, keep_mine * power * other + mine, keep_other * power * mine + other
        )
        self.payload = jnp.where(
            self.lane < width,
            carried,
            jnp.where(self.lane < width + LANE, mine * other, mine + other),
        )
        self.power = self.power * self.power

    def arrived(self, k):
        return self.before[k * self.high : (k + 1) * self.high]

    def sums(self):
        return self.payload[:, self.width + LANE :]


class SumAll:
    def __init__(self, value):
        self.value = value
        self.bits = steps_of(lax.axis_size("tm"))

    def step(self, times=1):
        for _ in range(min(times, len(self.bits))):
            self.value = self.value + swap(self.value, self.bits.pop(0))


def in_order(value, bits, slots):
    count = len(bits)
    axes = [count - bit.bit_length() for bit in bits]
    shape = (2,) * count + (slots, value.shape[1])
    return value.reshape(shape).transpose(axes + [count, count + 1]).reshape(value.shape)


def pad_lanes(value, padded):
    gap = padded - value.shape[-1]
    return jnp.pad(value, [(0, 0)] * (value.ndim - 1) + [(0, gap)])


def flat_places(shard, width, padded):
    size = lax.axis_size("tm")
    members = size * LANE // padded
    slots = LANE // members
    return members, slots, slots * width - shard


def to_block(flat, width, padded):
    size, mine = lax.axis_size("tm"), lax.axis_index("tm")
    members, slots, excess = flat_places(flat.shape[0], width, padded)
    lacking = excess * (members - 1)
    pairs = [(i + 1, i) for i in range(size - 1) if (i + 1) % members]
    extra = lax.ppermute(flat[:lacking], "tm", pairs)
    tail = jnp.zeros((excess,), flat.dtype)
    held = jnp.concatenate([flat, extra, tail])
    return lax.dynamic_slice_in_dim(held, excess * (mine % members), slots * width).reshape(
        slots, width
    )


def from_block(block, shard, padded):
    width = block.shape[1]
    size, mine = lax.axis_size("tm"), lax.axis_index("tm")
    members, slots, excess = flat_places(shard, width, padded)
    lacking = excess * (members - 1)
    pairs = [(i, i + 1) for i in range(size - 1) if (i + 1) % members]
    flat = block.reshape(-1)
    extra = lax.ppermute(flat[slots * width - lacking :], "tm", pairs)
    held = jnp.concatenate([extra, flat])
    return lax.dynamic_slice_in_dim(held, lacking - excess * (mine % members), shard)


def own_heads(shard, width, padded):
    members, slots, _ = flat_places(shard, width, padded)
    half = padded // 2
    group = LANE // 2
    if members == 2:
        lacking = slots - shard // width
        kept = -(-(lacking) // 16) * 16
        return [(0, group), (half + group - kept, kept)]
    return [(0, group), (half, group)]


def own_flat(found, shard, width, padded):
    mine = lax.axis_index("tm")
    members, slots, excess = flat_places(shard, width, padded)
    member = mine % members
    if members == 2:
        own, other = found[:slots].reshape(-1), found[slots:].reshape(-1)
        low = own[:shard]
        high = jnp.concatenate([other[other.shape[0] - excess :], own[: shard - excess]])
        return jnp.where(member == 0, low, high)
    near = found.reshape(members, slots * width)
    placed = jnp.take(near, jnp.arange(members) ^ member, axis=0).reshape(-1)
    return lax.dynamic_slice_in_dim(placed, shard * member, shard)


def per_device(
    inputs,
    clip_start,
    shallow_weight,
    shallow_momentum,
    deep_weight,
    deep_momentum,
    unit_params,
    unit_first,
    unit_second,
    out_grad,
):
    devices = lax.axis_size("tm")
    rows, frames, feats = inputs.shape
    width = shallow_weight.shape[1]
    padded = -(-width // WIDE) * WIDE
    group = width // (padded // LANE)
    count = rows * frames
    keep_mask = (1 - clip_start).astype(jnp.float32)
    flags = jnp.min(keep_mask, axis=1)
    keep = jnp.broadcast_to(keep_mask.T.reshape(count, 1), (count, LANE))
    params = pad_lanes(unit_params, padded)
    rates = jnp.maximum(1.0 - jnp.exp(-params[:, 0:1]), DECAY_FLOOR)
    powers = rates
    for _ in range(frames.bit_length() - 1):
        powers = powers * powers

    deep_block = pad_lanes(to_block(deep_weight.astype(jnp.bfloat16), width, padded), padded)
    momentum_block = pad_lanes(to_block(deep_momentum, width, padded), padded)

    shares = [3 * padded // 8, 3 * padded // 8, padded // 4]
    parts = [(sum(shares[:p]), shares[p]) for p in range(3)]
    side = bit_of(side_bit()).astype(jnp.int32).reshape(1)
    chunks = padded // WIDE
    orders = orders_of(devices)
    gather = Gather([deep_block[:, first : first + lanes] for first, lanes in parts], False)
    gather.step()
    x, proj_one, stat_one, gram = front(
        inputs.reshape(count, feats), shallow_weight, rows, frames
    )
    stats = Stats(stat_one, count)
    (stats.stat,) = gather.join(stats.stat)
    grad_rows = out_grad.reshape(count, width)
    delta = None
    for k in range(chunks):
        if k % 2 == 0:
            (stats.stat,) = gather.step(stats.stat)
        stats.step()
        delta = delta_two(k, delta, grad_rows, keep, params[1], rows, frames, padded)
        delta, (stats.stat,) = tie(delta, [stats.stat])
        if k % 2 == 1:
            (stats.stat,) = gather.join(stats.stat)
    delta_local, delta_end = delta
    (stats.stat,) = gather.step(stats.stat)
    stats.step(len(stats.bits))
    (stat_one,), (momentum_block,) = tie([stats.stat], [momentum_block])
    state_local, state_end = local_states(
        proj_one, keep, params[0], stat_one, rows, frames, devices
    )
    carries = Exchange(
        flags, [(state_end, powers[0], False), (delta_end, powers[1], True)], [gram]
    )
    carries.step(2)
    (carries.payload,) = gather.join(carries.payload)
    while gather.orders[0]:
        gather.step()
    deep_own, deep_other, (carries.payload,) = gather.finish(carries.payload)
    carries.step(len(carries.bits))
    state_in, delta_in, gram = carries.arrived(0), carries.arrived(1), carries.sums()
    low_one, mean_one = low_one_of(
        state_local, state_in, keep, params[0], rows, frames, width, group
    )
    (proj_own,) = second_forward(side, low_one, deep_own, parts)
    (proj_own,), deep_other = tie([proj_own], deep_other)
    proj_two, stat_two = second_forward(side, low_one, deep_other, parts, proj_own)
    stats = Stats(jnp.concatenate([stat_two, mean_one], axis=0), count)
    hidden = [None, None]
    sources = [(state_local, state_in, params[0]), None]

    def next_hidden(layer, places, waiting):
        states, start, layer_params = sources[layer]
        for k in places:
            hidden[layer] = hidden_of(
                k, hidden[layer], states, start, keep, layer_params, rows, frames, width
            )
        hidden[layer], waiting = tie(hidden[layer], waiting)
        return waiting

    for k in range(chunks):
        stats.step()
        (stats.stat,) = next_hidden(0, [k], [stats.stat])
    stats.step(len(stats.bits))
    stat_two, mean_one = stats.stat[:2], stats.stat[2:]
    gate, sums_two = gate_two(
        proj_two, delta_local, delta_in, keep, params[1], stat_two, rows, frames, devices
    )
    sums = SumAll(sums_two)
    turned = None
    for k in range(chunks):
        sums.step()
        turned = turn(k, turned, low_one, mean_one)
        turned, (sums.value,) = tie(turned, [sums.value])
    sums.step(len(sums.bits))
    sums_two = sums.value
    slots = padded // devices
    weights = [index_bits(order) for order in orders]
    aligned = slots % 16 == 0
    grad_two, total_two, keeps, sends = deep_term(
        parts, weights if aligned else None, side, gate, proj_two, params[1], stat_two,
        sums_two, turned[0], rows, frames, devices,
    )
    if not aligned:
        keeps = [in_order(keep, order, slots) for keep, order in zip(keeps, weights)]
        sends = [in_order(send, order, slots) for send, order in zip(sends, weights)]
    scatter = Scatter(keeps, sends)
    back = back_one(grad_two, deep_own, deep_other, parts)
    back = scatter.join(*back)
    back = scatter.step(*back)
    back_local, back_end = delta_one(
        side, *back, keep, params[0], rows, frames, width, group
    )
    second_local, second_end, second_decay = states_two(
        proj_two, delta_local, delta_in, keep, params[1], stat_two, rows, frames, devices
    )
    back_end, second_end = scatter.join(back_end, second_end)
    tall = 2 * rows
    back_end, second_end = scatter.step(back_end, second_end)
    carries = Exchange(
        flags,
        [(back_end, powers[0], True), (second_end, powers[1], False)],
        [total_two.reshape(tall, -1)],
    )
    carries.step(4)
    (carries.payload,) = scatter.join(carries.payload)
    (carries.payload,) = scatter.step(carries.payload)
    carries.step(len(carries.bits))
    back_in, second_in = carries.arrived(0), carries.arrived(1)
    sources[1] = (second_local, second_in, params[1])
    total_two = carries.sums().reshape(1, padded)
    gate_low, sums_one = gate_one(
        proj_one, state_local, state_in, back_local, back_in, keep, params[0], stat_one, x,
        rows, frames, devices, feats,
    )
    decay_two = jnp.sum(second_decay[:rows] + second_decay[rows:] * second_in, axis=0, keepdims=True)
    (sums_one,) = scatter.join(
        sums_one + jnp.pad(decay_two, ((feats + 3, SIDE - feats - 4), (0, 0)))
    )
    spread = SumSpread(sums_one)
    while scatter.orders[0]:
        (spread.value,) = scatter.step(spread.value)
        spread.step()
        (spread.value,) = scatter.join(spread.value)
    mine = lax.axis_index("tm")
    place = mine // (2 * side_bit()) * side_bit() + mine % side_bit()
    place = (side[0] * (devices // 2) + place) * slots
    mean_own = lax.dynamic_slice_in_dim(mean_one[0], place, slots)[:, None]
    grad_parts = [
        part + mean_own * total_two[:, first : first + lanes]
        for (first, lanes), part in zip(parts, scatter.result())
    ]
    gather = Gather(
        [
            (MUON_BETA * momentum_block[:, first : first + lanes] + part).astype(jnp.bfloat16)
            for (first, lanes), part in zip(parts, grad_parts)
        ],
        True,
    )
    for count_steps in (1, 2, 2, 3):
        (spread.value,) = gather.step(spread.value)
        spread.step(count_steps)
        (spread.value,) = gather.join(spread.value)
    while gather.orders[0]:
        gather.step()
    own, other, (spread.value,) = gather.finish(spread.value)
    spread.step(len(spread.steps))
    (spread.value,) = next_hidden(1, range(chunks), [spread.value])
    (hidden_one,), (hidden_two,) = hidden
    sums_one = spread.value
    shallow_grad, shallow_next, shallow_new, shallow_low = shallow_step(
        sums_one, gram, params[0], stat_one, shallow_weight, shallow_momentum,
        count * devices, count,
    )
    input_back = input_grad_of(
        gate_low, proj_one, params[0], stat_one, sums_one, shallow_weight, rows, frames, devices
    )
    input_grad = jnp.swapaxes(input_back.reshape(frames, rows, feats), 0, 1)
    grad_block = jnp.concatenate(grad_parts, axis=1)

    shard = deep_weight.shape[0]
    heads = own_heads(shard, width, padded)
    ortho = newton_rows(own, other, parts, heads)
    deep_ortho = own_flat(ortho[:, :width], shard, width, padded)
    deep_new = MUON_KEEP * deep_weight - MUON_RATE * deep_ortho.astype(jnp.float32)
    deep_grad = from_block(grad_block[:, :width], shard, padded)
    deep_next = MUON_BETA * deep_momentum + deep_grad

    unit_sums = sums_one[feats : feats + 4, :width]
    bias_gain_two = sums_two[:, :width]
    slope = jnp.where(
        1.0 - jnp.exp(-unit_params[:, 0]) > DECAY_FLOOR, jnp.exp(-unit_params[:, 0]), 0.0
    )
    unit_grad = jnp.stack(
        [
            jnp.stack([unit_sums[2] * slope[0], unit_sums[0], unit_sums[1], unit_sums[0]]),
            jnp.stack(
                [unit_sums[3] * slope[1], bias_gain_two[0], bias_gain_two[1], bias_gain_two[0]]
            ),
        ]
    )
    first_fix = 1.0 - FIRST_DECAY**STEP
    second_fix = 1.0 - SECOND_DECAY**STEP
    first_new = FIRST_DECAY * unit_first + (1.0 - FIRST_DECAY) * unit_grad
    second_new = SECOND_DECAY * unit_second + (1.0 - SECOND_DECAY) * unit_grad * unit_grad
    params_new = unit_params - ADAM_RATE * (first_new / first_fix) / (
        jnp.sqrt(second_new / second_fix) + ADAM_EPSILON
    )
    return (
        hidden_one.reshape(rows, frames, width),
        hidden_two.reshape(rows, frames, width),
        input_grad,
        shallow_grad,
        shallow_next,
        shallow_new,
        shallow_low,
        deep_grad,
        deep_next,
        deep_new,
        deep_new.astype(jnp.bfloat16),
        first_new,
        second_new,
        params_new,
    )


def solution(mesh):
    in_specs = (
        P(None, "tm", None),
        P(None, "tm"),
        P(),
        P(),
        P("tm"),
        P("tm"),
        P(),
        P(),
        P(),
        P(None, "tm", None),
    )
    out_specs = (
        P(None, "tm", None),
        P(None, "tm", None),
        P(None, "tm", None),
        P(),
        P(),
        P(),
        P(),
        P("tm"),
        P("tm"),
        P("tm"),
        P("tm"),
        P(),
        P(),
        P(),
    )
    return jax.shard_map(
        per_device, mesh=mesh, in_specs=in_specs, out_specs=out_specs, check_vma=False
    )
```

```python
import functools

import jax
import jax.numpy as jnp
from jax import lax
from jax.experimental import pallas as pl
from jax.experimental.pallas import tpu as pltpu
from jax.sharding import PartitionSpec as P

NS_STEPS = 2
STEP = 5


NORM_EPSILON = 1e-05
MUON_EPSILON = 1e-07
COEFF_A = 3.4445
COEFF_B = -4.775
COEFF_C = 2.0315
MUON_BETA = 0.5
MUON_RATE = 4.0
MUON_KEEP = 0.999
FIRST_DECAY = 0.9
SECOND_DECAY = 0.95
ADAM_RATE = 0.5
ADAM_EPSILON = 1e-08
DECAY_FLOOR = 0.9
LANE = 128
WIDE = 512
PART = 256
SIDE = 80


def kernel_call(body, grid, in_specs, out_specs, out_shape, scratch=(), flops=0, traffic=0):
    return pl.pallas_call(
        body,
        grid=grid,
        in_specs=in_specs,
        out_specs=out_specs,
        out_shape=out_shape,
        scratch_shapes=list(scratch),
        compiler_params=pltpu.CompilerParams(vmem_limit_bytes=56 * 1024 * 1024),
        cost_estimate=pl.CostEstimate(flops=flops, bytes_accessed=traffic, transcendentals=0),
    )


def shape_of(shape, dtype=jnp.float32):
    return jax.ShapeDtypeStruct(shape, dtype)


def whole(shape):
    return pl.BlockSpec(shape, lambda i: (0,) * len(shape))


def lanes_of(rows, width=WIDE):
    return pl.BlockSpec((rows, width), lambda i: (0, i))


def chunk_call(body, place, in_specs, out_specs, out_shape, arrays, previous, scratch=(), traffic=0):
    count = len(in_specs)
    before = list(previous) if previous is not None else []

    def run(*refs):
        body(*refs[:count], *refs[count + len(before) :])

    return pl.pallas_call(
        run,
        grid=(1,),
        in_specs=list(in_specs) + [pl.BlockSpec(memory_space=pl.ANY)] * len(before),
        out_specs=out_specs,
        out_shape=out_shape,
        scratch_shapes=list(scratch),
        input_output_aliases={count + k: k for k in range(len(before))},
        compiler_params=pltpu.CompilerParams(vmem_limit_bytes=56 * 1024 * 1024),
        cost_estimate=pl.CostEstimate(flops=0, bytes_accessed=traffic, transcendentals=0),
    )(*arrays, *before)


def chunk_at(rows, place):
    return pl.BlockSpec((rows, WIDE), lambda i: (0, place))


def rate_of(params):
    return jnp.maximum(1.0 - jnp.exp(-params[0:1]), DECAY_FLOOR)


def softened(value):
    return jnp.maximum(value, 0.0) + jnp.log(1.0 + jnp.exp(-jnp.abs(value)))


def sigmoid(value):
    return 0.5 * jnp.tanh(0.5 * value) + 0.5


def wide_keep(keep_ref, t, rows):
    keep = keep_ref[pl.ds(pl.multiple_of(t * rows, rows), rows), :]
    return jnp.concatenate([keep] * (WIDE // LANE), axis=1)


def rows_at(ref, t, rows):
    return ref[pl.ds(pl.multiple_of(t * rows, rows), rows), :]


def store_at(ref, t, rows, value):
    ref[pl.ds(pl.multiple_of(t * rows, rows), rows), :] = value


def valid_lanes(shape, total, step):
    return lax.broadcasted_iota(jnp.int32, shape, 1) + step * WIDE < total


def unit_terms(params_ref, stat_ref, total_devices, frames):
    params = params_ref[...]
    stat = stat_ref[...]
    centre = stat[0:1]
    inverse = lax.rsqrt(stat[1:2] / (total_devices * frames) + NORM_EPSILON)
    return centre, inverse, params[2:3], params[3:4] + params[1:2]


def front_body(rows, frames, width, x_ref, w_ref, xt_ref, proj_ref, stat_ref, gram_ref, padded_w):
    step = pl.program_id(0)
    count, feats = x_ref.shape

    @pl.when(step == 0)
    def _():
        i = lax.broadcasted_iota(jnp.int32, (count, count), 0)
        j = lax.broadcasted_iota(jnp.int32, (count, count), 1)
        move = (j == lax.rem(i, rows) * frames + lax.div(i, rows)).astype(jnp.bfloat16)
        moved = jnp.dot(move, x_ref[...], preferred_element_type=jnp.float32).astype(jnp.bfloat16)
        i = lax.broadcasted_iota(jnp.int32, (feats, LANE), 0)
        j = lax.broadcasted_iota(jnp.int32, (feats, LANE), 1)
        wide = jnp.dot(moved, (i == j).astype(jnp.bfloat16), preferred_element_type=jnp.float32)
        lane = lax.broadcasted_iota(jnp.int32, (count, LANE), 1)
        xt = jnp.where(lane == feats, 1.0, wide).astype(jnp.bfloat16)
        xt_ref[...] = xt
        gram = dot_tn(xt, xt)
        high = gram_ref.shape[0]
        for k in range(SIDE // high):
            gram_ref[:, k * LANE : (k + 1) * LANE] = gram[k * high : (k + 1) * high]
        padded_w[...] = jnp.zeros_like(padded_w)

    weight = w_ref[...]
    padded_w[0:feats, :] = jnp.where(valid_lanes(weight.shape, width, step), weight, 0.0)
    proj = jnp.dot(
        xt_ref[...], padded_w[...].astype(jnp.bfloat16), preferred_element_type=jnp.float32
    )
    proj_ref[...] = proj
    mean = jnp.sum(proj, axis=0, keepdims=True) * (1.0 / count)
    off = proj - mean
    stat_ref[0:1, :] = mean
    stat_ref[1:2, :] = jnp.sum(off * off, axis=0, keepdims=True)


def dot_tn(a, b):
    return lax.dot_general(a, b, (((0,), (0,)), ((), ())), preferred_element_type=jnp.float32)


def front(x, weight, rows, frames):
    count, feats = x.shape
    width = weight.shape[1]
    padded = -(-width // WIDE) * WIDE
    return kernel_call(
        functools.partial(front_body, rows, frames, width),
        (padded // WIDE,),
        [whole((count, feats)), lanes_of(feats)],
        [whole((count, LANE)), lanes_of(count), lanes_of(2), whole((rows, SIDE // rows * LANE))],
        [
            shape_of((count, LANE), jnp.bfloat16),
            shape_of((count, padded)),
            shape_of((2, padded)),
            shape_of((rows, SIDE // rows * LANE)),
        ],
        [pltpu.VMEM((LANE, WIDE), jnp.float32)],
    )(x, weight)


def delta_two_body(rows, frames, width, place, grad_ref, keep_ref, params_ref, delta_ref, end_ref, held):
    pieces = WIDE // LANE
    mask = valid_lanes((rows * frames, WIDE), width, place)
    grad = jnp.where(mask, grad_ref[...].astype(jnp.float32), 0.0)
    for g in range(pieces):
        held[g] = grad[:, g * LANE : (g + 1) * LANE]
    rate = rate_of(params_ref[...])

    def body(k, carried):
        t = frames - 1 - k
        own = jnp.concatenate(
            [held[g, pl.ds(t, rows, stride=frames), :] for g in range(pieces)], axis=1
        )
        delta = own + carried
        store_at(delta_ref, t, rows, delta)
        return rate * wide_keep(keep_ref, t, rows) * delta

    end_ref[...] = lax.fori_loop(
        0, frames, body, jnp.zeros((rows, WIDE), jnp.float32), unroll=8
    )


def delta_two(place, previous, out_grad, keep, params, rows, frames, padded):
    count, width = out_grad.shape
    return chunk_call(
        functools.partial(delta_two_body, rows, frames, width, place),
        place,
        [chunk_at(count, place), whole((count, LANE)), chunk_at(4, place)],
        [chunk_at(count, place), chunk_at(rows, place)],
        [shape_of((count, padded)), shape_of((rows, padded))],
        (out_grad, keep, params),
        previous,
        [pltpu.VMEM((WIDE // LANE, count, LANE), jnp.float32)],
    )


def states_body(
    rows, frames, devices, proj_ref, keep_ref, params_ref, stat_ref, state_ref, end_ref
):
    centre, inverse, gain, offset = unit_terms(params_ref, stat_ref, devices, rows * frames)
    rate = rate_of(params_ref[...])
    share = 1.0 - rate

    def body(t, carried):
        gate = (rows_at(proj_ref, t, rows) - centre) * inverse * gain + offset
        soft = softened(gate)
        carried = rate * wide_keep(keep_ref, t, rows) * carried + share * soft
        store_at(state_ref, t, rows, carried)
        return carried

    end_ref[...] = lax.fori_loop(
        0, frames, body, jnp.zeros((rows, WIDE), jnp.float32), unroll=8
    )


def local_states(proj, keep, params, stat, rows, frames, devices):
    count, padded = proj.shape
    return kernel_call(
        functools.partial(states_body, rows, frames, devices),
        (padded // WIDE,),
        [lanes_of(count), whole((count, LANE)), lanes_of(4), lanes_of(2)],
        [lanes_of(count), lanes_of(rows)],
        [shape_of((count, padded)), shape_of((rows, padded))],
    )(proj, keep, params, stat)


def to_slots(value, group):
    pieces = value.shape[1] // LANE
    lane = lax.broadcasted_iota(jnp.int32, (value.shape[0], LANE), 1)
    parts = [value[:, g * LANE : (g + 1) * LANE] for g in range(pieces)]
    out = []
    for g in range(pieces):
        moved = (LANE - group) * g
        if moved == 0:
            new = parts[g]
        else:
            new = jnp.where(
                lane < moved, pltpu.roll(parts[g - 1], moved, 1), pltpu.roll(parts[g], moved, 1)
            )
        out.append(jnp.where(lane < group, new, 0.0))
    return jnp.concatenate(out, axis=1)


def from_slots(value, group, width):
    pieces = value.shape[1] // LANE
    lane = lax.broadcasted_iota(jnp.int32, (value.shape[0], LANE), 1)
    parts = [value[:, g * LANE : (g + 1) * LANE] for g in range(pieces)]
    out = []
    for j in range(pieces):
        moved = (LANE - group) * j
        new = parts[j] if moved == 0 else pltpu.roll(parts[j], LANE - moved, 1)
        if j + 1 < pieces:
            new = jnp.where(lane < group - moved, new, pltpu.roll(parts[j + 1], group - moved, 1))
        left = width - j * LANE
        out.append(new if left >= LANE else jnp.where(lane < left, new, 0.0))
    return jnp.concatenate(out, axis=1)


def low_one_body(rows, frames, width, group, state_ref, start_ref, keep_ref, params_ref, low_ref, mean_ref):
    pieces = state_ref.shape[1] // LANE
    rate = rate_of(params_ref[...])

    def advance(t, carried):
        keep = rows_at(keep_ref, t, rows)
        carried = rate * jnp.concatenate([keep] * pieces, axis=1) * carried
        return carried, rows_at(state_ref, t, rows) + carried

    def body(k, both):
        carried, total = both
        t = 2 * k
        carried, first = advance(t, carried)
        carried, second = advance(t + 1, carried)
        place = pl.ds(pl.multiple_of(t * rows, 2 * rows), 2 * rows)
        slots = to_slots(jnp.concatenate([first, second], axis=0), group)
        low_ref[place, :] = slots.astype(jnp.bfloat16)
        return carried, total + slots[:rows] + slots[rows:]

    start = start_ref[...]
    _, total = lax.fori_loop(0, frames // 2, body, (start, jnp.zeros_like(start)), unroll=2)
    mean_ref[...] = jnp.sum(total, axis=0, keepdims=True) * (1.0 / (rows * frames))


def low_one_of(states, start, keep, params, rows, frames, width, group):
    count, padded = states.shape
    return kernel_call(
        functools.partial(low_one_body, rows, frames, width, group),
        (1,),
        [whole((count, padded)), whole((rows, padded)), whole((count, LANE)), whole((4, padded))],
        [whole((count, padded)), whole((1, padded))],
        [shape_of((count, padded), jnp.bfloat16), shape_of((1, padded))],
    )(states, start, keep, params)


def hidden_body(rows, frames, state_ref, start_ref, keep_ref, params_ref, hidden_ref, held):
    pieces = WIDE // LANE
    rate = rate_of(params_ref[...])

    def body(t, carry):
        carry = rate * wide_keep(keep_ref, t, rows) * carry
        state = rows_at(state_ref, t, rows) + carry
        for g in range(pieces):
            held[g, pl.ds(pl.multiple_of(t * rows, rows), rows), :] = state[
                :, g * LANE : (g + 1) * LANE
            ]
        return carry

    lax.fori_loop(0, frames, body, start_ref[...], unroll=8)
    for r in range(rows):
        for g in range(pieces):
            hidden_ref[r * frames : (r + 1) * frames, g * LANE : (g + 1) * LANE] = held[
                g, pl.ds(r, frames, stride=rows), :
            ]


def hidden_of(place, previous, states, start, keep, params, rows, frames, width):
    count, _ = states.shape
    return chunk_call(
        functools.partial(hidden_body, rows, frames),
        place,
        [chunk_at(count, place), chunk_at(rows, place), whole((count, LANE)), chunk_at(4, place)],
        [chunk_at(count, place)],
        [shape_of((count, width))],
        (states, start, keep, params),
        previous,
        [pltpu.VMEM((WIDE // LANE, count, LANE), jnp.float32)],
    )


def second_body(low_ref, weight_ref, proj_ref, stat_ref):
    proj = jnp.dot(low_ref[...], weight_ref[...], preferred_element_type=jnp.float32)
    proj_ref[...] = proj
    mean = jnp.sum(proj, axis=0, keepdims=True) * (1.0 / proj.shape[0])
    off = proj - mean
    stat_ref[0:1, :] = mean
    stat_ref[1:2, :] = jnp.sum(off * off, axis=0, keepdims=True)


def second_forward(low, weight):
    count, padded = low.shape
    return kernel_call(
        second_body,
        (padded // WIDE,),
        [whole((count, padded)), lanes_of(padded)],
        [lanes_of(count), lanes_of(2)],
        [shape_of((count, padded)), shape_of((2, padded))],
    )(low, weight)


def gate_two_body(
    rows, frames, devices, proj_ref, delta_ref, start_ref, keep_ref, params_ref, stat_ref, gate_ref, sums_ref
):
    centre, inverse, gain, offset = unit_terms(params_ref, stat_ref, devices, rows * frames)
    rate = rate_of(params_ref[...])
    share = 1.0 - rate
    none = jnp.zeros((rows, WIDE), jnp.float32)

    def body(k, carried):
        carry, bias_sum, gain_sum = carried
        t = frames - 1 - k
        delta = rows_at(delta_ref, t, rows) + carry
        normed = (rows_at(proj_ref, t, rows) - centre) * inverse
        gate = share * delta * sigmoid(normed * gain + offset)
        store_at(gate_ref, t, rows, gate)
        carry = rate * wide_keep(keep_ref, t, rows) * carry
        return carry, bias_sum + gate, gain_sum + gate * normed

    _, bias_sum, gain_sum = lax.fori_loop(
        0, frames, body, (start_ref[...], none, none), unroll=8
    )
    sums_ref[0:1, :] = jnp.sum(bias_sum, axis=0, keepdims=True)
    sums_ref[1:2, :] = jnp.sum(gain_sum, axis=0, keepdims=True)


def gate_two(proj, delta, start, keep, params, stat, rows, frames, devices):
    count, padded = proj.shape
    return kernel_call(
        functools.partial(gate_two_body, rows, frames, devices),
        (padded // WIDE,),
        [lanes_of(count), lanes_of(count), lanes_of(rows), whole((count, LANE)), lanes_of(4), lanes_of(2)],
        [lanes_of(count), lanes_of(2)],
        [shape_of((count, padded)), shape_of((2, padded))],
    )(proj, delta, start, keep, params, stat)


def states_two_body(
    rows, frames, devices, proj_ref, delta_ref, start_ref, keep_ref, params_ref, stat_ref,
    state_ref, end_ref, decay_ref, held,
):
    centre, inverse, gain, offset = unit_terms(params_ref, stat_ref, devices, rows * frames)
    rate = rate_of(params_ref[...])
    share = 1.0 - rate
    none = jnp.zeros((rows, WIDE), jnp.float32)

    def backward(k, carry):
        t = frames - 1 - k
        store_at(held, t, rows, rows_at(delta_ref, t, rows) + carry)
        return rate * wide_keep(keep_ref, t, rows) * carry

    lax.fori_loop(0, frames, backward, start_ref[...], unroll=8)

    def forward(t, carried):
        state, reach, decay, factor = carried
        keep = wide_keep(keep_ref, t, rows)
        delta = rows_at(held, t, rows)
        value = (rows_at(proj_ref, t, rows) - centre) * inverse * gain + offset
        soft = softened(value)
        decay = decay + delta * (keep * state - soft)
        factor = factor + delta * keep * reach
        state = rate * keep * state + share * soft
        reach = rate * keep * reach
        store_at(state_ref, t, rows, state)
        return state, reach, decay, factor

    state, _, decay, factor = lax.fori_loop(
        0, frames, forward, (none, jnp.ones_like(none), none, none), unroll=4
    )
    end_ref[...] = state
    decay_ref[0:rows, :] = decay
    decay_ref[rows : 2 * rows, :] = factor


def states_two(proj, delta, start, keep, params, stat, rows, frames, devices):
    count, padded = proj.shape
    return kernel_call(
        functools.partial(states_two_body, rows, frames, devices),
        (padded // WIDE,),
        [
            lanes_of(count),
            lanes_of(count),
            lanes_of(rows),
            whole((count, LANE)),
            lanes_of(4),
            lanes_of(2),
        ],
        [lanes_of(count), lanes_of(rows), lanes_of(2 * rows)],
        [shape_of((count, padded)), shape_of((rows, padded)), shape_of((2 * rows, padded))],
        [pltpu.VMEM((count, WIDE), jnp.float32)],
    )(proj, delta, start, keep, params, stat)


def turn_body(low_ref, mean_ref, turned_ref):
    half = LANE // 2
    turned = (low_ref[...].astype(jnp.float32) - mean_ref[...]).T.astype(jnp.bfloat16)
    for g in range(WIDE // LANE):
        for side in range(2):
            turned_ref[side, g * half : (g + 1) * half, :] = turned[
                g * LANE + side * half : g * LANE + (side + 1) * half
            ]


def turn(place, previous, low, mean):
    count, padded = low.shape
    return chunk_call(
        turn_body,
        place,
        [chunk_at(count, place), chunk_at(1, place)],
        [pl.BlockSpec((2, WIDE // 2, count), lambda i: (0, place, 0))],
        [shape_of((2, padded // 2, count), jnp.bfloat16)],
        (low, mean),
        previous,
    )


def deep_term_body(
    rows, frames, devices, parts, orders, side_ref, gate_ref, proj_ref, params_ref, stat_ref, sums_ref,
    turned_ref, grad_ref, total_ref, *outs,
):
    step = pl.program_id(0)
    total = devices * rows * frames
    centre, inverse, gain, _ = unit_terms(params_ref, stat_ref, devices, rows * frames)
    sums = sums_ref[...] * (1.0 / total)
    normed = (proj_ref[...] - centre) * inverse
    grad = (gain * inverse * (gate_ref[...] - sums[0:1] - normed * sums[1:2])).astype(jnp.bfloat16)
    grad_ref[...] = grad
    total_ref[...] = jnp.sum(grad.astype(jnp.float32), axis=0, keepdims=True)
    side = side_ref[0]
    half = turned_ref.shape[1]
    tile = 256
    for p, (first, lanes) in enumerate(parts):

        @pl.when((step >= first // PART) & (step < (first + lanes) // PART))
        def _():
            for which, out_ref in ((side, outs[p]), (1 - side, outs[len(parts) + p])):
                for k in range(half // tile):
                    part = jnp.dot(
                        turned_ref[which, k * tile : (k + 1) * tile, :],
                        grad_ref[...],
                        preferred_element_type=jnp.float32,
                    ).astype(out_ref.dtype)
                    if orders is None:
                        out_ref[k * tile : (k + 1) * tile, :] = part
                        continue
                    slots = half // 2 ** len(orders[p])
                    for b in range(tile // slots):
                        block = k * (tile // slots) + b
                        place = 0
                        for weight in orders[p]:
                            place = 2 * place + block // weight % 2
                        out_ref[place * slots : (place + 1) * slots, :] = part[
                            b * slots : (b + 1) * slots
                        ]


def deep_term(parts, orders, side, gate, proj, params, stat, sums, turned, rows, frames, devices):
    count, padded = proj.shape
    half = padded // 2

    def some(first, lanes):
        return pl.BlockSpec(
            (half, PART), lambda i: (0, jnp.clip(i - first // PART, 0, lanes // PART - 1))
        )

    found = kernel_call(
        functools.partial(deep_term_body, rows, frames, devices, parts, orders),
        (padded // PART,),
        [
            pl.BlockSpec(memory_space=pltpu.SMEM),
            lanes_of(count, PART),
            lanes_of(count, PART),
            lanes_of(4, PART),
            lanes_of(2, PART),
            lanes_of(2, PART),
            whole((2, half, count)),
        ],
        [lanes_of(count, PART), lanes_of(1, PART)] + [some(*part) for part in parts] * 2,
        [shape_of((count, padded), jnp.bfloat16), shape_of((1, padded))]
        + [shape_of((half, lanes)) for _, lanes in parts]
        + [shape_of((half, lanes), jnp.bfloat16) for _, lanes in parts],
    )(side, gate, proj, params, stat, sums, turned)
    return found[0], found[1], found[2 : 2 + len(parts)], found[2 + len(parts) :]


def back_body(grad_ref, weight_ref, back_ref):
    back_ref[...] = dot_nt(grad_ref[...], weight_ref[...])


def back_one(grad, weight):
    count, padded = grad.shape
    return kernel_call(
        back_body,
        (padded // WIDE,),
        [whole((count, padded)), pl.BlockSpec((WIDE, padded), lambda i: (i, 0))],
        lanes_of(count),
        shape_of((count, padded)),
    )(grad, weight)


def delta_one_body(rows, frames, width, group, back_ref, keep_ref, params_ref, delta_ref, end_ref):
    pieces = back_ref.shape[1] // LANE
    rate = rate_of(params_ref[...])

    def body(k, carried):
        t = frames - 1 - k
        delta = from_slots(rows_at(back_ref, t, rows), group, width) + carried
        store_at(delta_ref, t, rows, delta)
        keep = rows_at(keep_ref, t, rows)
        return rate * jnp.concatenate([keep] * pieces, axis=1) * delta

    end_ref[...] = lax.fori_loop(
        0, frames, body, jnp.zeros((rows, back_ref.shape[1]), jnp.float32), unroll=2
    )


def delta_one(back, keep, params, rows, frames, width, group):
    count, padded = back.shape
    return kernel_call(
        functools.partial(delta_one_body, rows, frames, width, group),
        (1,),
        [whole((count, padded)), whole((count, LANE)), whole((4, padded))],
        [whole((count, padded)), whole((rows, padded))],
        [shape_of((count, padded)), shape_of((rows, padded))],
    )(back, keep, params)


def gate_one_body(
    rows,
    frames,
    devices,
    feats,
    proj_ref,
    state_ref,
    first_ref,
    delta_ref,
    start_ref,
    keep_ref,
    params_ref,
    stat_ref,
    x_ref,
    gate_ref,
    sums_ref,
    held,
):
    centre, inverse, gain, offset = unit_terms(params_ref, stat_ref, devices, rows * frames)
    rate = rate_of(params_ref[...])
    share = 1.0 - rate
    none = jnp.zeros((rows, WIDE), jnp.float32)

    def backward(k, carry):
        t = frames - 1 - k
        store_at(held, t, rows, rows_at(delta_ref, t, rows) + carry)
        return rate * wide_keep(keep_ref, t, rows) * carry

    lax.fori_loop(0, frames, backward, start_ref[...], unroll=8)

    def forward(t, carried):
        carry, before, bias_sum, gain_sum, decay_sum = carried
        keep = wide_keep(keep_ref, t, rows)
        delta = rows_at(held, t, rows)
        normed = (rows_at(proj_ref, t, rows) - centre) * inverse
        value = normed * gain + offset
        soft = softened(value)
        gate = share * delta * sigmoid(value)
        store_at(gate_ref, t, rows, gate)
        decay_sum = decay_sum + delta * (keep * before - soft)
        carry = rate * keep * carry
        before = rows_at(state_ref, t, rows) + carry
        return carry, before, bias_sum + gate, gain_sum + gate * normed, decay_sum

    first = first_ref[...]
    _, _, bias_sum, gain_sum, decay_sum = lax.fori_loop(
        0, frames, forward, (first, first, none, none, none), unroll=4
    )
    bias = jnp.sum(bias_sum, axis=0, keepdims=True)
    mean = bias * (1.0 / (rows * frames))
    x = x_ref[...]
    ones = jnp.ones((rows * frames, LANE), jnp.bfloat16)
    total = jnp.concatenate([dot_tn(x, ones)] * (WIDE // LANE), axis=1)
    term = dot_tn(x, (gate_ref[...] - mean).astype(jnp.bfloat16)) + total * mean
    sums_ref[...] = term[: sums_ref.shape[0]]
    sums_ref[feats : feats + 1, :] = bias
    sums_ref[feats + 1 : feats + 2, :] = jnp.sum(gain_sum, axis=0, keepdims=True)
    sums_ref[feats + 2 : feats + 3, :] = jnp.sum(decay_sum, axis=0, keepdims=True)


def gate_one(proj, states, first, delta, start, keep, params, stat, x, rows, frames, devices, feats):
    count, padded = proj.shape
    return kernel_call(
        functools.partial(gate_one_body, rows, frames, devices, feats),
        (padded // WIDE,),
        [
            lanes_of(count),
            lanes_of(count),
            lanes_of(rows),
            lanes_of(count),
            lanes_of(rows),
            whole((count, LANE)),
            lanes_of(4),
            lanes_of(2),
            whole((count, LANE)),
        ],
        [lanes_of(count), lanes_of(SIDE)],
        [shape_of((count, padded)), shape_of((SIDE, padded))],
        [pltpu.VMEM((count, WIDE), jnp.float32)],
    )(proj, states, first, delta, start, keep, params, stat, x)


def input_grad_body(
    rows, frames, devices, width, feats, gate_ref, proj_ref, params_ref, stat_ref, sums_ref, w_ref, back_ref
):
    step = pl.program_id(0)
    total = devices * rows * frames
    centre, inverse, gain, _ = unit_terms(params_ref, stat_ref, devices, rows * frames)
    bias = sums_ref[feats : feats + 1, :] * (1.0 / total)
    slope = sums_ref[feats + 1 : feats + 2, :] * (1.0 / total)
    normed = (proj_ref[...] - centre) * inverse
    grad = (gain * inverse * (gate_ref[...] - bias - normed * slope)).astype(jnp.bfloat16)
    weight = w_ref[...]
    weight = jnp.where(valid_lanes(weight.shape, width, step), weight, 0.0).astype(jnp.bfloat16)
    part = dot_nt(grad, weight)

    @pl.when(step == 0)
    def _():
        back_ref[...] = part

    @pl.when(step > 0)
    def _():
        back_ref[...] += part


def input_grad_of(gate, proj, params, stat, sums, weight, rows, frames, devices):
    count, padded = proj.shape
    feats, width = weight.shape
    return kernel_call(
        functools.partial(input_grad_body, rows, frames, devices, width, feats),
        (padded // WIDE,),
        [lanes_of(count), lanes_of(count), lanes_of(4), lanes_of(2), lanes_of(SIDE), lanes_of(feats)],
        whole((count, feats)),
        shape_of((count, feats)),
    )(gate, proj, params, stat, sums, weight)


def dot_nt(a, b):
    return lax.dot_general(a, b, (((1,), (1,)), ((), ())), preferred_element_type=jnp.float32)


def shallow_body(
    total, frames, sums_ref, gram_ref, params_ref, stat_ref, w_ref, m_ref,
    grad_ref, next_ref, new_ref, low_ref, held,
):
    feats, width = w_ref.shape
    centre, inverse, gain, _ = unit_terms(params_ref, stat_ref, total // frames, frames)
    weight = w_ref[...]
    held[...] = jnp.zeros_like(held)
    held[0:feats, 0:width] = weight
    high = gram_ref.shape[0]
    gram = jnp.concatenate(
        [gram_ref[:, k * LANE : (k + 1) * LANE] for k in range(SIDE // high)], axis=0
    )
    lane = lax.broadcasted_iota(jnp.int32, gram.shape, 1)
    x_sum = jnp.sum(jnp.where(lane == feats, gram, 0.0), axis=1, keepdims=True)
    raw = jnp.dot(
        gram[:, :SIDE],
        held[...].astype(jnp.bfloat16).astype(jnp.float32),
        precision=lax.Precision.HIGHEST,
        preferred_element_type=jnp.float32,
    )
    normed = (raw - x_sum * centre) * inverse
    bias = sums_ref[feats : feats + 1, :] * (1.0 / total)
    slope = sums_ref[feats + 1 : feats + 2, :] * (1.0 / total)
    grad = gain * inverse * (sums_ref[...] - x_sum * bias - normed * slope)
    grad = grad[:feats, :width]
    grad_ref[...] = grad
    following = MUON_BETA * m_ref[...] + grad
    next_ref[...] = following
    held[0:feats, 0:width] = following
    m = held[...]
    current = (m / (jnp.sqrt(jnp.sum(m * m)) + MUON_EPSILON)).astype(jnp.bfloat16)
    for repeat in range(NS_STEPS):
        gram = dot_nt(current, current).astype(jnp.bfloat16)
        square = jnp.dot(gram, gram, preferred_element_type=jnp.float32)
        mixing = (COEFF_B * gram.astype(jnp.float32) + COEFF_C * square).astype(jnp.bfloat16)
        current = (
            COEFF_A * current.astype(jnp.float32)
            + jnp.dot(mixing, current, preferred_element_type=jnp.float32)
        ).astype(jnp.bfloat16)
    new = MUON_KEEP * weight - MUON_RATE * current[:feats, :width].astype(jnp.float32)
    new_ref[...] = new
    low_ref[...] = new.astype(jnp.bfloat16)


def shallow_step(sums, gram, params, stat, weight, momentum, total, frames):
    padded = sums.shape[1]
    some = shape_of(weight.shape)
    return kernel_call(
        functools.partial(shallow_body, total, frames),
        (1,),
        [whole(value.shape) for value in (sums, gram, params, stat, weight, momentum)],
        [whole(weight.shape)] * 4,
        [some, some, some, shape_of(weight.shape, jnp.bfloat16)],
        [pltpu.VMEM((SIDE, padded), jnp.float32)],
    )(sums, gram, params, stat, weight, momentum)


def newton_body(parts, heads, tile, *refs):
    blocks_refs, out_ref = refs[: 2 * len(parts)], refs[2 * len(parts)]
    m_ref, gram, mixing, sems = refs[2 * len(parts) + 1 :]
    size = m_ref.shape[0]
    half = size // 2
    blocks = size // tile
    copies = []
    for side in range(2):
        for p, (first, lanes) in enumerate(parts):
            copies.append(
                pltpu.make_async_copy(
                    blocks_refs[side * len(parts) + p],
                    m_ref.at[side * half : (side + 1) * half, first : first + lanes],
                    sems.at[side * len(parts) + p],
                )
            )
    for copy in copies:
        copy.start()
    for copy in copies:
        copy.wait()

    def place(k):
        return slice(k * tile, (k + 1) * tile)

    squares = jnp.zeros((8, size), jnp.float32)
    for k in range(blocks):
        value = m_ref[place(k), :].astype(jnp.float32)
        squares = squares + jnp.sum((value * value).reshape(tile // 8, 8, size), axis=0)
    scale = 1.0 / (jnp.sqrt(jnp.sum(squares)) + MUON_EPSILON)
    square_scale = scale * scale

    def gram_block(i, j):
        part = dot_nt(m_ref[place(i), :], m_ref[place(j), :]) * square_scale
        gram[place(i), place(j)] = part.astype(jnp.bfloat16)
        if i != j:
            gram[place(j), place(i)] = part.T.astype(jnp.bfloat16)

    for i in range(blocks):
        for j in range(i, blocks):
            gram_block(i, j)
    for i in range(blocks):
        for j in range(i, blocks):
            part = dot_nt(gram[place(i), :], gram[place(j), :])
            part = COEFF_B * gram[place(i), place(j)].astype(jnp.float32) + COEFF_C * part
            mixing[place(i), place(j)] = part.astype(jnp.bfloat16)
            if i != j:
                mixing[place(j), place(i)] = part.T.astype(jnp.bfloat16)

    def taken(ref):
        return jnp.concatenate([ref[first : first + count, :] for first, count in heads], axis=0)

    def times(value, ref):
        return jnp.dot(value.astype(jnp.bfloat16), ref[...], preferred_element_type=jnp.float32)

    def stepped(value):
        return COEFF_A * value + times(value, mixing)

    mixing_own = taken(mixing)
    gram_own = taken(gram).astype(jnp.float32)
    gram_own = stepped(COEFF_A * gram_own + times(mixing_own, gram))
    square_own = stepped(times(stepped(gram_own), gram))
    second_own = COEFF_B * gram_own + COEFF_C * square_own
    weights = COEFF_A * mixing_own.astype(jnp.float32) + stepped(second_own)
    result = COEFF_A * COEFF_A * taken(m_ref).astype(jnp.float32) + times(weights, m_ref)
    out_ref[...] = (scale * result).astype(jnp.bfloat16)


def newton_rows(own, other, parts, heads):
    size = 2 * own[0].shape[0]
    window = sum(count for _, count in heads)
    anywhere = pl.BlockSpec(memory_space=pl.ANY)
    return kernel_call(
        functools.partial(newton_body, parts, heads, 256),
        (1,),
        [anywhere] * (2 * len(parts)),
        whole((window, size)),
        shape_of((window, size), jnp.bfloat16),
        [pltpu.VMEM((size, size), jnp.bfloat16)] * 3 + [pltpu.SemaphoreType.DMA((2 * len(parts),))],
    )(*own, *other)


def swap(value, bit):
    size = lax.axis_size("tm")
    return lax.ppermute(value, "tm", [(i, i ^ bit) for i in range(size)])


def steps_of(size):
    bits = []
    bit = 1
    while bit < size:
        bits.append(bit)
        bit *= 2
    return bits


def bit_of(bit):
    return jnp.where((lax.axis_index("tm") & bit) != 0, 1, 0)


class SumSpread:
    def __init__(self, value):
        self.value = value
        self.steps = []
        lanes = value.shape[1]
        cuts = []
        for bit in steps_of(lax.axis_size("tm")):
            if lanes // 2 % LANE == 0:
                lanes //= 2
                self.steps.append((self.halve, bit))
                cuts.append(bit)
            else:
                self.steps.append((self.pair, bit))
        self.steps += [(self.join, bit) for bit in reversed(cuts)]

    def halve(self, bit):
        lanes = self.value.shape[1] // 2
        mine = lax.dynamic_slice_in_dim(self.value, bit_of(bit) * lanes, lanes, 1)
        away = lax.dynamic_slice_in_dim(self.value, (1 - bit_of(bit)) * lanes, lanes, 1)
        self.value = mine + swap(away, bit)

    def pair(self, bit):
        self.value = self.value + swap(self.value, bit)

    def join(self, bit):
        other = swap(self.value, bit)
        upper = bit_of(bit) == 1
        self.value = jnp.concatenate(
            [jnp.where(upper, other, self.value), jnp.where(upper, self.value, other)], axis=1
        )

    def step(self, times=1):
        for _ in range(times):
            if self.steps:
                action, bit = self.steps.pop(0)
                action(bit)


def tie(first, second):
    return lax.optimization_barrier((list(first), list(second)))


def side_bit():
    return lax.axis_size("tm") // 32


def orders_of(size):
    bits = [bit for bit in steps_of(size) if bit != side_bit()]
    return [bits[k * len(bits) // 3 :] + bits[: k * len(bits) // 3] for k in range(3)]


def index_bits(bits):
    return [bit if bit < side_bit() else bit // 2 for bit in bits]


class Scatter:
    def __init__(self, keeps, sends):
        self.orders = orders_of(lax.axis_size("tm"))
        self.current = list(keeps)
        self.received = [swap(send, side_bit()) for send in sends]

    def step(self, *waiting):
        sends = []
        for p, order in enumerate(self.orders):
            half = self.current[p].shape[0] // 2
            mine, away = [
                lax.dynamic_slice_in_dim(self.current[p], half * index, half)
                + lax.dynamic_slice_in_dim(self.received[p], half * index, half).astype(jnp.float32)
                for index in (bit_of(order[0]), 1 - bit_of(order[0]))
            ]
            self.current[p] = mine
            sends.append(away.astype(jnp.bfloat16))
        sends, waiting = tie(sends, waiting)
        self.received = [swap(send, order.pop(0)) for send, order in zip(sends, self.orders)]
        return waiting

    def join(self, *done):
        self.received, done = tie(self.received, done)
        return done

    def result(self):
        return [a + b.astype(jnp.float32) for a, b in zip(self.current, self.received)]


class Gather:
    def __init__(self, blocks, near):
        self.orders = orders_of(lax.axis_size("tm"))
        self.held = [[] for _ in blocks]
        self.current = list(blocks)
        self.received = None
        self.near = near

    def stack(self):
        if self.received is None:
            return
        for p, other in enumerate(self.received):
            bit, mine = self.held[p][-1], self.current[p]
            axis = sum(before > bit for before in self.held[p])
            if not self.near:
                upper = bit_of(bit) == 1
                mine, other = jnp.where(upper, other, mine), jnp.where(upper, mine, other)
            self.current[p] = jnp.stack([mine, other], axis=axis)

    def step(self, *waiting):
        self.stack()
        self.current, waiting = tie(self.current, waiting)
        self.received = []
        for p, order in enumerate(self.orders):
            bit = order.pop()
            self.held[p].append(bit)
            self.received.append(swap(self.current[p], bit))
        return waiting

    def join(self, *done):
        self.received, done = tie(self.received, done)
        return done

    def finish(self, *waiting):
        self.stack()
        own = [value.reshape(-1, value.shape[-1]) for value in self.current]
        own, waiting = tie(own, waiting)
        return own, [swap(value, side_bit()) for value in own], waiting


class Stats:
    def __init__(self, stat, count):
        self.stat = stat
        self.count = float(count)
        self.bits = steps_of(lax.axis_size("tm"))

    def step(self, times=1):
        for _ in range(min(times, len(self.bits))):
            stat = self.stat
            other = swap(stat, self.bits.pop(0))
            gap = stat[0:1] - other[0:1]
            mean = 0.5 * (stat[0:1] + other[0:1])
            square = (stat[1:2] + other[1:2]) + gap * gap * (0.5 * self.count)
            self.stat = jnp.concatenate([mean, square, 0.5 * (stat[2:] + other[2:])], axis=0)
            self.count *= 2


class Exchange:
    def __init__(self, flags, carries, sums=()):
        self.bits = steps_of(lax.axis_size("tm"))
        high, self.width = carries[0][0].shape
        rows = high * len(carries)
        flags = jnp.broadcast_to(jnp.tile(flags, len(carries))[:, None], (rows, LANE))
        ends = jnp.concatenate([ends for ends, _, _ in carries], axis=0)
        self.payload = jnp.concatenate([ends, flags, *sums], axis=1)
        self.power = jnp.concatenate(
            [jnp.broadcast_to(power, (high, self.width)) for _, power, _ in carries], axis=0
        )
        self.lane = lax.broadcasted_iota(jnp.int32, self.payload.shape, 1)
        self.high = high
        self.reverse = [reverse for _, _, reverse in carries]
        self.before = jnp.zeros_like(ends)
        self.before_keep = jnp.ones_like(ends)

    def step(self, times=1):
        for _ in range(min(times, len(self.bits))):
            self.one()

    def one(self):
        bit = self.bits.pop(0)
        width = self.width
        mine, other = self.payload, swap(self.payload, bit)
        upper = bit_of(bit)
        row = lax.broadcasted_iota(jnp.int32, (len(mine), 1), 0) // self.high
        turned = sum((row == k) * int(reverse) for k, reverse in enumerate(self.reverse))
        following = turned != upper
        other_total = other[:, :width]
        keep_mine, keep_other = mine[:, width : width + 1], other[:, width : width + 1]
        self.before = jnp.where(
            following, self.before_keep * other_total + self.before, self.before
        )
        self.before_keep = jnp.where(
            following, self.before_keep * keep_other * self.power, self.before_keep
        )
        power = jnp.pad(self.power, ((0, 0), (0, mine.shape[1] - width)))
        carried = jnp.where(
            following, keep_mine * power * other + mine, keep_other * power * mine + other
        )
        self.payload = jnp.where(
            self.lane < width,
            carried,
            jnp.where(self.lane < width + LANE, mine * other, mine + other),
        )
        self.power = self.power * self.power

    def arrived(self, k):
        return self.before[k * self.high : (k + 1) * self.high]

    def sums(self):
        return self.payload[:, self.width + LANE :]


class SumAll:
    def __init__(self, value):
        self.value = value
        self.bits = steps_of(lax.axis_size("tm"))

    def step(self, times=1):
        for _ in range(min(times, len(self.bits))):
            self.value = self.value + swap(self.value, self.bits.pop(0))


def in_order(value, bits, slots):
    count = len(bits)
    axes = [count - bit.bit_length() for bit in bits]
    shape = (2,) * count + (slots, value.shape[1])
    return value.reshape(shape).transpose(axes + [count, count + 1]).reshape(value.shape)


def pad_lanes(value, padded):
    gap = padded - value.shape[-1]
    return jnp.pad(value, [(0, 0)] * (value.ndim - 1) + [(0, gap)])


def flat_places(shard, width, padded):
    size = lax.axis_size("tm")
    members = size * LANE // padded
    slots = LANE // members
    return members, slots, slots * width - shard


def to_block(flat, width, padded):
    size, mine = lax.axis_size("tm"), lax.axis_index("tm")
    members, slots, excess = flat_places(flat.shape[0], width, padded)
    lacking = excess * (members - 1)
    pairs = [(i + 1, i) for i in range(size - 1) if (i + 1) % members]
    extra = lax.ppermute(flat[:lacking], "tm", pairs)
    tail = jnp.zeros((excess,), flat.dtype)
    held = jnp.concatenate([flat, extra, tail])
    return lax.dynamic_slice_in_dim(held, excess * (mine % members), slots * width).reshape(
        slots, width
    )


def from_block(block, shard, padded):
    width = block.shape[1]
    size, mine = lax.axis_size("tm"), lax.axis_index("tm")
    members, slots, excess = flat_places(shard, width, padded)
    lacking = excess * (members - 1)
    pairs = [(i, i + 1) for i in range(size - 1) if (i + 1) % members]
    flat = block.reshape(-1)
    extra = lax.ppermute(flat[slots * width - lacking :], "tm", pairs)
    held = jnp.concatenate([extra, flat])
    return lax.dynamic_slice_in_dim(held, lacking - excess * (mine % members), shard)


def own_heads(shard, width, padded):
    members, slots, _ = flat_places(shard, width, padded)
    half = padded // 2
    group = LANE // 2
    if members == 2:
        lacking = slots - shard // width
        kept = -(-(lacking) // 16) * 16
        return [(0, group), (half + group - kept, kept)]
    return [(0, group), (half, group)]


def own_flat(found, shard, width, padded):
    mine = lax.axis_index("tm")
    members, slots, excess = flat_places(shard, width, padded)
    member = mine % members
    if members == 2:
        own, other = found[:slots].reshape(-1), found[slots:].reshape(-1)
        low = own[:shard]
        high = jnp.concatenate([other[other.shape[0] - excess :], own[: shard - excess]])
        return jnp.where(member == 0, low, high)
    near = found.reshape(members, slots * width)
    placed = jnp.take(near, jnp.arange(members) ^ member, axis=0).reshape(-1)
    return lax.dynamic_slice_in_dim(placed, shard * member, shard)


def per_device(
    inputs,
    clip_start,
    shallow_weight,
    shallow_momentum,
    deep_weight,
    deep_momentum,
    unit_params,
    unit_first,
    unit_second,
    out_grad,
):
    devices = lax.axis_size("tm")
    rows, frames, feats = inputs.shape
    width = shallow_weight.shape[1]
    padded = -(-width // WIDE) * WIDE
    group = width // (padded // LANE)
    count = rows * frames
    keep_mask = (1 - clip_start).astype(jnp.float32)
    flags = jnp.min(keep_mask, axis=1)
    keep = jnp.broadcast_to(keep_mask.T.reshape(count, 1), (count, LANE))
    params = pad_lanes(unit_params, padded)
    rates = jnp.maximum(1.0 - jnp.exp(-params[:, 0:1]), DECAY_FLOOR)
    powers = rates
    for _ in range(frames.bit_length() - 1):
        powers = powers * powers

    deep_block = pad_lanes(to_block(deep_weight.astype(jnp.bfloat16), width, padded), padded)
    momentum_block = pad_lanes(to_block(deep_momentum, width, padded), padded)

    shares = [3 * padded // 8, 3 * padded // 8, padded // 4]
    parts = [(sum(shares[:p]), shares[p]) for p in range(3)]
    side = bit_of(side_bit()).astype(jnp.int32).reshape(1)
    chunks = padded // WIDE
    orders = orders_of(devices)
    x, proj_one, stat_one, gram = front(
        inputs.reshape(count, feats), shallow_weight, rows, frames
    )
    (deep_block,), (stat_one,) = tie([deep_block], [stat_one])
    deep_low = lax.all_gather(deep_block, "tm", axis=0, tiled=True)
    stats = Stats(stat_one, count)
    grad_rows = out_grad.reshape(count, width)
    delta = None
    for k in range(chunks):
        stats.step()
        delta = delta_two(k, delta, grad_rows, keep, params[1], rows, frames, padded)
        delta, (stats.stat,) = tie(delta, [stats.stat])
    delta_local, delta_end = delta
    stats.step(len(stats.bits))
    (stat_one,), (momentum_block,) = tie([stats.stat], [momentum_block])
    state_local, state_end = local_states(
        proj_one, keep, params[0], stat_one, rows, frames, devices
    )
    carries = Exchange(flags, [(state_end, powers[0], False)])
    carries.step(len(carries.bits))
    (state_in,), (delta_end,) = tie([carries.arrived(0)], [delta_end])
    later = Exchange(flags, [(delta_end, powers[1], True)], [gram])
    (deep_low,), (later.payload,) = tie([deep_low], [later.payload])
    later.step()
    low_one, mean_one = low_one_of(
        state_local, state_in, keep, params[0], rows, frames, width, group
    )
    proj_two, stat_two = second_forward(low_one, deep_low)
    (stat_two,), (later.payload, later.before) = tie([stat_two], [later.payload, later.before])
    stats = Stats(jnp.concatenate([stat_two, mean_one], axis=0), count)
    while later.bits:
        later.step()
        stats.step()
        (stats.stat,), (later.payload, later.before) = tie(
            [stats.stat], [later.payload, later.before]
        )
    stats.step(len(stats.bits))
    delta_in, gram = later.arrived(0), later.sums()
    hidden = [None, None]
    sources = [(state_local, state_in, params[0]), None]

    def next_hidden(layer, places, waiting):
        states, start, layer_params = sources[layer]
        for k in places:
            (start,), waiting = tie([start], waiting)
            hidden[layer] = hidden_of(
                k, hidden[layer], states, start, keep, layer_params, rows, frames, width
            )
        hidden[layer], waiting = tie(hidden[layer], waiting)
        return waiting

    stat_two, mean_one = stats.stat[:2], stats.stat[2:]
    gate, sums_two = gate_two(
        proj_two, delta_local, delta_in, keep, params[1], stat_two, rows, frames, devices
    )
    sums = SumAll(sums_two)
    turned = None
    for k in range(chunks):
        sums.step()
        turned = turn(k, turned, low_one, mean_one)
        turned, (sums.value,) = tie(turned, [sums.value])
    sums.step(len(sums.bits))
    sums_two = sums.value
    slots = padded // devices
    weights = [index_bits(order) for order in orders]
    aligned = slots % 16 == 0
    grad_two, total_two, keeps, sends = deep_term(
        parts, weights if aligned else None, side, gate, proj_two, params[1], stat_two,
        sums_two, turned[0], rows, frames, devices,
    )
    if not aligned:
        keeps = [in_order(keep, order, slots) for keep, order in zip(keeps, weights)]
        sends = [in_order(send, order, slots) for send, order in zip(sends, weights)]
    scatter = Scatter(keeps, sends)
    back = back_one(grad_two, deep_low)
    (back,) = scatter.join(back)
    (back,) = scatter.step(back)
    back_local, back_end = delta_one(back, keep, params[0], rows, frames, width, group)
    second_local, second_end, second_decay = states_two(
        proj_two, delta_local, delta_in, keep, params[1], stat_two, rows, frames, devices
    )
    back_end, second_end = scatter.join(back_end, second_end)
    tall = 2 * rows
    back_end, second_end = scatter.step(back_end, second_end)
    carries = Exchange(
        flags,
        [(back_end, powers[0], True), (second_end, powers[1], False)],
        [total_two.reshape(tall, -1)],
    )
    carries.step(2)
    (carries.payload,) = next_hidden(0, range(chunks), [carries.payload])
    (carries.payload,) = scatter.join(carries.payload)
    (carries.payload,) = scatter.step(carries.payload)
    carries.step(len(carries.bits))
    back_in, second_in = carries.arrived(0), carries.arrived(1)
    sources[1] = (second_local, second_in, params[1])
    total_two = carries.sums().reshape(1, padded)
    gate_low, sums_one = gate_one(
        proj_one, state_local, state_in, back_local, back_in, keep, params[0], stat_one, x,
        rows, frames, devices, feats,
    )
    decay_two = jnp.sum(second_decay[:rows] + second_decay[rows:] * second_in, axis=0, keepdims=True)
    sums_one = sums_one + jnp.pad(decay_two, ((feats + 3, SIDE - feats - 4), (0, 0)))
    (sums_one,) = scatter.join(sums_one)
    spread = SumSpread(sums_one)
    while scatter.orders[0]:
        (spread.value,) = scatter.step(spread.value)
        spread.step()
        (spread.value,) = scatter.join(spread.value)
    mine = lax.axis_index("tm")
    place = mine // (2 * side_bit()) * side_bit() + mine % side_bit()
    place = (side[0] * (devices // 2) + place) * slots
    mean_own = lax.dynamic_slice_in_dim(mean_one[0], place, slots)[:, None]
    grad_parts = [
        part + mean_own * total_two[:, first : first + lanes]
        for (first, lanes), part in zip(parts, scatter.result())
    ]
    gather = Gather(
        [
            (MUON_BETA * momentum_block[:, first : first + lanes] + part).astype(jnp.bfloat16)
            for (first, lanes), part in zip(parts, grad_parts)
        ],
        True,
    )
    for count_steps, places in ((1, []), (2, []), (2, [0, 1]), (2, [2, 3])):
        (spread.value,) = gather.step(spread.value)
        spread.step(count_steps)
        if places:
            (spread.value,) = next_hidden(1, places, [spread.value])
        (spread.value,) = gather.join(spread.value)
    while gather.orders[0]:
        gather.step()
    own, other, (spread.value,) = gather.finish(spread.value)
    spread.step(len(spread.steps))
    sums_one = spread.value
    (hidden_one,), (hidden_two,) = hidden
    shallow_grad, shallow_next, shallow_new, shallow_low = shallow_step(
        sums_one, gram, params[0], stat_one, shallow_weight, shallow_momentum,
        count * devices, count,
    )
    input_back = input_grad_of(
        gate_low, proj_one, params[0], stat_one, sums_one, shallow_weight, rows, frames, devices
    )
    input_grad = jnp.swapaxes(input_back.reshape(frames, rows, feats), 0, 1)
    grad_block = jnp.concatenate(grad_parts, axis=1)

    shard = deep_weight.shape[0]
    heads = own_heads(shard, width, padded)
    ortho = newton_rows(own, other, parts, heads)
    deep_ortho = own_flat(ortho[:, :width], shard, width, padded)
    deep_new = MUON_KEEP * deep_weight - MUON_RATE * deep_ortho.astype(jnp.float32)
    deep_grad = from_block(grad_block[:, :width], shard, padded)
    deep_next = MUON_BETA * deep_momentum + deep_grad

    unit_sums = sums_one[feats : feats + 4, :width]
    bias_gain_two = sums_two[:, :width]
    slope = jnp.where(
        1.0 - jnp.exp(-unit_params[:, 0]) > DECAY_FLOOR, jnp.exp(-unit_params[:, 0]), 0.0
    )
    unit_grad = jnp.stack(
        [
            jnp.stack([unit_sums[2] * slope[0], unit_sums[0], unit_sums[1], unit_sums[0]]),
            jnp.stack(
                [unit_sums[3] * slope[1], bias_gain_two[0], bias_gain_two[1], bias_gain_two[0]]
            ),
        ]
    )
    first_fix = 1.0 - FIRST_DECAY**STEP
    second_fix = 1.0 - SECOND_DECAY**STEP
    first_new = FIRST_DECAY * unit_first + (1.0 - FIRST_DECAY) * unit_grad
    second_new = SECOND_DECAY * unit_second + (1.0 - SECOND_DECAY) * unit_grad * unit_grad
    params_new = unit_params - ADAM_RATE * (first_new / first_fix) / (
        jnp.sqrt(second_new / second_fix) + ADAM_EPSILON
    )
    return (
        hidden_one.reshape(rows, frames, width),
        hidden_two.reshape(rows, frames, width),
        input_grad,
        shallow_grad,
        shallow_next,
        shallow_new,
        shallow_low,
        deep_grad,
        deep_next,
        deep_new,
        deep_new.astype(jnp.bfloat16),
        first_new,
        second_new,
        params_new,
    )


def solution(mesh):
    in_specs = (
        P(None, "tm", None),
        P(None, "tm"),
        P(),
        P(),
        P("tm"),
        P("tm"),
        P(),
        P(),
        P(),
        P(None, "tm", None),
    )
    out_specs = (
        P(None, "tm", None),
        P(None, "tm", None),
        P(None, "tm", None),
        P(),
        P(),
        P(),
        P(),
        P("tm"),
        P("tm"),
        P("tm"),
        P("tm"),
        P(),
        P(),
        P(),
    )
    return jax.shard_map(
        per_device, mesh=mesh, in_specs=in_specs, out_specs=out_specs, check_vma=False
    )
```

```python
import functools

import jax
import jax.numpy as jnp
from jax import lax
from jax.experimental import pallas as pl
from jax.experimental.pallas import tpu as pltpu
from jax.sharding import PartitionSpec as P

NS_STEPS = 2
STEP = 5


NORM_EPSILON = 1e-05
MUON_EPSILON = 1e-07
COEFF_A = 3.4445
COEFF_B = -4.775
COEFF_C = 2.0315
MUON_BETA = 0.5
MUON_RATE = 4.0
MUON_KEEP = 0.999
FIRST_DECAY = 0.9
SECOND_DECAY = 0.95
ADAM_RATE = 0.5
ADAM_EPSILON = 1e-08
DECAY_FLOOR = 0.9
LANE = 128
WIDE = 512
PART = 256
SIDE = 80


def kernel_call(body, grid, in_specs, out_specs, out_shape, scratch=(), flops=0, traffic=0):
    return pl.pallas_call(
        body,
        grid=grid,
        in_specs=in_specs,
        out_specs=out_specs,
        out_shape=out_shape,
        scratch_shapes=list(scratch),
        compiler_params=pltpu.CompilerParams(vmem_limit_bytes=56 * 1024 * 1024),
        cost_estimate=pl.CostEstimate(flops=flops, bytes_accessed=traffic, transcendentals=0),
    )


def shape_of(shape, dtype=jnp.float32):
    return jax.ShapeDtypeStruct(shape, dtype)


def whole(shape):
    return pl.BlockSpec(shape, lambda i: (0,) * len(shape))


def lanes_of(rows, width=WIDE):
    return pl.BlockSpec((rows, width), lambda i: (0, i))


def chunk_call(body, place, in_specs, out_specs, out_shape, arrays, previous, scratch=(), traffic=0):
    count = len(in_specs)
    before = list(previous) if previous is not None else []

    def run(*refs):
        body(*refs[:count], *refs[count + len(before) :])

    return pl.pallas_call(
        run,
        grid=(1,),
        in_specs=list(in_specs) + [pl.BlockSpec(memory_space=pl.ANY)] * len(before),
        out_specs=out_specs,
        out_shape=out_shape,
        scratch_shapes=list(scratch),
        input_output_aliases={count + k: k for k in range(len(before))},
        compiler_params=pltpu.CompilerParams(vmem_limit_bytes=56 * 1024 * 1024),
        cost_estimate=pl.CostEstimate(flops=0, bytes_accessed=traffic, transcendentals=0),
    )(*arrays, *before)


def chunk_at(rows, place):
    return pl.BlockSpec((rows, WIDE), lambda i: (0, place))


def rate_of(params):
    return jnp.maximum(1.0 - jnp.exp(-params[0:1]), DECAY_FLOOR)


def softened(value):
    return jnp.maximum(value, 0.0) + jnp.log(1.0 + jnp.exp(-jnp.abs(value)))


def sigmoid(value):
    return 0.5 * jnp.tanh(0.5 * value) + 0.5


def wide_keep(keep_ref, t, rows):
    keep = keep_ref[pl.ds(pl.multiple_of(t * rows, rows), rows), :]
    return jnp.concatenate([keep] * (WIDE // LANE), axis=1)


def rows_at(ref, t, rows):
    return ref[pl.ds(pl.multiple_of(t * rows, rows), rows), :]


def store_at(ref, t, rows, value):
    ref[pl.ds(pl.multiple_of(t * rows, rows), rows), :] = value


def valid_lanes(shape, total, step):
    return lax.broadcasted_iota(jnp.int32, shape, 1) + step * WIDE < total


def unit_terms(params_ref, stat_ref, total_devices, frames):
    params = params_ref[...]
    stat = stat_ref[...]
    centre = stat[0:1]
    inverse = lax.rsqrt(stat[1:2] / (total_devices * frames) + NORM_EPSILON)
    return centre, inverse, params[2:3], params[3:4] + params[1:2]


def front_body(rows, frames, width, x_ref, w_ref, xt_ref, proj_ref, stat_ref, gram_ref, padded_w):
    step = pl.program_id(0)
    count, feats = x_ref.shape

    @pl.when(step == 0)
    def _():
        i = lax.broadcasted_iota(jnp.int32, (count, count), 0)
        j = lax.broadcasted_iota(jnp.int32, (count, count), 1)
        move = (j == lax.rem(i, rows) * frames + lax.div(i, rows)).astype(jnp.bfloat16)
        moved = jnp.dot(move, x_ref[...], preferred_element_type=jnp.float32).astype(jnp.bfloat16)
        i = lax.broadcasted_iota(jnp.int32, (feats, LANE), 0)
        j = lax.broadcasted_iota(jnp.int32, (feats, LANE), 1)
        wide = jnp.dot(moved, (i == j).astype(jnp.bfloat16), preferred_element_type=jnp.float32)
        lane = lax.broadcasted_iota(jnp.int32, (count, LANE), 1)
        xt = jnp.where(lane == feats, 1.0, wide).astype(jnp.bfloat16)
        xt_ref[...] = xt
        gram = dot_tn(xt, xt)
        high = gram_ref.shape[0]
        for k in range(SIDE // high):
            gram_ref[:, k * LANE : (k + 1) * LANE] = gram[k * high : (k + 1) * high]
        padded_w[...] = jnp.zeros_like(padded_w)

    weight = w_ref[...]
    padded_w[0:feats, :] = jnp.where(valid_lanes(weight.shape, width, step), weight, 0.0)
    proj = jnp.dot(
        xt_ref[...], padded_w[...].astype(jnp.bfloat16), preferred_element_type=jnp.float32
    )
    proj_ref[...] = proj
    mean = jnp.sum(proj, axis=0, keepdims=True) * (1.0 / count)
    off = proj - mean
    stat_ref[0:1, :] = mean
    stat_ref[1:2, :] = jnp.sum(off * off, axis=0, keepdims=True)


def dot_tn(a, b):
    return lax.dot_general(a, b, (((0,), (0,)), ((), ())), preferred_element_type=jnp.float32)


def front(x, weight, rows, frames):
    count, feats = x.shape
    width = weight.shape[1]
    padded = -(-width // WIDE) * WIDE
    return kernel_call(
        functools.partial(front_body, rows, frames, width),
        (padded // WIDE,),
        [whole((count, feats)), lanes_of(feats)],
        [whole((count, LANE)), lanes_of(count), lanes_of(2), whole((rows, SIDE // rows * LANE))],
        [
            shape_of((count, LANE), jnp.bfloat16),
            shape_of((count, padded)),
            shape_of((2, padded)),
            shape_of((rows, SIDE // rows * LANE)),
        ],
        [pltpu.VMEM((LANE, WIDE), jnp.float32)],
    )(x, weight)


def delta_two_body(rows, frames, width, place, grad_ref, keep_ref, params_ref, delta_ref, end_ref, held):
    pieces = WIDE // LANE
    mask = valid_lanes((rows * frames, WIDE), width, place)
    grad = jnp.where(mask, grad_ref[...].astype(jnp.float32), 0.0)
    for g in range(pieces):
        held[g] = grad[:, g * LANE : (g + 1) * LANE]
    rate = rate_of(params_ref[...])

    def body(k, carried):
        t = frames - 1 - k
        own = jnp.concatenate(
            [held[g, pl.ds(t, rows, stride=frames), :] for g in range(pieces)], axis=1
        )
        delta = own + carried
        store_at(delta_ref, t, rows, delta)
        return rate * wide_keep(keep_ref, t, rows) * delta

    end_ref[...] = lax.fori_loop(
        0, frames, body, jnp.zeros((rows, WIDE), jnp.float32), unroll=8
    )


def delta_two(place, previous, out_grad, keep, params, rows, frames, padded):
    count, width = out_grad.shape
    return chunk_call(
        functools.partial(delta_two_body, rows, frames, width, place),
        place,
        [chunk_at(count, place), whole((count, LANE)), chunk_at(4, place)],
        [chunk_at(count, place), chunk_at(rows, place)],
        [shape_of((count, padded)), shape_of((rows, padded))],
        (out_grad, keep, params),
        previous,
        [pltpu.VMEM((WIDE // LANE, count, LANE), jnp.float32)],
    )


def states_body(
    rows, frames, devices, proj_ref, keep_ref, params_ref, stat_ref, state_ref, end_ref
):
    centre, inverse, gain, offset = unit_terms(params_ref, stat_ref, devices, rows * frames)
    rate = rate_of(params_ref[...])
    share = 1.0 - rate

    def body(t, carried):
        gate = (rows_at(proj_ref, t, rows) - centre) * inverse * gain + offset
        soft = softened(gate)
        carried = rate * wide_keep(keep_ref, t, rows) * carried + share * soft
        store_at(state_ref, t, rows, carried)
        return carried

    end_ref[...] = lax.fori_loop(
        0, frames, body, jnp.zeros((rows, WIDE), jnp.float32), unroll=8
    )


def local_states(proj, keep, params, stat, rows, frames, devices):
    count, padded = proj.shape
    return kernel_call(
        functools.partial(states_body, rows, frames, devices),
        (padded // WIDE,),
        [lanes_of(count), whole((count, LANE)), lanes_of(4), lanes_of(2)],
        [lanes_of(count), lanes_of(rows)],
        [shape_of((count, padded)), shape_of((rows, padded))],
    )(proj, keep, params, stat)


def to_slots(value, group):
    pieces = value.shape[1] // LANE
    lane = lax.broadcasted_iota(jnp.int32, (value.shape[0], LANE), 1)
    parts = [value[:, g * LANE : (g + 1) * LANE] for g in range(pieces)]
    out = []
    for g in range(pieces):
        moved = (LANE - group) * g
        if moved == 0:
            new = parts[g]
        else:
            new = jnp.where(
                lane < moved, pltpu.roll(parts[g - 1], moved, 1), pltpu.roll(parts[g], moved, 1)
            )
        out.append(jnp.where(lane < group, new, 0.0))
    half = LANE // 2
    low = [
        jnp.where(lane < half, out[g], pltpu.roll(out[g + 1], half, 1)) for g in range(0, pieces, 2)
    ]
    high = [
        jnp.where(lane < half, pltpu.roll(out[g], half, 1), out[g + 1]) for g in range(0, pieces, 2)
    ]
    return jnp.concatenate(low + high, axis=1)


def from_slots(value, group, width):
    pieces = value.shape[1] // LANE
    lane = lax.broadcasted_iota(jnp.int32, (value.shape[0], LANE), 1)
    half = LANE // 2
    parts = []
    for g in range(pieces // 2):
        low = value[:, g * LANE : (g + 1) * LANE]
        high = value[:, (g + pieces // 2) * LANE : (g + pieces // 2 + 1) * LANE]
        parts.append(jnp.where(lane < half, low, pltpu.roll(high, half, 1)))
        parts.append(jnp.where(lane < half, pltpu.roll(low, half, 1), high))
    out = []
    for j in range(pieces):
        moved = (LANE - group) * j
        new = parts[j] if moved == 0 else pltpu.roll(parts[j], LANE - moved, 1)
        if j + 1 < pieces:
            new = jnp.where(lane < group - moved, new, pltpu.roll(parts[j + 1], group - moved, 1))
        left = width - j * LANE
        out.append(new if left >= LANE else jnp.where(lane < left, new, 0.0))
    return jnp.concatenate(out, axis=1)


def low_one_body(rows, frames, width, group, state_ref, start_ref, keep_ref, params_ref, low_ref, mean_ref):
    pieces = state_ref.shape[1] // LANE
    rate = rate_of(params_ref[...])

    def advance(t, carried):
        keep = rows_at(keep_ref, t, rows)
        carried = rate * jnp.concatenate([keep] * pieces, axis=1) * carried
        return carried, rows_at(state_ref, t, rows) + carried

    def body(k, both):
        carried, total = both
        t = 2 * k
        carried, first = advance(t, carried)
        carried, second = advance(t + 1, carried)
        place = pl.ds(pl.multiple_of(t * rows, 2 * rows), 2 * rows)
        slots = to_slots(jnp.concatenate([first, second], axis=0), group)
        low_ref[place, :] = slots.astype(jnp.bfloat16)
        return carried, total + slots[:rows] + slots[rows:]

    start = start_ref[...]
    _, total = lax.fori_loop(0, frames // 2, body, (start, jnp.zeros_like(start)), unroll=2)
    mean_ref[...] = jnp.sum(total, axis=0, keepdims=True) * (1.0 / (rows * frames))


def low_one_of(states, start, keep, params, rows, frames, width, group):
    count, padded = states.shape
    return kernel_call(
        functools.partial(low_one_body, rows, frames, width, group),
        (1,),
        [whole((count, padded)), whole((rows, padded)), whole((count, LANE)), whole((4, padded))],
        [whole((count, padded)), whole((1, padded))],
        [shape_of((count, padded), jnp.bfloat16), shape_of((1, padded))],
    )(states, start, keep, params)


def hidden_body(rows, frames, state_ref, start_ref, keep_ref, params_ref, hidden_ref, held):
    pieces = WIDE // LANE
    rate = rate_of(params_ref[...])

    def body(t, carry):
        carry = rate * wide_keep(keep_ref, t, rows) * carry
        state = rows_at(state_ref, t, rows) + carry
        for g in range(pieces):
            held[g, pl.ds(pl.multiple_of(t * rows, rows), rows), :] = state[
                :, g * LANE : (g + 1) * LANE
            ]
        return carry

    lax.fori_loop(0, frames, body, start_ref[...], unroll=8)
    for r in range(rows):
        for g in range(pieces):
            hidden_ref[r * frames : (r + 1) * frames, g * LANE : (g + 1) * LANE] = held[
                g, pl.ds(r, frames, stride=rows), :
            ]


def hidden_of(place, previous, states, start, keep, params, rows, frames, width):
    count, _ = states.shape
    return chunk_call(
        functools.partial(hidden_body, rows, frames),
        place,
        [chunk_at(count, place), chunk_at(rows, place), whole((count, LANE)), chunk_at(4, place)],
        [chunk_at(count, place)],
        [shape_of((count, width))],
        (states, start, keep, params),
        previous,
        [pltpu.VMEM((WIDE // LANE, count, LANE), jnp.float32)],
    )


def second_body(parts, side_ref, low_ref, *refs):
    weights, (proj_ref, stat_ref, held, sems) = refs[: 2 * len(parts)], refs[2 * len(parts) :]
    half = held.shape[1]
    copies = []
    for k, weight in enumerate(weights):
        first, lanes = parts[k % len(parts)]
        copies.append(
            pltpu.make_async_copy(
                weight, held.at[k // len(parts), :, first : first + lanes], sems.at[k]
            )
        )
    for p in range(len(parts)):
        copies[p].start()
        copies[len(parts) + p].start()
    side = side_ref[0]
    own = low_ref[:, pl.ds(pl.multiple_of(side * half, half), half)]
    other = low_ref[:, pl.ds(pl.multiple_of((1 - side) * half, half), half)]
    for p, (first, lanes) in enumerate(parts):
        copies[p].wait()
        copies[len(parts) + p].wait()
        for at in range(first, first + lanes, PART):
            place = slice(at, at + PART)
            proj = jnp.dot(own, held[0, :, place], preferred_element_type=jnp.float32)
            proj += jnp.dot(other, held[1, :, place], preferred_element_type=jnp.float32)
            proj_ref[:, place] = proj
            mean = jnp.sum(proj, axis=0, keepdims=True) * (1.0 / proj.shape[0])
            off = proj - mean
            stat_ref[0:1, place] = mean
            stat_ref[1:2, place] = jnp.sum(off * off, axis=0, keepdims=True)


def second_forward(side, low, own, other, parts):
    count, padded = low.shape
    return kernel_call(
        functools.partial(second_body, parts),
        (1,),
        [pl.BlockSpec(memory_space=pltpu.SMEM), whole((count, padded))]
        + [pl.BlockSpec(memory_space=pl.ANY)] * (2 * len(parts)),
        [whole((count, padded)), whole((2, padded))],
        [shape_of((count, padded)), shape_of((2, padded))],
        [
            pltpu.VMEM((2, padded // 2, padded), jnp.bfloat16),
            pltpu.SemaphoreType.DMA((2 * len(parts),)),
        ],
    )(side, low, *own, *other)


def gate_two_body(
    rows, frames, devices, proj_ref, delta_ref, start_ref, keep_ref, params_ref, stat_ref, gate_ref, sums_ref
):
    centre, inverse, gain, offset = unit_terms(params_ref, stat_ref, devices, rows * frames)
    rate = rate_of(params_ref[...])
    share = 1.0 - rate
    none = jnp.zeros((rows, WIDE), jnp.float32)

    def body(k, carried):
        carry, bias_sum, gain_sum = carried
        t = frames - 1 - k
        delta = rows_at(delta_ref, t, rows) + carry
        normed = (rows_at(proj_ref, t, rows) - centre) * inverse
        gate = share * delta * sigmoid(normed * gain + offset)
        store_at(gate_ref, t, rows, gate)
        carry = rate * wide_keep(keep_ref, t, rows) * carry
        return carry, bias_sum + gate, gain_sum + gate * normed

    _, bias_sum, gain_sum = lax.fori_loop(
        0, frames, body, (start_ref[...], none, none), unroll=8
    )
    sums_ref[0:1, :] = jnp.sum(bias_sum, axis=0, keepdims=True)
    sums_ref[1:2, :] = jnp.sum(gain_sum, axis=0, keepdims=True)


def gate_two(proj, delta, start, keep, params, stat, rows, frames, devices):
    count, padded = proj.shape
    return kernel_call(
        functools.partial(gate_two_body, rows, frames, devices),
        (padded // WIDE,),
        [lanes_of(count), lanes_of(count), lanes_of(rows), whole((count, LANE)), lanes_of(4), lanes_of(2)],
        [lanes_of(count), lanes_of(2)],
        [shape_of((count, padded)), shape_of((2, padded))],
    )(proj, delta, start, keep, params, stat)


def states_two_body(
    rows, frames, devices, proj_ref, delta_ref, start_ref, keep_ref, params_ref, stat_ref,
    state_ref, end_ref, decay_ref, held,
):
    centre, inverse, gain, offset = unit_terms(params_ref, stat_ref, devices, rows * frames)
    rate = rate_of(params_ref[...])
    share = 1.0 - rate
    none = jnp.zeros((rows, WIDE), jnp.float32)

    def backward(k, carry):
        t = frames - 1 - k
        store_at(held, t, rows, rows_at(delta_ref, t, rows) + carry)
        return rate * wide_keep(keep_ref, t, rows) * carry

    lax.fori_loop(0, frames, backward, start_ref[...], unroll=8)

    def forward(t, carried):
        state, reach, decay, factor = carried
        keep = wide_keep(keep_ref, t, rows)
        delta = rows_at(held, t, rows)
        value = (rows_at(proj_ref, t, rows) - centre) * inverse * gain + offset
        soft = softened(value)
        decay = decay + delta * (keep * state - soft)
        factor = factor + delta * keep * reach
        state = rate * keep * state + share * soft
        reach = rate * keep * reach
        store_at(state_ref, t, rows, state)
        return state, reach, decay, factor

    state, _, decay, factor = lax.fori_loop(
        0, frames, forward, (none, jnp.ones_like(none), none, none), unroll=4
    )
    end_ref[...] = state
    decay_ref[0:rows, :] = decay
    decay_ref[rows : 2 * rows, :] = factor


def states_two(proj, delta, start, keep, params, stat, rows, frames, devices):
    count, padded = proj.shape
    return kernel_call(
        functools.partial(states_two_body, rows, frames, devices),
        (padded // WIDE,),
        [
            lanes_of(count),
            lanes_of(count),
            lanes_of(rows),
            whole((count, LANE)),
            lanes_of(4),
            lanes_of(2),
        ],
        [lanes_of(count), lanes_of(rows), lanes_of(2 * rows)],
        [shape_of((count, padded)), shape_of((rows, padded)), shape_of((2 * rows, padded))],
        [pltpu.VMEM((count, WIDE), jnp.float32)],
    )(proj, delta, start, keep, params, stat)


def turn_body(low_ref, mean_ref, turned_ref):
    turned_ref[...] = (low_ref[...].astype(jnp.float32) - mean_ref[...]).T.astype(jnp.bfloat16)


def turn(place, previous, low, mean):
    count, padded = low.shape
    return chunk_call(
        turn_body,
        place,
        [chunk_at(count, place), chunk_at(1, place)],
        [pl.BlockSpec((WIDE, count), lambda i: (place, 0))],
        [shape_of((padded, count), jnp.bfloat16)],
        (low, mean),
        previous,
    )


def deep_term_body(
    rows, frames, devices, parts, orders, side_ref, gate_ref, proj_ref, params_ref, stat_ref, sums_ref,
    turned_ref, grad_ref, total_ref, *outs,
):
    step = pl.program_id(0)
    total = devices * rows * frames
    centre, inverse, gain, _ = unit_terms(params_ref, stat_ref, devices, rows * frames)
    sums = sums_ref[...] * (1.0 / total)
    normed = (proj_ref[...] - centre) * inverse
    grad = (gain * inverse * (gate_ref[...] - sums[0:1] - normed * sums[1:2])).astype(jnp.bfloat16)
    grad_ref[...] = grad
    total_ref[...] = jnp.sum(grad.astype(jnp.float32), axis=0, keepdims=True)
    side = side_ref[0]
    half = turned_ref.shape[0] // 2
    tile = 256
    for p, (first, lanes) in enumerate(parts):

        @pl.when((step >= first // PART) & (step < (first + lanes) // PART))
        def _():
            for which, out_ref in ((side, outs[p]), (1 - side, outs[len(parts) + p])):
                for k in range(half // tile):
                    start = pl.multiple_of(which * half + k * tile, tile)
                    part = jnp.dot(
                        turned_ref[pl.ds(start, tile), :],
                        grad_ref[...],
                        preferred_element_type=jnp.float32,
                    ).astype(out_ref.dtype)
                    if orders is None:
                        out_ref[k * tile : (k + 1) * tile, :] = part
                        continue
                    slots = half // 2 ** len(orders[p])
                    for b in range(tile // slots):
                        block = k * (tile // slots) + b
                        place = 0
                        for weight in orders[p]:
                            place = 2 * place + block // weight % 2
                        out_ref[place * slots : (place + 1) * slots, :] = part[
                            b * slots : (b + 1) * slots
                        ]


def deep_term(parts, orders, side, gate, proj, params, stat, sums, turned, rows, frames, devices):
    count, padded = proj.shape
    half = padded // 2

    def some(first, lanes):
        return pl.BlockSpec(
            (half, PART), lambda i: (0, jnp.clip(i - first // PART, 0, lanes // PART - 1))
        )

    found = kernel_call(
        functools.partial(deep_term_body, rows, frames, devices, parts, orders),
        (padded // PART,),
        [
            pl.BlockSpec(memory_space=pltpu.SMEM),
            lanes_of(count, PART),
            lanes_of(count, PART),
            lanes_of(4, PART),
            lanes_of(2, PART),
            lanes_of(2, PART),
            whole((padded, count)),
        ],
        [lanes_of(count, PART), lanes_of(1, PART)] + [some(*part) for part in parts] * 2,
        [shape_of((count, padded), jnp.bfloat16), shape_of((1, padded))]
        + [shape_of((half, lanes), jnp.bfloat16) for _, lanes in parts] * 2,
    )(side, gate, proj, params, stat, sums, turned)
    return found[0], found[1], found[2 : 2 + len(parts)], found[2 + len(parts) :]


def back_body(parts, grad_ref, *refs):
    for side, back_ref in enumerate(refs[2 * len(parts) :]):
        total = 0.0
        for p, (first, lanes) in enumerate(parts):
            total += dot_nt(grad_ref[:, first : first + lanes], refs[side * len(parts) + p][...])
        back_ref[...] = total


def back_one(grad, own, other, parts):
    count, padded = grad.shape
    half = padded // 2
    return kernel_call(
        functools.partial(back_body, parts),
        (half // PART,),
        [whole(grad.shape)]
        + [pl.BlockSpec((PART, lanes), lambda i: (i, 0)) for _, lanes in parts] * 2,
        [lanes_of(count, PART)] * 2,
        [shape_of((count, half))] * 2,
    )(grad, *own, *other)


def delta_one_body(
    rows, frames, width, group, side_ref, own_ref, other_ref, keep_ref, params_ref, delta_ref, end_ref
):
    padded = delta_ref.shape[1]
    rate = rate_of(params_ref[...])
    straight = side_ref[0] == 0

    def body(k, carried):
        t = frames - 1 - k
        own, other = rows_at(own_ref, t, rows), rows_at(other_ref, t, rows)
        both = jnp.concatenate(
            [jnp.where(straight, own, other), jnp.where(straight, other, own)], axis=1
        )
        delta = from_slots(both, group, width) + carried
        store_at(delta_ref, t, rows, delta)
        keep = rows_at(keep_ref, t, rows)
        return rate * jnp.concatenate([keep] * (padded // LANE), axis=1) * delta

    end_ref[...] = lax.fori_loop(0, frames, body, jnp.zeros((rows, padded), jnp.float32), unroll=2)


def delta_one(side, own, other, keep, params, rows, frames, width, group):
    count, half = own.shape
    padded = 2 * half
    return kernel_call(
        functools.partial(delta_one_body, rows, frames, width, group),
        (1,),
        [
            pl.BlockSpec(memory_space=pltpu.SMEM),
            whole((count, half)),
            whole((count, half)),
            whole((count, LANE)),
            whole((4, padded)),
        ],
        [whole((count, padded)), whole((rows, padded))],
        [shape_of((count, padded)), shape_of((rows, padded))],
    )(side, own, other, keep, params)


def gate_one_body(
    rows,
    frames,
    devices,
    feats,
    proj_ref,
    state_ref,
    first_ref,
    delta_ref,
    start_ref,
    keep_ref,
    params_ref,
    stat_ref,
    x_ref,
    gate_ref,
    sums_ref,
    held,
):
    centre, inverse, gain, offset = unit_terms(params_ref, stat_ref, devices, rows * frames)
    rate = rate_of(params_ref[...])
    share = 1.0 - rate
    none = jnp.zeros((rows, WIDE), jnp.float32)

    def backward(k, carry):
        t = frames - 1 - k
        store_at(held, t, rows, rows_at(delta_ref, t, rows) + carry)
        return rate * wide_keep(keep_ref, t, rows) * carry

    lax.fori_loop(0, frames, backward, start_ref[...], unroll=8)

    def forward(t, carried):
        carry, before, bias_sum, gain_sum, decay_sum = carried
        keep = wide_keep(keep_ref, t, rows)
        delta = rows_at(held, t, rows)
        normed = (rows_at(proj_ref, t, rows) - centre) * inverse
        value = normed * gain + offset
        soft = softened(value)
        gate = share * delta * sigmoid(value)
        store_at(gate_ref, t, rows, gate)
        decay_sum = decay_sum + delta * (keep * before - soft)
        carry = rate * keep * carry
        before = rows_at(state_ref, t, rows) + carry
        return carry, before, bias_sum + gate, gain_sum + gate * normed, decay_sum

    first = first_ref[...]
    _, _, bias_sum, gain_sum, decay_sum = lax.fori_loop(
        0, frames, forward, (first, first, none, none, none), unroll=4
    )
    bias = jnp.sum(bias_sum, axis=0, keepdims=True)
    mean = bias * (1.0 / (rows * frames))
    x = x_ref[...]
    ones = jnp.ones((rows * frames, LANE), jnp.bfloat16)
    total = jnp.concatenate([dot_tn(x, ones)] * (WIDE // LANE), axis=1)
    term = dot_tn(x, (gate_ref[...] - mean).astype(jnp.bfloat16)) + total * mean
    sums_ref[...] = term[: sums_ref.shape[0]]
    sums_ref[feats : feats + 1, :] = bias
    sums_ref[feats + 1 : feats + 2, :] = jnp.sum(gain_sum, axis=0, keepdims=True)
    sums_ref[feats + 2 : feats + 3, :] = jnp.sum(decay_sum, axis=0, keepdims=True)


def gate_one(proj, states, first, delta, start, keep, params, stat, x, rows, frames, devices, feats):
    count, padded = proj.shape
    return kernel_call(
        functools.partial(gate_one_body, rows, frames, devices, feats),
        (padded // WIDE,),
        [
            lanes_of(count),
            lanes_of(count),
            lanes_of(rows),
            lanes_of(count),
            lanes_of(rows),
            whole((count, LANE)),
            lanes_of(4),
            lanes_of(2),
            whole((count, LANE)),
        ],
        [lanes_of(count), lanes_of(SIDE)],
        [shape_of((count, padded)), shape_of((SIDE, padded))],
        [pltpu.VMEM((count, WIDE), jnp.float32)],
    )(proj, states, first, delta, start, keep, params, stat, x)


def input_grad_body(
    rows, frames, devices, width, feats, gate_ref, proj_ref, params_ref, stat_ref, sums_ref, w_ref, back_ref
):
    step = pl.program_id(0)
    total = devices * rows * frames
    centre, inverse, gain, _ = unit_terms(params_ref, stat_ref, devices, rows * frames)
    bias = sums_ref[feats : feats + 1, :] * (1.0 / total)
    slope = sums_ref[feats + 1 : feats + 2, :] * (1.0 / total)
    normed = (proj_ref[...] - centre) * inverse
    grad = (gain * inverse * (gate_ref[...] - bias - normed * slope)).astype(jnp.bfloat16)
    weight = w_ref[...]
    weight = jnp.where(valid_lanes(weight.shape, width, step), weight, 0.0).astype(jnp.bfloat16)
    part = dot_nt(grad, weight)

    @pl.when(step == 0)
    def _():
        back_ref[...] = part

    @pl.when(step > 0)
    def _():
        back_ref[...] += part


def input_grad_of(gate, proj, params, stat, sums, weight, rows, frames, devices):
    count, padded = proj.shape
    feats, width = weight.shape
    return kernel_call(
        functools.partial(input_grad_body, rows, frames, devices, width, feats),
        (padded // WIDE,),
        [lanes_of(count), lanes_of(count), lanes_of(4), lanes_of(2), lanes_of(SIDE), lanes_of(feats)],
        whole((count, feats)),
        shape_of((count, feats)),
    )(gate, proj, params, stat, sums, weight)


def dot_nt(a, b):
    return lax.dot_general(a, b, (((1,), (1,)), ((), ())), preferred_element_type=jnp.float32)


def shallow_body(
    total, frames, sums_ref, gram_ref, params_ref, stat_ref, w_ref, m_ref,
    grad_ref, next_ref, new_ref, low_ref, held,
):
    feats, width = w_ref.shape
    centre, inverse, gain, _ = unit_terms(params_ref, stat_ref, total // frames, frames)
    weight = w_ref[...]
    held[...] = jnp.zeros_like(held)
    held[0:feats, 0:width] = weight
    high = gram_ref.shape[0]
    gram = jnp.concatenate(
        [gram_ref[:, k * LANE : (k + 1) * LANE] for k in range(SIDE // high)], axis=0
    )
    lane = lax.broadcasted_iota(jnp.int32, gram.shape, 1)
    x_sum = jnp.sum(jnp.where(lane == feats, gram, 0.0), axis=1, keepdims=True)
    raw = jnp.dot(
        gram[:, :SIDE],
        held[...].astype(jnp.bfloat16).astype(jnp.float32),
        precision=lax.Precision.HIGHEST,
        preferred_element_type=jnp.float32,
    )
    normed = (raw - x_sum * centre) * inverse
    bias = sums_ref[feats : feats + 1, :] * (1.0 / total)
    slope = sums_ref[feats + 1 : feats + 2, :] * (1.0 / total)
    grad = gain * inverse * (sums_ref[...] - x_sum * bias - normed * slope)
    grad = grad[:feats, :width]
    grad_ref[...] = grad
    following = MUON_BETA * m_ref[...] + grad
    next_ref[...] = following
    held[0:feats, 0:width] = following
    m = held[...]
    current = (m / (jnp.sqrt(jnp.sum(m * m)) + MUON_EPSILON)).astype(jnp.bfloat16)
    for repeat in range(NS_STEPS):
        gram = dot_nt(current, current).astype(jnp.bfloat16)
        square = jnp.dot(gram, gram, preferred_element_type=jnp.float32)
        mixing = (COEFF_B * gram.astype(jnp.float32) + COEFF_C * square).astype(jnp.bfloat16)
        current = (
            COEFF_A * current.astype(jnp.float32)
            + jnp.dot(mixing, current, preferred_element_type=jnp.float32)
        ).astype(jnp.bfloat16)
    new = MUON_KEEP * weight - MUON_RATE * current[:feats, :width].astype(jnp.float32)
    new_ref[...] = new
    low_ref[...] = new.astype(jnp.bfloat16)


def shallow_step(sums, gram, params, stat, weight, momentum, total, frames):
    padded = sums.shape[1]
    some = shape_of(weight.shape)
    return kernel_call(
        functools.partial(shallow_body, total, frames),
        (1,),
        [whole(value.shape) for value in (sums, gram, params, stat, weight, momentum)],
        [whole(weight.shape)] * 4,
        [some, some, some, shape_of(weight.shape, jnp.bfloat16)],
        [pltpu.VMEM((SIDE, padded), jnp.float32)],
    )(sums, gram, params, stat, weight, momentum)


def newton_body(parts, heads, tile, *refs):
    blocks_refs, out_ref = refs[: 2 * len(parts)], refs[2 * len(parts)]
    m_ref, gram, mixing, sems = refs[2 * len(parts) + 1 :]
    size = m_ref.shape[0]
    half = size // 2
    blocks = size // tile
    copies = []
    for side in range(2):
        for p, (first, lanes) in enumerate(parts):
            copies.append(
                pltpu.make_async_copy(
                    blocks_refs[side * len(parts) + p],
                    m_ref.at[side * half : (side + 1) * half, first : first + lanes],
                    sems.at[side * len(parts) + p],
                )
            )
    for copy in copies:
        copy.start()
    for copy in copies:
        copy.wait()

    def place(k):
        return slice(k * tile, (k + 1) * tile)

    squares = jnp.zeros((8, size), jnp.float32)
    for k in range(blocks):
        value = m_ref[place(k), :].astype(jnp.float32)
        squares = squares + jnp.sum((value * value).reshape(tile // 8, 8, size), axis=0)
    scale = 1.0 / (jnp.sqrt(jnp.sum(squares)) + MUON_EPSILON)
    square_scale = scale * scale

    def gram_block(i, j):
        part = dot_nt(m_ref[place(i), :], m_ref[place(j), :]) * square_scale
        gram[place(i), place(j)] = part.astype(jnp.bfloat16)
        if i != j:
            gram[place(j), place(i)] = part.T.astype(jnp.bfloat16)

    for i in range(blocks):
        for j in range(i, blocks):
            gram_block(i, j)
    for i in range(blocks):
        for j in range(i, blocks):
            part = dot_nt(gram[place(i), :], gram[place(j), :])
            part = COEFF_B * gram[place(i), place(j)].astype(jnp.float32) + COEFF_C * part
            mixing[place(i), place(j)] = part.astype(jnp.bfloat16)
            if i != j:
                mixing[place(j), place(i)] = part.T.astype(jnp.bfloat16)

    def taken(ref):
        return jnp.concatenate([ref[first : first + count, :] for first, count in heads], axis=0)

    def times(value, ref):
        return jnp.dot(value.astype(jnp.bfloat16), ref[...], preferred_element_type=jnp.float32)

    def stepped(value):
        return COEFF_A * value + times(value, mixing)

    mixing_own = taken(mixing)
    gram_own = taken(gram).astype(jnp.float32)
    gram_own = stepped(COEFF_A * gram_own + times(mixing_own, gram))
    square_own = stepped(times(stepped(gram_own), gram))
    second_own = COEFF_B * gram_own + COEFF_C * square_own
    weights = COEFF_A * mixing_own.astype(jnp.float32) + stepped(second_own)
    result = COEFF_A * COEFF_A * taken(m_ref).astype(jnp.float32) + times(weights, m_ref)
    out_ref[...] = (scale * result).astype(jnp.bfloat16)


def newton_rows(own, other, parts, heads):
    size = 2 * own[0].shape[0]
    window = sum(count for _, count in heads)
    anywhere = pl.BlockSpec(memory_space=pl.ANY)
    return kernel_call(
        functools.partial(newton_body, parts, heads, 256),
        (1,),
        [anywhere] * (2 * len(parts)),
        whole((window, size)),
        shape_of((window, size), jnp.bfloat16),
        [pltpu.VMEM((size, size), jnp.bfloat16)] * 3 + [pltpu.SemaphoreType.DMA((2 * len(parts),))],
    )(*own, *other)


def swap(value, bit):
    size = lax.axis_size("tm")
    return lax.ppermute(value, "tm", [(i, i ^ bit) for i in range(size)])


def steps_of(size):
    bits = []
    bit = 1
    while bit < size:
        bits.append(bit)
        bit *= 2
    return bits


def bit_of(bit):
    return jnp.where((lax.axis_index("tm") & bit) != 0, 1, 0)


class SumSpread:
    def __init__(self, value):
        self.value = value
        self.steps = []
        lanes = value.shape[1]
        cuts = []
        for bit in steps_of(lax.axis_size("tm")):
            if lanes // 2 % LANE == 0:
                lanes //= 2
                self.steps.append((self.halve, bit))
                cuts.append(bit)
            else:
                self.steps.append((self.pair, bit))
        self.steps += [(self.join, bit) for bit in reversed(cuts)]

    def halve(self, bit):
        lanes = self.value.shape[1] // 2
        mine = lax.dynamic_slice_in_dim(self.value, bit_of(bit) * lanes, lanes, 1)
        away = lax.dynamic_slice_in_dim(self.value, (1 - bit_of(bit)) * lanes, lanes, 1)
        self.value = mine + swap(away, bit)

    def pair(self, bit):
        self.value = self.value + swap(self.value, bit)

    def join(self, bit):
        other = swap(self.value, bit)
        upper = bit_of(bit) == 1
        self.value = jnp.concatenate(
            [jnp.where(upper, other, self.value), jnp.where(upper, self.value, other)], axis=1
        )

    def step(self, times=1):
        for _ in range(times):
            if self.steps:
                action, bit = self.steps.pop(0)
                action(bit)


def tie(first, second):
    return lax.optimization_barrier((list(first), list(second)))


def side_bit():
    return lax.axis_size("tm") // 32


def orders_of(size):
    bits = [bit for bit in steps_of(size) if bit != side_bit()]
    return [bits[k * len(bits) // 3 :] + bits[: k * len(bits) // 3] for k in range(3)]


def index_bits(bits):
    return [bit if bit < side_bit() else bit // 2 for bit in bits]


class Scatter:
    def __init__(self, keeps, sends):
        self.orders = orders_of(lax.axis_size("tm"))
        self.current = list(keeps)
        self.received = [swap(send, side_bit()) for send in sends]

    def step(self, *waiting):
        sends = []
        for p, order in enumerate(self.orders):
            half = self.current[p].shape[0] // 2
            mine, away = [
                lax.dynamic_slice_in_dim(self.current[p], half * index, half).astype(jnp.float32)
                + lax.dynamic_slice_in_dim(self.received[p], half * index, half).astype(jnp.float32)
                for index in (bit_of(order[0]), 1 - bit_of(order[0]))
            ]
            self.current[p] = mine
            sends.append(away.astype(jnp.bfloat16))
        sends, waiting = tie(sends, waiting)
        self.received = [swap(send, order.pop(0)) for send, order in zip(sends, self.orders)]
        return waiting

    def join(self, *done):
        self.received, done = tie(self.received, done)
        return done

    def result(self):
        return [a + b.astype(jnp.float32) for a, b in zip(self.current, self.received)]


class Gather:
    def __init__(self, blocks, near):
        self.orders = orders_of(lax.axis_size("tm"))
        self.held = [[] for _ in blocks]
        self.current = list(blocks)
        self.received = None
        self.near = near

    def stack(self):
        if self.received is None:
            return
        for p, other in enumerate(self.received):
            bit, mine = self.held[p][-1], self.current[p]
            axis = sum(before > bit for before in self.held[p])
            if not self.near:
                upper = bit_of(bit) == 1
                mine, other = jnp.where(upper, other, mine), jnp.where(upper, mine, other)
            self.current[p] = jnp.stack([mine, other], axis=axis)

    def step(self, *waiting):
        self.stack()
        self.current, waiting = tie(self.current, waiting)
        self.received = []
        for p, order in enumerate(self.orders):
            bit = order.pop()
            self.held[p].append(bit)
            self.received.append(swap(self.current[p], bit))
        return waiting

    def join(self, *done):
        self.received, done = tie(self.received, done)
        return done

    def finish(self, *waiting):
        self.stack()
        own = [value.reshape(-1, value.shape[-1]) for value in self.current]
        own, waiting = tie(own, waiting)
        return own, [swap(value, side_bit()) for value in own], waiting


class Stats:
    def __init__(self, stat, count):
        self.stat = stat
        self.count = float(count)
        self.bits = steps_of(lax.axis_size("tm"))

    def step(self, times=1):
        for _ in range(min(times, len(self.bits))):
            stat = self.stat
            other = swap(stat, self.bits.pop(0))
            gap = stat[0:1] - other[0:1]
            mean = 0.5 * (stat[0:1] + other[0:1])
            square = (stat[1:2] + other[1:2]) + gap * gap * (0.5 * self.count)
            self.stat = jnp.concatenate([mean, square, 0.5 * (stat[2:] + other[2:])], axis=0)
            self.count *= 2


class Exchange:
    def __init__(self, flags, carries, sums=()):
        self.bits = steps_of(lax.axis_size("tm"))
        high, self.width = carries[0][0].shape
        rows = high * len(carries)
        flags = jnp.broadcast_to(jnp.tile(flags, len(carries))[:, None], (rows, LANE))
        ends = jnp.concatenate([ends for ends, _, _ in carries], axis=0)
        self.payload = jnp.concatenate([ends, flags, *sums], axis=1)
        self.power = jnp.concatenate(
            [jnp.broadcast_to(power, (high, self.width)) for _, power, _ in carries], axis=0
        )
        self.lane = lax.broadcasted_iota(jnp.int32, self.payload.shape, 1)
        self.high = high
        self.reverse = [reverse for _, _, reverse in carries]
        self.before = jnp.zeros_like(ends)
        self.before_keep = jnp.ones_like(ends)

    def step(self, times=1):
        for _ in range(min(times, len(self.bits))):
            self.one()

    def one(self):
        bit = self.bits.pop(0)
        width = self.width
        mine, other = self.payload, swap(self.payload, bit)
        upper = bit_of(bit)
        row = lax.broadcasted_iota(jnp.int32, (len(mine), 1), 0) // self.high
        turned = sum((row == k) * int(reverse) for k, reverse in enumerate(self.reverse))
        following = turned != upper
        other_total = other[:, :width]
        keep_mine, keep_other = mine[:, width : width + 1], other[:, width : width + 1]
        self.before = jnp.where(
            following, self.before_keep * other_total + self.before, self.before
        )
        self.before_keep = jnp.where(
            following, self.before_keep * keep_other * self.power, self.before_keep
        )
        power = jnp.pad(self.power, ((0, 0), (0, mine.shape[1] - width)))
        carried = jnp.where(
            following, keep_mine * power * other + mine, keep_other * power * mine + other
        )
        self.payload = jnp.where(
            self.lane < width,
            carried,
            jnp.where(self.lane < width + LANE, mine * other, mine + other),
        )
        self.power = self.power * self.power

    def arrived(self, k):
        return self.before[k * self.high : (k + 1) * self.high]

    def sums(self):
        return self.payload[:, self.width + LANE :]


class SumAll:
    def __init__(self, value):
        self.value = value
        self.bits = steps_of(lax.axis_size("tm"))

    def step(self, times=1):
        for _ in range(min(times, len(self.bits))):
            self.value = self.value + swap(self.value, self.bits.pop(0))


def in_order(value, bits, slots):
    count = len(bits)
    axes = [count - bit.bit_length() for bit in bits]
    shape = (2,) * count + (slots, value.shape[1])
    return value.reshape(shape).transpose(axes + [count, count + 1]).reshape(value.shape)


def pad_lanes(value, padded):
    gap = padded - value.shape[-1]
    return jnp.pad(value, [(0, 0)] * (value.ndim - 1) + [(0, gap)])


def flat_places(shard, width, padded):
    size = lax.axis_size("tm")
    members = size * LANE // padded
    slots = LANE // members
    return members, slots, slots * width - shard


def to_block(flat, width, padded):
    size, mine = lax.axis_size("tm"), lax.axis_index("tm")
    members, slots, excess = flat_places(flat.shape[0], width, padded)
    lacking = excess * (members - 1)
    pairs = [(i + 1, i) for i in range(size - 1) if (i + 1) % members]
    extra = lax.ppermute(flat[:lacking], "tm", pairs)
    tail = jnp.zeros((excess,), flat.dtype)
    held = jnp.concatenate([flat, extra, tail])
    return lax.dynamic_slice_in_dim(held, excess * (mine % members), slots * width).reshape(
        slots, width
    )


def from_block(block, shard, padded):
    width = block.shape[1]
    size, mine = lax.axis_size("tm"), lax.axis_index("tm")
    members, slots, excess = flat_places(shard, width, padded)
    lacking = excess * (members - 1)
    pairs = [(i, i + 1) for i in range(size - 1) if (i + 1) % members]
    flat = block.reshape(-1)
    extra = lax.ppermute(flat[slots * width - lacking :], "tm", pairs)
    held = jnp.concatenate([extra, flat])
    return lax.dynamic_slice_in_dim(held, lacking - excess * (mine % members), shard)


def own_heads(shard, width, padded):
    members, slots, _ = flat_places(shard, width, padded)
    half = padded // 2
    group = LANE // 2
    if members == 2:
        lacking = slots - shard // width
        kept = -(-(lacking) // 16) * 16
        return [(0, group), (half + group - kept, kept)]
    return [(0, group), (half, group)]


def own_flat(found, shard, width, padded):
    mine = lax.axis_index("tm")
    members, slots, excess = flat_places(shard, width, padded)
    member = mine % members
    if members == 2:
        own, other = found[:slots].reshape(-1), found[slots:].reshape(-1)
        low = own[:shard]
        high = jnp.concatenate([other[other.shape[0] - excess :], own[: shard - excess]])
        return jnp.where(member == 0, low, high)
    near = found.reshape(members, slots * width)
    placed = jnp.take(near, jnp.arange(members) ^ member, axis=0).reshape(-1)
    return lax.dynamic_slice_in_dim(placed, shard * member, shard)


def per_device(
    inputs,
    clip_start,
    shallow_weight,
    shallow_momentum,
    deep_weight,
    deep_momentum,
    unit_params,
    unit_first,
    unit_second,
    out_grad,
):
    devices = lax.axis_size("tm")
    rows, frames, feats = inputs.shape
    width = shallow_weight.shape[1]
    padded = -(-width // WIDE) * WIDE
    group = width // (padded // LANE)
    count = rows * frames
    keep_mask = (1 - clip_start).astype(jnp.float32)
    flags = jnp.min(keep_mask, axis=1)
    keep = jnp.broadcast_to(keep_mask.T.reshape(count, 1), (count, LANE))
    params = pad_lanes(unit_params, padded)
    rates = jnp.maximum(1.0 - jnp.exp(-params[:, 0:1]), DECAY_FLOOR)
    powers = rates
    for _ in range(frames.bit_length() - 1):
        powers = powers * powers

    deep_block = pad_lanes(to_block(deep_weight.astype(jnp.bfloat16), width, padded), padded)
    momentum_block = pad_lanes(to_block(deep_momentum, width, padded), padded)

    shares = [3 * padded // 8, 3 * padded // 8, padded // 4]
    parts = [(sum(shares[:p]), shares[p]) for p in range(3)]
    side = bit_of(side_bit()).astype(jnp.int32).reshape(1)
    chunks = padded // WIDE
    orders = orders_of(devices)
    x, proj_one, stat_one, gram = front(
        inputs.reshape(count, feats), shallow_weight, rows, frames
    )
    gather = Gather([deep_block[:, first : first + lanes] for first, lanes in parts], False)
    grad_rows = out_grad.reshape(count, width)
    delta = None
    stats = Stats(stat_one, count)
    for places in ([], [0], [1, 2, 3]):
        (stats.stat,) = gather.step(stats.stat)
        stats.step()
        for k in places:
            (layer_params,), (stats.stat,) = tie([params[1]], [stats.stat])
            delta = delta_two(k, delta, grad_rows, keep, layer_params, rows, frames, padded)
            delta, (stats.stat,) = tie(delta, [stats.stat])
        (stats.stat,) = gather.join(stats.stat)
    delta_local, delta_end = delta
    (stats.stat,) = gather.step(stats.stat)
    stats.step(len(stats.bits))
    (stat_one,), (momentum_block,) = tie([stats.stat], [momentum_block])
    state_local, state_end = local_states(
        proj_one, keep, params[0], stat_one, rows, frames, devices
    )
    (state_end,) = gather.join(state_end)
    while gather.orders[0]:
        gather.step()
    deep_own, deep_other, (state_end,) = gather.finish(state_end)
    carries = Exchange(flags, [(state_end, powers[0], False)])
    later = Exchange(flags, [(delta_end, powers[1], True)], [gram])

    def tie_both(waiting):
        waiting, (later.payload, later.before) = tie(waiting, [later.payload, later.before])
        return waiting

    carries.step(3)
    deep_other, (carries.payload,) = tie(deep_other, [carries.payload])
    (carries.payload,) = tie_both([carries.payload])
    while carries.bits:
        later.step()
        carries.step()
        carries.payload, carries.before = tie_both([carries.payload, carries.before])
    state_in = carries.arrived(0)
    later.step()
    low_one, mean_one = low_one_of(
        state_local, state_in, keep, params[0], rows, frames, width, group
    )
    low_one, mean_one = tie_both([low_one, mean_one])
    later.step()
    proj_two, stat_two = second_forward(side, low_one, deep_own, deep_other, parts)
    proj_two, stat_two = tie_both([proj_two, stat_two])
    stats = Stats(jnp.concatenate([stat_two, mean_one], axis=0), count)
    while later.bits:
        later.step()
        stats.step()
        (stats.stat,) = tie_both([stats.stat])
    stats.step(len(stats.bits))
    delta_in, gram = later.arrived(0), later.sums()
    hidden = [None, None]
    sources = [(state_local, state_in, params[0]), None]

    def next_hidden(layer, places, waiting):
        states, start, layer_params = sources[layer]
        for k in places:
            (start,), waiting = tie([start], waiting)
            hidden[layer] = hidden_of(
                k, hidden[layer], states, start, keep, layer_params, rows, frames, width
            )
        hidden[layer], waiting = tie(hidden[layer], waiting)
        return waiting

    stat_two, mean_one = stats.stat[:2], stats.stat[2:]
    gate, sums_two = gate_two(
        proj_two, delta_local, delta_in, keep, params[1], stat_two, rows, frames, devices
    )
    sums = SumAll(sums_two)
    turned = None
    for k in range(chunks):
        sums.step()
        turned = turn(k, turned, low_one, mean_one)
        turned, (sums.value,) = tie(turned, [sums.value])
    sums.step(len(sums.bits))
    sums_two = sums.value
    slots = padded // devices
    weights = [index_bits(order) for order in orders]
    aligned = slots % 16 == 0
    grad_two, total_two, keeps, sends = deep_term(
        parts, weights if aligned else None, side, gate, proj_two, params[1], stat_two,
        sums_two, turned[0], rows, frames, devices,
    )
    if not aligned:
        keeps = [in_order(keep, order, slots) for keep, order in zip(keeps, weights)]
        sends = [in_order(send, order, slots) for send, order in zip(sends, weights)]
    scatter = Scatter(keeps, sends)
    back = back_one(grad_two, deep_own, deep_other, parts)
    back = scatter.join(*back)
    back = scatter.step(*back)
    back_local, back_end = delta_one(
        side, *back, keep, params[0], rows, frames, width, group
    )
    second_local, second_end, second_decay = states_two(
        proj_two, delta_local, delta_in, keep, params[1], stat_two, rows, frames, devices
    )
    back_end, second_end = scatter.join(back_end, second_end)
    tall = 2 * rows
    back_end, second_end = scatter.step(back_end, second_end)
    carries = Exchange(
        flags,
        [(back_end, powers[0], True), (second_end, powers[1], False)],
        [total_two.reshape(tall, -1)],
    )
    carries.step(2)
    (carries.payload,) = next_hidden(0, range(chunks), [carries.payload])
    (carries.payload,) = scatter.join(carries.payload)
    (carries.payload,) = scatter.step(carries.payload)
    carries.step(len(carries.bits))
    back_in, second_in = carries.arrived(0), carries.arrived(1)
    sources[1] = (second_local, second_in, params[1])
    total_two = carries.sums().reshape(1, padded)
    gate_low, sums_one = gate_one(
        proj_one, state_local, state_in, back_local, back_in, keep, params[0], stat_one, x,
        rows, frames, devices, feats,
    )
    decay_two = jnp.sum(second_decay[:rows] + second_decay[rows:] * second_in, axis=0, keepdims=True)
    sums_one = sums_one + jnp.pad(decay_two, ((feats + 3, SIDE - feats - 4), (0, 0)))
    (sums_one,) = scatter.join(sums_one)
    spread = SumSpread(sums_one)
    while scatter.orders[0]:
        (spread.value,) = scatter.step(spread.value)
        spread.step()
        (spread.value,) = scatter.join(spread.value)
    mine = lax.axis_index("tm")
    place = mine // (2 * side_bit()) * side_bit() + mine % side_bit()
    place = (side[0] * (devices // 2) + place) * slots
    mean_own = lax.dynamic_slice_in_dim(mean_one[0], place, slots)[:, None]
    grad_parts = [
        part + mean_own * total_two[:, first : first + lanes]
        for (first, lanes), part in zip(parts, scatter.result())
    ]
    gather = Gather(
        [
            (MUON_BETA * momentum_block[:, first : first + lanes] + part).astype(jnp.bfloat16)
            for (first, lanes), part in zip(parts, grad_parts)
        ],
        True,
    )
    for count_steps, places in ((1, []), (2, []), (2, [0, 1]), (2, [2, 3])):
        (spread.value,) = gather.step(spread.value)
        spread.step(count_steps)
        if places:
            (spread.value,) = next_hidden(1, places, [spread.value])
        (spread.value,) = gather.join(spread.value)
    while gather.orders[0]:
        gather.step()
    own, other, (spread.value,) = gather.finish(spread.value)
    spread.step(len(spread.steps))
    sums_one = spread.value
    (hidden_one,), (hidden_two,) = hidden
    shallow_grad, shallow_next, shallow_new, shallow_low = shallow_step(
        sums_one, gram, params[0], stat_one, shallow_weight, shallow_momentum,
        count * devices, count,
    )
    input_back = input_grad_of(
        gate_low, proj_one, params[0], stat_one, sums_one, shallow_weight, rows, frames, devices
    )
    input_grad = jnp.swapaxes(input_back.reshape(frames, rows, feats), 0, 1)
    grad_block = jnp.concatenate(grad_parts, axis=1)

    shard = deep_weight.shape[0]
    heads = own_heads(shard, width, padded)
    ortho = newton_rows(own, other, parts, heads)
    deep_ortho = own_flat(ortho[:, :width], shard, width, padded)
    deep_new = MUON_KEEP * deep_weight - MUON_RATE * deep_ortho.astype(jnp.float32)
    deep_grad = from_block(grad_block[:, :width], shard, padded)
    deep_next = MUON_BETA * deep_momentum + deep_grad

    unit_sums = sums_one[feats : feats + 4, :width]
    bias_gain_two = sums_two[:, :width]
    slope = jnp.where(
        1.0 - jnp.exp(-unit_params[:, 0]) > DECAY_FLOOR, jnp.exp(-unit_params[:, 0]), 0.0
    )
    unit_grad = jnp.stack(
        [
            jnp.stack([unit_sums[2] * slope[0], unit_sums[0], unit_sums[1], unit_sums[0]]),
            jnp.stack(
                [unit_sums[3] * slope[1], bias_gain_two[0], bias_gain_two[1], bias_gain_two[0]]
            ),
        ]
    )
    first_fix = 1.0 - FIRST_DECAY**STEP
    second_fix = 1.0 - SECOND_DECAY**STEP
    first_new = FIRST_DECAY * unit_first + (1.0 - FIRST_DECAY) * unit_grad
    second_new = SECOND_DECAY * unit_second + (1.0 - SECOND_DECAY) * unit_grad * unit_grad
    params_new = unit_params - ADAM_RATE * (first_new / first_fix) / (
        jnp.sqrt(second_new / second_fix) + ADAM_EPSILON
    )
    return (
        hidden_one.reshape(rows, frames, width),
        hidden_two.reshape(rows, frames, width),
        input_grad,
        shallow_grad,
        shallow_next,
        shallow_new,
        shallow_low,
        deep_grad,
        deep_next,
        deep_new,
        deep_new.astype(jnp.bfloat16),
        first_new,
        second_new,
        params_new,
    )


def solution(mesh):
    in_specs = (
        P(None, "tm", None),
        P(None, "tm"),
        P(),
        P(),
        P("tm"),
        P("tm"),
        P(),
        P(),
        P(),
        P(None, "tm", None),
    )
    out_specs = (
        P(None, "tm", None),
        P(None, "tm", None),
        P(None, "tm", None),
        P(),
        P(),
        P(),
        P(),
        P("tm"),
        P("tm"),
        P("tm"),
        P("tm"),
        P(),
        P(),
        P(),
    )
    return jax.shard_map(
        per_device, mesh=mesh, in_specs=in_specs, out_specs=out_specs, check_vma=False
    )
```

```python
import functools

import jax
import jax.numpy as jnp
from jax import lax
from jax.experimental import pallas as pl
from jax.experimental.pallas import tpu as pltpu
from jax.sharding import PartitionSpec as P

NS_STEPS = 2
STEP = 5


NORM_EPSILON = 1e-05
MUON_EPSILON = 1e-07
COEFF_A = 3.4445
COEFF_B = -4.775
COEFF_C = 2.0315
MUON_BETA = 0.5
MUON_RATE = 4.0
MUON_KEEP = 0.999
FIRST_DECAY = 0.9
SECOND_DECAY = 0.95
ADAM_RATE = 0.5
ADAM_EPSILON = 1e-08
DECAY_FLOOR = 0.9
LANE = 128
WIDE = 512
PART = 256
SIDE = 80


def kernel_call(body, grid, in_specs, out_specs, out_shape, scratch=(), flops=0, traffic=0):
    return pl.pallas_call(
        body,
        grid=grid,
        in_specs=in_specs,
        out_specs=out_specs,
        out_shape=out_shape,
        scratch_shapes=list(scratch),
        compiler_params=pltpu.CompilerParams(vmem_limit_bytes=56 * 1024 * 1024),
        cost_estimate=pl.CostEstimate(flops=flops, bytes_accessed=traffic, transcendentals=0),
    )


def shape_of(shape, dtype=jnp.float32):
    return jax.ShapeDtypeStruct(shape, dtype)


def whole(shape):
    return pl.BlockSpec(shape, lambda i: (0,) * len(shape))


def lanes_of(rows, width=WIDE):
    return pl.BlockSpec((rows, width), lambda i: (0, i))


def chunk_call(body, place, in_specs, out_specs, out_shape, arrays, previous, scratch=(), traffic=0):
    count = len(in_specs)
    before = list(previous) if previous is not None else []

    def run(*refs):
        body(*refs[:count], *refs[count + len(before) :])

    return pl.pallas_call(
        run,
        grid=(1,),
        in_specs=list(in_specs) + [pl.BlockSpec(memory_space=pl.ANY)] * len(before),
        out_specs=out_specs,
        out_shape=out_shape,
        scratch_shapes=list(scratch),
        input_output_aliases={count + k: k for k in range(len(before))},
        compiler_params=pltpu.CompilerParams(vmem_limit_bytes=56 * 1024 * 1024),
        cost_estimate=pl.CostEstimate(flops=0, bytes_accessed=traffic, transcendentals=0),
    )(*arrays, *before)


def chunk_at(rows, place):
    return pl.BlockSpec((rows, WIDE), lambda i: (0, place))


def rate_of(params):
    return jnp.maximum(1.0 - jnp.exp(-params[0:1]), DECAY_FLOOR)


def softened(value):
    return jnp.maximum(value, 0.0) + jnp.log(1.0 + jnp.exp(-jnp.abs(value)))


def sigmoid(value):
    return 0.5 * jnp.tanh(0.5 * value) + 0.5


def wide_keep(keep_ref, t, rows):
    keep = keep_ref[pl.ds(pl.multiple_of(t * rows, rows), rows), :]
    return jnp.concatenate([keep] * (WIDE // LANE), axis=1)


def rows_at(ref, t, rows):
    return ref[pl.ds(pl.multiple_of(t * rows, rows), rows), :]


def store_at(ref, t, rows, value):
    ref[pl.ds(pl.multiple_of(t * rows, rows), rows), :] = value


def valid_lanes(shape, total, step):
    return lax.broadcasted_iota(jnp.int32, shape, 1) + step * WIDE < total


def unit_terms(params_ref, stat_ref, total_devices, frames):
    params = params_ref[...]
    stat = stat_ref[...]
    centre = stat[0:1]
    inverse = lax.rsqrt(stat[1:2] / (total_devices * frames) + NORM_EPSILON)
    return centre, inverse, params[2:3], params[3:4] + params[1:2]


def front_body(rows, frames, width, x_ref, w_ref, xt_ref, proj_ref, stat_ref, gram_ref, padded_w):
    step = pl.program_id(0)
    count, feats = x_ref.shape

    @pl.when(step == 0)
    def _():
        i = lax.broadcasted_iota(jnp.int32, (count, count), 0)
        j = lax.broadcasted_iota(jnp.int32, (count, count), 1)
        move = (j == lax.rem(i, rows) * frames + lax.div(i, rows)).astype(jnp.bfloat16)
        moved = jnp.dot(move, x_ref[...], preferred_element_type=jnp.float32).astype(jnp.bfloat16)
        i = lax.broadcasted_iota(jnp.int32, (feats, LANE), 0)
        j = lax.broadcasted_iota(jnp.int32, (feats, LANE), 1)
        wide = jnp.dot(moved, (i == j).astype(jnp.bfloat16), preferred_element_type=jnp.float32)
        lane = lax.broadcasted_iota(jnp.int32, (count, LANE), 1)
        xt = jnp.where(lane == feats, 1.0, wide).astype(jnp.bfloat16)
        xt_ref[...] = xt
        gram = dot_tn(xt, xt)
        high = gram_ref.shape[0]
        for k in range(SIDE // high):
            gram_ref[:, k * LANE : (k + 1) * LANE] = gram[k * high : (k + 1) * high]
        padded_w[...] = jnp.zeros_like(padded_w)

    weight = w_ref[...]
    padded_w[0:feats, :] = jnp.where(valid_lanes(weight.shape, width, step), weight, 0.0)
    proj = jnp.dot(
        xt_ref[...], padded_w[...].astype(jnp.bfloat16), preferred_element_type=jnp.float32
    )
    proj_ref[...] = proj
    mean = jnp.sum(proj, axis=0, keepdims=True) * (1.0 / count)
    off = proj - mean
    stat_ref[0:1, :] = mean
    stat_ref[1:2, :] = jnp.sum(off * off, axis=0, keepdims=True)


def dot_tn(a, b):
    return lax.dot_general(a, b, (((0,), (0,)), ((), ())), preferred_element_type=jnp.float32)


def front(x, weight, rows, frames):
    count, feats = x.shape
    width = weight.shape[1]
    padded = -(-width // WIDE) * WIDE
    return kernel_call(
        functools.partial(front_body, rows, frames, width),
        (padded // WIDE,),
        [whole((count, feats)), lanes_of(feats)],
        [whole((count, LANE)), lanes_of(count), lanes_of(2), whole((rows, SIDE // rows * LANE))],
        [
            shape_of((count, LANE), jnp.bfloat16),
            shape_of((count, padded)),
            shape_of((2, padded)),
            shape_of((rows, SIDE // rows * LANE)),
        ],
        [pltpu.VMEM((LANE, WIDE), jnp.float32)],
    )(x, weight)


def delta_two_body(rows, frames, width, grad_ref, keep_ref, params_ref, delta_ref, end_ref, held):
    place = pl.program_id(0)
    pieces = WIDE // LANE
    mask = valid_lanes((rows * frames, WIDE), width, place)
    grad = jnp.where(mask, grad_ref[...].astype(jnp.float32), 0.0)
    for g in range(pieces):
        held[g] = grad[:, g * LANE : (g + 1) * LANE]
    rate = rate_of(params_ref[...])

    def body(k, carried):
        t = frames - 1 - k
        own = jnp.concatenate(
            [held[g, pl.ds(t, rows, stride=frames), :] for g in range(pieces)], axis=1
        )
        delta = own + carried
        store_at(delta_ref, t, rows, delta)
        return rate * wide_keep(keep_ref, t, rows) * delta

    end_ref[...] = lax.fori_loop(
        0, frames, body, jnp.zeros((rows, WIDE), jnp.float32), unroll=8
    )


def delta_two(out_grad, keep, params, rows, frames, padded):
    count, width = out_grad.shape
    return kernel_call(
        functools.partial(delta_two_body, rows, frames, width),
        (padded // WIDE,),
        [lanes_of(count), whole((count, LANE)), lanes_of(4)],
        [lanes_of(count), lanes_of(rows)],
        [shape_of((count, padded)), shape_of((rows, padded))],
        [pltpu.VMEM((WIDE // LANE, count, LANE), jnp.float32)],
    )(out_grad, keep, params)


def states_body(
    rows, frames, devices, proj_ref, keep_ref, params_ref, stat_ref, state_ref, end_ref
):
    centre, inverse, gain, offset = unit_terms(params_ref, stat_ref, devices, rows * frames)
    rate = rate_of(params_ref[...])
    share = 1.0 - rate

    def body(t, carried):
        gate = (rows_at(proj_ref, t, rows) - centre) * inverse * gain + offset
        soft = softened(gate)
        carried = rate * wide_keep(keep_ref, t, rows) * carried + share * soft
        store_at(state_ref, t, rows, carried)
        return carried

    end_ref[...] = lax.fori_loop(
        0, frames, body, jnp.zeros((rows, WIDE), jnp.float32), unroll=8
    )


def local_states(proj, keep, params, stat, rows, frames, devices):
    count, padded = proj.shape
    return kernel_call(
        functools.partial(states_body, rows, frames, devices),
        (padded // WIDE,),
        [lanes_of(count), whole((count, LANE)), lanes_of(4), lanes_of(2)],
        [lanes_of(count), lanes_of(rows)],
        [shape_of((count, padded)), shape_of((rows, padded))],
    )(proj, keep, params, stat)


def to_slots(value, group):
    pieces = value.shape[1] // LANE
    lane = lax.broadcasted_iota(jnp.int32, (value.shape[0], LANE), 1)
    parts = [value[:, g * LANE : (g + 1) * LANE] for g in range(pieces)]
    out = []
    for g in range(pieces):
        moved = (LANE - group) * g
        if moved == 0:
            new = parts[g]
        else:
            new = jnp.where(
                lane < moved, pltpu.roll(parts[g - 1], moved, 1), pltpu.roll(parts[g], moved, 1)
            )
        out.append(jnp.where(lane < group, new, 0.0))
    return jnp.concatenate(out, axis=1)


def from_slots(value, group, width):
    pieces = value.shape[1] // LANE
    lane = lax.broadcasted_iota(jnp.int32, (value.shape[0], LANE), 1)
    parts = [value[:, g * LANE : (g + 1) * LANE] for g in range(pieces)]
    out = []
    for j in range(pieces):
        moved = (LANE - group) * j
        new = parts[j] if moved == 0 else pltpu.roll(parts[j], LANE - moved, 1)
        if j + 1 < pieces:
            new = jnp.where(lane < group - moved, new, pltpu.roll(parts[j + 1], group - moved, 1))
        left = width - j * LANE
        out.append(new if left >= LANE else jnp.where(lane < left, new, 0.0))
    return jnp.concatenate(out, axis=1)


def low_one_body(rows, frames, width, group, state_ref, start_ref, keep_ref, params_ref, low_ref, mean_ref):
    pieces = state_ref.shape[1] // LANE
    rate = rate_of(params_ref[...])

    def advance(t, carried):
        keep = rows_at(keep_ref, t, rows)
        carried = rate * jnp.concatenate([keep] * pieces, axis=1) * carried
        return carried, rows_at(state_ref, t, rows) + carried

    def body(k, both):
        carried, total = both
        t = 2 * k
        carried, first = advance(t, carried)
        carried, second = advance(t + 1, carried)
        place = pl.ds(pl.multiple_of(t * rows, 2 * rows), 2 * rows)
        slots = to_slots(jnp.concatenate([first, second], axis=0), group)
        low_ref[place, :] = slots.astype(jnp.bfloat16)
        return carried, total + slots[:rows] + slots[rows:]

    start = start_ref[...]
    _, total = lax.fori_loop(0, frames // 2, body, (start, jnp.zeros_like(start)), unroll=2)
    mean_ref[...] = jnp.sum(total, axis=0, keepdims=True) * (1.0 / (rows * frames))


def low_one_of(states, start, keep, params, rows, frames, width, group):
    count, padded = states.shape
    return kernel_call(
        functools.partial(low_one_body, rows, frames, width, group),
        (1,),
        [whole((count, padded)), whole((rows, padded)), whole((count, LANE)), whole((4, padded))],
        [whole((count, padded)), whole((1, padded))],
        [shape_of((count, padded), jnp.bfloat16), shape_of((1, padded))],
    )(states, start, keep, params)


def hidden_body(rows, frames, state_ref, start_ref, keep_ref, params_ref, hidden_ref, held):
    pieces = WIDE // LANE
    rate = rate_of(params_ref[...])

    def body(t, carry):
        carry = rate * wide_keep(keep_ref, t, rows) * carry
        state = rows_at(state_ref, t, rows) + carry
        for g in range(pieces):
            held[g, pl.ds(pl.multiple_of(t * rows, rows), rows), :] = state[
                :, g * LANE : (g + 1) * LANE
            ]
        return carry

    lax.fori_loop(0, frames, body, start_ref[...], unroll=8)
    for r in range(rows):
        for g in range(pieces):
            hidden_ref[r * frames : (r + 1) * frames, g * LANE : (g + 1) * LANE] = held[
                g, pl.ds(r, frames, stride=rows), :
            ]


def hidden_of(place, previous, states, start, keep, params, rows, frames, width):
    count, _ = states.shape
    return chunk_call(
        functools.partial(hidden_body, rows, frames),
        place,
        [chunk_at(count, place), chunk_at(rows, place), whole((count, LANE)), chunk_at(4, place)],
        [chunk_at(count, place)],
        [shape_of((count, width))],
        (states, start, keep, params),
        previous,
        [pltpu.VMEM((WIDE // LANE, count, LANE), jnp.float32)],
    )


def second_body(low_ref, weight_ref, proj_ref, stat_ref):
    proj = jnp.dot(low_ref[...], weight_ref[...], preferred_element_type=jnp.float32)
    proj_ref[...] = proj
    mean = jnp.sum(proj, axis=0, keepdims=True) * (1.0 / proj.shape[0])
    off = proj - mean
    stat_ref[0:1, :] = mean
    stat_ref[1:2, :] = jnp.sum(off * off, axis=0, keepdims=True)


def second_forward(low, weight):
    count, padded = low.shape
    return kernel_call(
        second_body,
        (padded // WIDE,),
        [whole((count, padded)), lanes_of(padded)],
        [lanes_of(count), lanes_of(2)],
        [shape_of((count, padded)), shape_of((2, padded))],
    )(low, weight)


def gate_two_body(
    rows, frames, devices, proj_ref, delta_ref, start_ref, keep_ref, params_ref, stat_ref, gate_ref, sums_ref
):
    centre, inverse, gain, offset = unit_terms(params_ref, stat_ref, devices, rows * frames)
    rate = rate_of(params_ref[...])
    share = 1.0 - rate
    none = jnp.zeros((rows, WIDE), jnp.float32)

    def body(k, carried):
        carry, bias_sum, gain_sum = carried
        t = frames - 1 - k
        delta = rows_at(delta_ref, t, rows) + carry
        normed = (rows_at(proj_ref, t, rows) - centre) * inverse
        gate = share * delta * sigmoid(normed * gain + offset)
        store_at(gate_ref, t, rows, gate)
        carry = rate * wide_keep(keep_ref, t, rows) * carry
        return carry, bias_sum + gate, gain_sum + gate * normed

    _, bias_sum, gain_sum = lax.fori_loop(
        0, frames, body, (start_ref[...], none, none), unroll=8
    )
    sums_ref[0:1, :] = jnp.sum(bias_sum, axis=0, keepdims=True)
    sums_ref[1:2, :] = jnp.sum(gain_sum, axis=0, keepdims=True)


def gate_two(proj, delta, start, keep, params, stat, rows, frames, devices):
    count, padded = proj.shape
    return kernel_call(
        functools.partial(gate_two_body, rows, frames, devices),
        (padded // WIDE,),
        [lanes_of(count), lanes_of(count), lanes_of(rows), whole((count, LANE)), lanes_of(4), lanes_of(2)],
        [lanes_of(count), lanes_of(2)],
        [shape_of((count, padded)), shape_of((2, padded))],
    )(proj, delta, start, keep, params, stat)


def states_two_body(
    rows, frames, devices, proj_ref, delta_ref, start_ref, keep_ref, params_ref, stat_ref,
    state_ref, end_ref, decay_ref, held,
):
    centre, inverse, gain, offset = unit_terms(params_ref, stat_ref, devices, rows * frames)
    rate = rate_of(params_ref[...])
    share = 1.0 - rate
    none = jnp.zeros((rows, WIDE), jnp.float32)

    def backward(k, carry):
        t = frames - 1 - k
        store_at(held, t, rows, rows_at(delta_ref, t, rows) + carry)
        return rate * wide_keep(keep_ref, t, rows) * carry

    lax.fori_loop(0, frames, backward, start_ref[...], unroll=8)

    def forward(t, carried):
        state, reach, decay, factor = carried
        keep = wide_keep(keep_ref, t, rows)
        delta = rows_at(held, t, rows)
        value = (rows_at(proj_ref, t, rows) - centre) * inverse * gain + offset
        soft = softened(value)
        decay = decay + delta * (keep * state - soft)
        factor = factor + delta * keep * reach
        state = rate * keep * state + share * soft
        reach = rate * keep * reach
        store_at(state_ref, t, rows, state)
        return state, reach, decay, factor

    state, _, decay, factor = lax.fori_loop(
        0, frames, forward, (none, jnp.ones_like(none), none, none), unroll=4
    )
    end_ref[...] = state
    decay_ref[0:rows, :] = decay
    decay_ref[rows : 2 * rows, :] = factor


def states_two(proj, delta, start, keep, params, stat, rows, frames, devices):
    count, padded = proj.shape
    return kernel_call(
        functools.partial(states_two_body, rows, frames, devices),
        (padded // WIDE,),
        [
            lanes_of(count),
            lanes_of(count),
            lanes_of(rows),
            whole((count, LANE)),
            lanes_of(4),
            lanes_of(2),
        ],
        [lanes_of(count), lanes_of(rows), lanes_of(2 * rows)],
        [shape_of((count, padded)), shape_of((rows, padded)), shape_of((2 * rows, padded))],
        [pltpu.VMEM((count, WIDE), jnp.float32)],
    )(proj, delta, start, keep, params, stat)


def turn_body(low_ref, mean_ref, turned_ref):
    half = LANE // 2
    turned = (low_ref[...].astype(jnp.float32) - mean_ref[...]).T.astype(jnp.bfloat16)
    for g in range(WIDE // LANE):
        for side in range(2):
            turned_ref[side, g * half : (g + 1) * half, :] = turned[
                g * LANE + side * half : g * LANE + (side + 1) * half
            ]


def turn(place, previous, low, mean):
    count, padded = low.shape
    return chunk_call(
        turn_body,
        place,
        [chunk_at(count, place), chunk_at(1, place)],
        [pl.BlockSpec((2, WIDE // 2, count), lambda i: (0, place, 0))],
        [shape_of((2, padded // 2, count), jnp.bfloat16)],
        (low, mean),
        previous,
    )


def deep_term_body(
    rows, frames, devices, parts, orders, side_ref, gate_ref, proj_ref, params_ref, stat_ref, sums_ref,
    turned_ref, grad_ref, total_ref, *outs,
):
    step = pl.program_id(0)
    total = devices * rows * frames
    centre, inverse, gain, _ = unit_terms(params_ref, stat_ref, devices, rows * frames)
    sums = sums_ref[...] * (1.0 / total)
    normed = (proj_ref[...] - centre) * inverse
    grad = (gain * inverse * (gate_ref[...] - sums[0:1] - normed * sums[1:2])).astype(jnp.bfloat16)
    grad_ref[...] = grad
    total_ref[...] = jnp.sum(grad.astype(jnp.float32), axis=0, keepdims=True)
    side = side_ref[0]
    half = turned_ref.shape[1]
    tile = 256
    for p, (first, lanes) in enumerate(parts):

        @pl.when((step >= first // PART) & (step < (first + lanes) // PART))
        def _():
            for which, out_ref in ((side, outs[p]), (1 - side, outs[len(parts) + p])):
                for k in range(half // tile):
                    part = jnp.dot(
                        turned_ref[which, k * tile : (k + 1) * tile, :],
                        grad_ref[...],
                        preferred_element_type=jnp.float32,
                    ).astype(out_ref.dtype)
                    if orders is None:
                        out_ref[k * tile : (k + 1) * tile, :] = part
                        continue
                    slots = half // 2 ** len(orders[p])
                    for b in range(tile // slots):
                        block = k * (tile // slots) + b
                        place = 0
                        for weight in orders[p]:
                            place = 2 * place + block // weight % 2
                        out_ref[place * slots : (place + 1) * slots, :] = part[
                            b * slots : (b + 1) * slots
                        ]


def deep_term(parts, orders, side, gate, proj, params, stat, sums, turned, rows, frames, devices):
    count, padded = proj.shape
    half = padded // 2

    def some(first, lanes):
        return pl.BlockSpec(
            (half, PART), lambda i: (0, jnp.clip(i - first // PART, 0, lanes // PART - 1))
        )

    found = kernel_call(
        functools.partial(deep_term_body, rows, frames, devices, parts, orders),
        (padded // PART,),
        [
            pl.BlockSpec(memory_space=pltpu.SMEM),
            lanes_of(count, PART),
            lanes_of(count, PART),
            lanes_of(4, PART),
            lanes_of(2, PART),
            lanes_of(2, PART),
            whole((2, half, count)),
        ],
        [lanes_of(count, PART), lanes_of(1, PART)] + [some(*part) for part in parts] * 2,
        [shape_of((count, padded), jnp.bfloat16), shape_of((1, padded))]
        + [shape_of((half, lanes), jnp.bfloat16) for _, lanes in parts] * 2,
    )(side, gate, proj, params, stat, sums, turned)
    return found[0], found[1], found[2 : 2 + len(parts)], found[2 + len(parts) :]


def back_body(grad_ref, weight_ref, back_ref):
    back_ref[...] = dot_nt(grad_ref[...], weight_ref[...])


def back_one(grad, weight):
    count, padded = grad.shape
    return kernel_call(
        back_body,
        (padded // WIDE,),
        [whole((count, padded)), pl.BlockSpec((WIDE, padded), lambda i: (i, 0))],
        lanes_of(count),
        shape_of((count, padded)),
    )(grad, weight)


def delta_one_body(rows, frames, width, group, back_ref, keep_ref, params_ref, delta_ref, end_ref):
    pieces = back_ref.shape[1] // LANE
    rate = rate_of(params_ref[...])

    def body(k, carried):
        t = frames - 1 - k
        delta = from_slots(rows_at(back_ref, t, rows), group, width) + carried
        store_at(delta_ref, t, rows, delta)
        keep = rows_at(keep_ref, t, rows)
        return rate * jnp.concatenate([keep] * pieces, axis=1) * delta

    end_ref[...] = lax.fori_loop(
        0, frames, body, jnp.zeros((rows, back_ref.shape[1]), jnp.float32), unroll=2
    )


def delta_one(back, keep, params, rows, frames, width, group):
    count, padded = back.shape
    return kernel_call(
        functools.partial(delta_one_body, rows, frames, width, group),
        (1,),
        [whole((count, padded)), whole((count, LANE)), whole((4, padded))],
        [whole((count, padded)), whole((rows, padded))],
        [shape_of((count, padded)), shape_of((rows, padded))],
    )(back, keep, params)


def gate_one_body(
    rows,
    frames,
    devices,
    feats,
    proj_ref,
    state_ref,
    first_ref,
    delta_ref,
    start_ref,
    keep_ref,
    params_ref,
    stat_ref,
    x_ref,
    gate_ref,
    sums_ref,
    held,
):
    centre, inverse, gain, offset = unit_terms(params_ref, stat_ref, devices, rows * frames)
    rate = rate_of(params_ref[...])
    share = 1.0 - rate
    none = jnp.zeros((rows, WIDE), jnp.float32)

    def backward(k, carry):
        t = frames - 1 - k
        store_at(held, t, rows, rows_at(delta_ref, t, rows) + carry)
        return rate * wide_keep(keep_ref, t, rows) * carry

    lax.fori_loop(0, frames, backward, start_ref[...], unroll=8)

    def forward(t, carried):
        carry, before, bias_sum, gain_sum, decay_sum = carried
        keep = wide_keep(keep_ref, t, rows)
        delta = rows_at(held, t, rows)
        normed = (rows_at(proj_ref, t, rows) - centre) * inverse
        value = normed * gain + offset
        soft = softened(value)
        gate = share * delta * sigmoid(value)
        store_at(gate_ref, t, rows, gate)
        decay_sum = decay_sum + delta * (keep * before - soft)
        carry = rate * keep * carry
        before = rows_at(state_ref, t, rows) + carry
        return carry, before, bias_sum + gate, gain_sum + gate * normed, decay_sum

    first = first_ref[...]
    _, _, bias_sum, gain_sum, decay_sum = lax.fori_loop(
        0, frames, forward, (first, first, none, none, none), unroll=4
    )
    bias = jnp.sum(bias_sum, axis=0, keepdims=True)
    mean = bias * (1.0 / (rows * frames))
    x = x_ref[...]
    ones = jnp.ones((rows * frames, LANE), jnp.bfloat16)
    total = jnp.concatenate([dot_tn(x, ones)] * (WIDE // LANE), axis=1)
    term = dot_tn(x, (gate_ref[...] - mean).astype(jnp.bfloat16)) + total * mean
    sums_ref[...] = term[: sums_ref.shape[0]]
    sums_ref[feats : feats + 1, :] = bias
    sums_ref[feats + 1 : feats + 2, :] = jnp.sum(gain_sum, axis=0, keepdims=True)
    sums_ref[feats + 2 : feats + 3, :] = jnp.sum(decay_sum, axis=0, keepdims=True)


def gate_one(proj, states, first, delta, start, keep, params, stat, x, rows, frames, devices, feats):
    count, padded = proj.shape
    return kernel_call(
        functools.partial(gate_one_body, rows, frames, devices, feats),
        (padded // WIDE,),
        [
            lanes_of(count),
            lanes_of(count),
            lanes_of(rows),
            lanes_of(count),
            lanes_of(rows),
            whole((count, LANE)),
            lanes_of(4),
            lanes_of(2),
            whole((count, LANE)),
        ],
        [lanes_of(count), lanes_of(SIDE)],
        [shape_of((count, padded)), shape_of((SIDE, padded))],
        [pltpu.VMEM((count, WIDE), jnp.float32)],
    )(proj, states, first, delta, start, keep, params, stat, x)


def input_grad_body(
    rows, frames, devices, width, feats, gate_ref, proj_ref, params_ref, stat_ref, sums_ref, w_ref, back_ref
):
    step = pl.program_id(0)
    total = devices * rows * frames
    centre, inverse, gain, _ = unit_terms(params_ref, stat_ref, devices, rows * frames)
    bias = sums_ref[feats : feats + 1, :] * (1.0 / total)
    slope = sums_ref[feats + 1 : feats + 2, :] * (1.0 / total)
    normed = (proj_ref[...] - centre) * inverse
    grad = (gain * inverse * (gate_ref[...] - bias - normed * slope)).astype(jnp.bfloat16)
    weight = w_ref[...]
    weight = jnp.where(valid_lanes(weight.shape, width, step), weight, 0.0).astype(jnp.bfloat16)
    part = dot_nt(grad, weight)

    @pl.when(step == 0)
    def _():
        back_ref[...] = part

    @pl.when(step > 0)
    def _():
        back_ref[...] += part


def input_grad_of(gate, proj, params, stat, sums, weight, rows, frames, devices):
    count, padded = proj.shape
    feats, width = weight.shape
    return kernel_call(
        functools.partial(input_grad_body, rows, frames, devices, width, feats),
        (padded // WIDE,),
        [lanes_of(count), lanes_of(count), lanes_of(4), lanes_of(2), lanes_of(SIDE), lanes_of(feats)],
        whole((count, feats)),
        shape_of((count, feats)),
    )(gate, proj, params, stat, sums, weight)


def dot_nt(a, b):
    return lax.dot_general(a, b, (((1,), (1,)), ((), ())), preferred_element_type=jnp.float32)


def shallow_body(
    total, frames, sums_ref, gram_ref, params_ref, stat_ref, w_ref, m_ref,
    grad_ref, next_ref, new_ref, low_ref, held,
):
    feats, width = w_ref.shape
    centre, inverse, gain, _ = unit_terms(params_ref, stat_ref, total // frames, frames)
    weight = w_ref[...]
    held[...] = jnp.zeros_like(held)
    held[0:feats, 0:width] = weight
    high = gram_ref.shape[0]
    gram = jnp.concatenate(
        [gram_ref[:, k * LANE : (k + 1) * LANE] for k in range(SIDE // high)], axis=0
    )
    lane = lax.broadcasted_iota(jnp.int32, gram.shape, 1)
    x_sum = jnp.sum(jnp.where(lane == feats, gram, 0.0), axis=1, keepdims=True)
    raw = jnp.dot(
        gram[:, :SIDE],
        held[...].astype(jnp.bfloat16).astype(jnp.float32),
        precision=lax.Precision.HIGHEST,
        preferred_element_type=jnp.float32,
    )
    normed = (raw - x_sum * centre) * inverse
    bias = sums_ref[feats : feats + 1, :] * (1.0 / total)
    slope = sums_ref[feats + 1 : feats + 2, :] * (1.0 / total)
    grad = gain * inverse * (sums_ref[...] - x_sum * bias - normed * slope)
    grad = grad[:feats, :width]
    grad_ref[...] = grad
    following = MUON_BETA * m_ref[...] + grad
    next_ref[...] = following
    held[0:feats, 0:width] = following
    m = held[...]
    current = (m / (jnp.sqrt(jnp.sum(m * m)) + MUON_EPSILON)).astype(jnp.bfloat16)
    for repeat in range(NS_STEPS):
        gram = dot_nt(current, current).astype(jnp.bfloat16)
        square = jnp.dot(gram, gram, preferred_element_type=jnp.float32)
        mixing = (COEFF_B * gram.astype(jnp.float32) + COEFF_C * square).astype(jnp.bfloat16)
        current = (
            COEFF_A * current.astype(jnp.float32)
            + jnp.dot(mixing, current, preferred_element_type=jnp.float32)
        ).astype(jnp.bfloat16)
    new = MUON_KEEP * weight - MUON_RATE * current[:feats, :width].astype(jnp.float32)
    new_ref[...] = new
    low_ref[...] = new.astype(jnp.bfloat16)


def shallow_step(sums, gram, params, stat, weight, momentum, total, frames):
    padded = sums.shape[1]
    some = shape_of(weight.shape)
    return kernel_call(
        functools.partial(shallow_body, total, frames),
        (1,),
        [whole(value.shape) for value in (sums, gram, params, stat, weight, momentum)],
        [whole(weight.shape)] * 4,
        [some, some, some, shape_of(weight.shape, jnp.bfloat16)],
        [pltpu.VMEM((SIDE, padded), jnp.float32)],
    )(sums, gram, params, stat, weight, momentum)


def newton_body(parts, heads, tile, *refs):
    blocks_refs, out_ref = refs[: 2 * len(parts)], refs[2 * len(parts)]
    m_ref, gram, mixing, sems = refs[2 * len(parts) + 1 :]
    size = m_ref.shape[0]
    half = size // 2
    blocks = size // tile
    copies = []
    for side in range(2):
        for p, (first, lanes) in enumerate(parts):
            copies.append(
                pltpu.make_async_copy(
                    blocks_refs[side * len(parts) + p],
                    m_ref.at[side * half : (side + 1) * half, first : first + lanes],
                    sems.at[side * len(parts) + p],
                )
            )
    for copy in copies:
        copy.start()
    for copy in copies:
        copy.wait()

    def place(k):
        return slice(k * tile, (k + 1) * tile)

    squares = jnp.zeros((8, size), jnp.float32)
    for k in range(blocks):
        value = m_ref[place(k), :].astype(jnp.float32)
        squares = squares + jnp.sum((value * value).reshape(tile // 8, 8, size), axis=0)
    scale = 1.0 / (jnp.sqrt(jnp.sum(squares)) + MUON_EPSILON)
    square_scale = scale * scale

    def gram_block(i, j):
        part = dot_nt(m_ref[place(i), :], m_ref[place(j), :]) * square_scale
        gram[place(i), place(j)] = part.astype(jnp.bfloat16)
        if i != j:
            gram[place(j), place(i)] = part.T.astype(jnp.bfloat16)

    for i in range(blocks):
        for j in range(i, blocks):
            gram_block(i, j)
    for i in range(blocks):
        for j in range(i, blocks):
            part = dot_nt(gram[place(i), :], gram[place(j), :])
            part = COEFF_B * gram[place(i), place(j)].astype(jnp.float32) + COEFF_C * part
            mixing[place(i), place(j)] = part.astype(jnp.bfloat16)
            if i != j:
                mixing[place(j), place(i)] = part.T.astype(jnp.bfloat16)

    def taken(ref):
        return jnp.concatenate([ref[first : first + count, :] for first, count in heads], axis=0)

    def times(value, ref):
        return jnp.dot(value.astype(jnp.bfloat16), ref[...], preferred_element_type=jnp.float32)

    def stepped(value):
        return COEFF_A * value + times(value, mixing)

    mixing_own = taken(mixing)
    gram_own = taken(gram).astype(jnp.float32)
    gram_own = stepped(COEFF_A * gram_own + times(mixing_own, gram))
    square_own = stepped(times(stepped(gram_own), gram))
    second_own = COEFF_B * gram_own + COEFF_C * square_own
    weights = COEFF_A * mixing_own.astype(jnp.float32) + stepped(second_own)
    result = COEFF_A * COEFF_A * taken(m_ref).astype(jnp.float32) + times(weights, m_ref)
    out_ref[...] = (scale * result).astype(jnp.bfloat16)


def newton_rows(own, other, parts, heads):
    size = 2 * own[0].shape[0]
    window = sum(count for _, count in heads)
    anywhere = pl.BlockSpec(memory_space=pl.ANY)
    return kernel_call(
        functools.partial(newton_body, parts, heads, 256),
        (1,),
        [anywhere] * (2 * len(parts)),
        whole((window, size)),
        shape_of((window, size), jnp.bfloat16),
        [pltpu.VMEM((size, size), jnp.bfloat16)] * 3 + [pltpu.SemaphoreType.DMA((2 * len(parts),))],
    )(*own, *other)


def swap(value, bit):
    size = lax.axis_size("tm")
    return lax.ppermute(value, "tm", [(i, i ^ bit) for i in range(size)])


def steps_of(size):
    bits = []
    bit = 1
    while bit < size:
        bits.append(bit)
        bit *= 2
    return bits


def bit_of(bit):
    return jnp.where((lax.axis_index("tm") & bit) != 0, 1, 0)


class SumSpread:
    def __init__(self, value):
        self.value = value
        self.steps = []
        lanes = value.shape[1]
        cuts = []
        for bit in steps_of(lax.axis_size("tm")):
            if lanes // 2 % LANE == 0:
                lanes //= 2
                self.steps.append((self.halve, bit))
                cuts.append(bit)
            else:
                self.steps.append((self.pair, bit))
        self.steps += [(self.join, bit) for bit in reversed(cuts)]

    def halve(self, bit):
        lanes = self.value.shape[1] // 2
        mine = lax.dynamic_slice_in_dim(self.value, bit_of(bit) * lanes, lanes, 1)
        away = lax.dynamic_slice_in_dim(self.value, (1 - bit_of(bit)) * lanes, lanes, 1)
        self.value = mine + swap(away, bit)

    def pair(self, bit):
        self.value = self.value + swap(self.value, bit)

    def join(self, bit):
        other = swap(self.value, bit)
        upper = bit_of(bit) == 1
        self.value = jnp.concatenate(
            [jnp.where(upper, other, self.value), jnp.where(upper, self.value, other)], axis=1
        )

    def step(self, times=1):
        for _ in range(times):
            if self.steps:
                action, bit = self.steps.pop(0)
                action(bit)


def tie(first, second):
    return lax.optimization_barrier((list(first), list(second)))


def side_bit():
    return lax.axis_size("tm") // 32


def orders_of(size):
    bits = [bit for bit in steps_of(size) if bit != side_bit()]
    return [bits[k * len(bits) // 3 :] + bits[: k * len(bits) // 3] for k in range(3)]


def index_bits(bits):
    return [bit if bit < side_bit() else bit // 2 for bit in bits]


def combine_body(count, bits_ref, *refs):
    ins, outs = refs[: 4 * count], refs[4 * count :]
    for p in range(count):
        mine, mine_got, away, away_got = [ref[0].astype(jnp.float32) for ref in ins[4 * p : 4 * p + 4]]
        outs[2 * p][...] = mine + mine_got
        outs[2 * p + 1][...] = (away + away_got).astype(jnp.bfloat16)


def combine(bits, current, received):
    count = len(current)
    half = current[0].shape[0] // 2
    tile = min(half, 128)
    in_specs, out_specs, out_shape, arrays = [], [], [], []
    for p in range(count):
        lanes = current[p].shape[1]
        for away in (0, 1):
            for value in (current[p], received[p]):
                in_specs.append(
                    pl.BlockSpec(
                        (1, tile, lanes),
                        lambda i, bits_ref, p=p, away=away: (bits_ref[p] ^ away, i, 0),
                    )
                )
                arrays.append(value.reshape(2, half, lanes))
        for dtype in (jnp.float32, jnp.bfloat16):
            out_specs.append(pl.BlockSpec((tile, lanes), lambda i, bits_ref: (i, 0)))
            out_shape.append(shape_of((half, lanes), dtype))
    found = pl.pallas_call(
        functools.partial(combine_body, count),
        grid_spec=pltpu.PrefetchScalarGridSpec(
            num_scalar_prefetch=1, grid=(half // tile,), in_specs=in_specs, out_specs=out_specs
        ),
        out_shape=out_shape,
        compiler_params=pltpu.CompilerParams(vmem_limit_bytes=56 * 1024 * 1024),
        cost_estimate=pl.CostEstimate(flops=0, bytes_accessed=0, transcendentals=0),
    )(bits, *arrays)
    return found[0::2], found[1::2]


class Scatter:
    def __init__(self, keeps, sends):
        self.orders = orders_of(lax.axis_size("tm"))
        self.current = list(keeps)
        self.received = [swap(send, side_bit()) for send in sends]

    def step(self, *waiting):
        half = self.current[0].shape[0] // 2
        bits = [order[0] for order in self.orders]
        if half % 32 == 0:
            index = jnp.stack([bit_of(bit) for bit in bits]).astype(jnp.int32)
            self.current, sends = combine(index, self.current, self.received)
        else:
            sends = []
            for p, bit in enumerate(bits):
                mine, away = [
                    lax.dynamic_slice_in_dim(self.current[p], half * index, half)
                    + lax.dynamic_slice_in_dim(self.received[p], half * index, half).astype(
                        jnp.float32
                    )
                    for index in (bit_of(bit), 1 - bit_of(bit))
                ]
                self.current[p] = mine
                sends.append(away.astype(jnp.bfloat16))
        sends, waiting = tie(sends, waiting)
        self.current = list(self.current)
        self.received = [swap(send, order.pop(0)) for send, order in zip(sends, self.orders)]
        return waiting

    def join(self, *done):
        self.received, done = tie(self.received, done)
        return done

    def result(self):
        return [a + b.astype(jnp.float32) for a, b in zip(self.current, self.received)]


class Gather:
    def __init__(self, blocks, near):
        self.orders = orders_of(lax.axis_size("tm"))
        self.held = [[] for _ in blocks]
        self.current = list(blocks)
        self.received = None
        self.near = near

    def stack(self):
        if self.received is None:
            return
        for p, other in enumerate(self.received):
            bit, mine = self.held[p][-1], self.current[p]
            axis = sum(before > bit for before in self.held[p])
            if not self.near:
                upper = bit_of(bit) == 1
                mine, other = jnp.where(upper, other, mine), jnp.where(upper, mine, other)
            self.current[p] = jnp.stack([mine, other], axis=axis)

    def step(self, *waiting):
        self.stack()
        self.current, waiting = tie(self.current, waiting)
        self.received = []
        for p, order in enumerate(self.orders):
            bit = order.pop()
            self.held[p].append(bit)
            self.received.append(swap(self.current[p], bit))
        return waiting

    def join(self, *done):
        self.received, done = tie(self.received, done)
        return done

    def finish(self, *waiting):
        self.stack()
        own = [value.reshape(-1, value.shape[-1]) for value in self.current]
        own, waiting = tie(own, waiting)
        return own, [swap(value, side_bit()) for value in own], waiting


class Stats:
    def __init__(self, stat, count):
        self.stat = stat
        self.count = float(count)
        self.bits = steps_of(lax.axis_size("tm"))

    def step(self, times=1):
        for _ in range(min(times, len(self.bits))):
            stat = self.stat
            other = swap(stat, self.bits.pop(0))
            gap = stat[0:1] - other[0:1]
            mean = 0.5 * (stat[0:1] + other[0:1])
            square = (stat[1:2] + other[1:2]) + gap * gap * (0.5 * self.count)
            self.stat = jnp.concatenate([mean, square, 0.5 * (stat[2:] + other[2:])], axis=0)
            self.count *= 2


class Exchange:
    def __init__(self, flags, carries, sums=()):
        self.bits = steps_of(lax.axis_size("tm"))
        high, self.width = carries[0][0].shape
        rows = high * len(carries)
        flags = jnp.broadcast_to(jnp.tile(flags, len(carries))[:, None], (rows, LANE))
        ends = jnp.concatenate([ends for ends, _, _ in carries], axis=0)
        self.payload = jnp.concatenate([ends, flags, *sums], axis=1)
        self.power = jnp.concatenate(
            [jnp.broadcast_to(power, (high, self.width)) for _, power, _ in carries], axis=0
        )
        self.lane = lax.broadcasted_iota(jnp.int32, self.payload.shape, 1)
        self.high = high
        self.reverse = [reverse for _, _, reverse in carries]
        self.before = jnp.zeros_like(ends)
        self.before_keep = jnp.ones_like(ends)

    def step(self, times=1):
        for _ in range(min(times, len(self.bits))):
            self.one()

    def one(self):
        bit = self.bits.pop(0)
        width = self.width
        mine, other = self.payload, swap(self.payload, bit)
        upper = bit_of(bit)
        row = lax.broadcasted_iota(jnp.int32, (len(mine), 1), 0) // self.high
        turned = sum((row == k) * int(reverse) for k, reverse in enumerate(self.reverse))
        following = turned != upper
        other_total = other[:, :width]
        keep_mine, keep_other = mine[:, width : width + 1], other[:, width : width + 1]
        self.before = jnp.where(
            following, self.before_keep * other_total + self.before, self.before
        )
        self.before_keep = jnp.where(
            following, self.before_keep * keep_other * self.power, self.before_keep
        )
        power = jnp.pad(self.power, ((0, 0), (0, mine.shape[1] - width)))
        carried = jnp.where(
            following, keep_mine * power * other + mine, keep_other * power * mine + other
        )
        self.payload = jnp.where(
            self.lane < width,
            carried,
            jnp.where(self.lane < width + LANE, mine * other, mine + other),
        )
        self.power = self.power * self.power

    def arrived(self, k):
        return self.before[k * self.high : (k + 1) * self.high]

    def sums(self):
        return self.payload[:, self.width + LANE :]


class SumAll:
    def __init__(self, value):
        self.value = value
        self.bits = steps_of(lax.axis_size("tm"))

    def step(self, times=1):
        for _ in range(min(times, len(self.bits))):
            self.value = self.value + swap(self.value, self.bits.pop(0))


def in_order(value, bits, slots):
    count = len(bits)
    axes = [count - bit.bit_length() for bit in bits]
    shape = (2,) * count + (slots, value.shape[1])
    return value.reshape(shape).transpose(axes + [count, count + 1]).reshape(value.shape)


def pad_lanes(value, padded):
    gap = padded - value.shape[-1]
    return jnp.pad(value, [(0, 0)] * (value.ndim - 1) + [(0, gap)])


def flat_places(shard, width, padded):
    size = lax.axis_size("tm")
    members = size * LANE // padded
    slots = LANE // members
    return members, slots, slots * width - shard


def to_block(flat, width, padded):
    size, mine = lax.axis_size("tm"), lax.axis_index("tm")
    members, slots, excess = flat_places(flat.shape[0], width, padded)
    lacking = excess * (members - 1)
    pairs = [(i + 1, i) for i in range(size - 1) if (i + 1) % members]
    extra = lax.ppermute(flat[:lacking], "tm", pairs)
    tail = jnp.zeros((excess,), flat.dtype)
    held = jnp.concatenate([flat, extra, tail])
    return lax.dynamic_slice_in_dim(held, excess * (mine % members), slots * width).reshape(
        slots, width
    )


def from_block(block, shard, padded):
    width = block.shape[1]
    size, mine = lax.axis_size("tm"), lax.axis_index("tm")
    members, slots, excess = flat_places(shard, width, padded)
    lacking = excess * (members - 1)
    pairs = [(i, i + 1) for i in range(size - 1) if (i + 1) % members]
    flat = block.reshape(-1)
    extra = lax.ppermute(flat[slots * width - lacking :], "tm", pairs)
    held = jnp.concatenate([extra, flat])
    return lax.dynamic_slice_in_dim(held, lacking - excess * (mine % members), shard)


def own_heads(shard, width, padded):
    members, slots, _ = flat_places(shard, width, padded)
    half = padded // 2
    group = LANE // 2
    if members == 2:
        lacking = slots - shard // width
        kept = -(-(lacking) // 16) * 16
        return [(0, group), (half + group - kept, kept)]
    return [(0, group), (half, group)]


def own_flat(found, shard, width, padded):
    mine = lax.axis_index("tm")
    members, slots, excess = flat_places(shard, width, padded)
    member = mine % members
    if members == 2:
        own, other = found[:slots].reshape(-1), found[slots:].reshape(-1)
        low = own[:shard]
        high = jnp.concatenate([other[other.shape[0] - excess :], own[: shard - excess]])
        return jnp.where(member == 0, low, high)
    near = found.reshape(members, slots * width)
    placed = jnp.take(near, jnp.arange(members) ^ member, axis=0).reshape(-1)
    return lax.dynamic_slice_in_dim(placed, shard * member, shard)


def per_device(
    inputs,
    clip_start,
    shallow_weight,
    shallow_momentum,
    deep_weight,
    deep_momentum,
    unit_params,
    unit_first,
    unit_second,
    out_grad,
):
    devices = lax.axis_size("tm")
    rows, frames, feats = inputs.shape
    width = shallow_weight.shape[1]
    padded = -(-width // WIDE) * WIDE
    group = width // (padded // LANE)
    count = rows * frames
    keep_mask = (1 - clip_start).astype(jnp.float32)
    flags = jnp.min(keep_mask, axis=1)
    keep = jnp.broadcast_to(keep_mask.T.reshape(count, 1), (count, LANE))
    params = pad_lanes(unit_params, padded)
    rates = jnp.maximum(1.0 - jnp.exp(-params[:, 0:1]), DECAY_FLOOR)
    powers = rates
    for _ in range(frames.bit_length() - 1):
        powers = powers * powers

    deep_block = pad_lanes(to_block(deep_weight.astype(jnp.bfloat16), width, padded), padded)
    momentum_block = pad_lanes(to_block(deep_momentum, width, padded), padded)

    shares = [3 * padded // 8, 3 * padded // 8, padded // 4]
    parts = [(sum(shares[:p]), shares[p]) for p in range(3)]
    side = bit_of(side_bit()).astype(jnp.int32).reshape(1)
    chunks = padded // WIDE
    orders = orders_of(devices)
    delta_local, delta_end = delta_two(
        out_grad.reshape(count, width), keep, params[1], rows, frames, padded
    )
    (deep_block, flat_inputs), (delta_end,) = tie(
        [deep_block, inputs.reshape(count, feats)], [delta_end]
    )
    deep_low = lax.all_gather(deep_block, "tm", axis=0, tiled=True)
    x, proj_one, stat_one, gram = front(flat_inputs, shallow_weight, rows, frames)
    stats = Stats(stat_one, count)
    (stats.stat,), (delta_end,) = tie([stats.stat], [delta_end])
    later = Exchange(flags, [(delta_end, powers[1], True)], [gram])
    while later.bits:
        later.step()
        stats.step()
        (stats.stat,), (later.payload, later.before) = tie(
            [stats.stat], [later.payload, later.before]
        )
    delta_in, gram = later.arrived(0), later.sums()
    (stat_one,), (momentum_block,) = tie([stats.stat], [momentum_block])
    state_local, state_end = local_states(
        proj_one, keep, params[0], stat_one, rows, frames, devices
    )
    carries = Exchange(flags, [(state_end, powers[0], False)])
    carries.step(len(carries.bits))
    state_in = carries.arrived(0)
    low_one, mean_one = low_one_of(
        state_local, state_in, keep, params[0], rows, frames, width, group
    )
    proj_two, stat_two = second_forward(low_one, deep_low)
    stats = Stats(jnp.concatenate([stat_two, mean_one], axis=0), count)
    stats.step(len(stats.bits))
    hidden = [None, None]
    sources = [(state_local, state_in, params[0]), None]

    def next_hidden(layer, places, waiting):
        states, start, layer_params = sources[layer]
        for k in places:
            (start,), waiting = tie([start], waiting)
            hidden[layer] = hidden_of(
                k, hidden[layer], states, start, keep, layer_params, rows, frames, width
            )
        hidden[layer], waiting = tie(hidden[layer], waiting)
        return waiting

    stat_two, mean_one = stats.stat[:2], stats.stat[2:]
    gate, sums_two = gate_two(
        proj_two, delta_local, delta_in, keep, params[1], stat_two, rows, frames, devices
    )
    sums = SumAll(sums_two)
    turned = None
    for k in range(chunks):
        sums.step()
        turned = turn(k, turned, low_one, mean_one)
        turned, (sums.value,) = tie(turned, [sums.value])
    sums.step(len(sums.bits))
    sums_two = sums.value
    slots = padded // devices
    weights = [index_bits(order) for order in orders]
    aligned = slots % 16 == 0
    grad_two, total_two, keeps, sends = deep_term(
        parts, weights if aligned else None, side, gate, proj_two, params[1], stat_two,
        sums_two, turned[0], rows, frames, devices,
    )
    if not aligned:
        keeps = [in_order(keep, order, slots) for keep, order in zip(keeps, weights)]
        sends = [in_order(send, order, slots) for send, order in zip(sends, weights)]
    scatter = Scatter(keeps, sends)
    back = back_one(grad_two, deep_low)
    (back,) = scatter.join(back)
    (back,) = scatter.step(back)
    back_local, back_end = delta_one(back, keep, params[0], rows, frames, width, group)
    second_local, second_end, second_decay = states_two(
        proj_two, delta_local, delta_in, keep, params[1], stat_two, rows, frames, devices
    )
    back_end, second_end = scatter.join(back_end, second_end)
    tall = 2 * rows
    back_end, second_end = scatter.step(back_end, second_end)
    carries = Exchange(
        flags,
        [(back_end, powers[0], True), (second_end, powers[1], False)],
        [total_two.reshape(tall, -1)],
    )
    carries.step(2)
    (carries.payload,) = next_hidden(0, range(chunks), [carries.payload])
    (carries.payload,) = scatter.join(carries.payload)
    (carries.payload,) = scatter.step(carries.payload)
    carries.step(len(carries.bits))
    back_in, second_in = carries.arrived(0), carries.arrived(1)
    sources[1] = (second_local, second_in, params[1])
    total_two = carries.sums().reshape(1, padded)
    gate_low, sums_one = gate_one(
        proj_one, state_local, state_in, back_local, back_in, keep, params[0], stat_one, x,
        rows, frames, devices, feats,
    )
    decay_two = jnp.sum(second_decay[:rows] + second_decay[rows:] * second_in, axis=0, keepdims=True)
    sums_one = sums_one + jnp.pad(decay_two, ((feats + 3, SIDE - feats - 4), (0, 0)))
    (sums_one,) = scatter.join(sums_one)
    spread = SumSpread(sums_one)
    while scatter.orders[0]:
        (spread.value,) = scatter.step(spread.value)
        spread.step()
        (spread.value,) = scatter.join(spread.value)
    mine = lax.axis_index("tm")
    place = mine // (2 * side_bit()) * side_bit() + mine % side_bit()
    place = (side[0] * (devices // 2) + place) * slots
    mean_own = lax.dynamic_slice_in_dim(mean_one[0], place, slots)[:, None]
    grad_parts = [
        part + mean_own * total_two[:, first : first + lanes]
        for (first, lanes), part in zip(parts, scatter.result())
    ]
    gather = Gather(
        [
            (MUON_BETA * momentum_block[:, first : first + lanes] + part).astype(jnp.bfloat16)
            for (first, lanes), part in zip(parts, grad_parts)
        ],
        True,
    )
    for count_steps, places in ((1, []), (2, []), (2, [0, 1]), (2, [2, 3])):
        (spread.value,) = gather.step(spread.value)
        spread.step(count_steps)
        if places:
            (spread.value,) = next_hidden(1, places, [spread.value])
        (spread.value,) = gather.join(spread.value)
    while gather.orders[0]:
        gather.step()
    own, other, (spread.value,) = gather.finish(spread.value)
    spread.step(len(spread.steps))
    sums_one = spread.value
    (hidden_one,), (hidden_two,) = hidden
    shallow_grad, shallow_next, shallow_new, shallow_low = shallow_step(
        sums_one, gram, params[0], stat_one, shallow_weight, shallow_momentum,
        count * devices, count,
    )
    input_back = input_grad_of(
        gate_low, proj_one, params[0], stat_one, sums_one, shallow_weight, rows, frames, devices
    )
    input_grad = jnp.swapaxes(input_back.reshape(frames, rows, feats), 0, 1)
    grad_block = jnp.concatenate(grad_parts, axis=1)

    shard = deep_weight.shape[0]
    heads = own_heads(shard, width, padded)
    ortho = newton_rows(own, other, parts, heads)
    deep_ortho = own_flat(ortho[:, :width], shard, width, padded)
    deep_new = MUON_KEEP * deep_weight - MUON_RATE * deep_ortho.astype(jnp.float32)
    deep_grad = from_block(grad_block[:, :width], shard, padded)
    deep_next = MUON_BETA * deep_momentum + deep_grad

    unit_sums = sums_one[feats : feats + 4, :width]
    bias_gain_two = sums_two[:, :width]
    slope = jnp.where(
        1.0 - jnp.exp(-unit_params[:, 0]) > DECAY_FLOOR, jnp.exp(-unit_params[:, 0]), 0.0
    )
    unit_grad = jnp.stack(
        [
            jnp.stack([unit_sums[2] * slope[0], unit_sums[0], unit_sums[1], unit_sums[0]]),
            jnp.stack(
                [unit_sums[3] * slope[1], bias_gain_two[0], bias_gain_two[1], bias_gain_two[0]]
            ),
        ]
    )
    first_fix = 1.0 - FIRST_DECAY**STEP
    second_fix = 1.0 - SECOND_DECAY**STEP
    first_new = FIRST_DECAY * unit_first + (1.0 - FIRST_DECAY) * unit_grad
    second_new = SECOND_DECAY * unit_second + (1.0 - SECOND_DECAY) * unit_grad * unit_grad
    params_new = unit_params - ADAM_RATE * (first_new / first_fix) / (
        jnp.sqrt(second_new / second_fix) + ADAM_EPSILON
    )
    return (
        hidden_one.reshape(rows, frames, width),
        hidden_two.reshape(rows, frames, width),
        input_grad,
        shallow_grad,
        shallow_next,
        shallow_new,
        shallow_low,
        deep_grad,
        deep_next,
        deep_new,
        deep_new.astype(jnp.bfloat16),
        first_new,
        second_new,
        params_new,
    )


def solution(mesh):
    in_specs = (
        P(None, "tm", None),
        P(None, "tm"),
        P(),
        P(),
        P("tm"),
        P("tm"),
        P(),
        P(),
        P(),
        P(None, "tm", None),
    )
    out_specs = (
        P(None, "tm", None),
        P(None, "tm", None),
        P(None, "tm", None),
        P(),
        P(),
        P(),
        P(),
        P("tm"),
        P("tm"),
        P("tm"),
        P("tm"),
        P(),
        P(),
        P(),
    )
    return jax.shard_map(
        per_device, mesh=mesh, in_specs=in_specs, out_specs=out_specs, check_vma=False
    )
```

```python
import functools

import jax
import jax.numpy as jnp
from jax import lax
from jax.experimental import pallas as pl
from jax.experimental.pallas import tpu as pltpu
from jax.sharding import PartitionSpec as P

NS_STEPS = 2
STEP = 5


NORM_EPSILON = 1e-05
MUON_EPSILON = 1e-07
COEFF_A = 3.4445
COEFF_B = -4.775
COEFF_C = 2.0315
MUON_BETA = 0.5
MUON_RATE = 4.0
MUON_KEEP = 0.999
FIRST_DECAY = 0.9
SECOND_DECAY = 0.95
ADAM_RATE = 0.5
ADAM_EPSILON = 1e-08
DECAY_FLOOR = 0.9
LANE = 128
WIDE = 512
PART = 256
SIDE = 80


def kernel_call(body, grid, in_specs, out_specs, out_shape, scratch=(), flops=0, traffic=0):
    return pl.pallas_call(
        body,
        grid=grid,
        in_specs=in_specs,
        out_specs=out_specs,
        out_shape=out_shape,
        scratch_shapes=list(scratch),
        compiler_params=pltpu.CompilerParams(vmem_limit_bytes=56 * 1024 * 1024),
        cost_estimate=pl.CostEstimate(flops=flops, bytes_accessed=traffic, transcendentals=0),
    )


def shape_of(shape, dtype=jnp.float32):
    return jax.ShapeDtypeStruct(shape, dtype)


def whole(shape):
    return pl.BlockSpec(shape, lambda i: (0,) * len(shape))


def lanes_of(rows, width=WIDE):
    return pl.BlockSpec((rows, width), lambda i: (0, i))


def chunk_call(body, place, in_specs, out_specs, out_shape, arrays, previous, scratch=(), traffic=0):
    count = len(in_specs)
    before = list(previous) if previous is not None else []

    def run(*refs):
        body(*refs[:count], *refs[count + len(before) :])

    return pl.pallas_call(
        run,
        grid=(1,),
        in_specs=list(in_specs) + [pl.BlockSpec(memory_space=pl.ANY)] * len(before),
        out_specs=out_specs,
        out_shape=out_shape,
        scratch_shapes=list(scratch),
        input_output_aliases={count + k: k for k in range(len(before))},
        compiler_params=pltpu.CompilerParams(vmem_limit_bytes=56 * 1024 * 1024),
        cost_estimate=pl.CostEstimate(flops=0, bytes_accessed=traffic, transcendentals=0),
    )(*arrays, *before)


def chunk_at(rows, place):
    return pl.BlockSpec((rows, WIDE), lambda i: (0, place))


def rate_of(params):
    return jnp.maximum(1.0 - jnp.exp(-params[0:1]), DECAY_FLOOR)


def softened(value):
    return jnp.maximum(value, 0.0) + jnp.log(1.0 + jnp.exp(-jnp.abs(value)))


def sigmoid(value):
    return 0.5 * jnp.tanh(0.5 * value) + 0.5


def wide_keep(keep_ref, t, rows):
    keep = keep_ref[pl.ds(pl.multiple_of(t * rows, rows), rows), :]
    return jnp.concatenate([keep] * (WIDE // LANE), axis=1)


def rows_at(ref, t, rows):
    return ref[pl.ds(pl.multiple_of(t * rows, rows), rows), :]


def store_at(ref, t, rows, value):
    ref[pl.ds(pl.multiple_of(t * rows, rows), rows), :] = value


def valid_lanes(shape, total, step):
    return lax.broadcasted_iota(jnp.int32, shape, 1) + step * WIDE < total


def unit_terms(params_ref, stat_ref, total_devices, frames):
    params = params_ref[...]
    stat = stat_ref[...]
    centre = stat[0:1]
    inverse = lax.rsqrt(stat[1:2] / (total_devices * frames) + NORM_EPSILON)
    return centre, inverse, params[2:3], params[3:4] + params[1:2]


def front_body(rows, frames, width, x_ref, w_ref, xt_ref, proj_ref, stat_ref, gram_ref, padded_w):
    step = pl.program_id(0)
    count, feats = x_ref.shape

    @pl.when(step == 0)
    def _():
        i = lax.broadcasted_iota(jnp.int32, (count, count), 0)
        j = lax.broadcasted_iota(jnp.int32, (count, count), 1)
        move = (j == lax.rem(i, rows) * frames + lax.div(i, rows)).astype(jnp.bfloat16)
        moved = jnp.dot(move, x_ref[...], preferred_element_type=jnp.float32).astype(jnp.bfloat16)
        i = lax.broadcasted_iota(jnp.int32, (feats, LANE), 0)
        j = lax.broadcasted_iota(jnp.int32, (feats, LANE), 1)
        wide = jnp.dot(moved, (i == j).astype(jnp.bfloat16), preferred_element_type=jnp.float32)
        lane = lax.broadcasted_iota(jnp.int32, (count, LANE), 1)
        xt = jnp.where(lane == feats, 1.0, wide).astype(jnp.bfloat16)
        xt_ref[...] = xt
        gram = dot_tn(xt, xt)
        high = gram_ref.shape[0]
        for k in range(SIDE // high):
            gram_ref[:, k * LANE : (k + 1) * LANE] = gram[k * high : (k + 1) * high]
        padded_w[...] = jnp.zeros_like(padded_w)

    weight = w_ref[...]
    padded_w[0:feats, :] = jnp.where(valid_lanes(weight.shape, width, step), weight, 0.0)
    proj = jnp.dot(
        xt_ref[...], padded_w[...].astype(jnp.bfloat16), preferred_element_type=jnp.float32
    )
    proj_ref[...] = proj
    mean = jnp.sum(proj, axis=0, keepdims=True) * (1.0 / count)
    off = proj - mean
    stat_ref[0:1, :] = mean
    stat_ref[1:2, :] = jnp.sum(off * off, axis=0, keepdims=True)


def dot_tn(a, b):
    return lax.dot_general(a, b, (((0,), (0,)), ((), ())), preferred_element_type=jnp.float32)


def front(x, weight, rows, frames):
    count, feats = x.shape
    width = weight.shape[1]
    padded = -(-width // WIDE) * WIDE
    return kernel_call(
        functools.partial(front_body, rows, frames, width),
        (padded // WIDE,),
        [whole((count, feats)), lanes_of(feats)],
        [whole((count, LANE)), lanes_of(count), lanes_of(2), whole((2 * rows, SIDE // (2 * rows) * LANE))],
        [
            shape_of((count, LANE), jnp.bfloat16),
            shape_of((count, padded)),
            shape_of((2, padded)),
            shape_of((2 * rows, SIDE // (2 * rows) * LANE)),
        ],
        [pltpu.VMEM((LANE, WIDE), jnp.float32)],
    )(x, weight)


def delta_two_body(rows, frames, width, place, grad_ref, keep_ref, params_ref, delta_ref, end_ref, held):
    pieces = WIDE // LANE
    mask = valid_lanes((rows * frames, WIDE), width, place)
    grad = jnp.where(mask, grad_ref[...].astype(jnp.float32), 0.0)
    for g in range(pieces):
        held[g] = grad[:, g * LANE : (g + 1) * LANE]
    rate = rate_of(params_ref[...])

    def body(k, carried):
        t = frames - 1 - k
        own = jnp.concatenate(
            [held[g, pl.ds(t, rows, stride=frames), :] for g in range(pieces)], axis=1
        )
        delta = own + carried
        store_at(delta_ref, t, rows, delta)
        return rate * wide_keep(keep_ref, t, rows) * delta

    end_ref[...] = lax.fori_loop(
        0, frames, body, jnp.zeros((rows, WIDE), jnp.float32), unroll=8
    )


def delta_two(place, previous, out_grad, keep, params, rows, frames, padded):
    count, width = out_grad.shape
    return chunk_call(
        functools.partial(delta_two_body, rows, frames, width, place),
        place,
        [chunk_at(count, place), whole((count, LANE)), chunk_at(4, place)],
        [chunk_at(count, place), chunk_at(rows, place)],
        [shape_of((count, padded)), shape_of((rows, padded))],
        (out_grad, keep, params),
        previous,
        [pltpu.VMEM((WIDE // LANE, count, LANE), jnp.float32)],
    )


def states_body(
    rows, frames, devices, proj_ref, keep_ref, params_ref, stat_ref, state_ref, end_ref
):
    centre, inverse, gain, offset = unit_terms(params_ref, stat_ref, devices, rows * frames)
    rate = rate_of(params_ref[...])
    share = 1.0 - rate

    def body(t, carried):
        gate = (rows_at(proj_ref, t, rows) - centre) * inverse * gain + offset
        soft = softened(gate)
        carried = rate * wide_keep(keep_ref, t, rows) * carried + share * soft
        store_at(state_ref, t, rows, carried)
        return carried

    end_ref[...] = lax.fori_loop(
        0, frames, body, jnp.zeros((rows, WIDE), jnp.float32), unroll=8
    )


def local_states(proj, keep, params, stat, rows, frames, devices):
    count, padded = proj.shape
    return kernel_call(
        functools.partial(states_body, rows, frames, devices),
        (padded // WIDE,),
        [lanes_of(count), whole((count, LANE)), lanes_of(4), lanes_of(2)],
        [lanes_of(count), lanes_of(rows)],
        [shape_of((count, padded)), shape_of((rows, padded))],
    )(proj, keep, params, stat)


def to_slots(value, group):
    pieces = value.shape[1] // LANE
    lane = lax.broadcasted_iota(jnp.int32, (value.shape[0], LANE), 1)
    parts = [value[:, g * LANE : (g + 1) * LANE] for g in range(pieces)]
    out = []
    for g in range(pieces):
        moved = (LANE - group) * g
        if moved == 0:
            new = parts[g]
        else:
            new = jnp.where(
                lane < moved, pltpu.roll(parts[g - 1], moved, 1), pltpu.roll(parts[g], moved, 1)
            )
        out.append(jnp.where(lane < group, new, 0.0))
    return jnp.concatenate(out, axis=1)


def from_slots(value, group, width):
    pieces = value.shape[1] // LANE
    lane = lax.broadcasted_iota(jnp.int32, (value.shape[0], LANE), 1)
    parts = [value[:, g * LANE : (g + 1) * LANE] for g in range(pieces)]
    out = []
    for j in range(pieces):
        moved = (LANE - group) * j
        new = parts[j] if moved == 0 else pltpu.roll(parts[j], LANE - moved, 1)
        if j + 1 < pieces:
            new = jnp.where(lane < group - moved, new, pltpu.roll(parts[j + 1], group - moved, 1))
        left = width - j * LANE
        out.append(new if left >= LANE else jnp.where(lane < left, new, 0.0))
    return jnp.concatenate(out, axis=1)


def low_one_body(rows, frames, width, group, state_ref, start_ref, keep_ref, params_ref, low_ref, mean_ref):
    pieces = state_ref.shape[1] // LANE
    rate = rate_of(params_ref[...])

    def advance(t, carried):
        keep = rows_at(keep_ref, t, rows)
        carried = rate * jnp.concatenate([keep] * pieces, axis=1) * carried
        return carried, rows_at(state_ref, t, rows) + carried

    def body(k, both):
        carried, total = both
        t = 2 * k
        carried, first = advance(t, carried)
        carried, second = advance(t + 1, carried)
        place = pl.ds(pl.multiple_of(t * rows, 2 * rows), 2 * rows)
        slots = to_slots(jnp.concatenate([first, second], axis=0), group)
        low_ref[place, :] = slots.astype(jnp.bfloat16)
        return carried, total + slots[:rows] + slots[rows:]

    start = start_ref[...]
    _, total = lax.fori_loop(0, frames // 2, body, (start, jnp.zeros_like(start)), unroll=2)
    mean_ref[...] = jnp.sum(total, axis=0, keepdims=True) * (1.0 / (rows * frames))


def low_one_of(states, start, keep, params, rows, frames, width, group):
    count, padded = states.shape
    return kernel_call(
        functools.partial(low_one_body, rows, frames, width, group),
        (1,),
        [whole((count, padded)), whole((rows, padded)), whole((count, LANE)), whole((4, padded))],
        [whole((count, padded)), whole((1, padded))],
        [shape_of((count, padded), jnp.bfloat16), shape_of((1, padded))],
    )(states, start, keep, params)


def hidden_body(rows, frames, state_ref, start_ref, keep_ref, params_ref, hidden_ref, held):
    pieces = WIDE // LANE
    rate = rate_of(params_ref[...])

    def body(t, carry):
        carry = rate * wide_keep(keep_ref, t, rows) * carry
        state = rows_at(state_ref, t, rows) + carry
        for g in range(pieces):
            held[g, pl.ds(pl.multiple_of(t * rows, rows), rows), :] = state[
                :, g * LANE : (g + 1) * LANE
            ]
        return carry

    lax.fori_loop(0, frames, body, start_ref[...], unroll=8)
    for r in range(rows):
        for g in range(pieces):
            hidden_ref[r * frames : (r + 1) * frames, g * LANE : (g + 1) * LANE] = held[
                g, pl.ds(r, frames, stride=rows), :
            ]


def hidden_of(place, previous, states, start, keep, params, rows, frames, width):
    count, _ = states.shape
    return chunk_call(
        functools.partial(hidden_body, rows, frames),
        place,
        [chunk_at(count, place), chunk_at(rows, place), whole((count, LANE)), chunk_at(4, place)],
        [chunk_at(count, place)],
        [shape_of((count, width))],
        (states, start, keep, params),
        previous,
        [pltpu.VMEM((WIDE // LANE, count, LANE), jnp.float32)],
    )


def second_body(low_ref, weight_ref, proj_ref, stat_ref):
    proj = jnp.dot(low_ref[...], weight_ref[...], preferred_element_type=jnp.float32)
    proj_ref[...] = proj
    mean = jnp.sum(proj, axis=0, keepdims=True) * (1.0 / proj.shape[0])
    off = proj - mean
    stat_ref[0:1, :] = mean
    stat_ref[1:2, :] = jnp.sum(off * off, axis=0, keepdims=True)


def second_forward(low, weight):
    count, padded = low.shape
    return kernel_call(
        second_body,
        (padded // WIDE,),
        [whole((count, padded)), lanes_of(padded)],
        [lanes_of(count), lanes_of(2)],
        [shape_of((count, padded)), shape_of((2, padded))],
    )(low, weight)


def gate_two_body(
    rows, frames, devices, proj_ref, delta_ref, start_ref, keep_ref, params_ref, stat_ref, gate_ref, sums_ref
):
    centre, inverse, gain, offset = unit_terms(params_ref, stat_ref, devices, rows * frames)
    rate = rate_of(params_ref[...])
    share = 1.0 - rate
    none = jnp.zeros((rows, WIDE), jnp.float32)

    def body(k, carried):
        carry, bias_sum, gain_sum = carried
        t = frames - 1 - k
        delta = rows_at(delta_ref, t, rows) + carry
        normed = (rows_at(proj_ref, t, rows) - centre) * inverse
        gate = share * delta * sigmoid(normed * gain + offset)
        store_at(gate_ref, t, rows, gate)
        carry = rate * wide_keep(keep_ref, t, rows) * carry
        return carry, bias_sum + gate, gain_sum + gate * normed

    _, bias_sum, gain_sum = lax.fori_loop(
        0, frames, body, (start_ref[...], none, none), unroll=8
    )
    sums_ref[0:1, :] = jnp.sum(bias_sum, axis=0, keepdims=True)
    sums_ref[1:2, :] = jnp.sum(gain_sum, axis=0, keepdims=True)


def gate_two(proj, delta, start, keep, params, stat, rows, frames, devices):
    count, padded = proj.shape
    return kernel_call(
        functools.partial(gate_two_body, rows, frames, devices),
        (padded // WIDE,),
        [lanes_of(count), lanes_of(count), lanes_of(rows), whole((count, LANE)), lanes_of(4), lanes_of(2)],
        [lanes_of(count), lanes_of(2)],
        [shape_of((count, padded)), shape_of((2, padded))],
    )(proj, delta, start, keep, params, stat)


def states_two_body(
    rows, frames, devices, proj_ref, delta_ref, start_ref, keep_ref, params_ref, stat_ref,
    state_ref, end_ref, decay_ref, held,
):
    centre, inverse, gain, offset = unit_terms(params_ref, stat_ref, devices, rows * frames)
    rate = rate_of(params_ref[...])
    share = 1.0 - rate
    none = jnp.zeros((rows, WIDE), jnp.float32)

    def backward(k, carry):
        t = frames - 1 - k
        store_at(held, t, rows, rows_at(delta_ref, t, rows) + carry)
        return rate * wide_keep(keep_ref, t, rows) * carry

    lax.fori_loop(0, frames, backward, start_ref[...], unroll=8)

    def forward(t, carried):
        state, reach, decay, factor = carried
        keep = wide_keep(keep_ref, t, rows)
        delta = rows_at(held, t, rows)
        value = (rows_at(proj_ref, t, rows) - centre) * inverse * gain + offset
        soft = softened(value)
        decay = decay + delta * (keep * state - soft)
        factor = factor + delta * keep * reach
        state = rate * keep * state + share * soft
        reach = rate * keep * reach
        store_at(state_ref, t, rows, state)
        return state, reach, decay, factor

    state, _, decay, factor = lax.fori_loop(
        0, frames, forward, (none, jnp.ones_like(none), none, none), unroll=4
    )
    end_ref[...] = state
    decay_ref[0:rows, :] = decay
    decay_ref[rows : 2 * rows, :] = factor


def states_two(proj, delta, start, keep, params, stat, rows, frames, devices):
    count, padded = proj.shape
    return kernel_call(
        functools.partial(states_two_body, rows, frames, devices),
        (padded // WIDE,),
        [
            lanes_of(count),
            lanes_of(count),
            lanes_of(rows),
            whole((count, LANE)),
            lanes_of(4),
            lanes_of(2),
        ],
        [lanes_of(count), lanes_of(rows), lanes_of(2 * rows)],
        [shape_of((count, padded)), shape_of((rows, padded)), shape_of((2 * rows, padded))],
        [pltpu.VMEM((count, WIDE), jnp.float32)],
    )(proj, delta, start, keep, params, stat)


def turn_body(low_ref, mean_ref, turned_ref):
    half = LANE // 2
    turned = (low_ref[...].astype(jnp.float32) - mean_ref[...]).T.astype(jnp.bfloat16)
    for g in range(WIDE // LANE):
        for side in range(2):
            turned_ref[side, g * half : (g + 1) * half, :] = turned[
                g * LANE + side * half : g * LANE + (side + 1) * half
            ]


def turn(place, previous, low, mean):
    count, padded = low.shape
    return chunk_call(
        turn_body,
        place,
        [chunk_at(count, place), chunk_at(1, place)],
        [pl.BlockSpec((2, WIDE // 2, count), lambda i: (0, place, 0))],
        [shape_of((2, padded // 2, count), jnp.bfloat16)],
        (low, mean),
        previous,
    )


def deep_term_body(
    rows, frames, devices, parts, orders, side_ref, gate_ref, proj_ref, params_ref, stat_ref, sums_ref,
    turned_ref, grad_ref, total_ref, *outs,
):
    step = pl.program_id(0)
    total = devices * rows * frames
    centre, inverse, gain, _ = unit_terms(params_ref, stat_ref, devices, rows * frames)
    sums = sums_ref[...] * (1.0 / total)
    normed = (proj_ref[...] - centre) * inverse
    grad = (gain * inverse * (gate_ref[...] - sums[0:1] - normed * sums[1:2])).astype(jnp.bfloat16)
    grad_ref[...] = grad
    total_ref[...] = jnp.sum(grad.astype(jnp.float32), axis=0, keepdims=True)
    side = side_ref[0]
    half = turned_ref.shape[1]
    tile = 256
    for p, (first, lanes) in enumerate(parts):

        @pl.when((step >= first // PART) & (step < (first + lanes) // PART))
        def _():
            for which, out_ref in ((side, outs[p]), (1 - side, outs[len(parts) + p])):
                for k in range(half // tile):
                    part = jnp.dot(
                        turned_ref[which, k * tile : (k + 1) * tile, :],
                        grad_ref[...],
                        preferred_element_type=jnp.float32,
                    ).astype(out_ref.dtype)
                    if orders is None:
                        out_ref[k * tile : (k + 1) * tile, :] = part
                        continue
                    slots = half // 2 ** len(orders[p])
                    for b in range(tile // slots):
                        block = k * (tile // slots) + b
                        place = 0
                        for weight in orders[p]:
                            place = 2 * place + block // weight % 2
                        out_ref[place * slots : (place + 1) * slots, :] = part[
                            b * slots : (b + 1) * slots
                        ]


def deep_term(parts, orders, side, gate, proj, params, stat, sums, turned, rows, frames, devices):
    count, padded = proj.shape
    half = padded // 2

    def some(first, lanes):
        return pl.BlockSpec(
            (half, PART), lambda i: (0, jnp.clip(i - first // PART, 0, lanes // PART - 1))
        )

    found = kernel_call(
        functools.partial(deep_term_body, rows, frames, devices, parts, orders),
        (padded // PART,),
        [
            pl.BlockSpec(memory_space=pltpu.SMEM),
            lanes_of(count, PART),
            lanes_of(count, PART),
            lanes_of(4, PART),
            lanes_of(2, PART),
            lanes_of(2, PART),
            whole((2, half, count)),
        ],
        [lanes_of(count, PART), lanes_of(1, PART)] + [some(*part) for part in parts] * 2,
        [shape_of((count, padded), jnp.bfloat16), shape_of((1, padded))]
        + [shape_of((half, lanes), jnp.bfloat16) for _, lanes in parts] * 2,
    )(side, gate, proj, params, stat, sums, turned)
    return found[0], found[1], found[2 : 2 + len(parts)], found[2 + len(parts) :]


def back_body(grad_ref, weight_ref, back_ref):
    back_ref[...] = dot_nt(grad_ref[...], weight_ref[...])


def back_one(grad, weight):
    count, padded = grad.shape
    return kernel_call(
        back_body,
        (padded // WIDE,),
        [whole((count, padded)), pl.BlockSpec((WIDE, padded), lambda i: (i, 0))],
        lanes_of(count),
        shape_of((count, padded)),
    )(grad, weight)


def delta_one_body(rows, frames, width, group, back_ref, keep_ref, params_ref, delta_ref, end_ref):
    pieces = back_ref.shape[1] // LANE
    rate = rate_of(params_ref[...])

    def body(k, carried):
        t = frames - 1 - k
        delta = from_slots(rows_at(back_ref, t, rows), group, width) + carried
        store_at(delta_ref, t, rows, delta)
        keep = rows_at(keep_ref, t, rows)
        return rate * jnp.concatenate([keep] * pieces, axis=1) * delta

    end_ref[...] = lax.fori_loop(
        0, frames, body, jnp.zeros((rows, back_ref.shape[1]), jnp.float32), unroll=2
    )


def delta_one(back, keep, params, rows, frames, width, group):
    count, padded = back.shape
    return kernel_call(
        functools.partial(delta_one_body, rows, frames, width, group),
        (1,),
        [whole((count, padded)), whole((count, LANE)), whole((4, padded))],
        [whole((count, padded)), whole((rows, padded))],
        [shape_of((count, padded)), shape_of((rows, padded))],
    )(back, keep, params)


def gate_one_body(
    rows,
    frames,
    devices,
    feats,
    proj_ref,
    state_ref,
    first_ref,
    delta_ref,
    start_ref,
    keep_ref,
    params_ref,
    stat_ref,
    x_ref,
    gate_ref,
    sums_ref,
    held,
):
    centre, inverse, gain, offset = unit_terms(params_ref, stat_ref, devices, rows * frames)
    rate = rate_of(params_ref[...])
    share = 1.0 - rate
    none = jnp.zeros((rows, WIDE), jnp.float32)

    def backward(k, carry):
        t = frames - 1 - k
        store_at(held, t, rows, rows_at(delta_ref, t, rows) + carry)
        return rate * wide_keep(keep_ref, t, rows) * carry

    lax.fori_loop(0, frames, backward, start_ref[...], unroll=8)

    def forward(t, carried):
        carry, before, bias_sum, gain_sum, decay_sum = carried
        keep = wide_keep(keep_ref, t, rows)
        delta = rows_at(held, t, rows)
        normed = (rows_at(proj_ref, t, rows) - centre) * inverse
        value = normed * gain + offset
        soft = softened(value)
        gate = share * delta * sigmoid(value)
        store_at(gate_ref, t, rows, gate)
        decay_sum = decay_sum + delta * (keep * before - soft)
        carry = rate * keep * carry
        before = rows_at(state_ref, t, rows) + carry
        return carry, before, bias_sum + gate, gain_sum + gate * normed, decay_sum

    first = first_ref[...]
    _, _, bias_sum, gain_sum, decay_sum = lax.fori_loop(
        0, frames, forward, (first, first, none, none, none), unroll=4
    )
    bias = jnp.sum(bias_sum, axis=0, keepdims=True)
    mean = bias * (1.0 / (rows * frames))
    x = x_ref[...]
    ones = jnp.ones((rows * frames, LANE), jnp.bfloat16)
    total = jnp.concatenate([dot_tn(x, ones)] * (WIDE // LANE), axis=1)
    term = dot_tn(x, (gate_ref[...] - mean).astype(jnp.bfloat16)) + total * mean
    sums_ref[...] = term[: sums_ref.shape[0]]
    sums_ref[feats : feats + 1, :] = bias
    sums_ref[feats + 1 : feats + 2, :] = jnp.sum(gain_sum, axis=0, keepdims=True)
    sums_ref[feats + 2 : feats + 3, :] = jnp.sum(decay_sum, axis=0, keepdims=True)


def gate_one(proj, states, first, delta, start, keep, params, stat, x, rows, frames, devices, feats):
    count, padded = proj.shape
    return kernel_call(
        functools.partial(gate_one_body, rows, frames, devices, feats),
        (padded // WIDE,),
        [
            lanes_of(count),
            lanes_of(count),
            lanes_of(rows),
            lanes_of(count),
            lanes_of(rows),
            whole((count, LANE)),
            lanes_of(4),
            lanes_of(2),
            whole((count, LANE)),
        ],
        [lanes_of(count), lanes_of(SIDE)],
        [shape_of((count, padded)), shape_of((SIDE, padded))],
        [pltpu.VMEM((count, WIDE), jnp.float32)],
    )(proj, states, first, delta, start, keep, params, stat, x)


def input_grad_body(
    rows, frames, devices, width, feats, gate_ref, proj_ref, params_ref, stat_ref, sums_ref, w_ref, back_ref
):
    step = pl.program_id(0)
    total = devices * rows * frames
    centre, inverse, gain, _ = unit_terms(params_ref, stat_ref, devices, rows * frames)
    bias = sums_ref[feats : feats + 1, :] * (1.0 / total)
    slope = sums_ref[feats + 1 : feats + 2, :] * (1.0 / total)
    normed = (proj_ref[...] - centre) * inverse
    grad = (gain * inverse * (gate_ref[...] - bias - normed * slope)).astype(jnp.bfloat16)
    weight = w_ref[...]
    weight = jnp.where(valid_lanes(weight.shape, width, step), weight, 0.0).astype(jnp.bfloat16)
    part = dot_nt(grad, weight)

    @pl.when(step == 0)
    def _():
        back_ref[...] = part

    @pl.when(step > 0)
    def _():
        back_ref[...] += part


def input_grad_of(gate, proj, params, stat, sums, weight, rows, frames, devices):
    count, padded = proj.shape
    feats, width = weight.shape
    return kernel_call(
        functools.partial(input_grad_body, rows, frames, devices, width, feats),
        (padded // WIDE,),
        [lanes_of(count), lanes_of(count), lanes_of(4), lanes_of(2), lanes_of(SIDE), lanes_of(feats)],
        whole((count, feats)),
        shape_of((count, feats)),
    )(gate, proj, params, stat, sums, weight)


def dot_nt(a, b):
    return lax.dot_general(a, b, (((1,), (1,)), ((), ())), preferred_element_type=jnp.float32)


def shallow_body(
    total, frames, sums_ref, gram_ref, params_ref, stat_ref, w_ref, m_ref,
    grad_ref, next_ref, new_ref, low_ref, held,
):
    feats, width = w_ref.shape
    centre, inverse, gain, _ = unit_terms(params_ref, stat_ref, total // frames, frames)
    weight = w_ref[...]
    held[...] = jnp.zeros_like(held)
    held[0:feats, 0:width] = weight
    high = gram_ref.shape[0]
    gram = jnp.concatenate(
        [gram_ref[:, k * LANE : (k + 1) * LANE] for k in range(SIDE // high)], axis=0
    )
    lane = lax.broadcasted_iota(jnp.int32, gram.shape, 1)
    x_sum = jnp.sum(jnp.where(lane == feats, gram, 0.0), axis=1, keepdims=True)
    raw = jnp.dot(
        gram[:, :SIDE],
        held[...].astype(jnp.bfloat16).astype(jnp.float32),
        precision=lax.Precision.HIGHEST,
        preferred_element_type=jnp.float32,
    )
    normed = (raw - x_sum * centre) * inverse
    bias = sums_ref[feats : feats + 1, :] * (1.0 / total)
    slope = sums_ref[feats + 1 : feats + 2, :] * (1.0 / total)
    grad = gain * inverse * (sums_ref[...] - x_sum * bias - normed * slope)
    grad = grad[:feats, :width]
    grad_ref[...] = grad
    following = MUON_BETA * m_ref[...] + grad
    next_ref[...] = following
    held[0:feats, 0:width] = following
    m = held[...]
    current = (m / (jnp.sqrt(jnp.sum(m * m)) + MUON_EPSILON)).astype(jnp.bfloat16)
    for repeat in range(NS_STEPS):
        gram = dot_nt(current, current).astype(jnp.bfloat16)
        square = jnp.dot(gram, gram, preferred_element_type=jnp.float32)
        mixing = (COEFF_B * gram.astype(jnp.float32) + COEFF_C * square).astype(jnp.bfloat16)
        current = (
            COEFF_A * current.astype(jnp.float32)
            + jnp.dot(mixing, current, preferred_element_type=jnp.float32)
        ).astype(jnp.bfloat16)
    new = MUON_KEEP * weight - MUON_RATE * current[:feats, :width].astype(jnp.float32)
    new_ref[...] = new
    low_ref[...] = new.astype(jnp.bfloat16)


def shallow_step(sums, gram, params, stat, weight, momentum, total, frames):
    padded = sums.shape[1]
    some = shape_of(weight.shape)
    return kernel_call(
        functools.partial(shallow_body, total, frames),
        (1,),
        [whole(value.shape) for value in (sums, gram, params, stat, weight, momentum)],
        [whole(weight.shape)] * 4,
        [some, some, some, shape_of(weight.shape, jnp.bfloat16)],
        [pltpu.VMEM((SIDE, padded), jnp.float32)],
    )(sums, gram, params, stat, weight, momentum)


def newton_body(parts, heads, tile, *refs):
    blocks_refs, out_ref = refs[: 2 * len(parts)], refs[2 * len(parts)]
    m_ref, gram, mixing, sems = refs[2 * len(parts) + 1 :]
    size = m_ref.shape[0]
    half = size // 2
    blocks = size // tile
    copies = []
    for side in range(2):
        for p, (first, lanes) in enumerate(parts):
            copies.append(
                pltpu.make_async_copy(
                    blocks_refs[side * len(parts) + p],
                    m_ref.at[side * half : (side + 1) * half, first : first + lanes],
                    sems.at[side * len(parts) + p],
                )
            )
    for copy in copies:
        copy.start()
    for copy in copies:
        copy.wait()

    def place(k):
        return slice(k * tile, (k + 1) * tile)

    squares = jnp.zeros((8, size), jnp.float32)
    for k in range(blocks):
        value = m_ref[place(k), :].astype(jnp.float32)
        squares = squares + jnp.sum((value * value).reshape(tile // 8, 8, size), axis=0)
    scale = 1.0 / (jnp.sqrt(jnp.sum(squares)) + MUON_EPSILON)
    square_scale = scale * scale

    def gram_block(i, j):
        part = dot_nt(m_ref[place(i), :], m_ref[place(j), :]) * square_scale
        gram[place(i), place(j)] = part.astype(jnp.bfloat16)
        if i != j:
            gram[place(j), place(i)] = part.T.astype(jnp.bfloat16)

    for i in range(blocks):
        for j in range(i, blocks):
            gram_block(i, j)
    for i in range(blocks):
        for j in range(i, blocks):
            part = dot_nt(gram[place(i), :], gram[place(j), :])
            part = COEFF_B * gram[place(i), place(j)].astype(jnp.float32) + COEFF_C * part
            mixing[place(i), place(j)] = part.astype(jnp.bfloat16)
            if i != j:
                mixing[place(j), place(i)] = part.T.astype(jnp.bfloat16)

    def taken(ref):
        return jnp.concatenate([ref[first : first + count, :] for first, count in heads], axis=0)

    def times(value, ref):
        return jnp.dot(value.astype(jnp.bfloat16), ref[...], preferred_element_type=jnp.float32)

    def stepped(value):
        return COEFF_A * value + times(value, mixing)

    mixing_own = taken(mixing)
    gram_own = taken(gram).astype(jnp.float32)
    gram_own = stepped(COEFF_A * gram_own + times(mixing_own, gram))
    square_own = stepped(times(stepped(gram_own), gram))
    second_own = COEFF_B * gram_own + COEFF_C * square_own
    weights = COEFF_A * mixing_own.astype(jnp.float32) + stepped(second_own)
    result = COEFF_A * COEFF_A * taken(m_ref).astype(jnp.float32) + times(weights, m_ref)
    out_ref[...] = (scale * result).astype(jnp.bfloat16)


def newton_rows(own, other, parts, heads):
    size = 2 * own[0].shape[0]
    window = sum(count for _, count in heads)
    anywhere = pl.BlockSpec(memory_space=pl.ANY)
    return kernel_call(
        functools.partial(newton_body, parts, heads, 256),
        (1,),
        [anywhere] * (2 * len(parts)),
        whole((window, size)),
        shape_of((window, size), jnp.bfloat16),
        [pltpu.VMEM((size, size), jnp.bfloat16)] * 3 + [pltpu.SemaphoreType.DMA((2 * len(parts),))],
    )(*own, *other)


def swap(value, bit):
    size = lax.axis_size("tm")
    return lax.ppermute(value, "tm", [(i, i ^ bit) for i in range(size)])


def steps_of(size):
    bits = []
    bit = 1
    while bit < size:
        bits.append(bit)
        bit *= 2
    return bits


def bit_of(bit):
    return jnp.where((lax.axis_index("tm") & bit) != 0, 1, 0)


class SumSpread:
    def __init__(self, value):
        self.value = value
        self.steps = []
        lanes = value.shape[1]
        cuts = []
        for bit in steps_of(lax.axis_size("tm")):
            if lanes // 2 % LANE == 0:
                lanes //= 2
                self.steps.append((self.halve, bit))
                cuts.append(bit)
            else:
                self.steps.append((self.pair, bit))
        self.steps += [(self.join, bit) for bit in reversed(cuts)]

    def halve(self, bit):
        lanes = self.value.shape[1] // 2
        mine = lax.dynamic_slice_in_dim(self.value, bit_of(bit) * lanes, lanes, 1)
        away = lax.dynamic_slice_in_dim(self.value, (1 - bit_of(bit)) * lanes, lanes, 1)
        self.value = mine + swap(away, bit)

    def pair(self, bit):
        self.value = self.value + swap(self.value, bit)

    def join(self, bit):
        other = swap(self.value, bit)
        upper = bit_of(bit) == 1
        self.value = jnp.concatenate(
            [jnp.where(upper, other, self.value), jnp.where(upper, self.value, other)], axis=1
        )

    def step(self, times=1):
        for _ in range(times):
            if self.steps:
                action, bit = self.steps.pop(0)
                action(bit)


def tie(first, second):
    return lax.optimization_barrier((list(first), list(second)))


def side_bit():
    return lax.axis_size("tm") // 32


def orders_of(size):
    bits = [bit for bit in steps_of(size) if bit != side_bit()]
    return [bits[k * len(bits) // 3 :] + bits[: k * len(bits) // 3] for k in range(3)]


def index_bits(bits):
    return [bit if bit < side_bit() else bit // 2 for bit in bits]


class Scatter:
    def __init__(self, keeps, sends):
        self.orders = orders_of(lax.axis_size("tm"))
        self.current = list(keeps)
        self.received = [swap(send, side_bit()) for send in sends]

    def step(self, *waiting):
        sends = []
        for p, order in enumerate(self.orders):
            half = self.current[p].shape[0] // 2
            mine, away = [
                lax.dynamic_slice_in_dim(self.current[p], half * index, half).astype(jnp.float32)
                + lax.dynamic_slice_in_dim(self.received[p], half * index, half).astype(jnp.float32)
                for index in (bit_of(order[0]), 1 - bit_of(order[0]))
            ]
            self.current[p] = mine
            sends.append(away.astype(jnp.bfloat16))
        sends, waiting = tie(sends, waiting)
        self.received = [swap(send, order.pop(0)) for send, order in zip(sends, self.orders)]
        return waiting

    def join(self, *done):
        self.received, done = tie(self.received, done)
        return done

    def result(self):
        return [a + b.astype(jnp.float32) for a, b in zip(self.current, self.received)]


class Gather:
    def __init__(self, blocks, near):
        self.orders = orders_of(lax.axis_size("tm"))
        self.held = [[] for _ in blocks]
        self.current = list(blocks)
        self.received = None
        self.near = near

    def stack(self):
        if self.received is None:
            return
        for p, other in enumerate(self.received):
            bit, mine = self.held[p][-1], self.current[p]
            axis = sum(before > bit for before in self.held[p])
            if not self.near:
                upper = bit_of(bit) == 1
                mine, other = jnp.where(upper, other, mine), jnp.where(upper, mine, other)
            self.current[p] = jnp.stack([mine, other], axis=axis)

    def step(self, *waiting):
        self.stack()
        self.current, waiting = tie(self.current, waiting)
        self.received = []
        for p, order in enumerate(self.orders):
            bit = order.pop()
            self.held[p].append(bit)
            self.received.append(swap(self.current[p], bit))
        return waiting

    def join(self, *done):
        self.received, done = tie(self.received, done)
        return done

    def finish(self, *waiting):
        self.stack()
        own = [value.reshape(-1, value.shape[-1]) for value in self.current]
        own, waiting = tie(own, waiting)
        return own, [swap(value, side_bit()) for value in own], waiting


class Stats:
    def __init__(self, stat, count):
        self.stat = stat
        self.count = float(count)
        self.bits = steps_of(lax.axis_size("tm"))

    def step(self, times=1):
        for _ in range(min(times, len(self.bits))):
            stat = self.stat
            other = swap(stat, self.bits.pop(0))
            gap = stat[0:1] - other[0:1]
            mean = 0.5 * (stat[0:1] + other[0:1])
            square = (stat[1:2] + other[1:2]) + gap * gap * (0.5 * self.count)
            self.stat = jnp.concatenate([mean, square, 0.5 * (stat[2:] + other[2:])], axis=0)
            self.count *= 2


class Exchange:
    def __init__(self, flags, carries, sums=()):
        self.bits = steps_of(lax.axis_size("tm"))
        high, self.width = carries[0][0].shape
        rows = high * len(carries)
        flags = jnp.broadcast_to(jnp.tile(flags, len(carries))[:, None], (rows, LANE))
        ends = jnp.concatenate([ends for ends, _, _ in carries], axis=0)
        self.payload = jnp.concatenate([ends, flags, *sums], axis=1)
        self.power = jnp.concatenate(
            [jnp.broadcast_to(power, (high, self.width)) for _, power, _ in carries], axis=0
        )
        self.lane = lax.broadcasted_iota(jnp.int32, self.payload.shape, 1)
        self.high = high
        self.reverse = [reverse for _, _, reverse in carries]
        self.before = jnp.zeros_like(ends)
        self.before_keep = jnp.ones_like(ends)

    def step(self, times=1):
        for _ in range(min(times, len(self.bits))):
            self.one()

    def one(self):
        bit = self.bits.pop(0)
        width = self.width
        mine, other = self.payload, swap(self.payload, bit)
        upper = bit_of(bit)
        row = lax.broadcasted_iota(jnp.int32, (len(mine), 1), 0) // self.high
        turned = sum((row == k) * int(reverse) for k, reverse in enumerate(self.reverse))
        following = turned != upper
        other_total = other[:, :width]
        keep_mine, keep_other = mine[:, width : width + 1], other[:, width : width + 1]
        self.before = jnp.where(
            following, self.before_keep * other_total + self.before, self.before
        )
        self.before_keep = jnp.where(
            following, self.before_keep * keep_other * self.power, self.before_keep
        )
        power = jnp.pad(self.power, ((0, 0), (0, mine.shape[1] - width)))
        carried = jnp.where(
            following, keep_mine * power * other + mine, keep_other * power * mine + other
        )
        self.payload = jnp.where(
            self.lane < width,
            carried,
            jnp.where(self.lane < width + LANE, mine * other, mine + other),
        )
        self.power = self.power * self.power

    def arrived(self, k):
        return self.before[k * self.high : (k + 1) * self.high]

    def sums(self):
        return self.payload[:, self.width + LANE :]


class SumAll:
    def __init__(self, value):
        self.value = value
        self.bits = steps_of(lax.axis_size("tm"))

    def step(self, times=1):
        for _ in range(min(times, len(self.bits))):
            self.value = self.value + swap(self.value, self.bits.pop(0))


def in_order(value, bits, slots):
    count = len(bits)
    axes = [count - bit.bit_length() for bit in bits]
    shape = (2,) * count + (slots, value.shape[1])
    return value.reshape(shape).transpose(axes + [count, count + 1]).reshape(value.shape)


def pad_lanes(value, padded):
    gap = padded - value.shape[-1]
    return jnp.pad(value, [(0, 0)] * (value.ndim - 1) + [(0, gap)])


def flat_places(shard, width, padded):
    size = lax.axis_size("tm")
    members = size * LANE // padded
    slots = LANE // members
    return members, slots, slots * width - shard


def to_block(flat, width, padded):
    size, mine = lax.axis_size("tm"), lax.axis_index("tm")
    members, slots, excess = flat_places(flat.shape[0], width, padded)
    lacking = excess * (members - 1)
    pairs = [(i + 1, i) for i in range(size - 1) if (i + 1) % members]
    extra = lax.ppermute(flat[:lacking], "tm", pairs)
    tail = jnp.zeros((excess,), flat.dtype)
    held = jnp.concatenate([flat, extra, tail])
    return lax.dynamic_slice_in_dim(held, excess * (mine % members), slots * width).reshape(
        slots, width
    )


def from_block(block, shard, padded):
    width = block.shape[1]
    size, mine = lax.axis_size("tm"), lax.axis_index("tm")
    members, slots, excess = flat_places(shard, width, padded)
    lacking = excess * (members - 1)
    pairs = [(i, i + 1) for i in range(size - 1) if (i + 1) % members]
    flat = block.reshape(-1)
    extra = lax.ppermute(flat[slots * width - lacking :], "tm", pairs)
    held = jnp.concatenate([extra, flat])
    return lax.dynamic_slice_in_dim(held, lacking - excess * (mine % members), shard)


def own_heads(shard, width, padded):
    members, slots, _ = flat_places(shard, width, padded)
    half = padded // 2
    group = LANE // 2
    if members == 2:
        lacking = slots - shard // width
        kept = -(-(lacking) // 16) * 16
        return [(0, group), (half + group - kept, kept)]
    return [(0, group), (half, group)]


def own_flat(found, shard, width, padded):
    mine = lax.axis_index("tm")
    members, slots, excess = flat_places(shard, width, padded)
    member = mine % members
    if members == 2:
        own, other = found[:slots].reshape(-1), found[slots:].reshape(-1)
        low = own[:shard]
        high = jnp.concatenate([other[other.shape[0] - excess :], own[: shard - excess]])
        return jnp.where(member == 0, low, high)
    near = found.reshape(members, slots * width)
    placed = jnp.take(near, jnp.arange(members) ^ member, axis=0).reshape(-1)
    return lax.dynamic_slice_in_dim(placed, shard * member, shard)


def per_device(
    inputs,
    clip_start,
    shallow_weight,
    shallow_momentum,
    deep_weight,
    deep_momentum,
    unit_params,
    unit_first,
    unit_second,
    out_grad,
):
    devices = lax.axis_size("tm")
    rows, frames, feats = inputs.shape
    width = shallow_weight.shape[1]
    padded = -(-width // WIDE) * WIDE
    group = width // (padded // LANE)
    count = rows * frames
    keep_mask = (1 - clip_start).astype(jnp.float32)
    flags = jnp.min(keep_mask, axis=1)
    keep = jnp.broadcast_to(keep_mask.T.reshape(count, 1), (count, LANE))
    params = pad_lanes(unit_params, padded)
    rates = jnp.maximum(1.0 - jnp.exp(-params[:, 0:1]), DECAY_FLOOR)
    powers = rates
    for _ in range(frames.bit_length() - 1):
        powers = powers * powers

    deep_block = pad_lanes(to_block(deep_weight.astype(jnp.bfloat16), width, padded), padded)
    momentum_block = pad_lanes(to_block(deep_momentum, width, padded), padded)

    shares = [3 * padded // 8, 3 * padded // 8, padded // 4]
    parts = [(sum(shares[:p]), shares[p]) for p in range(3)]
    side = bit_of(side_bit()).astype(jnp.int32).reshape(1)
    chunks = padded // WIDE
    orders = orders_of(devices)
    x, proj_one, stat_one, gram = front(
        inputs.reshape(count, feats), shallow_weight, rows, frames
    )
    (deep_block,), (stat_one,) = tie([deep_block], [stat_one])
    deep_low = lax.all_gather(deep_block, "tm", axis=0, tiled=True)
    stats = Stats(stat_one, count)
    grad_rows = out_grad.reshape(count, width)
    delta = None
    for k in range(chunks):
        stats.step()
        delta = delta_two(k, delta, grad_rows, keep, params[1], rows, frames, padded)
        delta, (stats.stat,) = tie(delta, [stats.stat])
    delta_local, delta_end = delta
    stats.step(len(stats.bits))
    (stat_one,), (momentum_block,) = tie([stats.stat], [momentum_block])
    state_local, state_end = local_states(
        proj_one, keep, params[0], stat_one, rows, frames, devices
    )
    carries = Exchange(flags, [(state_end, powers[0], False), (delta_end, powers[1], True)])
    carries.step(len(carries.bits))
    state_in, delta_in = carries.arrived(0), carries.arrived(1)
    low_one, mean_one = low_one_of(
        state_local, state_in, keep, params[0], rows, frames, width, group
    )
    proj_two, stat_two = second_forward(low_one, deep_low)
    stats = Stats(jnp.concatenate([stat_two, mean_one], axis=0), count)
    stats.step(len(stats.bits))
    hidden = [None, None]
    sources = [(state_local, state_in, params[0]), None]

    def next_hidden(layer, places, waiting):
        states, start, layer_params = sources[layer]
        for k in places:
            (start,), waiting = tie([start], waiting)
            hidden[layer] = hidden_of(
                k, hidden[layer], states, start, keep, layer_params, rows, frames, width
            )
        hidden[layer], waiting = tie(hidden[layer], waiting)
        return waiting

    stat_two, mean_one = stats.stat[:2], stats.stat[2:]
    gate, sums_two = gate_two(
        proj_two, delta_local, delta_in, keep, params[1], stat_two, rows, frames, devices
    )
    sums = SumAll(sums_two)
    turned = None
    for k in range(chunks):
        sums.step()
        turned = turn(k, turned, low_one, mean_one)
        turned, (sums.value,) = tie(turned, [sums.value])
    sums.step(len(sums.bits))
    sums_two = sums.value
    slots = padded // devices
    weights = [index_bits(order) for order in orders]
    aligned = slots % 16 == 0
    grad_two, total_two, keeps, sends = deep_term(
        parts, weights if aligned else None, side, gate, proj_two, params[1], stat_two,
        sums_two, turned[0], rows, frames, devices,
    )
    if not aligned:
        keeps = [in_order(keep, order, slots) for keep, order in zip(keeps, weights)]
        sends = [in_order(send, order, slots) for send, order in zip(sends, weights)]
    scatter = Scatter(keeps, sends)
    back = back_one(grad_two, deep_low)
    (back,) = scatter.join(back)
    (back,) = scatter.step(back)
    back_local, back_end = delta_one(back, keep, params[0], rows, frames, width, group)
    second_local, second_end, second_decay = states_two(
        proj_two, delta_local, delta_in, keep, params[1], stat_two, rows, frames, devices
    )
    back_end, second_end = scatter.join(back_end, second_end)
    tall = 2 * rows
    back_end, second_end = scatter.step(back_end, second_end)
    carries = Exchange(
        flags,
        [(back_end, powers[0], True), (second_end, powers[1], False)],
        [total_two.reshape(tall, -1), gram],
    )
    carries.step(2)
    (carries.payload,) = next_hidden(0, range(chunks), [carries.payload])
    (carries.payload,) = scatter.join(carries.payload)
    while len(scatter.orders[0]) > 1:
        (carries.payload,) = scatter.step(carries.payload)
        carries.step()
        (carries.payload,) = scatter.join(carries.payload)
    (carries.payload,) = scatter.step(carries.payload)
    carries.step(len(carries.bits))
    carries.payload, carries.before = scatter.join(carries.payload, carries.before)
    back_in, second_in = carries.arrived(0), carries.arrived(1)
    sources[1] = (second_local, second_in, params[1])
    total_two = carries.sums()[:, : padded // tall].reshape(1, padded)
    gram = carries.sums()[:, padded // tall :]
    mine = lax.axis_index("tm")
    place = mine // (2 * side_bit()) * side_bit() + mine % side_bit()
    place = (side[0] * (devices // 2) + place) * slots
    mean_own = lax.dynamic_slice_in_dim(mean_one[0], place, slots)[:, None]
    grad_parts = [
        part + mean_own * total_two[:, first : first + lanes]
        for (first, lanes), part in zip(parts, scatter.result())
    ]
    gather = Gather(
        [
            (MUON_BETA * momentum_block[:, first : first + lanes] + part).astype(jnp.bfloat16)
            for (first, lanes), part in zip(parts, grad_parts)
        ],
        True,
    )
    (back_in,) = gather.step(back_in)
    gate_low, sums_one = gate_one(
        proj_one, state_local, state_in, back_local, back_in, keep, params[0], stat_one, x,
        rows, frames, devices, feats,
    )
    decay_two = jnp.sum(second_decay[:rows] + second_decay[rows:] * second_in, axis=0, keepdims=True)
    sums_one = sums_one + jnp.pad(decay_two, ((feats + 3, SIDE - feats - 4), (0, 0)))
    (sums_one,) = gather.join(sums_one)
    spread = SumSpread(sums_one)
    for count_steps, places in ((3, [0, 1]), (3, [2]), (3, [3])):
        (spread.value,) = gather.step(spread.value)
        spread.step(count_steps)
        if places:
            (spread.value,) = next_hidden(1, places, [spread.value])
        (spread.value,) = gather.join(spread.value)
    while gather.orders[0]:
        gather.step()
    own, other, (spread.value,) = gather.finish(spread.value)
    spread.step(len(spread.steps))
    sums_one = spread.value
    (hidden_one,), (hidden_two,) = hidden
    shallow_grad, shallow_next, shallow_new, shallow_low = shallow_step(
        sums_one, gram, params[0], stat_one, shallow_weight, shallow_momentum,
        count * devices, count,
    )
    input_back = input_grad_of(
        gate_low, proj_one, params[0], stat_one, sums_one, shallow_weight, rows, frames, devices
    )
    input_grad = jnp.swapaxes(input_back.reshape(frames, rows, feats), 0, 1)
    grad_block = jnp.concatenate(grad_parts, axis=1)

    shard = deep_weight.shape[0]
    heads = own_heads(shard, width, padded)
    ortho = newton_rows(own, other, parts, heads)
    deep_ortho = own_flat(ortho[:, :width], shard, width, padded)
    deep_new = MUON_KEEP * deep_weight - MUON_RATE * deep_ortho.astype(jnp.float32)
    deep_grad = from_block(grad_block[:, :width], shard, padded)
    deep_next = MUON_BETA * deep_momentum + deep_grad

    unit_sums = sums_one[feats : feats + 4, :width]
    bias_gain_two = sums_two[:, :width]
    slope = jnp.where(
        1.0 - jnp.exp(-unit_params[:, 0]) > DECAY_FLOOR, jnp.exp(-unit_params[:, 0]), 0.0
    )
    unit_grad = jnp.stack(
        [
            jnp.stack([unit_sums[2] * slope[0], unit_sums[0], unit_sums[1], unit_sums[0]]),
            jnp.stack(
                [unit_sums[3] * slope[1], bias_gain_two[0], bias_gain_two[1], bias_gain_two[0]]
            ),
        ]
    )
    first_fix = 1.0 - FIRST_DECAY**STEP
    second_fix = 1.0 - SECOND_DECAY**STEP
    first_new = FIRST_DECAY * unit_first + (1.0 - FIRST_DECAY) * unit_grad
    second_new = SECOND_DECAY * unit_second + (1.0 - SECOND_DECAY) * unit_grad * unit_grad
    params_new = unit_params - ADAM_RATE * (first_new / first_fix) / (
        jnp.sqrt(second_new / second_fix) + ADAM_EPSILON
    )
    return (
        hidden_one.reshape(rows, frames, width),
        hidden_two.reshape(rows, frames, width),
        input_grad,
        shallow_grad,
        shallow_next,
        shallow_new,
        shallow_low,
        deep_grad,
        deep_next,
        deep_new,
        deep_new.astype(jnp.bfloat16),
        first_new,
        second_new,
        params_new,
    )


def solution(mesh):
    in_specs = (
        P(None, "tm", None),
        P(None, "tm"),
        P(),
        P(),
        P("tm"),
        P("tm"),
        P(),
        P(),
        P(),
        P(None, "tm", None),
    )
    out_specs = (
        P(None, "tm", None),
        P(None, "tm", None),
        P(None, "tm", None),
        P(),
        P(),
        P(),
        P(),
        P("tm"),
        P("tm"),
        P("tm"),
        P("tm"),
        P(),
        P(),
        P(),
    )
    return jax.shard_map(
        per_device, mesh=mesh, in_specs=in_specs, out_specs=out_specs, check_vma=False
    )
```

```python
import functools

import jax
import jax.numpy as jnp
from jax import lax
from jax.experimental import pallas as pl
from jax.experimental.pallas import tpu as pltpu
from jax.sharding import PartitionSpec as P

NS_STEPS = 2
STEP = 5


NORM_EPSILON = 1e-05
MUON_EPSILON = 1e-07
COEFF_A = 3.4445
COEFF_B = -4.775
COEFF_C = 2.0315
MUON_BETA = 0.5
MUON_RATE = 4.0
MUON_KEEP = 0.999
FIRST_DECAY = 0.9
SECOND_DECAY = 0.95
ADAM_RATE = 0.5
ADAM_EPSILON = 1e-08
DECAY_FLOOR = 0.9
LANE = 128
WIDE = 512
PART = 256
SIDE = 80


def kernel_call(body, grid, in_specs, out_specs, out_shape, scratch=(), flops=0, traffic=0):
    return pl.pallas_call(
        body,
        grid=grid,
        in_specs=in_specs,
        out_specs=out_specs,
        out_shape=out_shape,
        scratch_shapes=list(scratch),
        compiler_params=pltpu.CompilerParams(vmem_limit_bytes=56 * 1024 * 1024),
        cost_estimate=pl.CostEstimate(flops=flops, bytes_accessed=traffic, transcendentals=0),
    )


def shape_of(shape, dtype=jnp.float32):
    return jax.ShapeDtypeStruct(shape, dtype)


def whole(shape):
    return pl.BlockSpec(shape, lambda i: (0,) * len(shape))


def lanes_of(rows, width=WIDE):
    return pl.BlockSpec((rows, width), lambda i: (0, i))


def chunk_call(body, place, in_specs, out_specs, out_shape, arrays, previous, scratch=(), traffic=0):
    count = len(in_specs)
    before = list(previous) if previous is not None else []

    def run(*refs):
        body(*refs[:count], *refs[count + len(before) :])

    return pl.pallas_call(
        run,
        grid=(1,),
        in_specs=list(in_specs) + [pl.BlockSpec(memory_space=pl.ANY)] * len(before),
        out_specs=out_specs,
        out_shape=out_shape,
        scratch_shapes=list(scratch),
        input_output_aliases={count + k: k for k in range(len(before))},
        compiler_params=pltpu.CompilerParams(vmem_limit_bytes=56 * 1024 * 1024),
        cost_estimate=pl.CostEstimate(flops=0, bytes_accessed=traffic, transcendentals=0),
    )(*arrays, *before)


def chunk_at(rows, place):
    return pl.BlockSpec((rows, WIDE), lambda i: (0, place))


def rate_of(params):
    return jnp.maximum(1.0 - jnp.exp(-params[0:1]), DECAY_FLOOR)


def softened(value):
    return jnp.maximum(value, 0.0) + jnp.log(1.0 + jnp.exp(-jnp.abs(value)))


def sigmoid(value):
    return 0.5 * jnp.tanh(0.5 * value) + 0.5


def wide_keep(keep_ref, t, rows):
    keep = keep_ref[pl.ds(pl.multiple_of(t * rows, rows), rows), :]
    return jnp.concatenate([keep] * (WIDE // LANE), axis=1)


def rows_at(ref, t, rows):
    return ref[pl.ds(pl.multiple_of(t * rows, rows), rows), :]


def store_at(ref, t, rows, value):
    ref[pl.ds(pl.multiple_of(t * rows, rows), rows), :] = value


def valid_lanes(shape, total, step):
    return lax.broadcasted_iota(jnp.int32, shape, 1) + step * WIDE < total


def unit_terms(params_ref, stat_ref, total_devices, frames):
    params = params_ref[...]
    stat = stat_ref[...]
    centre = stat[0:1]
    inverse = lax.rsqrt(stat[1:2] / (total_devices * frames) + NORM_EPSILON)
    return centre, inverse, params[2:3], params[3:4] + params[1:2]


def front_body(rows, frames, width, x_ref, w_ref, xt_ref, proj_ref, stat_ref, gram_ref, padded_w):
    step = pl.program_id(0)
    count, feats = x_ref.shape

    @pl.when(step == 0)
    def _():
        i = lax.broadcasted_iota(jnp.int32, (count, count), 0)
        j = lax.broadcasted_iota(jnp.int32, (count, count), 1)
        move = (j == lax.rem(i, rows) * frames + lax.div(i, rows)).astype(jnp.bfloat16)
        moved = jnp.dot(move, x_ref[...], preferred_element_type=jnp.float32).astype(jnp.bfloat16)
        i = lax.broadcasted_iota(jnp.int32, (feats, LANE), 0)
        j = lax.broadcasted_iota(jnp.int32, (feats, LANE), 1)
        wide = jnp.dot(moved, (i == j).astype(jnp.bfloat16), preferred_element_type=jnp.float32)
        lane = lax.broadcasted_iota(jnp.int32, (count, LANE), 1)
        xt = jnp.where(lane == feats, 1.0, wide).astype(jnp.bfloat16)
        xt_ref[...] = xt
        gram = dot_tn(xt, xt)
        high = gram_ref.shape[0]
        for k in range(SIDE // high):
            gram_ref[:, k * LANE : (k + 1) * LANE] = gram[k * high : (k + 1) * high]
        padded_w[...] = jnp.zeros_like(padded_w)

    weight = w_ref[...]
    padded_w[0:feats, :] = jnp.where(valid_lanes(weight.shape, width, step), weight, 0.0)
    proj = jnp.dot(
        xt_ref[...], padded_w[...].astype(jnp.bfloat16), preferred_element_type=jnp.float32
    )
    proj_ref[...] = proj
    mean = jnp.sum(proj, axis=0, keepdims=True) * (1.0 / count)
    off = proj - mean
    stat_ref[0:1, :] = mean
    stat_ref[1:2, :] = jnp.sum(off * off, axis=0, keepdims=True)


def dot_tn(a, b):
    return lax.dot_general(a, b, (((0,), (0,)), ((), ())), preferred_element_type=jnp.float32)


def front(x, weight, rows, frames):
    count, feats = x.shape
    width = weight.shape[1]
    padded = -(-width // WIDE) * WIDE
    return kernel_call(
        functools.partial(front_body, rows, frames, width),
        (padded // WIDE,),
        [whole((count, feats)), lanes_of(feats)],
        [whole((count, LANE)), lanes_of(count), lanes_of(2), whole((2 * rows, SIDE // (2 * rows) * LANE))],
        [
            shape_of((count, LANE), jnp.bfloat16),
            shape_of((count, padded)),
            shape_of((2, padded)),
            shape_of((2 * rows, SIDE // (2 * rows) * LANE)),
        ],
        [pltpu.VMEM((LANE, WIDE), jnp.float32)],
    )(x, weight)


def delta_two_body(rows, frames, width, place, grad_ref, keep_ref, params_ref, delta_ref, end_ref, held):
    pieces = WIDE // LANE
    mask = valid_lanes((rows * frames, WIDE), width, place)
    grad = jnp.where(mask, grad_ref[...].astype(jnp.float32), 0.0)
    for g in range(pieces):
        held[g] = grad[:, g * LANE : (g + 1) * LANE]
    rate = rate_of(params_ref[...])

    def body(k, carried):
        t = frames - 1 - k
        own = jnp.concatenate(
            [held[g, pl.ds(t, rows, stride=frames), :] for g in range(pieces)], axis=1
        )
        delta = own + carried
        store_at(delta_ref, t, rows, delta)
        return rate * wide_keep(keep_ref, t, rows) * delta

    end_ref[...] = lax.fori_loop(
        0, frames, body, jnp.zeros((rows, WIDE), jnp.float32), unroll=8
    )


def delta_two(place, previous, out_grad, keep, params, rows, frames, padded):
    count, width = out_grad.shape
    return chunk_call(
        functools.partial(delta_two_body, rows, frames, width, place),
        place,
        [chunk_at(count, place), whole((count, LANE)), chunk_at(4, place)],
        [chunk_at(count, place), chunk_at(rows, place)],
        [shape_of((count, padded)), shape_of((rows, padded))],
        (out_grad, keep, params),
        previous,
        [pltpu.VMEM((WIDE // LANE, count, LANE), jnp.float32)],
    )


def states_body(
    rows, frames, devices, proj_ref, keep_ref, params_ref, stat_ref, state_ref, end_ref
):
    centre, inverse, gain, offset = unit_terms(params_ref, stat_ref, devices, rows * frames)
    rate = rate_of(params_ref[...])
    share = 1.0 - rate

    def body(t, carried):
        gate = (rows_at(proj_ref, t, rows) - centre) * inverse * gain + offset
        soft = softened(gate)
        carried = rate * wide_keep(keep_ref, t, rows) * carried + share * soft
        store_at(state_ref, t, rows, carried)
        return carried

    end_ref[...] = lax.fori_loop(
        0, frames, body, jnp.zeros((rows, WIDE), jnp.float32), unroll=8
    )


def local_states(proj, keep, params, stat, rows, frames, devices):
    count, padded = proj.shape
    return kernel_call(
        functools.partial(states_body, rows, frames, devices),
        (padded // WIDE,),
        [lanes_of(count), whole((count, LANE)), lanes_of(4), lanes_of(2)],
        [lanes_of(count), lanes_of(rows)],
        [shape_of((count, padded)), shape_of((rows, padded))],
    )(proj, keep, params, stat)


def to_slots(value, group):
    pieces = value.shape[1] // LANE
    lane = lax.broadcasted_iota(jnp.int32, (value.shape[0], LANE), 1)
    parts = [value[:, g * LANE : (g + 1) * LANE] for g in range(pieces)]
    out = []
    for g in range(pieces):
        moved = (LANE - group) * g
        if moved == 0:
            new = parts[g]
        else:
            new = jnp.where(
                lane < moved, pltpu.roll(parts[g - 1], moved, 1), pltpu.roll(parts[g], moved, 1)
            )
        out.append(jnp.where(lane < group, new, 0.0))
    return jnp.concatenate(out, axis=1)


def from_slots(value, group, width):
    pieces = value.shape[1] // LANE
    lane = lax.broadcasted_iota(jnp.int32, (value.shape[0], LANE), 1)
    parts = [value[:, g * LANE : (g + 1) * LANE] for g in range(pieces)]
    out = []
    for j in range(pieces):
        moved = (LANE - group) * j
        new = parts[j] if moved == 0 else pltpu.roll(parts[j], LANE - moved, 1)
        if j + 1 < pieces:
            new = jnp.where(lane < group - moved, new, pltpu.roll(parts[j + 1], group - moved, 1))
        left = width - j * LANE
        out.append(new if left >= LANE else jnp.where(lane < left, new, 0.0))
    return jnp.concatenate(out, axis=1)


def low_one_body(rows, frames, width, group, state_ref, start_ref, keep_ref, params_ref, low_ref, mean_ref):
    pieces = state_ref.shape[1] // LANE
    rate = rate_of(params_ref[...])

    def advance(t, carried):
        keep = rows_at(keep_ref, t, rows)
        carried = rate * jnp.concatenate([keep] * pieces, axis=1) * carried
        return carried, rows_at(state_ref, t, rows) + carried

    def body(k, both):
        carried, total = both
        t = 2 * k
        carried, first = advance(t, carried)
        carried, second = advance(t + 1, carried)
        place = pl.ds(pl.multiple_of(t * rows, 2 * rows), 2 * rows)
        slots = to_slots(jnp.concatenate([first, second], axis=0), group)
        low_ref[place, :] = slots.astype(jnp.bfloat16)
        return carried, total + slots[:rows] + slots[rows:]

    start = start_ref[...]
    _, total = lax.fori_loop(0, frames // 2, body, (start, jnp.zeros_like(start)), unroll=2)
    mean_ref[...] = jnp.sum(total, axis=0, keepdims=True) * (1.0 / (rows * frames))


def low_one_of(states, start, keep, params, rows, frames, width, group):
    count, padded = states.shape
    return kernel_call(
        functools.partial(low_one_body, rows, frames, width, group),
        (1,),
        [whole((count, padded)), whole((rows, padded)), whole((count, LANE)), whole((4, padded))],
        [whole((count, padded)), whole((1, padded))],
        [shape_of((count, padded), jnp.bfloat16), shape_of((1, padded))],
    )(states, start, keep, params)


def hidden_body(rows, frames, state_ref, start_ref, keep_ref, params_ref, hidden_ref, held):
    pieces = WIDE // LANE
    rate = rate_of(params_ref[...])

    def body(t, carry):
        carry = rate * wide_keep(keep_ref, t, rows) * carry
        state = rows_at(state_ref, t, rows) + carry
        for g in range(pieces):
            held[g, pl.ds(pl.multiple_of(t * rows, rows), rows), :] = state[
                :, g * LANE : (g + 1) * LANE
            ]
        return carry

    lax.fori_loop(0, frames, body, start_ref[...], unroll=8)
    for r in range(rows):
        for g in range(pieces):
            hidden_ref[r * frames : (r + 1) * frames, g * LANE : (g + 1) * LANE] = held[
                g, pl.ds(r, frames, stride=rows), :
            ]


def hidden_of(place, previous, states, start, keep, params, rows, frames, width):
    count, _ = states.shape
    return chunk_call(
        functools.partial(hidden_body, rows, frames),
        place,
        [chunk_at(count, place), chunk_at(rows, place), whole((count, LANE)), chunk_at(4, place)],
        [chunk_at(count, place)],
        [shape_of((count, width))],
        (states, start, keep, params),
        previous,
        [pltpu.VMEM((WIDE // LANE, count, LANE), jnp.float32)],
    )


def second_body(low_ref, weight_ref, proj_ref, stat_ref):
    tile = 256
    count = proj_ref.shape[0]
    for j in range(0, WIDE, tile):
        place = slice(j, j + tile)
        for i in range(0, count, tile):
            proj_ref[i : i + tile, place] = jnp.dot(
                low_ref[i : i + tile, :], weight_ref[:, place], preferred_element_type=jnp.float32
            )
        proj = proj_ref[:, place]
        mean = jnp.sum(proj, axis=0, keepdims=True) * (1.0 / count)
        off = proj - mean
        stat_ref[0:1, place] = mean
        stat_ref[1:2, place] = jnp.sum(off * off, axis=0, keepdims=True)


def second_forward(low, weight):
    count, padded = low.shape
    return kernel_call(
        second_body,
        (padded // WIDE,),
        [whole((count, padded)), lanes_of(padded)],
        [lanes_of(count), lanes_of(2)],
        [shape_of((count, padded)), shape_of((2, padded))],
    )(low, weight)


def gate_two_body(
    rows, frames, devices, proj_ref, delta_ref, start_ref, keep_ref, params_ref, stat_ref, gate_ref, sums_ref
):
    centre, inverse, gain, offset = unit_terms(params_ref, stat_ref, devices, rows * frames)
    rate = rate_of(params_ref[...])
    share = 1.0 - rate
    none = jnp.zeros((rows, WIDE), jnp.float32)

    def body(k, carried):
        carry, bias_sum, gain_sum = carried
        t = frames - 1 - k
        delta = rows_at(delta_ref, t, rows) + carry
        normed = (rows_at(proj_ref, t, rows) - centre) * inverse
        gate = share * delta * sigmoid(normed * gain + offset)
        store_at(gate_ref, t, rows, gate)
        carry = rate * wide_keep(keep_ref, t, rows) * carry
        return carry, bias_sum + gate, gain_sum + gate * normed

    _, bias_sum, gain_sum = lax.fori_loop(
        0, frames, body, (start_ref[...], none, none), unroll=8
    )
    sums_ref[0:1, :] = jnp.sum(bias_sum, axis=0, keepdims=True)
    sums_ref[1:2, :] = jnp.sum(gain_sum, axis=0, keepdims=True)


def gate_two(proj, delta, start, keep, params, stat, rows, frames, devices):
    count, padded = proj.shape
    return kernel_call(
        functools.partial(gate_two_body, rows, frames, devices),
        (padded // WIDE,),
        [lanes_of(count), lanes_of(count), lanes_of(rows), whole((count, LANE)), lanes_of(4), lanes_of(2)],
        [lanes_of(count), lanes_of(2)],
        [shape_of((count, padded)), shape_of((2, padded))],
    )(proj, delta, start, keep, params, stat)


def states_two_body(
    rows, frames, devices, proj_ref, delta_ref, start_ref, keep_ref, params_ref, stat_ref,
    state_ref, end_ref, decay_ref, held,
):
    centre, inverse, gain, offset = unit_terms(params_ref, stat_ref, devices, rows * frames)
    rate = rate_of(params_ref[...])
    share = 1.0 - rate
    none = jnp.zeros((rows, WIDE), jnp.float32)

    def backward(k, carry):
        t = frames - 1 - k
        store_at(held, t, rows, rows_at(delta_ref, t, rows) + carry)
        return rate * wide_keep(keep_ref, t, rows) * carry

    lax.fori_loop(0, frames, backward, start_ref[...], unroll=8)

    def forward(t, carried):
        state, reach, decay, factor = carried
        keep = wide_keep(keep_ref, t, rows)
        delta = rows_at(held, t, rows)
        value = (rows_at(proj_ref, t, rows) - centre) * inverse * gain + offset
        soft = softened(value)
        decay = decay + delta * (keep * state - soft)
        factor = factor + delta * keep * reach
        state = rate * keep * state + share * soft
        reach = rate * keep * reach
        store_at(state_ref, t, rows, state)
        return state, reach, decay, factor

    state, _, decay, factor = lax.fori_loop(
        0, frames, forward, (none, jnp.ones_like(none), none, none), unroll=4
    )
    end_ref[...] = state
    decay_ref[0:rows, :] = decay
    decay_ref[rows : 2 * rows, :] = factor


def states_two(proj, delta, start, keep, params, stat, rows, frames, devices):
    count, padded = proj.shape
    return kernel_call(
        functools.partial(states_two_body, rows, frames, devices),
        (padded // WIDE,),
        [
            lanes_of(count),
            lanes_of(count),
            lanes_of(rows),
            whole((count, LANE)),
            lanes_of(4),
            lanes_of(2),
        ],
        [lanes_of(count), lanes_of(rows), lanes_of(2 * rows)],
        [shape_of((count, padded)), shape_of((rows, padded)), shape_of((2 * rows, padded))],
        [pltpu.VMEM((count, WIDE), jnp.float32)],
    )(proj, delta, start, keep, params, stat)


def turn_body(low_ref, mean_ref, turned_ref):
    half = LANE // 2
    turned = (low_ref[...].astype(jnp.float32) - mean_ref[...]).T.astype(jnp.bfloat16)
    for g in range(WIDE // LANE):
        for side in range(2):
            turned_ref[side, g * half : (g + 1) * half, :] = turned[
                g * LANE + side * half : g * LANE + (side + 1) * half
            ]


def turn(place, previous, low, mean):
    count, padded = low.shape
    return chunk_call(
        turn_body,
        place,
        [chunk_at(count, place), chunk_at(1, place)],
        [pl.BlockSpec((2, WIDE // 2, count), lambda i: (0, place, 0))],
        [shape_of((2, padded // 2, count), jnp.bfloat16)],
        (low, mean),
        previous,
    )


def deep_term_body(
    rows, frames, devices, parts, orders, side_ref, gate_ref, proj_ref, params_ref, stat_ref, sums_ref,
    turned_ref, grad_ref, total_ref, *outs,
):
    step = pl.program_id(0)
    total = devices * rows * frames
    centre, inverse, gain, _ = unit_terms(params_ref, stat_ref, devices, rows * frames)
    sums = sums_ref[...] * (1.0 / total)
    normed = (proj_ref[...] - centre) * inverse
    grad = (gain * inverse * (gate_ref[...] - sums[0:1] - normed * sums[1:2])).astype(jnp.bfloat16)
    grad_ref[...] = grad
    total_ref[...] = jnp.sum(grad.astype(jnp.float32), axis=0, keepdims=True)
    side = side_ref[0]
    half = turned_ref.shape[1]
    tile = 256
    for p, (first, lanes) in enumerate(parts):

        @pl.when((step >= first // PART) & (step < (first + lanes) // PART))
        def _():
            for which, out_ref in ((side, outs[p]), (1 - side, outs[len(parts) + p])):
                for k in range(half // tile):
                    part = jnp.dot(
                        turned_ref[which, k * tile : (k + 1) * tile, :],
                        grad_ref[...],
                        preferred_element_type=jnp.float32,
                    ).astype(out_ref.dtype)
                    if orders is None:
                        out_ref[k * tile : (k + 1) * tile, :] = part
                        continue
                    slots = half // 2 ** len(orders[p])
                    for b in range(tile // slots):
                        block = k * (tile // slots) + b
                        place = 0
                        for weight in orders[p]:
                            place = 2 * place + block // weight % 2
                        out_ref[place * slots : (place + 1) * slots, :] = part[
                            b * slots : (b + 1) * slots
                        ]


def deep_term(parts, orders, side, gate, proj, params, stat, sums, turned, rows, frames, devices):
    count, padded = proj.shape
    half = padded // 2

    def some(first, lanes):
        return pl.BlockSpec(
            (half, PART), lambda i: (0, jnp.clip(i - first // PART, 0, lanes // PART - 1))
        )

    found = kernel_call(
        functools.partial(deep_term_body, rows, frames, devices, parts, orders),
        (padded // PART,),
        [
            pl.BlockSpec(memory_space=pltpu.SMEM),
            lanes_of(count, PART),
            lanes_of(count, PART),
            lanes_of(4, PART),
            lanes_of(2, PART),
            lanes_of(2, PART),
            whole((2, half, count)),
        ],
        [lanes_of(count, PART), lanes_of(1, PART)] + [some(*part) for part in parts] * 2,
        [shape_of((count, padded), jnp.bfloat16), shape_of((1, padded))]
        + [shape_of((half, lanes), jnp.bfloat16) for _, lanes in parts] * 2,
    )(side, gate, proj, params, stat, sums, turned)
    return found[0], found[1], found[2 : 2 + len(parts)], found[2 + len(parts) :]


def back_body(grad_ref, weight_ref, back_ref):
    back_ref[...] = dot_nt(grad_ref[...], weight_ref[...])


def back_one(grad, weight):
    count, padded = grad.shape
    return kernel_call(
        back_body,
        (padded // WIDE,),
        [whole((count, padded)), pl.BlockSpec((WIDE, padded), lambda i: (i, 0))],
        lanes_of(count),
        shape_of((count, padded)),
    )(grad, weight)


def delta_one_body(rows, frames, width, group, back_ref, keep_ref, params_ref, delta_ref, end_ref):
    pieces = back_ref.shape[1] // LANE
    rate = rate_of(params_ref[...])

    def body(k, carried):
        t = frames - 1 - k
        delta = from_slots(rows_at(back_ref, t, rows), group, width) + carried
        store_at(delta_ref, t, rows, delta)
        keep = rows_at(keep_ref, t, rows)
        return rate * jnp.concatenate([keep] * pieces, axis=1) * delta

    end_ref[...] = lax.fori_loop(
        0, frames, body, jnp.zeros((rows, back_ref.shape[1]), jnp.float32), unroll=2
    )


def delta_one(back, keep, params, rows, frames, width, group):
    count, padded = back.shape
    return kernel_call(
        functools.partial(delta_one_body, rows, frames, width, group),
        (1,),
        [whole((count, padded)), whole((count, LANE)), whole((4, padded))],
        [whole((count, padded)), whole((rows, padded))],
        [shape_of((count, padded)), shape_of((rows, padded))],
    )(back, keep, params)


def gate_one_body(
    rows,
    frames,
    devices,
    feats,
    proj_ref,
    state_ref,
    first_ref,
    delta_ref,
    start_ref,
    keep_ref,
    params_ref,
    stat_ref,
    x_ref,
    gate_ref,
    sums_ref,
    held,
):
    centre, inverse, gain, offset = unit_terms(params_ref, stat_ref, devices, rows * frames)
    rate = rate_of(params_ref[...])
    share = 1.0 - rate
    none = jnp.zeros((rows, WIDE), jnp.float32)

    def backward(k, carry):
        t = frames - 1 - k
        store_at(held, t, rows, rows_at(delta_ref, t, rows) + carry)
        return rate * wide_keep(keep_ref, t, rows) * carry

    lax.fori_loop(0, frames, backward, start_ref[...], unroll=8)

    def forward(t, carried):
        carry, before, bias_sum, gain_sum, decay_sum = carried
        keep = wide_keep(keep_ref, t, rows)
        delta = rows_at(held, t, rows)
        normed = (rows_at(proj_ref, t, rows) - centre) * inverse
        value = normed * gain + offset
        soft = softened(value)
        gate = share * delta * sigmoid(value)
        store_at(gate_ref, t, rows, gate)
        decay_sum = decay_sum + delta * (keep * before - soft)
        carry = rate * keep * carry
        before = rows_at(state_ref, t, rows) + carry
        return carry, before, bias_sum + gate, gain_sum + gate * normed, decay_sum

    first = first_ref[...]
    _, _, bias_sum, gain_sum, decay_sum = lax.fori_loop(
        0, frames, forward, (first, first, none, none, none), unroll=4
    )
    bias = jnp.sum(bias_sum, axis=0, keepdims=True)
    mean = bias * (1.0 / (rows * frames))
    x = x_ref[...]
    ones = jnp.ones((rows * frames, LANE), jnp.bfloat16)
    total = jnp.concatenate([dot_tn(x, ones)] * (WIDE // LANE), axis=1)
    term = dot_tn(x, (gate_ref[...] - mean).astype(jnp.bfloat16)) + total * mean
    sums_ref[...] = term[: sums_ref.shape[0]]
    sums_ref[feats : feats + 1, :] = bias
    sums_ref[feats + 1 : feats + 2, :] = jnp.sum(gain_sum, axis=0, keepdims=True)
    sums_ref[feats + 2 : feats + 3, :] = jnp.sum(decay_sum, axis=0, keepdims=True)


def gate_one(proj, states, first, delta, start, keep, params, stat, x, rows, frames, devices, feats):
    count, padded = proj.shape
    return kernel_call(
        functools.partial(gate_one_body, rows, frames, devices, feats),
        (padded // WIDE,),
        [
            lanes_of(count),
            lanes_of(count),
            lanes_of(rows),
            lanes_of(count),
            lanes_of(rows),
            whole((count, LANE)),
            lanes_of(4),
            lanes_of(2),
            whole((count, LANE)),
        ],
        [lanes_of(count), lanes_of(SIDE)],
        [shape_of((count, padded)), shape_of((SIDE, padded))],
        [pltpu.VMEM((count, WIDE), jnp.float32)],
    )(proj, states, first, delta, start, keep, params, stat, x)


def input_grad_body(
    rows, frames, devices, width, feats, gate_ref, proj_ref, params_ref, stat_ref, sums_ref, w_ref, back_ref
):
    step = pl.program_id(0)
    total = devices * rows * frames
    centre, inverse, gain, _ = unit_terms(params_ref, stat_ref, devices, rows * frames)
    bias = sums_ref[feats : feats + 1, :] * (1.0 / total)
    slope = sums_ref[feats + 1 : feats + 2, :] * (1.0 / total)
    normed = (proj_ref[...] - centre) * inverse
    grad = (gain * inverse * (gate_ref[...] - bias - normed * slope)).astype(jnp.bfloat16)
    weight = w_ref[...]
    weight = jnp.where(valid_lanes(weight.shape, width, step), weight, 0.0).astype(jnp.bfloat16)
    part = dot_nt(grad, weight)

    @pl.when(step == 0)
    def _():
        back_ref[...] = part

    @pl.when(step > 0)
    def _():
        back_ref[...] += part


def input_grad_of(gate, proj, params, stat, sums, weight, rows, frames, devices):
    count, padded = proj.shape
    feats, width = weight.shape
    return kernel_call(
        functools.partial(input_grad_body, rows, frames, devices, width, feats),
        (padded // WIDE,),
        [lanes_of(count), lanes_of(count), lanes_of(4), lanes_of(2), lanes_of(SIDE), lanes_of(feats)],
        whole((count, feats)),
        shape_of((count, feats)),
    )(gate, proj, params, stat, sums, weight)


def dot_nt(a, b):
    return lax.dot_general(a, b, (((1,), (1,)), ((), ())), preferred_element_type=jnp.float32)


def shallow_body(
    total, frames, sums_ref, gram_ref, params_ref, stat_ref, w_ref, m_ref,
    grad_ref, next_ref, new_ref, low_ref, held,
):
    feats, width = w_ref.shape
    centre, inverse, gain, _ = unit_terms(params_ref, stat_ref, total // frames, frames)
    weight = w_ref[...]
    held[...] = jnp.zeros_like(held)
    held[0:feats, 0:width] = weight
    high = gram_ref.shape[0]
    gram = jnp.concatenate(
        [gram_ref[:, k * LANE : (k + 1) * LANE] for k in range(SIDE // high)], axis=0
    )
    lane = lax.broadcasted_iota(jnp.int32, gram.shape, 1)
    x_sum = jnp.sum(jnp.where(lane == feats, gram, 0.0), axis=1, keepdims=True)
    raw = jnp.dot(
        gram[:, :SIDE],
        held[...].astype(jnp.bfloat16).astype(jnp.float32),
        precision=lax.Precision.HIGHEST,
        preferred_element_type=jnp.float32,
    )
    normed = (raw - x_sum * centre) * inverse
    bias = sums_ref[feats : feats + 1, :] * (1.0 / total)
    slope = sums_ref[feats + 1 : feats + 2, :] * (1.0 / total)
    grad = gain * inverse * (sums_ref[...] - x_sum * bias - normed * slope)
    grad = grad[:feats, :width]
    grad_ref[...] = grad
    following = MUON_BETA * m_ref[...] + grad
    next_ref[...] = following
    held[0:feats, 0:width] = following
    m = held[...]
    current = (m / (jnp.sqrt(jnp.sum(m * m)) + MUON_EPSILON)).astype(jnp.bfloat16)
    for repeat in range(NS_STEPS):
        gram = dot_nt(current, current).astype(jnp.bfloat16)
        square = jnp.dot(gram, gram, preferred_element_type=jnp.float32)
        mixing = (COEFF_B * gram.astype(jnp.float32) + COEFF_C * square).astype(jnp.bfloat16)
        current = (
            COEFF_A * current.astype(jnp.float32)
            + jnp.dot(mixing, current, preferred_element_type=jnp.float32)
        ).astype(jnp.bfloat16)
    new = MUON_KEEP * weight - MUON_RATE * current[:feats, :width].astype(jnp.float32)
    new_ref[...] = new
    low_ref[...] = new.astype(jnp.bfloat16)


def shallow_step(sums, gram, params, stat, weight, momentum, total, frames):
    padded = sums.shape[1]
    some = shape_of(weight.shape)
    return kernel_call(
        functools.partial(shallow_body, total, frames),
        (1,),
        [whole(value.shape) for value in (sums, gram, params, stat, weight, momentum)],
        [whole(weight.shape)] * 4,
        [some, some, some, shape_of(weight.shape, jnp.bfloat16)],
        [pltpu.VMEM((SIDE, padded), jnp.float32)],
    )(sums, gram, params, stat, weight, momentum)


def newton_body(window, tile, first_ref, start_ref, out_ref, m_ref, gram, mixing, sem):
    size = m_ref.shape[0]
    blocks = size // tile
    copy = pltpu.make_async_copy(start_ref, m_ref, sem)
    copy.start()
    copy.wait()

    def place(k):
        return slice(k * tile, (k + 1) * tile)

    squares = jnp.zeros((8, size), jnp.float32)
    for k in range(blocks):
        value = m_ref[place(k), :].astype(jnp.float32)
        squares = squares + jnp.sum((value * value).reshape(tile // 8, 8, size), axis=0)
    scale = 1.0 / (jnp.sqrt(jnp.sum(squares)) + MUON_EPSILON)
    square_scale = scale * scale

    def gram_block(i, j):
        part = dot_nt(m_ref[place(i), :], m_ref[place(j), :]) * square_scale
        gram[place(i), place(j)] = part.astype(jnp.bfloat16)
        if i != j:
            gram[place(j), place(i)] = part.T.astype(jnp.bfloat16)

    for i in range(blocks):
        for j in range(i, blocks):
            gram_block(i, j)
    for i in range(blocks):
        for j in range(i, blocks):
            part = dot_nt(gram[place(i), :], gram[place(j), :])
            part = COEFF_B * gram[place(i), place(j)].astype(jnp.float32) + COEFF_C * part
            mixing[place(i), place(j)] = part.astype(jnp.bfloat16)
            if i != j:
                mixing[place(j), place(i)] = part.T.astype(jnp.bfloat16)

    def taken(ref):
        return ref[pl.ds(pl.multiple_of(first_ref[0] * 16, 16), window), :]

    def times(value, ref):
        return jnp.dot(value.astype(jnp.bfloat16), ref[...], preferred_element_type=jnp.float32)

    def stepped(value):
        return COEFF_A * value + times(value, mixing)

    mixing_own = taken(mixing)
    gram_own = taken(gram).astype(jnp.float32)
    gram_own = stepped(COEFF_A * gram_own + times(mixing_own, gram))
    square_own = stepped(times(stepped(gram_own), gram))
    second_own = COEFF_B * gram_own + COEFF_C * square_own
    weights = COEFF_A * mixing_own.astype(jnp.float32) + stepped(second_own)
    result = COEFF_A * COEFF_A * taken(m_ref).astype(jnp.float32) + times(weights, m_ref)
    out_ref[...] = (scale * result).astype(jnp.bfloat16)


def newton_rows(start, first, window):
    size = start.shape[0]
    return kernel_call(
        functools.partial(newton_body, window, 256),
        (1,),
        [pl.BlockSpec(memory_space=pltpu.SMEM), pl.BlockSpec(memory_space=pl.ANY)],
        whole((window, size)),
        shape_of((window, size), jnp.bfloat16),
        [pltpu.VMEM((size, size), jnp.bfloat16)] * 3 + [pltpu.SemaphoreType.DMA],
    )(first, start)


def swap(value, bit):
    size = lax.axis_size("tm")
    return lax.ppermute(value, "tm", [(i, i ^ bit) for i in range(size)])


def steps_of(size):
    bits = []
    bit = 1
    while bit < size:
        bits.append(bit)
        bit *= 2
    return bits


def bit_of(bit):
    return jnp.where((lax.axis_index("tm") & bit) != 0, 1, 0)


class SumSpread:
    def __init__(self, value):
        self.value = value
        self.steps = []
        lanes = value.shape[1]
        cuts = []
        for bit in steps_of(lax.axis_size("tm")):
            if lanes // 2 % WIDE == 0:
                lanes //= 2
                self.steps.append((self.halve, bit))
                cuts.append(bit)
            else:
                self.steps.append((self.pair, bit))
        self.steps += [(self.join, bit) for bit in reversed(cuts)]

    def halve(self, bit):
        lanes = self.value.shape[1] // 2
        mine = lax.dynamic_slice_in_dim(self.value, bit_of(bit) * lanes, lanes, 1)
        away = lax.dynamic_slice_in_dim(self.value, (1 - bit_of(bit)) * lanes, lanes, 1)
        self.value = mine + swap(away, bit)

    def pair(self, bit):
        self.value = self.value + swap(self.value, bit)

    def join(self, bit):
        other = swap(self.value, bit)
        upper = bit_of(bit) == 1
        self.value = jnp.concatenate(
            [jnp.where(upper, other, self.value), jnp.where(upper, self.value, other)], axis=1
        )

    def step(self, times=1):
        for _ in range(times):
            if self.steps:
                action, bit = self.steps.pop(0)
                action(bit)


def tie(first, second):
    return lax.optimization_barrier((list(first), list(second)))


def side_bit():
    return lax.axis_size("tm") // 32


def orders_of(size):
    bits = [bit for bit in steps_of(size) if bit != side_bit()]
    return [bits[k * len(bits) // 3 :] + bits[: k * len(bits) // 3] for k in range(3)]


def index_bits(bits):
    return [bit if bit < side_bit() else bit // 2 for bit in bits]


class Scatter:
    def __init__(self, keeps, sends):
        self.orders = orders_of(lax.axis_size("tm"))
        self.current = list(keeps)
        self.received = [swap(send, side_bit()) for send in sends]

    def step(self, *waiting):
        sends = []
        for p, order in enumerate(self.orders):
            half = self.current[p].shape[0] // 2
            mine, away = [
                lax.dynamic_slice_in_dim(self.current[p], half * index, half).astype(jnp.float32)
                + lax.dynamic_slice_in_dim(self.received[p], half * index, half).astype(jnp.float32)
                for index in (bit_of(order[0]), 1 - bit_of(order[0]))
            ]
            self.current[p] = mine
            sends.append(away.astype(jnp.bfloat16))
        sends, waiting = tie(sends, waiting)
        self.received = [swap(send, order.pop(0)) for send, order in zip(sends, self.orders)]
        return waiting

    def join(self, *done):
        self.received, done = tie(self.received, done)
        return done

    def result(self):
        return [a + b.astype(jnp.float32) for a, b in zip(self.current, self.received)]


class Stats:
    def __init__(self, stat, count):
        self.stat = stat
        self.count = float(count)
        self.bits = steps_of(lax.axis_size("tm"))

    def step(self, times=1):
        for _ in range(min(times, len(self.bits))):
            stat = self.stat
            other = swap(stat, self.bits.pop(0))
            gap = stat[0:1] - other[0:1]
            mean = 0.5 * (stat[0:1] + other[0:1])
            square = (stat[1:2] + other[1:2]) + gap * gap * (0.5 * self.count)
            self.stat = jnp.concatenate([mean, square, 0.5 * (stat[2:] + other[2:])], axis=0)
            self.count *= 2


class Exchange:
    def __init__(self, flags, carries, sums=()):
        self.bits = steps_of(lax.axis_size("tm"))
        high, self.width = carries[0][0].shape
        rows = high * len(carries)
        flags = jnp.broadcast_to(jnp.tile(flags, len(carries))[:, None], (rows, LANE))
        ends = jnp.concatenate([ends for ends, _, _ in carries], axis=0)
        self.payload = jnp.concatenate([ends, flags, *sums], axis=1)
        self.power = jnp.concatenate(
            [jnp.broadcast_to(power, (high, self.width)) for _, power, _ in carries], axis=0
        )
        self.lane = lax.broadcasted_iota(jnp.int32, self.payload.shape, 1)
        self.high = high
        self.reverse = [reverse for _, _, reverse in carries]
        self.before = jnp.zeros_like(ends)
        self.before_keep = jnp.ones_like(ends)

    def step(self, times=1):
        for _ in range(min(times, len(self.bits))):
            self.one()

    def one(self):
        bit = self.bits.pop(0)
        width = self.width
        mine, other = self.payload, swap(self.payload, bit)
        upper = bit_of(bit)
        row = lax.broadcasted_iota(jnp.int32, (len(mine), 1), 0) // self.high
        turned = sum((row == k) * int(reverse) for k, reverse in enumerate(self.reverse))
        following = turned != upper
        other_total = other[:, :width]
        keep_mine, keep_other = mine[:, width : width + 1], other[:, width : width + 1]
        self.before = jnp.where(
            following, self.before_keep * other_total + self.before, self.before
        )
        self.before_keep = jnp.where(
            following, self.before_keep * keep_other * self.power, self.before_keep
        )
        power = jnp.pad(self.power, ((0, 0), (0, mine.shape[1] - width)))
        carried = jnp.where(
            following, keep_mine * power * other + mine, keep_other * power * mine + other
        )
        self.payload = jnp.where(
            self.lane < width,
            carried,
            jnp.where(self.lane < width + LANE, mine * other, mine + other),
        )
        self.power = self.power * self.power

    def arrived(self, k):
        return self.before[k * self.high : (k + 1) * self.high]

    def sums(self):
        return self.payload[:, self.width + LANE :]


class SumAll:
    def __init__(self, value):
        self.value = value
        self.bits = steps_of(lax.axis_size("tm"))

    def step(self, times=1):
        for _ in range(min(times, len(self.bits))):
            self.value = self.value + swap(self.value, self.bits.pop(0))


def in_order(value, bits, slots):
    count = len(bits)
    axes = [count - bit.bit_length() for bit in bits]
    shape = (2,) * count + (slots, value.shape[1])
    return value.reshape(shape).transpose(axes + [count, count + 1]).reshape(value.shape)


def pad_lanes(value, padded):
    gap = padded - value.shape[-1]
    return jnp.pad(value, [(0, 0)] * (value.ndim - 1) + [(0, gap)])


def flat_places(shard, width, padded):
    size = lax.axis_size("tm")
    members = size * LANE // padded
    slots = LANE // members
    return members, slots, slots * width - shard


def to_block(flat, width, padded):
    size, mine = lax.axis_size("tm"), lax.axis_index("tm")
    members, slots, excess = flat_places(flat.shape[0], width, padded)
    lacking = excess * (members - 1)
    pairs = [(i + 1, i) for i in range(size - 1) if (i + 1) % members]
    extra = lax.ppermute(flat[:lacking], "tm", pairs)
    tail = jnp.zeros((excess,), flat.dtype)
    held = jnp.concatenate([flat, extra, tail])
    return lax.dynamic_slice_in_dim(held, excess * (mine % members), slots * width).reshape(
        slots, width
    )


def from_block(block, shard, padded):
    width = block.shape[1]
    size, mine = lax.axis_size("tm"), lax.axis_index("tm")
    members, slots, excess = flat_places(shard, width, padded)
    lacking = excess * (members - 1)
    pairs = [(i, i + 1) for i in range(size - 1) if (i + 1) % members]
    flat = block.reshape(-1)
    extra = lax.ppermute(flat[slots * width - lacking :], "tm", pairs)
    held = jnp.concatenate([extra, flat])
    return lax.dynamic_slice_in_dim(held, lacking - excess * (mine % members), shard)


def own_window(shard, width, padded):
    mine = lax.axis_index("tm")
    members, _, _ = flat_places(shard, width, padded)
    window = 16
    for k in range(members):
        first = shard * k // width // 16 * 16
        last = -(-shard * (k + 1) // width)
        window = max(window, -(-(last - first) // 16) * 16)
    member = mine % members
    first = jnp.minimum(shard * member // width // 16 * 16, LANE - window)
    return window, LANE * (mine // members) + first, shard * member - first * width


def per_device(
    inputs,
    clip_start,
    shallow_weight,
    shallow_momentum,
    deep_weight,
    deep_momentum,
    unit_params,
    unit_first,
    unit_second,
    out_grad,
):
    devices = lax.axis_size("tm")
    rows, frames, feats = inputs.shape
    width = shallow_weight.shape[1]
    padded = -(-width // WIDE) * WIDE
    group = width // (padded // LANE)
    count = rows * frames
    keep_mask = (1 - clip_start).astype(jnp.float32)
    flags = jnp.min(keep_mask, axis=1)
    keep = jnp.broadcast_to(keep_mask.T.reshape(count, 1), (count, LANE))
    params = pad_lanes(unit_params, padded)
    rates = jnp.maximum(1.0 - jnp.exp(-params[:, 0:1]), DECAY_FLOOR)
    powers = rates
    for _ in range(frames.bit_length() - 1):
        powers = powers * powers

    deep_block = pad_lanes(to_block(deep_weight.astype(jnp.bfloat16), width, padded), padded)
    momentum_block = pad_lanes(to_block(deep_momentum, width, padded), padded)

    shares = [3 * padded // 8, 3 * padded // 8, padded // 4]
    parts = [(sum(shares[:p]), shares[p]) for p in range(3)]
    side = bit_of(side_bit()).astype(jnp.int32).reshape(1)
    chunks = padded // WIDE
    orders = orders_of(devices)
    x, proj_one, stat_one, gram = front(
        inputs.reshape(count, feats), shallow_weight, rows, frames
    )
    (deep_block,), (stat_one,) = tie([deep_block], [stat_one])
    deep_low = lax.all_gather(deep_block, "tm", axis=0, tiled=True)
    stats = Stats(stat_one, count)
    grad_rows = out_grad.reshape(count, width)
    delta = None
    for k in range(chunks):
        stats.step()
        delta = delta_two(k, delta, grad_rows, keep, params[1], rows, frames, padded)
        delta, (stats.stat,) = tie(delta, [stats.stat])
    delta_local, delta_end = delta
    stats.step(len(stats.bits))
    (stat_one,), (momentum_block,) = tie([stats.stat], [momentum_block])
    state_local, state_end = local_states(
        proj_one, keep, params[0], stat_one, rows, frames, devices
    )
    carries = Exchange(flags, [(state_end, powers[0], False), (delta_end, powers[1], True)])
    carries.step(len(carries.bits))
    state_in, delta_in = carries.arrived(0), carries.arrived(1)
    low_one, mean_one = low_one_of(
        state_local, state_in, keep, params[0], rows, frames, width, group
    )
    proj_two, stat_two = second_forward(low_one, deep_low)
    stats = Stats(jnp.concatenate([stat_two, mean_one], axis=0), count)
    stats.step(len(stats.bits))
    hidden = [None, None]
    sources = [(state_local, state_in, params[0]), None]

    def next_hidden(layer, places, waiting):
        states, start, layer_params = sources[layer]
        for k in places:
            (start,), waiting = tie([start], waiting)
            hidden[layer] = hidden_of(
                k, hidden[layer], states, start, keep, layer_params, rows, frames, width
            )
        hidden[layer], waiting = tie(hidden[layer], waiting)
        return waiting

    stat_two, mean_one = stats.stat[:2], stats.stat[2:]
    gate, sums_two = gate_two(
        proj_two, delta_local, delta_in, keep, params[1], stat_two, rows, frames, devices
    )
    sums = SumAll(sums_two)
    turned = None
    for k in range(chunks):
        sums.step()
        turned = turn(k, turned, low_one, mean_one)
        turned, (sums.value,) = tie(turned, [sums.value])
    sums.step(len(sums.bits))
    sums_two = sums.value
    slots = padded // devices
    weights = [index_bits(order) for order in orders]
    aligned = slots % 16 == 0
    grad_two, total_two, keeps, sends = deep_term(
        parts, weights if aligned else None, side, gate, proj_two, params[1], stat_two,
        sums_two, turned[0], rows, frames, devices,
    )
    if not aligned:
        keeps = [in_order(keep, order, slots) for keep, order in zip(keeps, weights)]
        sends = [in_order(send, order, slots) for send, order in zip(sends, weights)]
    scatter = Scatter(keeps, sends)
    back = back_one(grad_two, deep_low)
    (back,) = scatter.join(back)
    (back,) = scatter.step(back)
    back_local, back_end = delta_one(back, keep, params[0], rows, frames, width, group)
    second_local, second_end, second_decay = states_two(
        proj_two, delta_local, delta_in, keep, params[1], stat_two, rows, frames, devices
    )
    back_end, second_end = scatter.join(back_end, second_end)
    tall = 2 * rows
    back_end, second_end = scatter.step(back_end, second_end)
    carries = Exchange(
        flags,
        [(back_end, powers[0], True), (second_end, powers[1], False)],
        [total_two.reshape(tall, -1), gram],
    )
    carries.step(2)
    (carries.payload,) = next_hidden(0, range(chunks), [carries.payload])
    (carries.payload,) = scatter.join(carries.payload)
    while len(scatter.orders[0]) > 1:
        (carries.payload,) = scatter.step(carries.payload)
        carries.step()
        (carries.payload,) = scatter.join(carries.payload)
    (carries.payload,) = scatter.step(carries.payload)
    carries.step(len(carries.bits))
    carries.payload, carries.before = scatter.join(carries.payload, carries.before)
    back_in, second_in = carries.arrived(0), carries.arrived(1)
    sources[1] = (second_local, second_in, params[1])
    total_two = carries.sums()[:, : padded // tall].reshape(1, padded)
    gram = carries.sums()[:, padded // tall :]
    mine = lax.axis_index("tm")
    place = mine // (2 * side_bit()) * side_bit() + mine % side_bit()
    place = (side[0] * (devices // 2) + place) * slots
    mean_own = lax.dynamic_slice_in_dim(mean_one[0], place, slots)[:, None]
    grad_parts = [
        part + mean_own * total_two[:, first : first + lanes]
        for (first, lanes), part in zip(parts, scatter.result())
    ]
    grad_block = jnp.concatenate(grad_parts, axis=1)
    start_block = (MUON_BETA * momentum_block + grad_block).astype(jnp.bfloat16)
    (start_block,), (back_in,) = tie([start_block], [back_in])
    gathered = lax.all_gather(start_block, "tm", axis=0, tiled=True)
    gate_low, sums_one = gate_one(
        proj_one, state_local, state_in, back_local, back_in, keep, params[0], stat_one, x,
        rows, frames, devices, feats,
    )
    decay_two = jnp.sum(second_decay[:rows] + second_decay[rows:] * second_in, axis=0, keepdims=True)
    sums_one = sums_one + jnp.pad(decay_two, ((feats + 3, SIDE - feats - 4), (0, 0)))
    spread = SumSpread(sums_one)
    for k in range(chunks):
        spread.step()
        (spread.value,) = next_hidden(1, [k], [spread.value])
    spread.step(len(spread.steps))
    sums_one = spread.value
    (hidden_one,), (hidden_two,) = hidden
    shallow_grad, shallow_next, shallow_new, shallow_low = shallow_step(
        sums_one, gram, params[0], stat_one, shallow_weight, shallow_momentum,
        count * devices, count,
    )
    input_back = input_grad_of(
        gate_low, proj_one, params[0], stat_one, sums_one, shallow_weight, rows, frames, devices
    )
    input_grad = jnp.swapaxes(input_back.reshape(frames, rows, feats), 0, 1)

    (gathered,), (shallow_low, input_grad) = tie([gathered], [shallow_low, input_grad])
    shard = deep_weight.shape[0]
    window, first_row, offset = own_window(shard, width, padded)
    ortho = newton_rows(
        gathered, (first_row // 16).astype(jnp.int32).reshape(1), window
    )
    deep_ortho = lax.dynamic_slice_in_dim(ortho[:, :width].reshape(-1), offset, shard)
    deep_new = MUON_KEEP * deep_weight - MUON_RATE * deep_ortho.astype(jnp.float32)
    deep_grad = from_block(grad_block[:, :width], shard, padded)
    deep_next = MUON_BETA * deep_momentum + deep_grad

    unit_sums = sums_one[feats : feats + 4, :width]
    bias_gain_two = sums_two[:, :width]
    slope = jnp.where(
        1.0 - jnp.exp(-unit_params[:, 0]) > DECAY_FLOOR, jnp.exp(-unit_params[:, 0]), 0.0
    )
    unit_grad = jnp.stack(
        [
            jnp.stack([unit_sums[2] * slope[0], unit_sums[0], unit_sums[1], unit_sums[0]]),
            jnp.stack(
                [unit_sums[3] * slope[1], bias_gain_two[0], bias_gain_two[1], bias_gain_two[0]]
            ),
        ]
    )
    first_fix = 1.0 - FIRST_DECAY**STEP
    second_fix = 1.0 - SECOND_DECAY**STEP
    first_new = FIRST_DECAY * unit_first + (1.0 - FIRST_DECAY) * unit_grad
    second_new = SECOND_DECAY * unit_second + (1.0 - SECOND_DECAY) * unit_grad * unit_grad
    params_new = unit_params - ADAM_RATE * (first_new / first_fix) / (
        jnp.sqrt(second_new / second_fix) + ADAM_EPSILON
    )
    return (
        hidden_one.reshape(rows, frames, width),
        hidden_two.reshape(rows, frames, width),
        input_grad,
        shallow_grad,
        shallow_next,
        shallow_new,
        shallow_low,
        deep_grad,
        deep_next,
        deep_new,
        deep_new.astype(jnp.bfloat16),
        first_new,
        second_new,
        params_new,
    )


def solution(mesh):
    in_specs = (
        P(None, "tm", None),
        P(None, "tm"),
        P(),
        P(),
        P("tm"),
        P("tm"),
        P(),
        P(),
        P(),
        P(None, "tm", None),
    )
    out_specs = (
        P(None, "tm", None),
        P(None, "tm", None),
        P(None, "tm", None),
        P(),
        P(),
        P(),
        P(),
        P("tm"),
        P("tm"),
        P("tm"),
        P("tm"),
        P(),
        P(),
        P(),
    )
    return jax.shard_map(
        per_device, mesh=mesh, in_specs=in_specs, out_specs=out_specs, check_vma=False
    )
```

```python
import functools

import jax
import jax.numpy as jnp
from jax import lax
from jax.experimental import pallas as pl
from jax.experimental.pallas import tpu as pltpu
from jax.sharding import PartitionSpec as P

NS_STEPS = 2
STEP = 5


NORM_EPSILON = 1e-05
MUON_EPSILON = 1e-07
COEFF_A = 3.4445
COEFF_B = -4.775
COEFF_C = 2.0315
MUON_BETA = 0.5
MUON_RATE = 4.0
MUON_KEEP = 0.999
FIRST_DECAY = 0.9
SECOND_DECAY = 0.95
ADAM_RATE = 0.5
ADAM_EPSILON = 1e-08
DECAY_FLOOR = 0.9
LANE = 128
WIDE = 512
PART = 256
SIDE = 80


def kernel_call(body, grid, in_specs, out_specs, out_shape, scratch=(), flops=0, traffic=0):
    return pl.pallas_call(
        body,
        grid=grid,
        in_specs=in_specs,
        out_specs=out_specs,
        out_shape=out_shape,
        scratch_shapes=list(scratch),
        compiler_params=pltpu.CompilerParams(vmem_limit_bytes=56 * 1024 * 1024),
        cost_estimate=pl.CostEstimate(flops=flops, bytes_accessed=traffic, transcendentals=0),
    )


def shape_of(shape, dtype=jnp.float32):
    return jax.ShapeDtypeStruct(shape, dtype)


def whole(shape):
    return pl.BlockSpec(shape, lambda i: (0,) * len(shape))


def lanes_of(rows, width=WIDE):
    return pl.BlockSpec((rows, width), lambda i: (0, i))


def chunk_call(body, place, in_specs, out_specs, out_shape, arrays, previous, scratch=(), traffic=0):
    count = len(in_specs)
    before = list(previous) if previous is not None else []

    def run(*refs):
        body(*refs[:count], *refs[count + len(before) :])

    return pl.pallas_call(
        run,
        grid=(1,),
        in_specs=list(in_specs) + [pl.BlockSpec(memory_space=pl.ANY)] * len(before),
        out_specs=out_specs,
        out_shape=out_shape,
        scratch_shapes=list(scratch),
        input_output_aliases={count + k: k for k in range(len(before))},
        compiler_params=pltpu.CompilerParams(vmem_limit_bytes=56 * 1024 * 1024),
        cost_estimate=pl.CostEstimate(flops=0, bytes_accessed=traffic, transcendentals=0),
    )(*arrays, *before)


def chunk_at(rows, place):
    return pl.BlockSpec((rows, WIDE), lambda i: (0, place))


def rate_of(params):
    return jnp.maximum(1.0 - jnp.exp(-params[0:1]), DECAY_FLOOR)


def softened(value):
    return jnp.maximum(value, 0.0) + jnp.log(1.0 + jnp.exp(-jnp.abs(value)))


def sigmoid(value):
    return 0.5 * jnp.tanh(0.5 * value) + 0.5


def wide_keep(keep_ref, t, rows):
    keep = keep_ref[pl.ds(pl.multiple_of(t * rows, rows), rows), :]
    return jnp.concatenate([keep] * (WIDE // LANE), axis=1)


def rows_at(ref, t, rows):
    return ref[pl.ds(pl.multiple_of(t * rows, rows), rows), :]


def store_at(ref, t, rows, value):
    ref[pl.ds(pl.multiple_of(t * rows, rows), rows), :] = value


def valid_lanes(shape, total, step):
    return lax.broadcasted_iota(jnp.int32, shape, 1) + step * WIDE < total


def unit_terms(params_ref, stat_ref, total_devices, frames):
    params = params_ref[...]
    stat = stat_ref[...]
    centre = stat[0:1]
    inverse = lax.rsqrt(stat[1:2] / (total_devices * frames) + NORM_EPSILON)
    return centre, inverse, params[2:3], params[3:4] + params[1:2]


def front_body(rows, frames, width, x_ref, w_ref, xt_ref, proj_ref, stat_ref, gram_ref, padded_w):
    step = pl.program_id(0)
    count, feats = x_ref.shape

    @pl.when(step == 0)
    def _():
        i = lax.broadcasted_iota(jnp.int32, (count, count), 0)
        j = lax.broadcasted_iota(jnp.int32, (count, count), 1)
        move = (j == lax.rem(i, rows) * frames + lax.div(i, rows)).astype(jnp.bfloat16)
        moved = jnp.dot(move, x_ref[...], preferred_element_type=jnp.float32).astype(jnp.bfloat16)
        i = lax.broadcasted_iota(jnp.int32, (feats, LANE), 0)
        j = lax.broadcasted_iota(jnp.int32, (feats, LANE), 1)
        wide = jnp.dot(moved, (i == j).astype(jnp.bfloat16), preferred_element_type=jnp.float32)
        lane = lax.broadcasted_iota(jnp.int32, (count, LANE), 1)
        xt = jnp.where(lane == feats, 1.0, wide).astype(jnp.bfloat16)
        xt_ref[...] = xt
        gram = dot_tn(xt, xt)
        high = gram_ref.shape[0]
        for k in range(SIDE // high):
            gram_ref[:, k * LANE : (k + 1) * LANE] = gram[k * high : (k + 1) * high]
        padded_w[...] = jnp.zeros_like(padded_w)

    weight = w_ref[...]
    padded_w[0:feats, :] = jnp.where(valid_lanes(weight.shape, width, step), weight, 0.0)
    proj = jnp.dot(
        xt_ref[...], padded_w[...].astype(jnp.bfloat16), preferred_element_type=jnp.float32
    )
    proj_ref[...] = proj
    mean = jnp.sum(proj, axis=0, keepdims=True) * (1.0 / count)
    off = proj - mean
    stat_ref[0:1, :] = mean
    stat_ref[1:2, :] = jnp.sum(off * off, axis=0, keepdims=True)


def dot_tn(a, b):
    return lax.dot_general(a, b, (((0,), (0,)), ((), ())), preferred_element_type=jnp.float32)


def front(x, weight, rows, frames):
    count, feats = x.shape
    width = weight.shape[1]
    padded = -(-width // WIDE) * WIDE
    return kernel_call(
        functools.partial(front_body, rows, frames, width),
        (padded // WIDE,),
        [whole((count, feats)), lanes_of(feats)],
        [whole((count, LANE)), lanes_of(count), lanes_of(2), whole((2 * rows, SIDE // (2 * rows) * LANE))],
        [
            shape_of((count, LANE), jnp.bfloat16),
            shape_of((count, padded)),
            shape_of((2, padded)),
            shape_of((2 * rows, SIDE // (2 * rows) * LANE)),
        ],
        [pltpu.VMEM((LANE, WIDE), jnp.float32)],
    )(x, weight)


def delta_two_body(rows, frames, width, grad_ref, keep_ref, params_ref, delta_ref, end_ref, held):
    place = pl.program_id(0)
    pieces = WIDE // LANE
    mask = valid_lanes((rows * frames, WIDE), width, place)
    grad = jnp.where(mask, grad_ref[...].astype(jnp.float32), 0.0)
    for g in range(pieces):
        held[g] = grad[:, g * LANE : (g + 1) * LANE]
    rate = rate_of(params_ref[...])

    def body(k, carried):
        t = frames - 1 - k
        own = jnp.concatenate(
            [held[g, pl.ds(t, rows, stride=frames), :] for g in range(pieces)], axis=1
        )
        delta = own + carried
        store_at(delta_ref, t, rows, delta)
        return rate * wide_keep(keep_ref, t, rows) * delta

    end_ref[...] = lax.fori_loop(
        0, frames, body, jnp.zeros((rows, WIDE), jnp.float32), unroll=8
    )


def delta_two(out_grad, keep, params, rows, frames, padded):
    count, width = out_grad.shape
    return kernel_call(
        functools.partial(delta_two_body, rows, frames, width),
        (padded // WIDE,),
        [lanes_of(count), whole((count, LANE)), lanes_of(4)],
        [lanes_of(count), lanes_of(rows)],
        [shape_of((count, padded)), shape_of((rows, padded))],
        [pltpu.VMEM((WIDE // LANE, count, LANE), jnp.float32)],
    )(out_grad, keep, params)


def states_body(
    rows, frames, devices, proj_ref, keep_ref, params_ref, stat_ref, state_ref, end_ref
):
    centre, inverse, gain, offset = unit_terms(params_ref, stat_ref, devices, rows * frames)
    rate = rate_of(params_ref[...])
    share = 1.0 - rate

    def body(t, carried):
        gate = (rows_at(proj_ref, t, rows) - centre) * inverse * gain + offset
        soft = softened(gate)
        carried = rate * wide_keep(keep_ref, t, rows) * carried + share * soft
        store_at(state_ref, t, rows, carried)
        return carried

    end_ref[...] = lax.fori_loop(
        0, frames, body, jnp.zeros((rows, WIDE), jnp.float32), unroll=8
    )


def local_states(proj, keep, params, stat, rows, frames, devices):
    count, padded = proj.shape
    return kernel_call(
        functools.partial(states_body, rows, frames, devices),
        (padded // WIDE,),
        [lanes_of(count), whole((count, LANE)), lanes_of(4), lanes_of(2)],
        [lanes_of(count), lanes_of(rows)],
        [shape_of((count, padded)), shape_of((rows, padded))],
    )(proj, keep, params, stat)


def to_slots(value, group):
    pieces = value.shape[1] // LANE
    lane = lax.broadcasted_iota(jnp.int32, (value.shape[0], LANE), 1)
    parts = [value[:, g * LANE : (g + 1) * LANE] for g in range(pieces)]
    out = []
    for g in range(pieces):
        moved = (LANE - group) * g
        if moved == 0:
            new = parts[g]
        else:
            new = jnp.where(
                lane < moved, pltpu.roll(parts[g - 1], moved, 1), pltpu.roll(parts[g], moved, 1)
            )
        out.append(jnp.where(lane < group, new, 0.0))
    return jnp.concatenate(out, axis=1)


def from_slots(value, group, width):
    pieces = value.shape[1] // LANE
    lane = lax.broadcasted_iota(jnp.int32, (value.shape[0], LANE), 1)
    parts = [value[:, g * LANE : (g + 1) * LANE] for g in range(pieces)]
    out = []
    for j in range(pieces):
        moved = (LANE - group) * j
        new = parts[j] if moved == 0 else pltpu.roll(parts[j], LANE - moved, 1)
        if j + 1 < pieces:
            new = jnp.where(lane < group - moved, new, pltpu.roll(parts[j + 1], group - moved, 1))
        left = width - j * LANE
        out.append(new if left >= LANE else jnp.where(lane < left, new, 0.0))
    return jnp.concatenate(out, axis=1)


def low_one_body(rows, frames, width, group, state_ref, start_ref, keep_ref, params_ref, low_ref, mean_ref):
    pieces = state_ref.shape[1] // LANE
    rate = rate_of(params_ref[...])

    def advance(t, carried):
        keep = rows_at(keep_ref, t, rows)
        carried = rate * jnp.concatenate([keep] * pieces, axis=1) * carried
        return carried, rows_at(state_ref, t, rows) + carried

    def body(k, both):
        carried, total = both
        t = 2 * k
        carried, first = advance(t, carried)
        carried, second = advance(t + 1, carried)
        place = pl.ds(pl.multiple_of(t * rows, 2 * rows), 2 * rows)
        slots = to_slots(jnp.concatenate([first, second], axis=0), group)
        low_ref[place, :] = slots.astype(jnp.bfloat16)
        return carried, total + slots[:rows] + slots[rows:]

    start = start_ref[...]
    _, total = lax.fori_loop(0, frames // 2, body, (start, jnp.zeros_like(start)), unroll=2)
    mean_ref[...] = jnp.sum(total, axis=0, keepdims=True) * (1.0 / (rows * frames))


def low_one_of(states, start, keep, params, rows, frames, width, group):
    count, padded = states.shape
    return kernel_call(
        functools.partial(low_one_body, rows, frames, width, group),
        (1,),
        [whole((count, padded)), whole((rows, padded)), whole((count, LANE)), whole((4, padded))],
        [whole((count, padded)), whole((1, padded))],
        [shape_of((count, padded), jnp.bfloat16), shape_of((1, padded))],
    )(states, start, keep, params)


def hidden_body(rows, frames, state_ref, start_ref, keep_ref, params_ref, hidden_ref, held):
    pieces = WIDE // LANE
    rate = rate_of(params_ref[...])

    def body(t, carry):
        carry = rate * wide_keep(keep_ref, t, rows) * carry
        state = rows_at(state_ref, t, rows) + carry
        for g in range(pieces):
            held[g, pl.ds(pl.multiple_of(t * rows, rows), rows), :] = state[
                :, g * LANE : (g + 1) * LANE
            ]
        return carry

    lax.fori_loop(0, frames, body, start_ref[...], unroll=8)
    for r in range(rows):
        for g in range(pieces):
            hidden_ref[r * frames : (r + 1) * frames, g * LANE : (g + 1) * LANE] = held[
                g, pl.ds(r, frames, stride=rows), :
            ]


def hidden_of(place, previous, states, start, keep, params, rows, frames, width):
    count, _ = states.shape
    return chunk_call(
        functools.partial(hidden_body, rows, frames),
        place,
        [chunk_at(count, place), chunk_at(rows, place), whole((count, LANE)), chunk_at(4, place)],
        [chunk_at(count, place)],
        [shape_of((count, width))],
        (states, start, keep, params),
        previous,
        [pltpu.VMEM((WIDE // LANE, count, LANE), jnp.float32)],
    )


def second_body(low_ref, weight_ref, proj_ref, stat_ref):
    tile = 256
    count = proj_ref.shape[0]
    for j in range(0, WIDE, tile):
        place = slice(j, j + tile)
        for i in range(0, count, tile):
            proj_ref[i : i + tile, place] = jnp.dot(
                low_ref[i : i + tile, :], weight_ref[:, place], preferred_element_type=jnp.float32
            )
        proj = proj_ref[:, place]
        mean = jnp.sum(proj, axis=0, keepdims=True) * (1.0 / count)
        off = proj - mean
        stat_ref[0:1, place] = mean
        stat_ref[1:2, place] = jnp.sum(off * off, axis=0, keepdims=True)


def second_forward(low, weight):
    count, padded = low.shape
    return kernel_call(
        second_body,
        (padded // WIDE,),
        [whole((count, padded)), lanes_of(padded)],
        [lanes_of(count), lanes_of(2)],
        [shape_of((count, padded)), shape_of((2, padded))],
    )(low, weight)


def gate_two_body(
    rows, frames, devices, proj_ref, delta_ref, start_ref, keep_ref, params_ref, stat_ref, gate_ref, sums_ref
):
    centre, inverse, gain, offset = unit_terms(params_ref, stat_ref, devices, rows * frames)
    rate = rate_of(params_ref[...])
    share = 1.0 - rate
    none = jnp.zeros((rows, WIDE), jnp.float32)

    def body(k, carried):
        carry, bias_sum, gain_sum = carried
        t = frames - 1 - k
        delta = rows_at(delta_ref, t, rows) + carry
        normed = (rows_at(proj_ref, t, rows) - centre) * inverse
        gate = share * delta * sigmoid(normed * gain + offset)
        store_at(gate_ref, t, rows, gate)
        carry = rate * wide_keep(keep_ref, t, rows) * carry
        return carry, bias_sum + gate, gain_sum + gate * normed

    _, bias_sum, gain_sum = lax.fori_loop(
        0, frames, body, (start_ref[...], none, none), unroll=8
    )
    sums_ref[0:1, :] = jnp.sum(bias_sum, axis=0, keepdims=True)
    sums_ref[1:2, :] = jnp.sum(gain_sum, axis=0, keepdims=True)


def gate_two(proj, delta, start, keep, params, stat, rows, frames, devices):
    count, padded = proj.shape
    return kernel_call(
        functools.partial(gate_two_body, rows, frames, devices),
        (padded // WIDE,),
        [lanes_of(count), lanes_of(count), lanes_of(rows), whole((count, LANE)), lanes_of(4), lanes_of(2)],
        [lanes_of(count), lanes_of(2)],
        [shape_of((count, padded)), shape_of((2, padded))],
    )(proj, delta, start, keep, params, stat)


def states_two_body(
    rows, frames, devices, proj_ref, delta_ref, start_ref, keep_ref, params_ref, stat_ref,
    state_ref, end_ref, decay_ref, held,
):
    centre, inverse, gain, offset = unit_terms(params_ref, stat_ref, devices, rows * frames)
    rate = rate_of(params_ref[...])
    share = 1.0 - rate
    none = jnp.zeros((rows, WIDE), jnp.float32)

    def backward(k, carry):
        t = frames - 1 - k
        store_at(held, t, rows, rows_at(delta_ref, t, rows) + carry)
        return rate * wide_keep(keep_ref, t, rows) * carry

    lax.fori_loop(0, frames, backward, start_ref[...], unroll=8)

    def forward(t, carried):
        state, reach, decay, factor = carried
        keep = wide_keep(keep_ref, t, rows)
        delta = rows_at(held, t, rows)
        value = (rows_at(proj_ref, t, rows) - centre) * inverse * gain + offset
        soft = softened(value)
        decay = decay + delta * (keep * state - soft)
        factor = factor + delta * keep * reach
        state = rate * keep * state + share * soft
        reach = rate * keep * reach
        store_at(state_ref, t, rows, state)
        return state, reach, decay, factor

    state, _, decay, factor = lax.fori_loop(
        0, frames, forward, (none, jnp.ones_like(none), none, none), unroll=4
    )
    end_ref[...] = state
    decay_ref[0:rows, :] = decay
    decay_ref[rows : 2 * rows, :] = factor


def states_two(proj, delta, start, keep, params, stat, rows, frames, devices):
    count, padded = proj.shape
    return kernel_call(
        functools.partial(states_two_body, rows, frames, devices),
        (padded // WIDE,),
        [
            lanes_of(count),
            lanes_of(count),
            lanes_of(rows),
            whole((count, LANE)),
            lanes_of(4),
            lanes_of(2),
        ],
        [lanes_of(count), lanes_of(rows), lanes_of(2 * rows)],
        [shape_of((count, padded)), shape_of((rows, padded)), shape_of((2 * rows, padded))],
        [pltpu.VMEM((count, WIDE), jnp.float32)],
    )(proj, delta, start, keep, params, stat)


def turn_body(low_ref, mean_ref, turned_ref):
    half = LANE // 2
    turned = (low_ref[...].astype(jnp.float32) - mean_ref[...]).T.astype(jnp.bfloat16)
    for g in range(WIDE // LANE):
        for side in range(2):
            turned_ref[side, g * half : (g + 1) * half, :] = turned[
                g * LANE + side * half : g * LANE + (side + 1) * half
            ]


def turn(place, previous, low, mean):
    count, padded = low.shape
    return chunk_call(
        turn_body,
        place,
        [chunk_at(count, place), chunk_at(1, place)],
        [pl.BlockSpec((2, WIDE // 2, count), lambda i: (0, place, 0))],
        [shape_of((2, padded // 2, count), jnp.bfloat16)],
        (low, mean),
        previous,
    )


def deep_term_body(
    rows, frames, devices, parts, orders, side_ref, gate_ref, proj_ref, params_ref, stat_ref, sums_ref,
    turned_ref, grad_ref, total_ref, *outs,
):
    step = pl.program_id(0)
    total = devices * rows * frames
    centre, inverse, gain, _ = unit_terms(params_ref, stat_ref, devices, rows * frames)
    sums = sums_ref[...] * (1.0 / total)
    normed = (proj_ref[...] - centre) * inverse
    grad = (gain * inverse * (gate_ref[...] - sums[0:1] - normed * sums[1:2])).astype(jnp.bfloat16)
    grad_ref[...] = grad
    total_ref[...] = jnp.sum(grad.astype(jnp.float32), axis=0, keepdims=True)
    side = side_ref[0]
    half = turned_ref.shape[1]
    tile = 256
    for p, (first, lanes) in enumerate(parts):

        @pl.when((step >= first // PART) & (step < (first + lanes) // PART))
        def _():
            for which, out_ref in ((side, outs[p]), (1 - side, outs[len(parts) + p])):
                for k in range(half // tile):
                    part = jnp.dot(
                        turned_ref[which, k * tile : (k + 1) * tile, :],
                        grad_ref[...],
                        preferred_element_type=jnp.float32,
                    ).astype(out_ref.dtype)
                    if orders is None:
                        out_ref[k * tile : (k + 1) * tile, :] = part
                        continue
                    slots = half // 2 ** len(orders[p])
                    for b in range(tile // slots):
                        block = k * (tile // slots) + b
                        place = 0
                        for weight in orders[p]:
                            place = 2 * place + block // weight % 2
                        out_ref[place * slots : (place + 1) * slots, :] = part[
                            b * slots : (b + 1) * slots
                        ]


def deep_term(parts, orders, side, gate, proj, params, stat, sums, turned, rows, frames, devices):
    count, padded = proj.shape
    half = padded // 2

    def some(first, lanes):
        return pl.BlockSpec(
            (half, PART), lambda i: (0, jnp.clip(i - first // PART, 0, lanes // PART - 1))
        )

    found = kernel_call(
        functools.partial(deep_term_body, rows, frames, devices, parts, orders),
        (padded // PART,),
        [
            pl.BlockSpec(memory_space=pltpu.SMEM),
            lanes_of(count, PART),
            lanes_of(count, PART),
            lanes_of(4, PART),
            lanes_of(2, PART),
            lanes_of(2, PART),
            whole((2, half, count)),
        ],
        [lanes_of(count, PART), lanes_of(1, PART)] + [some(*part) for part in parts] * 2,
        [shape_of((count, padded), jnp.bfloat16), shape_of((1, padded))]
        + [shape_of((half, lanes), jnp.bfloat16) for _, lanes in parts] * 2,
    )(side, gate, proj, params, stat, sums, turned)
    return found[0], found[1], found[2 : 2 + len(parts)], found[2 + len(parts) :]


def back_body(grad_ref, weight_ref, back_ref):
    back_ref[...] = dot_nt(grad_ref[...], weight_ref[...])


def back_one(grad, weight):
    count, padded = grad.shape
    return kernel_call(
        back_body,
        (padded // WIDE,),
        [whole((count, padded)), pl.BlockSpec((WIDE, padded), lambda i: (i, 0))],
        lanes_of(count),
        shape_of((count, padded)),
    )(grad, weight)


def delta_one_body(rows, frames, width, group, back_ref, keep_ref, params_ref, delta_ref, end_ref):
    pieces = back_ref.shape[1] // LANE
    rate = rate_of(params_ref[...])

    def body(k, carried):
        t = frames - 1 - k
        delta = from_slots(rows_at(back_ref, t, rows), group, width) + carried
        store_at(delta_ref, t, rows, delta)
        keep = rows_at(keep_ref, t, rows)
        return rate * jnp.concatenate([keep] * pieces, axis=1) * delta

    end_ref[...] = lax.fori_loop(
        0, frames, body, jnp.zeros((rows, back_ref.shape[1]), jnp.float32), unroll=2
    )


def delta_one(back, keep, params, rows, frames, width, group):
    count, padded = back.shape
    return kernel_call(
        functools.partial(delta_one_body, rows, frames, width, group),
        (1,),
        [whole((count, padded)), whole((count, LANE)), whole((4, padded))],
        [whole((count, padded)), whole((rows, padded))],
        [shape_of((count, padded)), shape_of((rows, padded))],
    )(back, keep, params)


def gate_one_body(
    rows,
    frames,
    devices,
    feats,
    width,
    proj_ref,
    state_ref,
    first_ref,
    delta_ref,
    start_ref,
    keep_ref,
    params_ref,
    stat_ref,
    x_ref,
    w_ref,
    sums_ref,
    back_ref,
    mean_ref,
    held,
    gate_ref,
    padded_w,
):
    step = pl.program_id(0)
    centre, inverse, gain, offset = unit_terms(params_ref, stat_ref, devices, rows * frames)
    rate = rate_of(params_ref[...])
    share = 1.0 - rate
    none = jnp.zeros((rows, WIDE), jnp.float32)

    def backward(k, carry):
        t = frames - 1 - k
        store_at(held, t, rows, rows_at(delta_ref, t, rows) + carry)
        return rate * wide_keep(keep_ref, t, rows) * carry

    lax.fori_loop(0, frames, backward, start_ref[...], unroll=8)

    def forward(t, carried):
        carry, before, bias_sum, gain_sum, decay_sum = carried
        keep = wide_keep(keep_ref, t, rows)
        delta = rows_at(held, t, rows)
        normed = (rows_at(proj_ref, t, rows) - centre) * inverse
        value = normed * gain + offset
        soft = softened(value)
        gate = share * delta * sigmoid(value)
        store_at(gate_ref, t, rows, gate)
        decay_sum = decay_sum + delta * (keep * before - soft)
        carry = rate * keep * carry
        before = rows_at(state_ref, t, rows) + carry
        return carry, before, bias_sum + gate, gain_sum + gate * normed, decay_sum

    first = first_ref[...]
    _, _, bias_sum, gain_sum, decay_sum = lax.fori_loop(
        0, frames, forward, (first, first, none, none, none), unroll=4
    )
    bias = jnp.sum(bias_sum, axis=0, keepdims=True)
    mean = bias * (1.0 / (rows * frames))
    x = x_ref[...]
    ones = jnp.ones((rows * frames, LANE), jnp.bfloat16)
    total = jnp.concatenate([dot_tn(x, ones)] * (WIDE // LANE), axis=1)
    centred = gate_ref[...] - mean
    term = dot_tn(x, centred.astype(jnp.bfloat16)) + total * mean
    sums_ref[...] = term[: sums_ref.shape[0]]
    sums_ref[feats : feats + 1, :] = bias
    sums_ref[feats + 1 : feats + 2, :] = jnp.sum(gain_sum, axis=0, keepdims=True)
    sums_ref[feats + 2 : feats + 3, :] = jnp.sum(decay_sum, axis=0, keepdims=True)
    mean_ref[...] = mean
    weight = w_ref[...]
    padded_w[...] = jnp.zeros_like(padded_w)
    padded_w[0:feats, :] = jnp.where(valid_lanes(weight.shape, width, step), weight, 0.0)
    part = dot_nt(
        (gain * inverse * centred).astype(jnp.bfloat16), padded_w[...].astype(jnp.bfloat16)
    )

    @pl.when(step == 0)
    def _():
        back_ref[...] = part

    @pl.when(step > 0)
    def _():
        back_ref[...] += part


def gate_one(proj, states, first, delta, start, keep, params, stat, x, weight, rows, frames, devices):
    count, padded = proj.shape
    feats, width = weight.shape
    return kernel_call(
        functools.partial(gate_one_body, rows, frames, devices, feats, width),
        (padded // WIDE,),
        [
            lanes_of(count),
            lanes_of(count),
            lanes_of(rows),
            lanes_of(count),
            lanes_of(rows),
            whole((count, LANE)),
            lanes_of(4),
            lanes_of(2),
            whole((count, LANE)),
            lanes_of(feats),
        ],
        [lanes_of(SIDE), whole((count, LANE)), lanes_of(1)],
        [shape_of((SIDE, padded)), shape_of((count, LANE)), shape_of((1, padded))],
        [
            pltpu.VMEM((count, WIDE), jnp.float32),
            pltpu.VMEM((count, WIDE), jnp.float32),
            pltpu.VMEM((LANE, WIDE), jnp.float32),
        ],
    )(proj, states, first, delta, start, keep, params, stat, x, weight)


def dot_nt(a, b):
    return lax.dot_general(a, b, (((1,), (1,)), ((), ())), preferred_element_type=jnp.float32)


def shallow_body(
    total, rows, frames, sums_ref, gram_ref, params_ref, stat_ref, w_ref, m_ref, x_ref, back_ref, mean_ref,
    grad_ref, next_ref, new_ref, low_ref, input_ref, held, moved,
):
    feats, width = w_ref.shape
    count = rows * frames
    centre, inverse, gain, _ = unit_terms(params_ref, stat_ref, total // count, count)
    weight = w_ref[...]
    held[...] = jnp.zeros_like(held)
    held[0:feats, 0:width] = weight
    low = held[...].astype(jnp.bfloat16).astype(jnp.float32)
    high = gram_ref.shape[0]
    gram = jnp.concatenate(
        [gram_ref[:, k * LANE : (k + 1) * LANE] for k in range(SIDE // high)], axis=0
    )
    lane = lax.broadcasted_iota(jnp.int32, gram.shape, 1)
    x_sum = jnp.sum(jnp.where(lane == feats, gram, 0.0), axis=1, keepdims=True)
    raw = jnp.dot(
        gram, low, precision=lax.Precision.HIGHEST, preferred_element_type=jnp.float32
    )
    normed = (raw - x_sum * centre) * inverse
    bias = sums_ref[feats : feats + 1, :] * (1.0 / total)
    slope = sums_ref[feats + 1 : feats + 2, :] * (1.0 / total)
    scaled = gain * inverse
    grad = scaled * (sums_ref[...] - x_sum * bias - normed * slope)
    grad = grad[:feats, :width]
    grad_ref[...] = grad

    row = lax.broadcasted_iota(jnp.int32, low.shape, 0)
    turn = slope * inverse
    left = jnp.where(
        row == feats, scaled * (mean_ref[...] - bias + turn * centre), -low * (scaled * turn)
    )
    matrix = lax.dot_general(
        left, low, (((1,), (1,)), ((), ())),
        precision=lax.Precision.HIGHEST, preferred_element_type=jnp.float32,
    )
    moved[...] = back_ref[...] + jnp.dot(
        x_ref[...].astype(jnp.float32), matrix,
        precision=lax.Precision.HIGHEST, preferred_element_type=jnp.float32,
    )
    for r in range(rows):
        input_ref[r * frames : (r + 1) * frames, :] = moved[pl.ds(r, frames, stride=rows), :][:, :feats]

    following = MUON_BETA * m_ref[...] + grad
    next_ref[...] = following
    held[0:feats, 0:width] = following
    m = held[0:SIDE, :]
    current = (m / (jnp.sqrt(jnp.sum(m * m)) + MUON_EPSILON)).astype(jnp.bfloat16)
    for repeat in range(NS_STEPS):
        gram = dot_nt(current, current).astype(jnp.bfloat16)
        square = jnp.dot(gram, gram, preferred_element_type=jnp.float32)
        mixing = (COEFF_B * gram.astype(jnp.float32) + COEFF_C * square).astype(jnp.bfloat16)
        current = (
            COEFF_A * current.astype(jnp.float32)
            + jnp.dot(mixing, current, preferred_element_type=jnp.float32)
        ).astype(jnp.bfloat16)
    new = MUON_KEEP * weight - MUON_RATE * current[:feats, :width].astype(jnp.float32)
    new_ref[...] = new
    low_ref[...] = new.astype(jnp.bfloat16)


def shallow_step(sums, gram, params, stat, weight, momentum, x, back, mean, total, rows, frames):
    padded = sums.shape[1]
    some = shape_of(weight.shape)
    feats = weight.shape[0]
    arrays = (sums, gram, params, stat, weight, momentum, x, back, mean)
    return kernel_call(
        functools.partial(shallow_body, total, rows, frames),
        (1,),
        [whole(value.shape) for value in arrays],
        [whole(weight.shape)] * 4 + [whole((rows * frames, feats))],
        [some, some, some, shape_of(weight.shape, jnp.bfloat16), shape_of((rows * frames, feats))],
        [pltpu.VMEM((LANE, padded), jnp.float32), pltpu.VMEM((rows * frames, LANE), jnp.float32)],
    )(*arrays)


def newton_body(window, tile, first_ref, scale_ref, start_ref, out_ref, m_ref, gram, mixing, sems):
    size = m_ref.shape[0]
    blocks = size // tile

    def place(k):
        return slice(k * tile, (k + 1) * tile)

    copies = [
        pltpu.make_async_copy(start_ref.at[place(k), :], m_ref.at[place(k), :], sems.at[k])
        for k in range(blocks)
    ]
    for copy in copies:
        copy.start()
    scale = scale_ref[0]
    square_scale = scale * scale
    for j in range(blocks):
        copies[j].wait()
        for i in range(j + 1):
            part = dot_nt(m_ref[place(i), :], m_ref[place(j), :]) * square_scale
            gram[place(i), place(j)] = part.astype(jnp.bfloat16)
            if i != j:
                gram[place(j), place(i)] = part.T.astype(jnp.bfloat16)
    for i in range(blocks):
        for j in range(i, blocks):
            part = dot_nt(gram[place(i), :], gram[place(j), :])
            part = COEFF_B * gram[place(i), place(j)].astype(jnp.float32) + COEFF_C * part
            mixing[place(i), place(j)] = part.astype(jnp.bfloat16)
            if i != j:
                mixing[place(j), place(i)] = part.T.astype(jnp.bfloat16)

    def taken(ref):
        return ref[pl.ds(pl.multiple_of(first_ref[0] * 16, 16), window), :]

    def times(value, ref):
        return jnp.dot(value.astype(jnp.bfloat16), ref[...], preferred_element_type=jnp.float32)

    def stepped(value):
        return COEFF_A * value + times(value, mixing)

    mixing_own = taken(mixing)
    gram_own = taken(gram).astype(jnp.float32)
    gram_own = stepped(COEFF_A * gram_own + times(mixing_own, gram))
    square_own = stepped(times(stepped(gram_own), gram))
    second_own = COEFF_B * gram_own + COEFF_C * square_own
    weights = COEFF_A * mixing_own.astype(jnp.float32) + stepped(second_own)
    result = COEFF_A * COEFF_A * taken(m_ref).astype(jnp.float32) + times(weights, m_ref)
    out_ref[...] = (scale * result).astype(jnp.bfloat16)


def newton_rows(start, scale, first, window):
    size = start.shape[0]
    tile = 256
    scalar = pl.BlockSpec(memory_space=pltpu.SMEM)
    return kernel_call(
        functools.partial(newton_body, window, tile),
        (1,),
        [scalar, scalar, pl.BlockSpec(memory_space=pl.ANY)],
        whole((window, size)),
        shape_of((window, size), jnp.bfloat16),
        [pltpu.VMEM((size, size), jnp.bfloat16)] * 3 + [pltpu.SemaphoreType.DMA((size // tile,))],
    )(first, scale, start)


def swap(value, bit):
    size = lax.axis_size("tm")
    return lax.ppermute(value, "tm", [(i, i ^ bit) for i in range(size)])


def steps_of(size):
    bits = []
    bit = 1
    while bit < size:
        bits.append(bit)
        bit *= 2
    return bits


def bit_of(bit):
    return jnp.where((lax.axis_index("tm") & bit) != 0, 1, 0)


class SumSpread:
    def __init__(self, value):
        self.value = value
        self.steps = []
        lanes = value.shape[1]
        cuts = []
        for bit in steps_of(lax.axis_size("tm")):
            if lanes // 2 % WIDE == 0:
                lanes //= 2
                self.steps.append((self.halve, bit))
                cuts.append(bit)
            else:
                self.steps.append((self.pair, bit))
        self.steps += [(self.join, bit) for bit in reversed(cuts)]

    def halve(self, bit):
        lanes = self.value.shape[1] // 2
        mine = lax.dynamic_slice_in_dim(self.value, bit_of(bit) * lanes, lanes, 1)
        away = lax.dynamic_slice_in_dim(self.value, (1 - bit_of(bit)) * lanes, lanes, 1)
        self.value = mine + swap(away, bit)

    def pair(self, bit):
        self.value = self.value + swap(self.value, bit)

    def join(self, bit):
        other = swap(self.value, bit)
        upper = bit_of(bit) == 1
        self.value = jnp.concatenate(
            [jnp.where(upper, other, self.value), jnp.where(upper, self.value, other)], axis=1
        )

    def step(self, times=1):
        for _ in range(times):
            if self.steps:
                action, bit = self.steps.pop(0)
                action(bit)


def tie(first, second):
    return lax.optimization_barrier((list(first), list(second)))


def side_bit():
    return lax.axis_size("tm") // 32


def orders_of(size):
    bits = [bit for bit in steps_of(size) if bit != side_bit()]
    return [bits[k * len(bits) // 3 :] + bits[: k * len(bits) // 3] for k in range(3)]


def index_bits(bits):
    return [bit if bit < side_bit() else bit // 2 for bit in bits]


class Scatter:
    def __init__(self, keeps, sends):
        self.orders = orders_of(lax.axis_size("tm"))
        self.current = list(keeps)
        self.received = [swap(send, side_bit()) for send in sends]

    def step(self, *waiting):
        sends = []
        for p, order in enumerate(self.orders):
            half = self.current[p].shape[0] // 2
            mine, away = [
                lax.dynamic_slice_in_dim(self.current[p], half * index, half).astype(jnp.float32)
                + lax.dynamic_slice_in_dim(self.received[p], half * index, half).astype(jnp.float32)
                for index in (bit_of(order[0]), 1 - bit_of(order[0]))
            ]
            self.current[p] = mine
            sends.append(away.astype(jnp.bfloat16))
        sends, waiting = tie(sends, waiting)
        self.received = [swap(send, order.pop(0)) for send, order in zip(sends, self.orders)]
        return waiting

    def join(self, *done):
        self.received, done = tie(self.received, done)
        return done

    def result(self):
        return [a + b.astype(jnp.float32) for a, b in zip(self.current, self.received)]


class Stats:
    def __init__(self, stat, count):
        self.stat = stat
        self.count = float(count)
        self.bits = steps_of(lax.axis_size("tm"))

    def step(self, times=1):
        for _ in range(min(times, len(self.bits))):
            stat = self.stat
            other = swap(stat, self.bits.pop(0))
            gap = stat[0:1] - other[0:1]
            mean = 0.5 * (stat[0:1] + other[0:1])
            square = (stat[1:2] + other[1:2]) + gap * gap * (0.5 * self.count)
            self.stat = jnp.concatenate([mean, square, 0.5 * (stat[2:] + other[2:])], axis=0)
            self.count *= 2


class Exchange:
    def __init__(self, flags, carries, sums=()):
        self.bits = steps_of(lax.axis_size("tm"))
        high, self.width = carries[0][0].shape
        rows = high * len(carries)
        flags = jnp.broadcast_to(jnp.tile(flags, len(carries))[:, None], (rows, LANE))
        ends = jnp.concatenate([ends for ends, _, _ in carries], axis=0)
        self.payload = jnp.concatenate([ends, flags, *sums], axis=1)
        self.power = jnp.concatenate(
            [jnp.broadcast_to(power, (high, self.width)) for _, power, _ in carries], axis=0
        )
        self.lane = lax.broadcasted_iota(jnp.int32, self.payload.shape, 1)
        self.high = high
        self.reverse = [reverse for _, _, reverse in carries]
        self.before = jnp.zeros_like(ends)
        self.before_keep = jnp.ones_like(ends)

    def step(self, times=1):
        for _ in range(min(times, len(self.bits))):
            self.one()

    def one(self):
        bit = self.bits.pop(0)
        width = self.width
        mine, other = self.payload, swap(self.payload, bit)
        upper = bit_of(bit)
        row = lax.broadcasted_iota(jnp.int32, (len(mine), 1), 0) // self.high
        turned = sum((row == k) * int(reverse) for k, reverse in enumerate(self.reverse))
        following = turned != upper
        other_total = other[:, :width]
        keep_mine, keep_other = mine[:, width : width + 1], other[:, width : width + 1]
        self.before = jnp.where(
            following, self.before_keep * other_total + self.before, self.before
        )
        self.before_keep = jnp.where(
            following, self.before_keep * keep_other * self.power, self.before_keep
        )
        power = jnp.pad(self.power, ((0, 0), (0, mine.shape[1] - width)))
        carried = jnp.where(
            following, keep_mine * power * other + mine, keep_other * power * mine + other
        )
        self.payload = jnp.where(
            self.lane < width,
            carried,
            jnp.where(self.lane < width + LANE, mine * other, mine + other),
        )
        self.power = self.power * self.power

    def arrived(self, k):
        return self.before[k * self.high : (k + 1) * self.high]

    def sums(self):
        return self.payload[:, self.width + LANE :]


class SumAll:
    def __init__(self, value):
        self.value = value
        self.bits = steps_of(lax.axis_size("tm"))

    def step(self, times=1):
        for _ in range(min(times, len(self.bits))):
            self.value = self.value + swap(self.value, self.bits.pop(0))


def in_order(value, bits, slots):
    count = len(bits)
    axes = [count - bit.bit_length() for bit in bits]
    shape = (2,) * count + (slots, value.shape[1])
    return value.reshape(shape).transpose(axes + [count, count + 1]).reshape(value.shape)


def pad_lanes(value, padded):
    gap = padded - value.shape[-1]
    return jnp.pad(value, [(0, 0)] * (value.ndim - 1) + [(0, gap)])


def flat_places(shard, width, padded):
    size = lax.axis_size("tm")
    members = size * LANE // padded
    slots = LANE // members
    return members, slots, slots * width - shard


def to_block(flat, width, padded):
    size, mine = lax.axis_size("tm"), lax.axis_index("tm")
    members, slots, excess = flat_places(flat.shape[0], width, padded)
    lacking = excess * (members - 1)
    pairs = [(i + 1, i) for i in range(size - 1) if (i + 1) % members]
    extra = lax.ppermute(flat[:lacking], "tm", pairs)
    tail = jnp.zeros((excess,), flat.dtype)
    held = jnp.concatenate([flat, extra, tail])
    return lax.dynamic_slice_in_dim(held, excess * (mine % members), slots * width).reshape(
        slots, width
    )


def from_block(block, shard, padded):
    width = block.shape[1]
    size, mine = lax.axis_size("tm"), lax.axis_index("tm")
    members, slots, excess = flat_places(shard, width, padded)
    lacking = excess * (members - 1)
    pairs = [(i, i + 1) for i in range(size - 1) if (i + 1) % members]
    flat = block.reshape(-1)
    extra = lax.ppermute(flat[slots * width - lacking :], "tm", pairs)
    held = jnp.concatenate([extra, flat])
    return lax.dynamic_slice_in_dim(held, lacking - excess * (mine % members), shard)


def own_window(shard, width, padded):
    mine = lax.axis_index("tm")
    members, _, _ = flat_places(shard, width, padded)
    window = 16
    for k in range(members):
        first = shard * k // width // 16 * 16
        last = -(-shard * (k + 1) // width)
        window = max(window, -(-(last - first) // 16) * 16)
    member = mine % members
    first = jnp.minimum(shard * member // width // 16 * 16, LANE - window)
    return window, LANE * (mine // members) + first, shard * member - first * width


def per_device(
    inputs,
    clip_start,
    shallow_weight,
    shallow_momentum,
    deep_weight,
    deep_momentum,
    unit_params,
    unit_first,
    unit_second,
    out_grad,
):
    devices = lax.axis_size("tm")
    rows, frames, feats = inputs.shape
    width = shallow_weight.shape[1]
    padded = -(-width // WIDE) * WIDE
    group = width // (padded // LANE)
    count = rows * frames
    keep_mask = (1 - clip_start).astype(jnp.float32)
    flags = jnp.min(keep_mask, axis=1)
    keep = jnp.broadcast_to(keep_mask.T.reshape(count, 1), (count, LANE))
    params = pad_lanes(unit_params, padded)
    rates = jnp.maximum(1.0 - jnp.exp(-params[:, 0:1]), DECAY_FLOOR)
    powers = rates
    for _ in range(frames.bit_length() - 1):
        powers = powers * powers

    deep_block = pad_lanes(to_block(deep_weight.astype(jnp.bfloat16), width, padded), padded)
    momentum_block = pad_lanes(to_block(deep_momentum, width, padded), padded)

    shares = [3 * padded // 8, 3 * padded // 8, padded // 4]
    parts = [(sum(shares[:p]), shares[p]) for p in range(3)]
    side = bit_of(side_bit()).astype(jnp.int32).reshape(1)
    chunks = padded // WIDE
    orders = orders_of(devices)
    x, proj_one, stat_one, gram = front(
        inputs.reshape(count, feats), shallow_weight, rows, frames
    )
    (deep_block,), (stat_one,) = tie([deep_block], [stat_one])
    deep_low = lax.all_gather(deep_block, "tm", axis=0, tiled=True)
    stats = Stats(stat_one, count)
    stats.step()
    delta_local, delta_end = delta_two(
        out_grad.reshape(count, width), keep, params[1], rows, frames, padded
    )
    (delta_local, delta_end), (stats.stat,) = tie([delta_local, delta_end], [stats.stat])
    stats.step(len(stats.bits))
    (stat_one,), (momentum_block,) = tie([stats.stat], [momentum_block])
    state_local, state_end = local_states(
        proj_one, keep, params[0], stat_one, rows, frames, devices
    )
    carries = Exchange(flags, [(state_end, powers[0], False), (delta_end, powers[1], True)])
    carries.step(len(carries.bits))
    state_in, delta_in = carries.arrived(0), carries.arrived(1)
    low_one, mean_one = low_one_of(
        state_local, state_in, keep, params[0], rows, frames, width, group
    )
    proj_two, stat_two = second_forward(low_one, deep_low)
    stats = Stats(jnp.concatenate([stat_two, mean_one], axis=0), count)
    stats.step(len(stats.bits))
    hidden = [None, None]
    sources = [(state_local, state_in, params[0]), None]

    def next_hidden(layer, places, waiting):
        states, start, layer_params = sources[layer]
        for k in places:
            (start,), waiting = tie([start], waiting)
            hidden[layer] = hidden_of(
                k, hidden[layer], states, start, keep, layer_params, rows, frames, width
            )
        hidden[layer], waiting = tie(hidden[layer], waiting)
        return waiting

    stat_two, mean_one = stats.stat[:2], stats.stat[2:]
    gate, sums_two = gate_two(
        proj_two, delta_local, delta_in, keep, params[1], stat_two, rows, frames, devices
    )
    sums = SumAll(sums_two)
    turned = None
    for k in range(chunks):
        sums.step()
        turned = turn(k, turned, low_one, mean_one)
        turned, (sums.value,) = tie(turned, [sums.value])
    sums.step(len(sums.bits))
    sums_two = sums.value
    slots = padded // devices
    weights = [index_bits(order) for order in orders]
    aligned = slots % 16 == 0
    grad_two, total_two, keeps, sends = deep_term(
        parts, weights if aligned else None, side, gate, proj_two, params[1], stat_two,
        sums_two, turned[0], rows, frames, devices,
    )
    if not aligned:
        keeps = [in_order(keep, order, slots) for keep, order in zip(keeps, weights)]
        sends = [in_order(send, order, slots) for send, order in zip(sends, weights)]
    scatter = Scatter(keeps, sends)
    back = back_one(grad_two, deep_low)
    (back,) = scatter.join(back)
    (back,) = scatter.step(back)
    back_local, back_end = delta_one(back, keep, params[0], rows, frames, width, group)
    second_local, second_end, second_decay = states_two(
        proj_two, delta_local, delta_in, keep, params[1], stat_two, rows, frames, devices
    )
    back_end, second_end = scatter.join(back_end, second_end)
    tall = 2 * rows
    back_end, second_end = scatter.step(back_end, second_end)
    carries = Exchange(
        flags,
        [(back_end, powers[0], True), (second_end, powers[1], False)],
        [total_two.reshape(tall, -1), gram],
    )
    carries.step(2)
    (carries.payload,) = next_hidden(0, range(chunks), [carries.payload])
    (carries.payload,) = scatter.join(carries.payload)
    while len(scatter.orders[0]) > 1:
        (carries.payload,) = scatter.step(carries.payload)
        carries.step()
        (carries.payload,) = scatter.join(carries.payload)
    (carries.payload,) = scatter.step(carries.payload)
    carries.step(len(carries.bits))
    carries.payload, carries.before = scatter.join(carries.payload, carries.before)
    back_in, second_in = carries.arrived(0), carries.arrived(1)
    sources[1] = (second_local, second_in, params[1])
    total_two = carries.sums()[:, : padded // tall].reshape(1, padded)
    gram = carries.sums()[:, padded // tall :]
    mine = lax.axis_index("tm")
    place = mine // (2 * side_bit()) * side_bit() + mine % side_bit()
    place = (side[0] * (devices // 2) + place) * slots
    mean_own = lax.dynamic_slice_in_dim(mean_one[0], place, slots)[:, None]
    grad_parts = [
        part + mean_own * total_two[:, first : first + lanes]
        for (first, lanes), part in zip(parts, scatter.result())
    ]
    grad_block = jnp.concatenate(grad_parts, axis=1)
    momentum_new = MUON_BETA * momentum_block + grad_block
    start_block = momentum_new.astype(jnp.bfloat16)
    (start_block,), (back_in,) = tie([start_block], [back_in])
    gathered = lax.all_gather(start_block, "tm", axis=0, tiled=True)
    sums_one, input_part, gate_mean = gate_one(
        proj_one, state_local, state_in, back_local, back_in, keep, params[0], stat_one, x,
        shallow_weight, rows, frames, devices,
    )
    decay_two = jnp.sum(second_decay[:rows] + second_decay[rows:] * second_in, axis=0, keepdims=True)
    square = jnp.sum(momentum_new * momentum_new).reshape(1, 1)
    sums_one = (
        sums_one
        + jnp.pad(decay_two, ((feats + 3, SIDE - feats - 4), (0, 0)))
        + jnp.pad(square, ((feats + 4, SIDE - feats - 5), (0, padded - 1)))
    )
    spread = SumSpread(sums_one)
    for k in range(chunks):
        spread.step()
        (spread.value,) = next_hidden(1, [k], [spread.value])
    spread.step(len(spread.steps))
    sums_one = spread.value
    (hidden_one,), (hidden_two,) = hidden
    shallow_grad, shallow_next, shallow_new, shallow_low, input_grad = shallow_step(
        sums_one, gram, params[0], stat_one, shallow_weight, shallow_momentum, x, input_part, gate_mean,
        count * devices, rows, frames,
    )
    (gathered,), (shallow_low,) = tie([gathered], [shallow_low])
    input_grad = input_grad.reshape(rows, frames, feats)
    scale = 1.0 / (jnp.sqrt(sums_one[feats + 4, :1]) + MUON_EPSILON)
    shard = deep_weight.shape[0]
    window, first_row, offset = own_window(shard, width, padded)
    ortho = newton_rows(
        gathered, scale, (first_row // 16).astype(jnp.int32).reshape(1), window
    )
    deep_ortho = lax.dynamic_slice_in_dim(ortho[:, :width].reshape(-1), offset, shard)
    deep_new = MUON_KEEP * deep_weight - MUON_RATE * deep_ortho.astype(jnp.float32)
    deep_grad = from_block(grad_block[:, :width], shard, padded)
    deep_next = MUON_BETA * deep_momentum + deep_grad

    unit_sums = sums_one[feats : feats + 4, :width]
    bias_gain_two = sums_two[:, :width]
    slope = jnp.where(
        1.0 - jnp.exp(-unit_params[:, 0]) > DECAY_FLOOR, jnp.exp(-unit_params[:, 0]), 0.0
    )
    unit_grad = jnp.stack(
        [
            jnp.stack([unit_sums[2] * slope[0], unit_sums[0], unit_sums[1], unit_sums[0]]),
            jnp.stack(
                [unit_sums[3] * slope[1], bias_gain_two[0], bias_gain_two[1], bias_gain_two[0]]
            ),
        ]
    )
    first_fix = 1.0 - FIRST_DECAY**STEP
    second_fix = 1.0 - SECOND_DECAY**STEP
    first_new = FIRST_DECAY * unit_first + (1.0 - FIRST_DECAY) * unit_grad
    second_new = SECOND_DECAY * unit_second + (1.0 - SECOND_DECAY) * unit_grad * unit_grad
    params_new = unit_params - ADAM_RATE * (first_new / first_fix) / (
        jnp.sqrt(second_new / second_fix) + ADAM_EPSILON
    )
    return (
        hidden_one.reshape(rows, frames, width),
        hidden_two.reshape(rows, frames, width),
        input_grad,
        shallow_grad,
        shallow_next,
        shallow_new,
        shallow_low,
        deep_grad,
        deep_next,
        deep_new,
        deep_new.astype(jnp.bfloat16),
        first_new,
        second_new,
        params_new,
    )


def solution(mesh):
    in_specs = (
        P(None, "tm", None),
        P(None, "tm"),
        P(),
        P(),
        P("tm"),
        P("tm"),
        P(),
        P(),
        P(),
        P(None, "tm", None),
    )
    out_specs = (
        P(None, "tm", None),
        P(None, "tm", None),
        P(None, "tm", None),
        P(),
        P(),
        P(),
        P(),
        P("tm"),
        P("tm"),
        P("tm"),
        P("tm"),
        P(),
        P(),
        P(),
    )
    return jax.shard_map(
        per_device, mesh=mesh, in_specs=in_specs, out_specs=out_specs, check_vma=False
    )
```

```python
import functools

import jax
import jax.numpy as jnp
from jax import lax
from jax.experimental import pallas as pl
from jax.experimental.pallas import tpu as pltpu
from jax.sharding import PartitionSpec as P

NS_STEPS = 2
STEP = 5


NORM_EPSILON = 1e-05
MUON_EPSILON = 1e-07
COEFF_A = 3.4445
COEFF_B = -4.775
COEFF_C = 2.0315
MUON_BETA = 0.5
MUON_RATE = 4.0
MUON_KEEP = 0.999
FIRST_DECAY = 0.9
SECOND_DECAY = 0.95
ADAM_RATE = 0.5
ADAM_EPSILON = 1e-08
DECAY_FLOOR = 0.9
LANE = 128
WIDE = 512
PART = 256
SIDE = 80


def kernel_call(body, grid, in_specs, out_specs, out_shape, scratch=(), flops=0, traffic=0):
    return pl.pallas_call(
        body,
        grid=grid,
        in_specs=in_specs,
        out_specs=out_specs,
        out_shape=out_shape,
        scratch_shapes=list(scratch),
        compiler_params=pltpu.CompilerParams(vmem_limit_bytes=56 * 1024 * 1024),
        cost_estimate=pl.CostEstimate(flops=flops, bytes_accessed=traffic, transcendentals=0),
    )


def shape_of(shape, dtype=jnp.float32):
    return jax.ShapeDtypeStruct(shape, dtype)


def whole(shape):
    return pl.BlockSpec(shape, lambda i: (0,) * len(shape))


def lanes_of(rows, width=WIDE):
    return pl.BlockSpec((rows, width), lambda i: (0, i))


def chunk_call(body, place, in_specs, out_specs, out_shape, arrays, previous, scratch=(), traffic=0):
    count = len(in_specs)
    before = list(previous) if previous is not None else []

    def run(*refs):
        body(*refs[:count], *refs[count + len(before) :])

    return pl.pallas_call(
        run,
        grid=(1,),
        in_specs=list(in_specs) + [pl.BlockSpec(memory_space=pl.ANY)] * len(before),
        out_specs=out_specs,
        out_shape=out_shape,
        scratch_shapes=list(scratch),
        input_output_aliases={count + k: k for k in range(len(before))},
        compiler_params=pltpu.CompilerParams(vmem_limit_bytes=56 * 1024 * 1024),
        cost_estimate=pl.CostEstimate(flops=0, bytes_accessed=traffic, transcendentals=0),
    )(*arrays, *before)


def chunk_at(rows, place):
    return pl.BlockSpec((rows, WIDE), lambda i: (0, place))


def rate_of(params):
    return jnp.maximum(1.0 - jnp.exp(-params[0:1]), DECAY_FLOOR)


def softened(value):
    return jnp.maximum(value, 0.0) + jnp.log(1.0 + jnp.exp(-jnp.abs(value)))


def sigmoid(value):
    return 0.5 * jnp.tanh(0.5 * value) + 0.5


def wide_keep(keep_ref, t, rows):
    keep = keep_ref[pl.ds(pl.multiple_of(t * rows, rows), rows), :]
    return jnp.concatenate([keep] * (WIDE // LANE), axis=1)


def rows_at(ref, t, rows):
    return ref[pl.ds(pl.multiple_of(t * rows, rows), rows), :]


def store_at(ref, t, rows, value):
    ref[pl.ds(pl.multiple_of(t * rows, rows), rows), :] = value


def valid_lanes(shape, total, step):
    return lax.broadcasted_iota(jnp.int32, shape, 1) + step * WIDE < total


def unit_terms(params_ref, stat_ref, total_devices, frames):
    params = params_ref[...]
    stat = stat_ref[...]
    centre = stat[0:1]
    inverse = lax.rsqrt(stat[1:2] / (total_devices * frames) + NORM_EPSILON)
    return centre, inverse, params[2:3], params[3:4] + params[1:2]


def front_body(rows, frames, width, x_ref, w_ref, xt_ref, proj_ref, stat_ref, gram_ref, padded_w):
    step = pl.program_id(0)
    count, feats = x_ref.shape

    @pl.when(step == 0)
    def _():
        i = lax.broadcasted_iota(jnp.int32, (count, count), 0)
        j = lax.broadcasted_iota(jnp.int32, (count, count), 1)
        move = (j == lax.rem(i, rows) * frames + lax.div(i, rows)).astype(jnp.bfloat16)
        moved = jnp.dot(move, x_ref[...], preferred_element_type=jnp.float32).astype(jnp.bfloat16)
        i = lax.broadcasted_iota(jnp.int32, (feats, LANE), 0)
        j = lax.broadcasted_iota(jnp.int32, (feats, LANE), 1)
        wide = jnp.dot(moved, (i == j).astype(jnp.bfloat16), preferred_element_type=jnp.float32)
        lane = lax.broadcasted_iota(jnp.int32, (count, LANE), 1)
        xt = jnp.where(lane == feats, 1.0, wide).astype(jnp.bfloat16)
        xt_ref[...] = xt
        gram = dot_tn(xt, xt)
        high = gram_ref.shape[0]
        for k in range(SIDE // high):
            gram_ref[:, k * LANE : (k + 1) * LANE] = gram[k * high : (k + 1) * high]
        padded_w[...] = jnp.zeros_like(padded_w)

    weight = w_ref[...]
    padded_w[0:feats, :] = jnp.where(valid_lanes(weight.shape, width, step), weight, 0.0)
    proj = jnp.dot(
        xt_ref[...], padded_w[...].astype(jnp.bfloat16), preferred_element_type=jnp.float32
    )
    proj_ref[...] = proj
    mean = jnp.sum(proj, axis=0, keepdims=True) * (1.0 / count)
    off = proj - mean
    stat_ref[0:1, :] = mean
    stat_ref[1:2, :] = jnp.sum(off * off, axis=0, keepdims=True)


def dot_tn(a, b):
    return lax.dot_general(a, b, (((0,), (0,)), ((), ())), preferred_element_type=jnp.float32)


def front(x, weight, rows, frames):
    count, feats = x.shape
    width = weight.shape[1]
    padded = -(-width // WIDE) * WIDE
    return kernel_call(
        functools.partial(front_body, rows, frames, width),
        (padded // WIDE,),
        [whole((count, feats)), lanes_of(feats)],
        [whole((count, LANE)), lanes_of(count), lanes_of(2), whole((2 * rows, SIDE // (2 * rows) * LANE))],
        [
            shape_of((count, LANE), jnp.bfloat16),
            shape_of((count, padded)),
            shape_of((2, padded)),
            shape_of((2 * rows, SIDE // (2 * rows) * LANE)),
        ],
        [pltpu.VMEM((LANE, WIDE), jnp.float32)],
    )(x, weight)


def delta_two_body(rows, frames, width, grad_ref, keep_ref, params_ref, delta_ref, end_ref, held):
    place = pl.program_id(0)
    pieces = WIDE // LANE
    mask = valid_lanes((rows * frames, WIDE), width, place)
    grad = jnp.where(mask, grad_ref[...].astype(jnp.float32), 0.0)
    for g in range(pieces):
        held[g] = grad[:, g * LANE : (g + 1) * LANE]
    rate = rate_of(params_ref[...])

    def body(k, carried):
        t = frames - 1 - k
        own = jnp.concatenate(
            [held[g, pl.ds(t, rows, stride=frames), :] for g in range(pieces)], axis=1
        )
        delta = own + carried
        store_at(delta_ref, t, rows, delta)
        return rate * wide_keep(keep_ref, t, rows) * delta

    end_ref[...] = lax.fori_loop(
        0, frames, body, jnp.zeros((rows, WIDE), jnp.float32), unroll=8
    )


def delta_two(out_grad, keep, params, rows, frames, padded):
    count, width = out_grad.shape
    return kernel_call(
        functools.partial(delta_two_body, rows, frames, width),
        (padded // WIDE,),
        [lanes_of(count), whole((count, LANE)), lanes_of(4)],
        [lanes_of(count), lanes_of(rows)],
        [shape_of((count, padded)), shape_of((rows, padded))],
        [pltpu.VMEM((WIDE // LANE, count, LANE), jnp.float32)],
    )(out_grad, keep, params)


def states_body(
    rows, frames, devices, proj_ref, keep_ref, params_ref, stat_ref, state_ref, end_ref
):
    centre, inverse, gain, offset = unit_terms(params_ref, stat_ref, devices, rows * frames)
    rate = rate_of(params_ref[...])
    share = 1.0 - rate

    def body(t, carried):
        gate = (rows_at(proj_ref, t, rows) - centre) * inverse * gain + offset
        soft = softened(gate)
        carried = rate * wide_keep(keep_ref, t, rows) * carried + share * soft
        store_at(state_ref, t, rows, carried)
        return carried

    end_ref[...] = lax.fori_loop(
        0, frames, body, jnp.zeros((rows, WIDE), jnp.float32), unroll=8
    )


def local_states(proj, keep, params, stat, rows, frames, devices):
    count, padded = proj.shape
    return kernel_call(
        functools.partial(states_body, rows, frames, devices),
        (padded // WIDE,),
        [lanes_of(count), whole((count, LANE)), lanes_of(4), lanes_of(2)],
        [lanes_of(count), lanes_of(rows)],
        [shape_of((count, padded)), shape_of((rows, padded))],
    )(proj, keep, params, stat)


def to_slots(value, group):
    pieces = value.shape[1] // LANE
    lane = lax.broadcasted_iota(jnp.int32, (value.shape[0], LANE), 1)
    parts = [value[:, g * LANE : (g + 1) * LANE] for g in range(pieces)]
    out = []
    for g in range(pieces):
        moved = (LANE - group) * g
        if moved == 0:
            new = parts[g]
        else:
            new = jnp.where(
                lane < moved, pltpu.roll(parts[g - 1], moved, 1), pltpu.roll(parts[g], moved, 1)
            )
        out.append(jnp.where(lane < group, new, 0.0))
    return jnp.concatenate(out, axis=1)


def from_slots(value, group, width):
    pieces = value.shape[1] // LANE
    lane = lax.broadcasted_iota(jnp.int32, (value.shape[0], LANE), 1)
    parts = [value[:, g * LANE : (g + 1) * LANE] for g in range(pieces)]
    out = []
    for j in range(pieces):
        moved = (LANE - group) * j
        new = parts[j] if moved == 0 else pltpu.roll(parts[j], LANE - moved, 1)
        if j + 1 < pieces:
            new = jnp.where(lane < group - moved, new, pltpu.roll(parts[j + 1], group - moved, 1))
        left = width - j * LANE
        out.append(new if left >= LANE else jnp.where(lane < left, new, 0.0))
    return jnp.concatenate(out, axis=1)


def low_one_body(rows, frames, width, group, state_ref, start_ref, keep_ref, params_ref, low_ref, mean_ref):
    pieces = state_ref.shape[1] // LANE
    rate = rate_of(params_ref[...])

    def advance(t, carried):
        keep = rows_at(keep_ref, t, rows)
        carried = rate * jnp.concatenate([keep] * pieces, axis=1) * carried
        return carried, rows_at(state_ref, t, rows) + carried

    def body(k, both):
        carried, total = both
        t = 2 * k
        carried, first = advance(t, carried)
        carried, second = advance(t + 1, carried)
        place = pl.ds(pl.multiple_of(t * rows, 2 * rows), 2 * rows)
        slots = to_slots(jnp.concatenate([first, second], axis=0), group)
        low_ref[place, :] = slots.astype(jnp.bfloat16)
        return carried, total + slots[:rows] + slots[rows:]

    start = start_ref[...]
    _, total = lax.fori_loop(0, frames // 2, body, (start, jnp.zeros_like(start)), unroll=4)
    mean_ref[...] = jnp.sum(total, axis=0, keepdims=True) * (1.0 / (rows * frames))


def low_one_of(states, start, keep, params, rows, frames, width, group):
    count, padded = states.shape
    return kernel_call(
        functools.partial(low_one_body, rows, frames, width, group),
        (1,),
        [whole((count, padded)), whole((rows, padded)), whole((count, LANE)), whole((4, padded))],
        [whole((count, padded)), whole((1, padded))],
        [shape_of((count, padded), jnp.bfloat16), shape_of((1, padded))],
    )(states, start, keep, params)


def hidden_body(rows, frames, state_ref, start_ref, keep_ref, params_ref, hidden_ref, held):
    pieces = WIDE // LANE
    rate = rate_of(params_ref[...])

    def body(t, carry):
        carry = rate * wide_keep(keep_ref, t, rows) * carry
        state = rows_at(state_ref, t, rows) + carry
        for g in range(pieces):
            held[g, pl.ds(pl.multiple_of(t * rows, rows), rows), :] = state[
                :, g * LANE : (g + 1) * LANE
            ]
        return carry

    lax.fori_loop(0, frames, body, start_ref[...], unroll=8)
    for r in range(rows):
        for g in range(pieces):
            hidden_ref[r * frames : (r + 1) * frames, g * LANE : (g + 1) * LANE] = held[
                g, pl.ds(r, frames, stride=rows), :
            ]


def hidden_of(place, previous, states, start, keep, params, rows, frames, width):
    count, _ = states.shape
    return chunk_call(
        functools.partial(hidden_body, rows, frames),
        place,
        [chunk_at(count, place), chunk_at(rows, place), whole((count, LANE)), chunk_at(4, place)],
        [chunk_at(count, place)],
        [shape_of((count, width))],
        (states, start, keep, params),
        previous,
        [pltpu.VMEM((WIDE // LANE, count, LANE), jnp.float32)],
    )


def second_body(low_ref, weight_ref, proj_ref, stat_ref):
    tile = 256
    count = proj_ref.shape[0]
    for j in range(0, WIDE, tile):
        place = slice(j, j + tile)
        for i in range(0, count, tile):
            proj_ref[i : i + tile, place] = jnp.dot(
                low_ref[i : i + tile, :], weight_ref[:, place], preferred_element_type=jnp.float32
            )
        proj = proj_ref[:, place]
        mean = jnp.sum(proj, axis=0, keepdims=True) * (1.0 / count)
        off = proj - mean
        stat_ref[0:1, place] = mean
        stat_ref[1:2, place] = jnp.sum(off * off, axis=0, keepdims=True)


def second_forward(low, weight):
    count, padded = low.shape
    return kernel_call(
        second_body,
        (padded // WIDE,),
        [whole((count, padded)), lanes_of(padded)],
        [lanes_of(count), lanes_of(2)],
        [shape_of((count, padded)), shape_of((2, padded))],
    )(low, weight)


def gate_two_body(
    rows, frames, devices, proj_ref, delta_ref, start_ref, keep_ref, params_ref, stat_ref, gate_ref, sums_ref
):
    centre, inverse, gain, offset = unit_terms(params_ref, stat_ref, devices, rows * frames)
    rate = rate_of(params_ref[...])
    share = 1.0 - rate
    none = jnp.zeros((rows, WIDE), jnp.float32)

    def body(k, carried):
        carry, bias_sum, gain_sum = carried
        t = frames - 1 - k
        delta = rows_at(delta_ref, t, rows) + carry
        normed = (rows_at(proj_ref, t, rows) - centre) * inverse
        gate = share * delta * sigmoid(normed * gain + offset)
        store_at(gate_ref, t, rows, gate)
        carry = rate * wide_keep(keep_ref, t, rows) * carry
        return carry, bias_sum + gate, gain_sum + gate * normed

    _, bias_sum, gain_sum = lax.fori_loop(
        0, frames, body, (start_ref[...], none, none), unroll=8
    )
    sums_ref[0:1, :] = jnp.sum(bias_sum, axis=0, keepdims=True)
    sums_ref[1:2, :] = jnp.sum(gain_sum, axis=0, keepdims=True)


def gate_two(proj, delta, start, keep, params, stat, rows, frames, devices):
    count, padded = proj.shape
    return kernel_call(
        functools.partial(gate_two_body, rows, frames, devices),
        (padded // WIDE,),
        [lanes_of(count), lanes_of(count), lanes_of(rows), whole((count, LANE)), lanes_of(4), lanes_of(2)],
        [lanes_of(count), lanes_of(2)],
        [shape_of((count, padded)), shape_of((2, padded))],
    )(proj, delta, start, keep, params, stat)


def states_two_body(
    rows, frames, devices, proj_ref, delta_ref, start_ref, keep_ref, params_ref, stat_ref,
    state_ref, end_ref, decay_ref, held,
):
    centre, inverse, gain, offset = unit_terms(params_ref, stat_ref, devices, rows * frames)
    rate = rate_of(params_ref[...])
    share = 1.0 - rate
    none = jnp.zeros((rows, WIDE), jnp.float32)

    def backward(k, carry):
        t = frames - 1 - k
        store_at(held, t, rows, rows_at(delta_ref, t, rows) + carry)
        return rate * wide_keep(keep_ref, t, rows) * carry

    lax.fori_loop(0, frames, backward, start_ref[...], unroll=8)

    def forward(t, carried):
        state, reach, decay, factor = carried
        keep = wide_keep(keep_ref, t, rows)
        delta = rows_at(held, t, rows)
        value = (rows_at(proj_ref, t, rows) - centre) * inverse * gain + offset
        soft = softened(value)
        decay = decay + delta * (keep * state - soft)
        factor = factor + delta * keep * reach
        state = rate * keep * state + share * soft
        reach = rate * keep * reach
        store_at(state_ref, t, rows, state)
        return state, reach, decay, factor

    state, _, decay, factor = lax.fori_loop(
        0, frames, forward, (none, jnp.ones_like(none), none, none), unroll=4
    )
    end_ref[...] = state
    decay_ref[0:rows, :] = decay
    decay_ref[rows : 2 * rows, :] = factor


def states_two(proj, delta, start, keep, params, stat, rows, frames, devices):
    count, padded = proj.shape
    return kernel_call(
        functools.partial(states_two_body, rows, frames, devices),
        (padded // WIDE,),
        [
            lanes_of(count),
            lanes_of(count),
            lanes_of(rows),
            whole((count, LANE)),
            lanes_of(4),
            lanes_of(2),
        ],
        [lanes_of(count), lanes_of(rows), lanes_of(2 * rows)],
        [shape_of((count, padded)), shape_of((rows, padded)), shape_of((2 * rows, padded))],
        [pltpu.VMEM((count, WIDE), jnp.float32)],
    )(proj, delta, start, keep, params, stat)


def turn_body(low_ref, mean_ref, turned_ref):
    half = LANE // 2
    turned = (low_ref[...].astype(jnp.float32) - mean_ref[...]).T.astype(jnp.bfloat16)
    for g in range(WIDE // LANE):
        for side in range(2):
            turned_ref[side, g * half : (g + 1) * half, :] = turned[
                g * LANE + side * half : g * LANE + (side + 1) * half
            ]


def turn(place, previous, low, mean):
    count, padded = low.shape
    return chunk_call(
        turn_body,
        place,
        [chunk_at(count, place), chunk_at(1, place)],
        [pl.BlockSpec((2, WIDE // 2, count), lambda i: (0, place, 0))],
        [shape_of((2, padded // 2, count), jnp.bfloat16)],
        (low, mean),
        previous,
    )


def deep_term_body(
    rows, frames, devices, parts, orders, side_ref, gate_ref, proj_ref, params_ref, stat_ref, sums_ref,
    turned_ref, grad_ref, total_ref, *outs,
):
    step = pl.program_id(0)
    total = devices * rows * frames
    centre, inverse, gain, _ = unit_terms(params_ref, stat_ref, devices, rows * frames)
    sums = sums_ref[...] * (1.0 / total)
    normed = (proj_ref[...] - centre) * inverse
    grad = (gain * inverse * (gate_ref[...] - sums[0:1] - normed * sums[1:2])).astype(jnp.bfloat16)
    grad_ref[...] = grad
    total_ref[...] = jnp.sum(grad.astype(jnp.float32), axis=0, keepdims=True)
    side = side_ref[0]
    half = turned_ref.shape[1]
    tile = 256
    for p, (first, lanes) in enumerate(parts):

        @pl.when((step >= first // PART) & (step < (first + lanes) // PART))
        def _():
            for which, out_ref in ((side, outs[p]), (1 - side, outs[len(parts) + p])):
                for k in range(half // tile):
                    part = jnp.dot(
                        turned_ref[which, k * tile : (k + 1) * tile, :],
                        grad_ref[...],
                        preferred_element_type=jnp.float32,
                    ).astype(out_ref.dtype)
                    if orders is None:
                        out_ref[k * tile : (k + 1) * tile, :] = part
                        continue
                    slots = half // 2 ** len(orders[p])
                    for b in range(tile // slots):
                        block = k * (tile // slots) + b
                        place = 0
                        for weight in orders[p]:
                            place = 2 * place + block // weight % 2
                        out_ref[place * slots : (place + 1) * slots, :] = part[
                            b * slots : (b + 1) * slots
                        ]


def deep_term(parts, orders, side, gate, proj, params, stat, sums, turned, rows, frames, devices):
    count, padded = proj.shape
    half = padded // 2

    def some(first, lanes):
        return pl.BlockSpec(
            (half, PART), lambda i: (0, jnp.clip(i - first // PART, 0, lanes // PART - 1))
        )

    found = kernel_call(
        functools.partial(deep_term_body, rows, frames, devices, parts, orders),
        (padded // PART,),
        [
            pl.BlockSpec(memory_space=pltpu.SMEM),
            lanes_of(count, PART),
            lanes_of(count, PART),
            lanes_of(4, PART),
            lanes_of(2, PART),
            lanes_of(2, PART),
            whole((2, half, count)),
        ],
        [lanes_of(count, PART), lanes_of(1, PART)] + [some(*part) for part in parts] * 2,
        [shape_of((count, padded), jnp.bfloat16), shape_of((1, padded))]
        + [shape_of((half, lanes), jnp.bfloat16) for _, lanes in parts] * 2,
    )(side, gate, proj, params, stat, sums, turned)
    return found[0], found[1], found[2 : 2 + len(parts)], found[2 + len(parts) :]


def back_body(grad_ref, weight_ref, back_ref):
    back_ref[...] = dot_nt(grad_ref[...], weight_ref[...])


def back_one(grad, weight):
    count, padded = grad.shape
    return kernel_call(
        back_body,
        (padded // WIDE,),
        [whole((count, padded)), pl.BlockSpec((WIDE, padded), lambda i: (i, 0))],
        lanes_of(count),
        shape_of((count, padded)),
    )(grad, weight)


def delta_one_body(rows, frames, width, group, back_ref, keep_ref, params_ref, delta_ref, end_ref):
    pieces = back_ref.shape[1] // LANE
    rate = rate_of(params_ref[...])

    def body(k, carried):
        t = frames - 1 - k
        delta = from_slots(rows_at(back_ref, t, rows), group, width) + carried
        store_at(delta_ref, t, rows, delta)
        keep = rows_at(keep_ref, t, rows)
        return rate * jnp.concatenate([keep] * pieces, axis=1) * delta

    end_ref[...] = lax.fori_loop(
        0, frames, body, jnp.zeros((rows, back_ref.shape[1]), jnp.float32), unroll=2
    )


def delta_one(back, keep, params, rows, frames, width, group):
    count, padded = back.shape
    return kernel_call(
        functools.partial(delta_one_body, rows, frames, width, group),
        (1,),
        [whole((count, padded)), whole((count, LANE)), whole((4, padded))],
        [whole((count, padded)), whole((rows, padded))],
        [shape_of((count, padded)), shape_of((rows, padded))],
    )(back, keep, params)


def gate_one_body(
    rows,
    frames,
    devices,
    feats,
    width,
    proj_ref,
    state_ref,
    first_ref,
    delta_ref,
    start_ref,
    keep_ref,
    params_ref,
    stat_ref,
    x_ref,
    w_ref,
    sums_ref,
    back_ref,
    mean_ref,
    held,
    gate_ref,
    padded_w,
):
    step = pl.program_id(0)
    centre, inverse, gain, offset = unit_terms(params_ref, stat_ref, devices, rows * frames)
    rate = rate_of(params_ref[...])
    share = 1.0 - rate
    none = jnp.zeros((rows, WIDE), jnp.float32)

    def backward(k, carry):
        t = frames - 1 - k
        store_at(held, t, rows, rows_at(delta_ref, t, rows) + carry)
        return rate * wide_keep(keep_ref, t, rows) * carry

    lax.fori_loop(0, frames, backward, start_ref[...], unroll=8)

    def forward(t, carried):
        carry, before, bias_sum, gain_sum, decay_sum = carried
        keep = wide_keep(keep_ref, t, rows)
        delta = rows_at(held, t, rows)
        normed = (rows_at(proj_ref, t, rows) - centre) * inverse
        value = normed * gain + offset
        soft = softened(value)
        gate = share * delta * sigmoid(value)
        store_at(gate_ref, t, rows, gate)
        decay_sum = decay_sum + delta * (keep * before - soft)
        carry = rate * keep * carry
        before = rows_at(state_ref, t, rows) + carry
        return carry, before, bias_sum + gate, gain_sum + gate * normed, decay_sum

    first = first_ref[...]
    _, _, bias_sum, gain_sum, decay_sum = lax.fori_loop(
        0, frames, forward, (first, first, none, none, none), unroll=4
    )
    bias = jnp.sum(bias_sum, axis=0, keepdims=True)
    mean = bias * (1.0 / (rows * frames))
    x = x_ref[...]
    ones = jnp.ones((rows * frames, LANE), jnp.bfloat16)
    total = jnp.concatenate([dot_tn(x, ones)] * (WIDE // LANE), axis=1)
    centred = gate_ref[...] - mean
    term = dot_tn(x, centred.astype(jnp.bfloat16)) + total * mean
    sums_ref[...] = term[: sums_ref.shape[0]]
    sums_ref[feats : feats + 1, :] = bias
    sums_ref[feats + 1 : feats + 2, :] = jnp.sum(gain_sum, axis=0, keepdims=True)
    sums_ref[feats + 2 : feats + 3, :] = jnp.sum(decay_sum, axis=0, keepdims=True)
    mean_ref[...] = mean
    weight = w_ref[...]
    padded_w[...] = jnp.zeros_like(padded_w)
    padded_w[0:feats, :] = jnp.where(valid_lanes(weight.shape, width, step), weight, 0.0)
    part = dot_nt(
        (gain * inverse * centred).astype(jnp.bfloat16), padded_w[...].astype(jnp.bfloat16)
    )

    @pl.when(step == 0)
    def _():
        back_ref[...] = part

    @pl.when(step > 0)
    def _():
        back_ref[...] += part


def gate_one(proj, states, first, delta, start, keep, params, stat, x, weight, rows, frames, devices):
    count, padded = proj.shape
    feats, width = weight.shape
    return kernel_call(
        functools.partial(gate_one_body, rows, frames, devices, feats, width),
        (padded // WIDE,),
        [
            lanes_of(count),
            lanes_of(count),
            lanes_of(rows),
            lanes_of(count),
            lanes_of(rows),
            whole((count, LANE)),
            lanes_of(4),
            lanes_of(2),
            whole((count, LANE)),
            lanes_of(feats),
        ],
        [lanes_of(SIDE), whole((count, LANE)), lanes_of(1)],
        [shape_of((SIDE, padded)), shape_of((count, LANE)), shape_of((1, padded))],
        [
            pltpu.VMEM((count, WIDE), jnp.float32),
            pltpu.VMEM((count, WIDE), jnp.float32),
            pltpu.VMEM((LANE, WIDE), jnp.float32),
        ],
    )(proj, states, first, delta, start, keep, params, stat, x, weight)


def dot_nt(a, b):
    return lax.dot_general(a, b, (((1,), (1,)), ((), ())), preferred_element_type=jnp.float32)


def shallow_body(
    total, rows, frames, sums_ref, gram_ref, params_ref, stat_ref, w_ref, m_ref, x_ref, back_ref, mean_ref,
    grad_ref, next_ref, new_ref, low_ref, input_ref, held, moved,
):
    feats, width = w_ref.shape
    count = rows * frames
    centre, inverse, gain, _ = unit_terms(params_ref, stat_ref, total // count, count)
    weight = w_ref[...]
    held[...] = jnp.zeros_like(held)
    held[0:feats, 0:width] = weight
    low = held[...].astype(jnp.bfloat16).astype(jnp.float32)
    high = gram_ref.shape[0]
    gram = jnp.concatenate(
        [gram_ref[:, k * LANE : (k + 1) * LANE] for k in range(SIDE // high)], axis=0
    )
    lane = lax.broadcasted_iota(jnp.int32, gram.shape, 1)
    x_sum = jnp.sum(jnp.where(lane == feats, gram, 0.0), axis=1, keepdims=True)
    raw = jnp.dot(
        gram, low, precision=lax.Precision.HIGHEST, preferred_element_type=jnp.float32
    )
    normed = (raw - x_sum * centre) * inverse
    bias = sums_ref[feats : feats + 1, :] * (1.0 / total)
    slope = sums_ref[feats + 1 : feats + 2, :] * (1.0 / total)
    scaled = gain * inverse
    grad = scaled * (sums_ref[...] - x_sum * bias - normed * slope)
    grad = grad[:feats, :width]
    grad_ref[...] = grad

    row = lax.broadcasted_iota(jnp.int32, low.shape, 0)
    turn = slope * inverse
    left = jnp.where(
        row == feats, scaled * (mean_ref[...] - bias + turn * centre), -low * (scaled * turn)
    )
    matrix = lax.dot_general(
        left, low, (((1,), (1,)), ((), ())),
        precision=lax.Precision.HIGHEST, preferred_element_type=jnp.float32,
    )
    moved[...] = back_ref[...] + jnp.dot(
        x_ref[...].astype(jnp.float32), matrix,
        precision=lax.Precision.HIGHEST, preferred_element_type=jnp.float32,
    )
    for r in range(rows):
        input_ref[r * frames : (r + 1) * frames, :] = moved[pl.ds(r, frames, stride=rows), :][:, :feats]

    following = MUON_BETA * m_ref[...] + grad
    next_ref[...] = following
    held[0:feats, 0:width] = following
    m = held[0:SIDE, :]
    current = (m / (jnp.sqrt(jnp.sum(m * m)) + MUON_EPSILON)).astype(jnp.bfloat16)
    for repeat in range(NS_STEPS):
        gram = dot_nt(current, current).astype(jnp.bfloat16)
        square = jnp.dot(gram, gram, preferred_element_type=jnp.float32)
        mixing = (COEFF_B * gram.astype(jnp.float32) + COEFF_C * square).astype(jnp.bfloat16)
        current = (
            COEFF_A * current.astype(jnp.float32)
            + jnp.dot(mixing, current, preferred_element_type=jnp.float32)
        ).astype(jnp.bfloat16)
    new = MUON_KEEP * weight - MUON_RATE * current[:feats, :width].astype(jnp.float32)
    new_ref[...] = new
    low_ref[...] = new.astype(jnp.bfloat16)


def shallow_step(sums, gram, params, stat, weight, momentum, x, back, mean, total, rows, frames):
    padded = sums.shape[1]
    some = shape_of(weight.shape)
    feats = weight.shape[0]
    arrays = (sums, gram, params, stat, weight, momentum, x, back, mean)
    return kernel_call(
        functools.partial(shallow_body, total, rows, frames),
        (1,),
        [whole(value.shape) for value in arrays],
        [whole(weight.shape)] * 4 + [whole((rows * frames, feats))],
        [some, some, some, shape_of(weight.shape, jnp.bfloat16), shape_of((rows * frames, feats))],
        [pltpu.VMEM((LANE, padded), jnp.float32), pltpu.VMEM((rows * frames, LANE), jnp.float32)],
    )(*arrays)


def newton_body(window, tile, first_ref, scale_ref, start_ref, out_ref, m_ref, gram, sems):
    size = m_ref.shape[0]
    blocks = size // tile

    def place(k):
        return slice(k * tile, (k + 1) * tile)

    copies = [
        pltpu.make_async_copy(start_ref.at[place(k), :], m_ref.at[place(k), :], sems.at[k])
        for k in range(blocks)
    ]
    for copy in copies:
        copy.start()
    scale = scale_ref[0]
    square_scale = scale * scale
    for j in range(blocks):
        copies[j].wait()
        for i in range(j + 1):
            part = dot_nt(m_ref[place(i), :], m_ref[place(j), :]) * square_scale
            gram[place(i), place(j)] = part.astype(jnp.bfloat16)
            if i != j:
                gram[place(j), place(i)] = part.T.astype(jnp.bfloat16)
    def taken(ref):
        return ref[pl.ds(pl.multiple_of(first_ref[0] * 16, 16), window), :].astype(jnp.float32)

    def times(value, ref):
        return jnp.dot(value.astype(jnp.bfloat16), ref[...], preferred_element_type=jnp.float32)

    def mixed(once):
        return COEFF_B * once + COEFF_C * times(once, gram)

    def stepped(value):
        return COEFF_A * value + mixed(times(value, gram))

    gram_own = taken(gram)
    mixing_own = mixed(gram_own)
    gram_own = stepped(COEFF_A * gram_own + times(mixing_own, gram))
    square_own = stepped(times(stepped(gram_own), gram))
    second_own = COEFF_B * gram_own + COEFF_C * square_own
    weights = COEFF_A * mixing_own + stepped(second_own)
    result = COEFF_A * COEFF_A * taken(m_ref) + times(weights, m_ref)
    out_ref[...] = (scale * result).astype(jnp.bfloat16)


def newton_rows(start, scale, first, window):
    size = start.shape[0]
    tile = 256
    scalar = pl.BlockSpec(memory_space=pltpu.SMEM)
    return kernel_call(
        functools.partial(newton_body, window, tile),
        (1,),
        [scalar, scalar, pl.BlockSpec(memory_space=pl.ANY)],
        whole((window, size)),
        shape_of((window, size), jnp.bfloat16),
        [pltpu.VMEM((size, size), jnp.bfloat16)] * 2 + [pltpu.SemaphoreType.DMA((size // tile,))],
    )(first, scale, start)


def swap(value, bit):
    size = lax.axis_size("tm")
    return lax.ppermute(value, "tm", [(i, i ^ bit) for i in range(size)])


def steps_of(size):
    bits = []
    bit = 1
    while bit < size:
        bits.append(bit)
        bit *= 2
    return bits


def bit_of(bit):
    return jnp.where((lax.axis_index("tm") & bit) != 0, 1, 0)


class SumSpread:
    def __init__(self, value):
        self.value = value
        self.steps = []
        lanes = value.shape[1]
        cuts = []
        for bit in steps_of(lax.axis_size("tm")):
            if lanes // 2 % WIDE == 0:
                lanes //= 2
                self.steps.append((self.halve, bit))
                cuts.append(bit)
            else:
                self.steps.append((self.pair, bit))
        self.steps += [(self.join, bit) for bit in reversed(cuts)]

    def halve(self, bit):
        lanes = self.value.shape[1] // 2
        mine = lax.dynamic_slice_in_dim(self.value, bit_of(bit) * lanes, lanes, 1)
        away = lax.dynamic_slice_in_dim(self.value, (1 - bit_of(bit)) * lanes, lanes, 1)
        self.value = mine + swap(away, bit)

    def pair(self, bit):
        self.value = self.value + swap(self.value, bit)

    def join(self, bit):
        other = swap(self.value, bit)
        upper = bit_of(bit) == 1
        self.value = jnp.concatenate(
            [jnp.where(upper, other, self.value), jnp.where(upper, self.value, other)], axis=1
        )

    def step(self, times=1):
        for _ in range(times):
            if self.steps:
                action, bit = self.steps.pop(0)
                action(bit)


def tie(first, second):
    return lax.optimization_barrier((list(first), list(second)))


def side_bit():
    return lax.axis_size("tm") // 32


def orders_of(size):
    bits = [bit for bit in steps_of(size) if bit != side_bit()]
    return [bits[k * len(bits) // 3 :] + bits[: k * len(bits) // 3] for k in range(3)]


def index_bits(bits):
    return [bit if bit < side_bit() else bit // 2 for bit in bits]


class Scatter:
    def __init__(self, keeps, sends):
        self.orders = orders_of(lax.axis_size("tm"))
        self.current = list(keeps)
        self.received = [swap(send, side_bit()) for send in sends]

    def step(self, *waiting):
        sends = []
        for p, order in enumerate(self.orders):
            half = self.current[p].shape[0] // 2
            mine, away = [
                lax.dynamic_slice_in_dim(self.current[p], half * index, half).astype(jnp.float32)
                + lax.dynamic_slice_in_dim(self.received[p], half * index, half).astype(jnp.float32)
                for index in (bit_of(order[0]), 1 - bit_of(order[0]))
            ]
            self.current[p] = mine
            sends.append(away.astype(jnp.bfloat16))
        sends, waiting = tie(sends, waiting)
        self.received = [swap(send, order.pop(0)) for send, order in zip(sends, self.orders)]
        return waiting

    def join(self, *done):
        self.received, done = tie(self.received, done)
        return done

    def result(self):
        return [a + b.astype(jnp.float32) for a, b in zip(self.current, self.received)]


class Stats:
    def __init__(self, stat, count):
        self.stat = stat
        self.count = float(count)
        self.bits = steps_of(lax.axis_size("tm"))

    def step(self, times=1):
        for _ in range(min(times, len(self.bits))):
            stat = self.stat
            other = swap(stat, self.bits.pop(0))
            gap = stat[0:1] - other[0:1]
            mean = 0.5 * (stat[0:1] + other[0:1])
            square = (stat[1:2] + other[1:2]) + gap * gap * (0.5 * self.count)
            self.stat = jnp.concatenate([mean, square, 0.5 * (stat[2:] + other[2:])], axis=0)
            self.count *= 2


class Exchange:
    def __init__(self, flags, carries, sums=()):
        self.bits = steps_of(lax.axis_size("tm"))
        high, self.width = carries[0][0].shape
        rows = high * len(carries)
        flags = jnp.broadcast_to(jnp.tile(flags, len(carries))[:, None], (rows, LANE))
        ends = jnp.concatenate([ends for ends, _, _ in carries], axis=0)
        self.payload = jnp.concatenate([ends, flags, *sums], axis=1)
        self.power = jnp.concatenate(
            [jnp.broadcast_to(power, (high, self.width)) for _, power, _ in carries], axis=0
        )
        self.lane = lax.broadcasted_iota(jnp.int32, self.payload.shape, 1)
        self.high = high
        self.reverse = [reverse for _, _, reverse in carries]
        self.before = jnp.zeros_like(ends)
        self.before_keep = jnp.ones_like(ends)

    def step(self, times=1):
        for _ in range(min(times, len(self.bits))):
            self.one()

    def one(self):
        bit = self.bits.pop(0)
        width = self.width
        mine, other = self.payload, swap(self.payload, bit)
        upper = bit_of(bit)
        row = lax.broadcasted_iota(jnp.int32, (len(mine), 1), 0) // self.high
        turned = sum((row == k) * int(reverse) for k, reverse in enumerate(self.reverse))
        following = turned != upper
        other_total = other[:, :width]
        keep_mine, keep_other = mine[:, width : width + 1], other[:, width : width + 1]
        self.before = jnp.where(
            following, self.before_keep * other_total + self.before, self.before
        )
        self.before_keep = jnp.where(
            following, self.before_keep * keep_other * self.power, self.before_keep
        )
        power = jnp.pad(self.power, ((0, 0), (0, mine.shape[1] - width)))
        carried = jnp.where(
            following, keep_mine * power * other + mine, keep_other * power * mine + other
        )
        self.payload = jnp.where(
            self.lane < width,
            carried,
            jnp.where(self.lane < width + LANE, mine * other, mine + other),
        )
        self.power = self.power * self.power

    def arrived(self, k):
        return self.before[k * self.high : (k + 1) * self.high]

    def sums(self):
        return self.payload[:, self.width + LANE :]


class SumAll:
    def __init__(self, value):
        self.value = value
        self.bits = steps_of(lax.axis_size("tm"))

    def step(self, times=1):
        for _ in range(min(times, len(self.bits))):
            self.value = self.value + swap(self.value, self.bits.pop(0))


def in_order(value, bits, slots):
    count = len(bits)
    axes = [count - bit.bit_length() for bit in bits]
    shape = (2,) * count + (slots, value.shape[1])
    return value.reshape(shape).transpose(axes + [count, count + 1]).reshape(value.shape)


def pad_lanes(value, padded):
    gap = padded - value.shape[-1]
    return jnp.pad(value, [(0, 0)] * (value.ndim - 1) + [(0, gap)])


def flat_places(shard, width, padded):
    size = lax.axis_size("tm")
    members = size * LANE // padded
    slots = LANE // members
    return members, slots, slots * width - shard


def to_block(flat, width, padded):
    size, mine = lax.axis_size("tm"), lax.axis_index("tm")
    members, slots, excess = flat_places(flat.shape[0], width, padded)
    lacking = excess * (members - 1)
    pairs = [(i + 1, i) for i in range(size - 1) if (i + 1) % members]
    extra = lax.ppermute(flat[:lacking], "tm", pairs)
    tail = jnp.zeros((excess,), flat.dtype)
    held = jnp.concatenate([flat, extra, tail])
    return lax.dynamic_slice_in_dim(held, excess * (mine % members), slots * width).reshape(
        slots, width
    )


def from_block(block, shard, padded):
    width = block.shape[1]
    size, mine = lax.axis_size("tm"), lax.axis_index("tm")
    members, slots, excess = flat_places(shard, width, padded)
    lacking = excess * (members - 1)
    pairs = [(i, i + 1) for i in range(size - 1) if (i + 1) % members]
    flat = block.reshape(-1)
    extra = lax.ppermute(flat[slots * width - lacking :], "tm", pairs)
    held = jnp.concatenate([extra, flat])
    return lax.dynamic_slice_in_dim(held, lacking - excess * (mine % members), shard)


def own_window(shard, width, padded):
    mine = lax.axis_index("tm")
    members, _, _ = flat_places(shard, width, padded)
    window = 16
    for k in range(members):
        first = shard * k // width // 16 * 16
        last = -(-shard * (k + 1) // width)
        window = max(window, -(-(last - first) // 16) * 16)
    member = mine % members
    first = jnp.minimum(shard * member // width // 16 * 16, LANE - window)
    return window, LANE * (mine // members) + first, shard * member - first * width


def per_device(
    inputs,
    clip_start,
    shallow_weight,
    shallow_momentum,
    deep_weight,
    deep_momentum,
    unit_params,
    unit_first,
    unit_second,
    out_grad,
):
    devices = lax.axis_size("tm")
    rows, frames, feats = inputs.shape
    width = shallow_weight.shape[1]
    padded = -(-width // WIDE) * WIDE
    group = width // (padded // LANE)
    count = rows * frames
    keep_mask = (1 - clip_start).astype(jnp.float32)
    flags = jnp.min(keep_mask, axis=1)
    keep = jnp.broadcast_to(keep_mask.T.reshape(count, 1), (count, LANE))
    params = pad_lanes(unit_params, padded)
    rates = jnp.maximum(1.0 - jnp.exp(-params[:, 0:1]), DECAY_FLOOR)
    powers = rates
    for _ in range(frames.bit_length() - 1):
        powers = powers * powers

    deep_block = pad_lanes(to_block(deep_weight.astype(jnp.bfloat16), width, padded), padded)
    momentum_block = pad_lanes(to_block(deep_momentum, width, padded), padded)

    shares = [3 * padded // 8, 3 * padded // 8, padded // 4]
    parts = [(sum(shares[:p]), shares[p]) for p in range(3)]
    side = bit_of(side_bit()).astype(jnp.int32).reshape(1)
    chunks = padded // WIDE
    orders = orders_of(devices)
    x, proj_one, stat_one, gram = front(
        inputs.reshape(count, feats), shallow_weight, rows, frames
    )
    (deep_block,), (stat_one,) = tie([deep_block], [stat_one])
    deep_low = lax.all_gather(deep_block, "tm", axis=0, tiled=True)
    stats = Stats(stat_one, count)
    stats.step()
    delta_local, delta_end = delta_two(
        out_grad.reshape(count, width), keep, params[1], rows, frames, padded
    )
    (delta_local, delta_end), (stats.stat,) = tie([delta_local, delta_end], [stats.stat])
    stats.step(len(stats.bits))
    (stat_one,), (momentum_block,) = tie([stats.stat], [momentum_block])
    state_local, state_end = local_states(
        proj_one, keep, params[0], stat_one, rows, frames, devices
    )
    carries = Exchange(flags, [(state_end, powers[0], False), (delta_end, powers[1], True)])
    carries.step(len(carries.bits))
    state_in, delta_in = carries.arrived(0), carries.arrived(1)
    low_one, mean_one = low_one_of(
        state_local, state_in, keep, params[0], rows, frames, width, group
    )
    proj_two, stat_two = second_forward(low_one, deep_low)
    stats = Stats(jnp.concatenate([stat_two, mean_one], axis=0), count)
    stats.step(len(stats.bits))
    hidden = [None, None]
    sources = [(state_local, state_in, params[0]), None]

    def next_hidden(layer, places, waiting):
        states, start, layer_params = sources[layer]
        for k in places:
            (start,), waiting = tie([start], waiting)
            hidden[layer] = hidden_of(
                k, hidden[layer], states, start, keep, layer_params, rows, frames, width
            )
        hidden[layer], waiting = tie(hidden[layer], waiting)
        return waiting

    stat_two, mean_one = stats.stat[:2], stats.stat[2:]
    gate, sums_two = gate_two(
        proj_two, delta_local, delta_in, keep, params[1], stat_two, rows, frames, devices
    )
    sums = SumAll(sums_two)
    turned = None
    for k in range(chunks):
        sums.step()
        turned = turn(k, turned, low_one, mean_one)
        turned, (sums.value,) = tie(turned, [sums.value])
    sums.step(len(sums.bits))
    sums_two = sums.value
    slots = padded // devices
    weights = [index_bits(order) for order in orders]
    aligned = slots % 16 == 0
    grad_two, total_two, keeps, sends = deep_term(
        parts, weights if aligned else None, side, gate, proj_two, params[1], stat_two,
        sums_two, turned[0], rows, frames, devices,
    )
    if not aligned:
        keeps = [in_order(keep, order, slots) for keep, order in zip(keeps, weights)]
        sends = [in_order(send, order, slots) for send, order in zip(sends, weights)]
    scatter = Scatter(keeps, sends)
    back = back_one(grad_two, deep_low)
    (back,) = scatter.join(back)
    (back,) = scatter.step(back)
    back_local, back_end = delta_one(back, keep, params[0], rows, frames, width, group)
    second_local, second_end, second_decay = states_two(
        proj_two, delta_local, delta_in, keep, params[1], stat_two, rows, frames, devices
    )
    back_end, second_end = scatter.join(back_end, second_end)
    tall = 2 * rows
    back_end, second_end = scatter.step(back_end, second_end)
    carries = Exchange(
        flags,
        [(back_end, powers[0], True), (second_end, powers[1], False)],
        [total_two.reshape(tall, -1), gram],
    )
    carries.step(2)
    (carries.payload,) = next_hidden(0, range(chunks), [carries.payload])
    (carries.payload,) = scatter.join(carries.payload)
    while len(scatter.orders[0]) > 1:
        (carries.payload,) = scatter.step(carries.payload)
        carries.step()
        (carries.payload,) = scatter.join(carries.payload)
    (carries.payload,) = scatter.step(carries.payload)
    carries.step(len(carries.bits))
    carries.payload, carries.before = scatter.join(carries.payload, carries.before)
    back_in, second_in = carries.arrived(0), carries.arrived(1)
    sources[1] = (second_local, second_in, params[1])
    total_two = carries.sums()[:, : padded // tall].reshape(1, padded)
    gram = carries.sums()[:, padded // tall :]
    mine = lax.axis_index("tm")
    place = mine // (2 * side_bit()) * side_bit() + mine % side_bit()
    place = (side[0] * (devices // 2) + place) * slots
    mean_own = lax.dynamic_slice_in_dim(mean_one[0], place, slots)[:, None]
    grad_parts = [
        part + mean_own * total_two[:, first : first + lanes]
        for (first, lanes), part in zip(parts, scatter.result())
    ]
    grad_block = jnp.concatenate(grad_parts, axis=1)
    momentum_new = MUON_BETA * momentum_block + grad_block
    start_block = momentum_new.astype(jnp.bfloat16)
    (start_block,), (back_in,) = tie([start_block], [back_in])
    gathered = lax.all_gather(start_block, "tm", axis=0, tiled=True)
    sums_one, input_part, gate_mean = gate_one(
        proj_one, state_local, state_in, back_local, back_in, keep, params[0], stat_one, x,
        shallow_weight, rows, frames, devices,
    )
    decay_two = jnp.sum(second_decay[:rows] + second_decay[rows:] * second_in, axis=0, keepdims=True)
    square = jnp.sum(momentum_new * momentum_new).reshape(1, 1)
    sums_one = (
        sums_one
        + jnp.pad(decay_two, ((feats + 3, SIDE - feats - 4), (0, 0)))
        + jnp.pad(square, ((feats + 4, SIDE - feats - 5), (0, padded - 1)))
    )
    spread = SumSpread(sums_one)
    for k in range(chunks):
        spread.step()
        (spread.value,) = next_hidden(1, [k], [spread.value])
    spread.step(len(spread.steps))
    sums_one = spread.value
    (hidden_one,), (hidden_two,) = hidden
    shallow_grad, shallow_next, shallow_new, shallow_low, input_grad = shallow_step(
        sums_one, gram, params[0], stat_one, shallow_weight, shallow_momentum, x, input_part, gate_mean,
        count * devices, rows, frames,
    )
    (gathered,), (shallow_low,) = tie([gathered], [shallow_low])
    input_grad = input_grad.reshape(rows, frames, feats)
    scale = 1.0 / (jnp.sqrt(sums_one[feats + 4, :1]) + MUON_EPSILON)
    shard = deep_weight.shape[0]
    window, first_row, offset = own_window(shard, width, padded)
    ortho = newton_rows(
        gathered, scale, (first_row // 16).astype(jnp.int32).reshape(1), window
    )
    deep_ortho = lax.dynamic_slice_in_dim(ortho[:, :width].reshape(-1), offset, shard)
    deep_new = MUON_KEEP * deep_weight - MUON_RATE * deep_ortho.astype(jnp.float32)
    deep_grad = from_block(grad_block[:, :width], shard, padded)
    deep_next = MUON_BETA * deep_momentum + deep_grad

    unit_sums = sums_one[feats : feats + 4, :width]
    bias_gain_two = sums_two[:, :width]
    slope = jnp.where(
        1.0 - jnp.exp(-unit_params[:, 0]) > DECAY_FLOOR, jnp.exp(-unit_params[:, 0]), 0.0
    )
    unit_grad = jnp.stack(
        [
            jnp.stack([unit_sums[2] * slope[0], unit_sums[0], unit_sums[1], unit_sums[0]]),
            jnp.stack(
                [unit_sums[3] * slope[1], bias_gain_two[0], bias_gain_two[1], bias_gain_two[0]]
            ),
        ]
    )
    first_fix = 1.0 - FIRST_DECAY**STEP
    second_fix = 1.0 - SECOND_DECAY**STEP
    first_new = FIRST_DECAY * unit_first + (1.0 - FIRST_DECAY) * unit_grad
    second_new = SECOND_DECAY * unit_second + (1.0 - SECOND_DECAY) * unit_grad * unit_grad
    params_new = unit_params - ADAM_RATE * (first_new / first_fix) / (
        jnp.sqrt(second_new / second_fix) + ADAM_EPSILON
    )
    return (
        hidden_one.reshape(rows, frames, width),
        hidden_two.reshape(rows, frames, width),
        input_grad,
        shallow_grad,
        shallow_next,
        shallow_new,
        shallow_low,
        deep_grad,
        deep_next,
        deep_new,
        deep_new.astype(jnp.bfloat16),
        first_new,
        second_new,
        params_new,
    )


def solution(mesh):
    in_specs = (
        P(None, "tm", None),
        P(None, "tm"),
        P(),
        P(),
        P("tm"),
        P("tm"),
        P(),
        P(),
        P(),
        P(None, "tm", None),
    )
    out_specs = (
        P(None, "tm", None),
        P(None, "tm", None),
        P(None, "tm", None),
        P(),
        P(),
        P(),
        P(),
        P("tm"),
        P("tm"),
        P("tm"),
        P("tm"),
        P(),
        P(),
        P(),
    )
    return jax.shard_map(
        per_device, mesh=mesh, in_specs=in_specs, out_specs=out_specs, check_vma=False
    )
```

```python
import copy
import functools

import jax
import jax.numpy as jnp
from jax import lax
from jax.experimental import pallas as pl
from jax.experimental.pallas import tpu as pltpu
from jax.sharding import PartitionSpec as P

NS_STEPS = 2
STEP = 5


NORM_EPSILON = 1e-05
MUON_EPSILON = 1e-07
COEFF_A = 3.4445
COEFF_B = -4.775
COEFF_C = 2.0315
MUON_BETA = 0.5
MUON_RATE = 4.0
MUON_KEEP = 0.999
FIRST_DECAY = 0.9
SECOND_DECAY = 0.95
ADAM_RATE = 0.5
ADAM_EPSILON = 1e-08
DECAY_FLOOR = 0.9
LANE = 128
WIDE = 512
PART = 256
SIDE = 80


def kernel_call(body, grid, in_specs, out_specs, out_shape, scratch=(), flops=0, traffic=0):
    return pl.pallas_call(
        body,
        grid=grid,
        in_specs=in_specs,
        out_specs=out_specs,
        out_shape=out_shape,
        scratch_shapes=list(scratch),
        compiler_params=pltpu.CompilerParams(vmem_limit_bytes=56 * 1024 * 1024),
        cost_estimate=pl.CostEstimate(flops=flops, bytes_accessed=traffic, transcendentals=0),
    )


def shape_of(shape, dtype=jnp.float32):
    return jax.ShapeDtypeStruct(shape, dtype)


def whole(shape):
    return pl.BlockSpec(shape, lambda i: (0,) * len(shape))


def lanes_of(rows, width=WIDE):
    return pl.BlockSpec((rows, width), lambda i: (0, i))


def chunk_call(body, place, in_specs, out_specs, out_shape, arrays, previous, scratch=(), traffic=0):
    count = len(in_specs)
    before = list(previous) if previous is not None else []

    def run(*refs):
        body(*refs[:count], *refs[count + len(before) :])

    return pl.pallas_call(
        run,
        grid=(1,),
        in_specs=list(in_specs) + [pl.BlockSpec(memory_space=pl.ANY)] * len(before),
        out_specs=out_specs,
        out_shape=out_shape,
        scratch_shapes=list(scratch),
        input_output_aliases={count + k: k for k in range(len(before))},
        compiler_params=pltpu.CompilerParams(vmem_limit_bytes=56 * 1024 * 1024),
        cost_estimate=pl.CostEstimate(flops=0, bytes_accessed=traffic, transcendentals=0),
    )(*arrays, *before)


def chunk_at(rows, place):
    return pl.BlockSpec((rows, WIDE), lambda i: (0, place))


def rate_of(params):
    return jnp.maximum(1.0 - jnp.exp(-params[0:1]), DECAY_FLOOR)


def softened(value):
    return jnp.maximum(value, 0.0) + jnp.log(1.0 + jnp.exp(-jnp.abs(value)))


def sigmoid(value):
    return 0.5 * jnp.tanh(0.5 * value) + 0.5


def wide_keep(keep_ref, t, rows):
    keep = keep_ref[pl.ds(pl.multiple_of(t * rows, rows), rows), :]
    return jnp.concatenate([keep] * (WIDE // LANE), axis=1)


def rows_at(ref, t, rows):
    return ref[pl.ds(pl.multiple_of(t * rows, rows), rows), :]


def store_at(ref, t, rows, value):
    ref[pl.ds(pl.multiple_of(t * rows, rows), rows), :] = value


def valid_lanes(shape, total, step):
    return lax.broadcasted_iota(jnp.int32, shape, 1) + step * WIDE < total


def unit_terms(params_ref, stat_ref, total_devices, frames):
    params = params_ref[...]
    stat = stat_ref[...]
    centre = stat[0:1]
    inverse = lax.rsqrt(stat[1:2] / (total_devices * frames) + NORM_EPSILON)
    return centre, inverse, params[2:3], params[3:4] + params[1:2]


def front_body(rows, frames, width, x_ref, w_ref, xt_ref, proj_ref, stat_ref, gram_ref, padded_w):
    step = pl.program_id(0)
    count, feats = x_ref.shape

    @pl.when(step == 0)
    def _():
        i = lax.broadcasted_iota(jnp.int32, (count, count), 0)
        j = lax.broadcasted_iota(jnp.int32, (count, count), 1)
        move = (j == lax.rem(i, rows) * frames + lax.div(i, rows)).astype(jnp.bfloat16)
        moved = jnp.dot(move, x_ref[...], preferred_element_type=jnp.float32).astype(jnp.bfloat16)
        i = lax.broadcasted_iota(jnp.int32, (feats, LANE), 0)
        j = lax.broadcasted_iota(jnp.int32, (feats, LANE), 1)
        wide = jnp.dot(moved, (i == j).astype(jnp.bfloat16), preferred_element_type=jnp.float32)
        lane = lax.broadcasted_iota(jnp.int32, (count, LANE), 1)
        xt = jnp.where(lane == feats, 1.0, wide).astype(jnp.bfloat16)
        xt_ref[...] = xt
        gram = dot_tn(xt, xt)
        high = gram_ref.shape[0]
        for k in range(SIDE // high):
            gram_ref[:, k * LANE : (k + 1) * LANE] = gram[k * high : (k + 1) * high]
        padded_w[...] = jnp.zeros_like(padded_w)

    weight = w_ref[...]
    padded_w[0:feats, :] = jnp.where(valid_lanes(weight.shape, width, step), weight, 0.0)
    proj = jnp.dot(
        xt_ref[...], padded_w[...].astype(jnp.bfloat16), preferred_element_type=jnp.float32
    )
    proj_ref[...] = proj
    mean = jnp.sum(proj, axis=0, keepdims=True) * (1.0 / count)
    off = proj - mean
    stat_ref[0:1, :] = mean
    stat_ref[1:2, :] = jnp.sum(off * off, axis=0, keepdims=True)


def dot_tn(a, b):
    return lax.dot_general(a, b, (((0,), (0,)), ((), ())), preferred_element_type=jnp.float32)


def front(x, weight, rows, frames):
    count, feats = x.shape
    width = weight.shape[1]
    padded = -(-width // WIDE) * WIDE
    return kernel_call(
        functools.partial(front_body, rows, frames, width),
        (padded // WIDE,),
        [whole((count, feats)), lanes_of(feats)],
        [whole((count, LANE)), lanes_of(count), lanes_of(2), whole((2 * rows, SIDE // (2 * rows) * LANE))],
        [
            shape_of((count, LANE), jnp.bfloat16),
            shape_of((count, padded)),
            shape_of((2, padded)),
            shape_of((2 * rows, SIDE // (2 * rows) * LANE)),
        ],
        [pltpu.VMEM((LANE, WIDE), jnp.float32)],
    )(x, weight)


def delta_two_body(rows, frames, width, grad_ref, keep_ref, params_ref, delta_ref, end_ref, held):
    place = pl.program_id(0)
    pieces = WIDE // LANE
    mask = valid_lanes((rows * frames, WIDE), width, place)
    grad = jnp.where(mask, grad_ref[...].astype(jnp.float32), 0.0)
    for g in range(pieces):
        held[g] = grad[:, g * LANE : (g + 1) * LANE]
    rate = rate_of(params_ref[...])

    def body(k, carried):
        t = frames - 1 - k
        own = jnp.concatenate(
            [held[g, pl.ds(t, rows, stride=frames), :] for g in range(pieces)], axis=1
        )
        delta = own + carried
        store_at(delta_ref, t, rows, delta)
        return rate * wide_keep(keep_ref, t, rows) * delta

    end_ref[...] = lax.fori_loop(
        0, frames, body, jnp.zeros((rows, WIDE), jnp.float32), unroll=8
    )


def delta_two(out_grad, keep, params, rows, frames, padded):
    count, width = out_grad.shape
    return kernel_call(
        functools.partial(delta_two_body, rows, frames, width),
        (padded // WIDE,),
        [lanes_of(count), whole((count, LANE)), lanes_of(4)],
        [lanes_of(count), lanes_of(rows)],
        [shape_of((count, padded)), shape_of((rows, padded))],
        [pltpu.VMEM((WIDE // LANE, count, LANE), jnp.float32)],
    )(out_grad, keep, params)


def states_body(
    rows, frames, devices, proj_ref, keep_ref, params_ref, stat_ref, state_ref, end_ref
):
    centre, inverse, gain, offset = unit_terms(params_ref, stat_ref, devices, rows * frames)
    rate = rate_of(params_ref[...])
    share = 1.0 - rate

    def body(t, carried):
        gate = (rows_at(proj_ref, t, rows) - centre) * inverse * gain + offset
        soft = softened(gate)
        carried = rate * wide_keep(keep_ref, t, rows) * carried + share * soft
        store_at(state_ref, t, rows, carried)
        return carried

    end_ref[...] = lax.fori_loop(
        0, frames, body, jnp.zeros((rows, WIDE), jnp.float32), unroll=8
    )


def local_states(proj, keep, params, stat, rows, frames, devices):
    count, padded = proj.shape
    return kernel_call(
        functools.partial(states_body, rows, frames, devices),
        (padded // WIDE,),
        [lanes_of(count), whole((count, LANE)), lanes_of(4), lanes_of(2)],
        [lanes_of(count), lanes_of(rows)],
        [shape_of((count, padded)), shape_of((rows, padded))],
    )(proj, keep, params, stat)


def to_slots(value, group):
    pieces = value.shape[1] // LANE
    lane = lax.broadcasted_iota(jnp.int32, (value.shape[0], LANE), 1)
    parts = [value[:, g * LANE : (g + 1) * LANE] for g in range(pieces)]
    out = []
    for g in range(pieces):
        moved = (LANE - group) * g
        if moved == 0:
            new = parts[g]
        else:
            new = jnp.where(
                lane < moved, pltpu.roll(parts[g - 1], moved, 1), pltpu.roll(parts[g], moved, 1)
            )
        out.append(jnp.where(lane < group, new, 0.0))
    return jnp.concatenate(out, axis=1)


def from_slots(value, group, width):
    pieces = value.shape[1] // LANE
    lane = lax.broadcasted_iota(jnp.int32, (value.shape[0], LANE), 1)
    parts = [value[:, g * LANE : (g + 1) * LANE] for g in range(pieces)]
    out = []
    for j in range(pieces):
        moved = (LANE - group) * j
        new = parts[j] if moved == 0 else pltpu.roll(parts[j], LANE - moved, 1)
        if j + 1 < pieces:
            new = jnp.where(lane < group - moved, new, pltpu.roll(parts[j + 1], group - moved, 1))
        left = width - j * LANE
        out.append(new if left >= LANE else jnp.where(lane < left, new, 0.0))
    return jnp.concatenate(out, axis=1)


def low_one_body(rows, frames, width, group, state_ref, start_ref, keep_ref, params_ref, low_ref, mean_ref):
    pieces = state_ref.shape[1] // LANE
    rate = rate_of(params_ref[...])

    def advance(t, carried):
        keep = rows_at(keep_ref, t, rows)
        carried = rate * jnp.concatenate([keep] * pieces, axis=1) * carried
        return carried, rows_at(state_ref, t, rows) + carried

    def body(k, both):
        carried, total = both
        t = 2 * k
        carried, first = advance(t, carried)
        carried, second = advance(t + 1, carried)
        place = pl.ds(pl.multiple_of(t * rows, 2 * rows), 2 * rows)
        slots = to_slots(jnp.concatenate([first, second], axis=0), group)
        low_ref[place, :] = slots.astype(jnp.bfloat16)
        return carried, total + slots[:rows] + slots[rows:]

    start = start_ref[...]
    _, total = lax.fori_loop(0, frames // 2, body, (start, jnp.zeros_like(start)), unroll=4)
    mean_ref[...] = jnp.sum(total, axis=0, keepdims=True) * (1.0 / (rows * frames))


def low_one_of(states, start, keep, params, rows, frames, width, group):
    count, padded = states.shape
    return kernel_call(
        functools.partial(low_one_body, rows, frames, width, group),
        (1,),
        [whole((count, padded)), whole((rows, padded)), whole((count, LANE)), whole((4, padded))],
        [whole((count, padded)), whole((1, padded))],
        [shape_of((count, padded), jnp.bfloat16), shape_of((1, padded))],
    )(states, start, keep, params)


def hidden_body(rows, frames, state_ref, start_ref, keep_ref, params_ref, hidden_ref, held):
    pieces = WIDE // LANE
    rate = rate_of(params_ref[...])

    def body(t, carry):
        carry = rate * wide_keep(keep_ref, t, rows) * carry
        state = rows_at(state_ref, t, rows) + carry
        for g in range(pieces):
            held[g, pl.ds(pl.multiple_of(t * rows, rows), rows), :] = state[
                :, g * LANE : (g + 1) * LANE
            ]
        return carry

    lax.fori_loop(0, frames, body, start_ref[...], unroll=8)
    for r in range(rows):
        for g in range(pieces):
            hidden_ref[r * frames : (r + 1) * frames, g * LANE : (g + 1) * LANE] = held[
                g, pl.ds(r, frames, stride=rows), :
            ]


def hidden_of(place, previous, states, start, keep, params, rows, frames, width):
    count, _ = states.shape
    return chunk_call(
        functools.partial(hidden_body, rows, frames),
        place,
        [chunk_at(count, place), chunk_at(rows, place), whole((count, LANE)), chunk_at(4, place)],
        [chunk_at(count, place)],
        [shape_of((count, width))],
        (states, start, keep, params),
        previous,
        [pltpu.VMEM((WIDE // LANE, count, LANE), jnp.float32)],
    )


def second_body(low_ref, weight_ref, proj_ref, stat_ref):
    tile = 256
    count = proj_ref.shape[0]
    for j in range(0, WIDE, tile):
        place = slice(j, j + tile)
        for i in range(0, count, tile):
            proj_ref[i : i + tile, place] = jnp.dot(
                low_ref[i : i + tile, :], weight_ref[:, place], preferred_element_type=jnp.float32
            )
        proj = proj_ref[:, place]
        mean = jnp.sum(proj, axis=0, keepdims=True) * (1.0 / count)
        off = proj - mean
        stat_ref[0:1, place] = mean
        stat_ref[1:2, place] = jnp.sum(off * off, axis=0, keepdims=True)


def second_forward(low, weight):
    count, padded = low.shape
    return kernel_call(
        second_body,
        (padded // WIDE,),
        [whole((count, padded)), lanes_of(padded)],
        [lanes_of(count), lanes_of(2)],
        [shape_of((count, padded)), shape_of((2, padded))],
    )(low, weight)


def gate_two_body(
    rows, frames, devices, proj_ref, delta_ref, start_ref, keep_ref, params_ref, stat_ref, gate_ref, sums_ref
):
    centre, inverse, gain, offset = unit_terms(params_ref, stat_ref, devices, rows * frames)
    rate = rate_of(params_ref[...])
    share = 1.0 - rate
    none = jnp.zeros((rows, WIDE), jnp.float32)

    def body(k, carried):
        carry, bias_sum, gain_sum = carried
        t = frames - 1 - k
        delta = rows_at(delta_ref, t, rows) + carry
        normed = (rows_at(proj_ref, t, rows) - centre) * inverse
        gate = share * delta * sigmoid(normed * gain + offset)
        store_at(gate_ref, t, rows, gate)
        carry = rate * wide_keep(keep_ref, t, rows) * carry
        return carry, bias_sum + gate, gain_sum + gate * normed

    _, bias_sum, gain_sum = lax.fori_loop(
        0, frames, body, (start_ref[...], none, none), unroll=8
    )
    sums_ref[0:1, :] = jnp.sum(bias_sum, axis=0, keepdims=True)
    sums_ref[1:2, :] = jnp.sum(gain_sum, axis=0, keepdims=True)


def gate_two(proj, delta, start, keep, params, stat, rows, frames, devices):
    count, padded = proj.shape
    return kernel_call(
        functools.partial(gate_two_body, rows, frames, devices),
        (padded // WIDE,),
        [lanes_of(count), lanes_of(count), lanes_of(rows), whole((count, LANE)), lanes_of(4), lanes_of(2)],
        [lanes_of(count), lanes_of(2)],
        [shape_of((count, padded)), shape_of((2, padded))],
    )(proj, delta, start, keep, params, stat)


def states_two_body(
    rows, frames, devices, proj_ref, delta_ref, start_ref, keep_ref, params_ref, stat_ref,
    state_ref, end_ref, decay_ref, held,
):
    centre, inverse, gain, offset = unit_terms(params_ref, stat_ref, devices, rows * frames)
    rate = rate_of(params_ref[...])
    share = 1.0 - rate
    none = jnp.zeros((rows, WIDE), jnp.float32)

    def backward(k, carry):
        t = frames - 1 - k
        store_at(held, t, rows, rows_at(delta_ref, t, rows) + carry)
        return rate * wide_keep(keep_ref, t, rows) * carry

    lax.fori_loop(0, frames, backward, start_ref[...], unroll=8)

    def forward(t, carried):
        state, reach, decay, factor = carried
        keep = wide_keep(keep_ref, t, rows)
        delta = rows_at(held, t, rows)
        value = (rows_at(proj_ref, t, rows) - centre) * inverse * gain + offset
        soft = softened(value)
        decay = decay + delta * (keep * state - soft)
        factor = factor + delta * keep * reach
        state = rate * keep * state + share * soft
        reach = rate * keep * reach
        store_at(state_ref, t, rows, state)
        return state, reach, decay, factor

    state, _, decay, factor = lax.fori_loop(
        0, frames, forward, (none, jnp.ones_like(none), none, none), unroll=4
    )
    end_ref[...] = state
    decay_ref[0:rows, :] = decay
    decay_ref[rows : 2 * rows, :] = factor


def states_two(proj, delta, start, keep, params, stat, rows, frames, devices):
    count, padded = proj.shape
    return kernel_call(
        functools.partial(states_two_body, rows, frames, devices),
        (padded // WIDE,),
        [
            lanes_of(count),
            lanes_of(count),
            lanes_of(rows),
            whole((count, LANE)),
            lanes_of(4),
            lanes_of(2),
        ],
        [lanes_of(count), lanes_of(rows), lanes_of(2 * rows)],
        [shape_of((count, padded)), shape_of((rows, padded)), shape_of((2 * rows, padded))],
        [pltpu.VMEM((count, WIDE), jnp.float32)],
    )(proj, delta, start, keep, params, stat)


def turn_body(low_ref, mean_ref, turned_ref):
    half = LANE // 2
    turned = (low_ref[...].astype(jnp.float32) - mean_ref[...]).T.astype(jnp.bfloat16)
    for g in range(WIDE // LANE):
        for side in range(2):
            turned_ref[side, g * half : (g + 1) * half, :] = turned[
                g * LANE + side * half : g * LANE + (side + 1) * half
            ]


def turn(place, previous, low, mean):
    count, padded = low.shape
    return chunk_call(
        turn_body,
        place,
        [chunk_at(count, place), chunk_at(1, place)],
        [pl.BlockSpec((2, WIDE // 2, count), lambda i: (0, place, 0))],
        [shape_of((2, padded // 2, count), jnp.bfloat16)],
        (low, mean),
        previous,
    )


def deep_term_body(
    rows, frames, devices, parts, orders, side_ref, gate_ref, proj_ref, params_ref, stat_ref, sums_ref,
    turned_ref, grad_ref, total_ref, *outs,
):
    step = pl.program_id(0)
    total = devices * rows * frames
    centre, inverse, gain, _ = unit_terms(params_ref, stat_ref, devices, rows * frames)
    sums = sums_ref[...] * (1.0 / total)
    normed = (proj_ref[...] - centre) * inverse
    grad = (gain * inverse * (gate_ref[...] - sums[0:1] - normed * sums[1:2])).astype(jnp.bfloat16)
    grad_ref[...] = grad
    total_ref[...] = jnp.sum(grad.astype(jnp.float32), axis=0, keepdims=True)
    side = side_ref[0]
    half = turned_ref.shape[1]
    tile = 256
    for p, (first, lanes) in enumerate(parts):

        @pl.when((step >= first // PART) & (step < (first + lanes) // PART))
        def _():
            for which, out_ref in ((side, outs[p]), (1 - side, outs[len(parts) + p])):
                for k in range(half // tile):
                    part = jnp.dot(
                        turned_ref[which, k * tile : (k + 1) * tile, :],
                        grad_ref[...],
                        preferred_element_type=jnp.float32,
                    ).astype(out_ref.dtype)
                    if orders is None:
                        out_ref[k * tile : (k + 1) * tile, :] = part
                        continue
                    slots = half // 2 ** len(orders[p])
                    for b in range(tile // slots):
                        block = k * (tile // slots) + b
                        place = 0
                        for weight in orders[p]:
                            place = 2 * place + block // weight % 2
                        out_ref[place * slots : (place + 1) * slots, :] = part[
                            b * slots : (b + 1) * slots
                        ]


def deep_term(parts, orders, side, gate, proj, params, stat, sums, turned, rows, frames, devices):
    count, padded = proj.shape
    half = padded // 2

    def some(first, lanes):
        return pl.BlockSpec(
            (half, PART), lambda i: (0, jnp.clip(i - first // PART, 0, lanes // PART - 1))
        )

    found = kernel_call(
        functools.partial(deep_term_body, rows, frames, devices, parts, orders),
        (padded // PART,),
        [
            pl.BlockSpec(memory_space=pltpu.SMEM),
            lanes_of(count, PART),
            lanes_of(count, PART),
            lanes_of(4, PART),
            lanes_of(2, PART),
            lanes_of(2, PART),
            whole((2, half, count)),
        ],
        [lanes_of(count, PART), lanes_of(1, PART)] + [some(*part) for part in parts] * 2,
        [shape_of((count, padded), jnp.bfloat16), shape_of((1, padded))]
        + [shape_of((half, lanes), jnp.bfloat16) for _, lanes in parts] * 2,
    )(side, gate, proj, params, stat, sums, turned)
    return found[0], found[1], found[2 : 2 + len(parts)], found[2 + len(parts) :]


def back_body(grad_ref, weight_ref, back_ref):
    back_ref[...] = dot_nt(grad_ref[...], weight_ref[...])


def back_one(grad, weight):
    count, padded = grad.shape
    return kernel_call(
        back_body,
        (padded // WIDE,),
        [whole((count, padded)), pl.BlockSpec((WIDE, padded), lambda i: (i, 0))],
        lanes_of(count),
        shape_of((count, padded)),
    )(grad, weight)


def delta_one_body(rows, frames, width, group, back_ref, keep_ref, params_ref, delta_ref, end_ref):
    pieces = back_ref.shape[1] // LANE
    rate = rate_of(params_ref[...])

    def body(k, carried):
        t = frames - 1 - k
        delta = from_slots(rows_at(back_ref, t, rows), group, width) + carried
        store_at(delta_ref, t, rows, delta)
        keep = rows_at(keep_ref, t, rows)
        return rate * jnp.concatenate([keep] * pieces, axis=1) * delta

    end_ref[...] = lax.fori_loop(
        0, frames, body, jnp.zeros((rows, back_ref.shape[1]), jnp.float32), unroll=2
    )


def delta_one(back, keep, params, rows, frames, width, group):
    count, padded = back.shape
    return kernel_call(
        functools.partial(delta_one_body, rows, frames, width, group),
        (1,),
        [whole((count, padded)), whole((count, LANE)), whole((4, padded))],
        [whole((count, padded)), whole((rows, padded))],
        [shape_of((count, padded)), shape_of((rows, padded))],
    )(back, keep, params)


def gate_one_body(
    rows,
    frames,
    devices,
    feats,
    width,
    proj_ref,
    state_ref,
    first_ref,
    delta_ref,
    start_ref,
    keep_ref,
    params_ref,
    stat_ref,
    x_ref,
    w_ref,
    sums_ref,
    back_ref,
    mean_ref,
    held,
    gate_ref,
    padded_w,
):
    step = pl.program_id(0)
    centre, inverse, gain, offset = unit_terms(params_ref, stat_ref, devices, rows * frames)
    rate = rate_of(params_ref[...])
    share = 1.0 - rate
    none = jnp.zeros((rows, WIDE), jnp.float32)

    def backward(k, carry):
        t = frames - 1 - k
        store_at(held, t, rows, rows_at(delta_ref, t, rows) + carry)
        return rate * wide_keep(keep_ref, t, rows) * carry

    lax.fori_loop(0, frames, backward, start_ref[...], unroll=8)

    def forward(t, carried):
        carry, before, bias_sum, gain_sum, decay_sum = carried
        keep = wide_keep(keep_ref, t, rows)
        delta = rows_at(held, t, rows)
        normed = (rows_at(proj_ref, t, rows) - centre) * inverse
        value = normed * gain + offset
        soft = softened(value)
        gate = share * delta * sigmoid(value)
        store_at(gate_ref, t, rows, gate)
        decay_sum = decay_sum + delta * (keep * before - soft)
        carry = rate * keep * carry
        before = rows_at(state_ref, t, rows) + carry
        return carry, before, bias_sum + gate, gain_sum + gate * normed, decay_sum

    first = first_ref[...]
    _, _, bias_sum, gain_sum, decay_sum = lax.fori_loop(
        0, frames, forward, (first, first, none, none, none), unroll=4
    )
    bias = jnp.sum(bias_sum, axis=0, keepdims=True)
    mean = bias * (1.0 / (rows * frames))
    x = x_ref[...]
    ones = jnp.ones((rows * frames, LANE), jnp.bfloat16)
    total = jnp.concatenate([dot_tn(x, ones)] * (WIDE // LANE), axis=1)
    centred = gate_ref[...] - mean
    term = dot_tn(x, centred.astype(jnp.bfloat16)) + total * mean
    sums_ref[...] = term[: sums_ref.shape[0]]
    sums_ref[feats : feats + 1, :] = bias
    sums_ref[feats + 1 : feats + 2, :] = jnp.sum(gain_sum, axis=0, keepdims=True)
    sums_ref[feats + 2 : feats + 3, :] = jnp.sum(decay_sum, axis=0, keepdims=True)
    mean_ref[...] = mean
    weight = w_ref[...]
    padded_w[...] = jnp.zeros_like(padded_w)
    padded_w[0:feats, :] = jnp.where(valid_lanes(weight.shape, width, step), weight, 0.0)
    part = dot_nt(
        (gain * inverse * centred).astype(jnp.bfloat16), padded_w[...].astype(jnp.bfloat16)
    )

    @pl.when(step == 0)
    def _():
        back_ref[...] = part

    @pl.when(step > 0)
    def _():
        back_ref[...] += part


def gate_one(proj, states, first, delta, start, keep, params, stat, x, weight, rows, frames, devices):
    count, padded = proj.shape
    feats, width = weight.shape
    return kernel_call(
        functools.partial(gate_one_body, rows, frames, devices, feats, width),
        (padded // WIDE,),
        [
            lanes_of(count),
            lanes_of(count),
            lanes_of(rows),
            lanes_of(count),
            lanes_of(rows),
            whole((count, LANE)),
            lanes_of(4),
            lanes_of(2),
            whole((count, LANE)),
            lanes_of(feats),
        ],
        [lanes_of(SIDE), whole((count, LANE)), lanes_of(1)],
        [shape_of((SIDE, padded)), shape_of((count, LANE)), shape_of((1, padded))],
        [
            pltpu.VMEM((count, WIDE), jnp.float32),
            pltpu.VMEM((count, WIDE), jnp.float32),
            pltpu.VMEM((LANE, WIDE), jnp.float32),
        ],
    )(proj, states, first, delta, start, keep, params, stat, x, weight)


def dot_nt(a, b):
    return lax.dot_general(a, b, (((1,), (1,)), ((), ())), preferred_element_type=jnp.float32)


def shallow_body(
    total, rows, frames, sums_ref, gram_ref, params_ref, stat_ref, w_ref, m_ref, x_ref, back_ref, mean_ref,
    grad_ref, next_ref, new_ref, low_ref, input_ref, held, moved,
):
    feats, width = w_ref.shape
    count = rows * frames
    centre, inverse, gain, _ = unit_terms(params_ref, stat_ref, total // count, count)
    weight = w_ref[...]
    held[...] = jnp.zeros_like(held)
    held[0:feats, 0:width] = weight
    low = held[...].astype(jnp.bfloat16).astype(jnp.float32)
    high = gram_ref.shape[0]
    gram = jnp.concatenate(
        [gram_ref[:, k * LANE : (k + 1) * LANE] for k in range(SIDE // high)], axis=0
    )
    lane = lax.broadcasted_iota(jnp.int32, gram.shape, 1)
    x_sum = jnp.sum(jnp.where(lane == feats, gram, 0.0), axis=1, keepdims=True)
    raw = jnp.dot(
        gram, low, precision=lax.Precision.HIGHEST, preferred_element_type=jnp.float32
    )
    normed = (raw - x_sum * centre) * inverse
    bias = sums_ref[feats : feats + 1, :] * (1.0 / total)
    slope = sums_ref[feats + 1 : feats + 2, :] * (1.0 / total)
    scaled = gain * inverse
    grad = scaled * (sums_ref[...] - x_sum * bias - normed * slope)
    grad = grad[:feats, :width]
    grad_ref[...] = grad

    row = lax.broadcasted_iota(jnp.int32, low.shape, 0)
    turn = slope * inverse
    left = jnp.where(
        row == feats, scaled * (mean_ref[...] - bias + turn * centre), -low * (scaled * turn)
    )
    matrix = lax.dot_general(
        left, low, (((1,), (1,)), ((), ())),
        precision=lax.Precision.HIGHEST, preferred_element_type=jnp.float32,
    )
    moved[...] = back_ref[...] + jnp.dot(
        x_ref[...].astype(jnp.float32), matrix,
        precision=lax.Precision.HIGHEST, preferred_element_type=jnp.float32,
    )
    for r in range(rows):
        input_ref[r * frames : (r + 1) * frames, :] = moved[pl.ds(r, frames, stride=rows), :][:, :feats]

    following = MUON_BETA * m_ref[...] + grad
    next_ref[...] = following
    held[0:feats, 0:width] = following
    m = held[0:SIDE, :]
    current = (m / (jnp.sqrt(jnp.sum(m * m)) + MUON_EPSILON)).astype(jnp.bfloat16)
    for repeat in range(NS_STEPS):
        gram = dot_nt(current, current).astype(jnp.bfloat16)
        square = jnp.dot(gram, gram, preferred_element_type=jnp.float32)
        mixing = (COEFF_B * gram.astype(jnp.float32) + COEFF_C * square).astype(jnp.bfloat16)
        current = (
            COEFF_A * current.astype(jnp.float32)
            + jnp.dot(mixing, current, preferred_element_type=jnp.float32)
        ).astype(jnp.bfloat16)
    new = MUON_KEEP * weight - MUON_RATE * current[:feats, :width].astype(jnp.float32)
    new_ref[...] = new
    low_ref[...] = new.astype(jnp.bfloat16)


def shallow_step(sums, gram, params, stat, weight, momentum, x, back, mean, total, rows, frames):
    padded = sums.shape[1]
    some = shape_of(weight.shape)
    feats = weight.shape[0]
    arrays = (sums, gram, params, stat, weight, momentum, x, back, mean)
    return kernel_call(
        functools.partial(shallow_body, total, rows, frames),
        (1,),
        [whole(value.shape) for value in arrays],
        [whole(weight.shape)] * 4 + [whole((rows * frames, feats))],
        [some, some, some, shape_of(weight.shape, jnp.bfloat16), shape_of((rows * frames, feats))],
        [pltpu.VMEM((LANE, padded), jnp.float32), pltpu.VMEM((rows * frames, LANE), jnp.float32)],
    )(*arrays)


def newton_body(window, tile, first_ref, scale_ref, start_ref, out_ref, m_ref, gram, sems):
    size = m_ref.shape[0]
    blocks = size // tile

    def place(k):
        return slice(k * tile, (k + 1) * tile)

    copies = [
        pltpu.make_async_copy(start_ref.at[place(k), :], m_ref.at[place(k), :], sems.at[k])
        for k in range(blocks)
    ]
    for copy in copies:
        copy.start()
    scale = scale_ref[0]
    square_scale = scale * scale
    for j in range(blocks):
        copies[j].wait()
        for i in range(j + 1):
            part = dot_nt(m_ref[place(i), :], m_ref[place(j), :]) * square_scale
            gram[place(i), place(j)] = part.astype(jnp.bfloat16)
            if i != j:
                gram[place(j), place(i)] = part.T.astype(jnp.bfloat16)
    def taken(ref):
        return ref[pl.ds(pl.multiple_of(first_ref[0] * 16, 16), window), :].astype(jnp.float32)

    def times(value, ref):
        return jnp.dot(value.astype(jnp.bfloat16), ref[...], preferred_element_type=jnp.float32)

    def mixed(once):
        return COEFF_B * once + COEFF_C * times(once, gram)

    def stepped(value):
        return COEFF_A * value + mixed(times(value, gram))

    gram_own = taken(gram)
    mixing_own = mixed(gram_own)
    gram_own = stepped(COEFF_A * gram_own + times(mixing_own, gram))
    square_own = stepped(times(stepped(gram_own), gram))
    second_own = COEFF_B * gram_own + COEFF_C * square_own
    weights = COEFF_A * mixing_own + stepped(second_own)
    result = COEFF_A * COEFF_A * taken(m_ref) + times(weights, m_ref)
    out_ref[...] = (scale * result).astype(jnp.bfloat16)


def newton_rows(start, scale, first, window):
    size = start.shape[0]
    tile = 256
    scalar = pl.BlockSpec(memory_space=pltpu.SMEM)
    return kernel_call(
        functools.partial(newton_body, window, tile),
        (1,),
        [scalar, scalar, pl.BlockSpec(memory_space=pl.ANY)],
        whole((window, size)),
        shape_of((window, size), jnp.bfloat16),
        [pltpu.VMEM((size, size), jnp.bfloat16)] * 2 + [pltpu.SemaphoreType.DMA((size // tile,))],
    )(first, scale, start)


def swap(value, bit):
    size = lax.axis_size("tm")
    return lax.ppermute(value, "tm", [(i, i ^ bit) for i in range(size)])


def steps_of(size):
    bits = []
    bit = 1
    while bit < size:
        bits.append(bit)
        bit *= 2
    return bits


def bit_of(bit):
    return jnp.where((lax.axis_index("tm") & bit) != 0, 1, 0)


class SumSpread:
    def __init__(self, value):
        self.value = value
        self.steps = []
        lanes = value.shape[1]
        cuts = []
        for bit in steps_of(lax.axis_size("tm")):
            if lanes // 2 % WIDE == 0:
                lanes //= 2
                self.steps.append((self.halve, bit))
                cuts.append(bit)
            else:
                self.steps.append((self.pair, bit))
        self.steps += [(self.join, bit) for bit in reversed(cuts)]

    def halve(self, bit):
        lanes = self.value.shape[1] // 2
        mine = lax.dynamic_slice_in_dim(self.value, bit_of(bit) * lanes, lanes, 1)
        away = lax.dynamic_slice_in_dim(self.value, (1 - bit_of(bit)) * lanes, lanes, 1)
        self.value = mine + swap(away, bit)

    def pair(self, bit):
        self.value = self.value + swap(self.value, bit)

    def join(self, bit):
        other = swap(self.value, bit)
        upper = bit_of(bit) == 1
        self.value = jnp.concatenate(
            [jnp.where(upper, other, self.value), jnp.where(upper, self.value, other)], axis=1
        )

    def step(self, times=1):
        for _ in range(times):
            if self.steps:
                action, bit = self.steps.pop(0)
                action(bit)


def tie(first, second):
    return lax.optimization_barrier((list(first), list(second)))


def side_bit():
    return lax.axis_size("tm") // 32


def orders_of(size):
    bits = [bit for bit in steps_of(size) if bit != side_bit()]
    return [bits[k * len(bits) // 3 :] + bits[: k * len(bits) // 3] for k in range(3)]


def index_bits(bits):
    return [bit if bit < side_bit() else bit // 2 for bit in bits]


class Scatter:
    def __init__(self, keeps, sends):
        self.orders = orders_of(lax.axis_size("tm"))
        self.current = list(keeps)
        self.received = [swap(send, side_bit()) for send in sends]

    def step(self, *waiting):
        sends = []
        for p, order in enumerate(self.orders):
            half = self.current[p].shape[0] // 2
            mine, away = [
                lax.dynamic_slice_in_dim(self.current[p], half * index, half).astype(jnp.float32)
                + lax.dynamic_slice_in_dim(self.received[p], half * index, half).astype(jnp.float32)
                for index in (bit_of(order[0]), 1 - bit_of(order[0]))
            ]
            self.current[p] = mine
            sends.append(away.astype(jnp.bfloat16))
        sends, waiting = tie(sends, waiting)
        self.received = [swap(send, order.pop(0)) for send, order in zip(sends, self.orders)]
        return waiting

    def join(self, *done):
        self.received, done = tie(self.received, done)
        return done

    def result(self):
        return [a + b.astype(jnp.float32) for a, b in zip(self.current, self.received)]


class Stats:
    def __init__(self, stat, count):
        self.stat = stat
        self.count = float(count)
        self.bits = steps_of(lax.axis_size("tm"))

    def step(self, times=1):
        for _ in range(min(times, len(self.bits))):
            stat = self.stat
            other = swap(stat, self.bits.pop(0))
            gap = stat[0:1] - other[0:1]
            mean = 0.5 * (stat[0:1] + other[0:1])
            square = (stat[1:2] + other[1:2]) + gap * gap * (0.5 * self.count)
            self.stat = jnp.concatenate([mean, square, 0.5 * (stat[2:] + other[2:])], axis=0)
            self.count *= 2


class Exchange:
    def __init__(self, flags, carries, sums=()):
        self.bits = steps_of(lax.axis_size("tm"))
        high, self.width = carries[0][0].shape
        rows = high * len(carries)
        flags = jnp.broadcast_to(jnp.tile(flags, len(carries))[:, None], (rows, LANE))
        ends = jnp.concatenate([ends for ends, _, _ in carries], axis=0)
        self.payload = jnp.concatenate([ends, flags, *sums], axis=1)
        self.power = jnp.concatenate(
            [jnp.broadcast_to(power, (high, self.width)) for _, power, _ in carries], axis=0
        )
        self.lane = lax.broadcasted_iota(jnp.int32, self.payload.shape, 1)
        self.high = high
        self.reverse = [reverse for _, _, reverse in carries]
        self.before = jnp.zeros_like(ends)
        self.before_keep = jnp.ones_like(ends)

    def step(self, times=1):
        for _ in range(min(times, len(self.bits))):
            self.one()

    def one(self):
        bit = self.bits.pop(0)
        width = self.width
        mine, other = self.payload, swap(self.payload, bit)
        upper = bit_of(bit)
        row = lax.broadcasted_iota(jnp.int32, (len(mine), 1), 0) // self.high
        turned = sum((row == k) * int(reverse) for k, reverse in enumerate(self.reverse))
        following = turned != upper
        other_total = other[:, :width]
        keep_mine, keep_other = mine[:, width : width + 1], other[:, width : width + 1]
        self.before = jnp.where(
            following, self.before_keep * other_total + self.before, self.before
        )
        self.before_keep = jnp.where(
            following, self.before_keep * keep_other * self.power, self.before_keep
        )
        power = jnp.pad(self.power, ((0, 0), (0, mine.shape[1] - width)))
        carried = jnp.where(
            following, keep_mine * power * other + mine, keep_other * power * mine + other
        )
        self.payload = jnp.where(
            self.lane < width,
            carried,
            jnp.where(self.lane < width + LANE, mine * other, mine + other),
        )
        self.power = self.power * self.power

    def parts(self):
        found = []
        for k, reverse in enumerate(self.reverse):
            part = copy.copy(self)
            place = slice(k * self.high, (k + 1) * self.high)
            part.bits = list(self.bits)
            part.payload, part.power, part.lane = [
                value[place] for value in (self.payload, self.power, self.lane)
            ]
            part.before, part.before_keep = self.before[place], self.before_keep[place]
            part.reverse = [reverse]
            found.append(part)
        return found

    def arrived(self, k):
        return self.before[k * self.high : (k + 1) * self.high]

    def sums(self):
        return self.payload[:, self.width + LANE :]


class SumAll:
    def __init__(self, value):
        self.value = value
        self.bits = steps_of(lax.axis_size("tm"))

    def step(self, times=1):
        for _ in range(min(times, len(self.bits))):
            self.value = self.value + swap(self.value, self.bits.pop(0))


def in_order(value, bits, slots):
    count = len(bits)
    axes = [count - bit.bit_length() for bit in bits]
    shape = (2,) * count + (slots, value.shape[1])
    return value.reshape(shape).transpose(axes + [count, count + 1]).reshape(value.shape)


def pad_lanes(value, padded):
    gap = padded - value.shape[-1]
    return jnp.pad(value, [(0, 0)] * (value.ndim - 1) + [(0, gap)])


def flat_places(shard, width, padded):
    size = lax.axis_size("tm")
    members = size * LANE // padded
    slots = LANE // members
    return members, slots, slots * width - shard


def to_block(flat, width, padded):
    size, mine = lax.axis_size("tm"), lax.axis_index("tm")
    members, slots, excess = flat_places(flat.shape[0], width, padded)
    lacking = excess * (members - 1)
    pairs = [(i + 1, i) for i in range(size - 1) if (i + 1) % members]
    extra = lax.ppermute(flat[:lacking], "tm", pairs)
    tail = jnp.zeros((excess,), flat.dtype)
    held = jnp.concatenate([flat, extra, tail])
    return lax.dynamic_slice_in_dim(held, excess * (mine % members), slots * width).reshape(
        slots, width
    )


def from_block(block, shard, padded):
    width = block.shape[1]
    size, mine = lax.axis_size("tm"), lax.axis_index("tm")
    members, slots, excess = flat_places(shard, width, padded)
    lacking = excess * (members - 1)
    pairs = [(i, i + 1) for i in range(size - 1) if (i + 1) % members]
    flat = block.reshape(-1)
    extra = lax.ppermute(flat[slots * width - lacking :], "tm", pairs)
    held = jnp.concatenate([extra, flat])
    return lax.dynamic_slice_in_dim(held, lacking - excess * (mine % members), shard)


def own_window(shard, width, padded):
    mine = lax.axis_index("tm")
    members, _, _ = flat_places(shard, width, padded)
    window = 16
    for k in range(members):
        first = shard * k // width // 16 * 16
        last = -(-shard * (k + 1) // width)
        window = max(window, -(-(last - first) // 16) * 16)
    member = mine % members
    first = jnp.minimum(shard * member // width // 16 * 16, LANE - window)
    return window, LANE * (mine // members) + first, shard * member - first * width


def per_device(
    inputs,
    clip_start,
    shallow_weight,
    shallow_momentum,
    deep_weight,
    deep_momentum,
    unit_params,
    unit_first,
    unit_second,
    out_grad,
):
    devices = lax.axis_size("tm")
    rows, frames, feats = inputs.shape
    width = shallow_weight.shape[1]
    padded = -(-width // WIDE) * WIDE
    group = width // (padded // LANE)
    count = rows * frames
    keep_mask = (1 - clip_start).astype(jnp.float32)
    flags = jnp.min(keep_mask, axis=1)
    keep = jnp.broadcast_to(keep_mask.T.reshape(count, 1), (count, LANE))
    params = pad_lanes(unit_params, padded)
    rates = jnp.maximum(1.0 - jnp.exp(-params[:, 0:1]), DECAY_FLOOR)
    powers = rates
    for _ in range(frames.bit_length() - 1):
        powers = powers * powers

    deep_block = pad_lanes(to_block(deep_weight.astype(jnp.bfloat16), width, padded), padded)
    momentum_block = pad_lanes(to_block(deep_momentum, width, padded), padded)

    shares = [3 * padded // 8, 3 * padded // 8, padded // 4]
    parts = [(sum(shares[:p]), shares[p]) for p in range(3)]
    side = bit_of(side_bit()).astype(jnp.int32).reshape(1)
    chunks = padded // WIDE
    orders = orders_of(devices)
    x, proj_one, stat_one, gram = front(
        inputs.reshape(count, feats), shallow_weight, rows, frames
    )
    (deep_block,), (stat_one,) = tie([deep_block], [stat_one])
    deep_low = lax.all_gather(deep_block, "tm", axis=0, tiled=True)
    stats = Stats(stat_one, count)
    stats.step()
    delta_local, delta_end = delta_two(
        out_grad.reshape(count, width), keep, params[1], rows, frames, padded
    )
    (delta_local, delta_end), (stats.stat,) = tie([delta_local, delta_end], [stats.stat])
    stats.step(len(stats.bits))
    (stat_one,), (momentum_block,) = tie([stats.stat], [momentum_block])
    state_local, state_end = local_states(
        proj_one, keep, params[0], stat_one, rows, frames, devices
    )
    carries = Exchange(flags, [(state_end, powers[0], False), (delta_end, powers[1], True)])
    carries.step(len(carries.bits) - 2)
    carries, later = carries.parts()
    carries.step(len(carries.bits))
    (state_in,), (later.payload,) = tie([carries.arrived(0)], [later.payload])
    low_one, mean_one = low_one_of(
        state_local, state_in, keep, params[0], rows, frames, width, group
    )
    (low_one, mean_one), (later.payload,) = tie([low_one, mean_one], [later.payload])
    later.step()
    proj_two, stat_two = second_forward(low_one, deep_low)
    (stat_two,), (later.payload, later.before) = tie([stat_two], [later.payload, later.before])
    stats = Stats(jnp.concatenate([stat_two, mean_one], axis=0), count)
    later.step()
    stats.step()
    (stats.stat,), (later.payload, later.before) = tie([stats.stat], [later.payload, later.before])
    delta_in = later.arrived(0)
    hidden = [None, None]
    sources = [(state_local, state_in, params[0]), None]

    def next_hidden(layer, places, waiting, beside=False):
        states, start, layer_params = sources[layer]
        for k in places:
            if not beside:
                (start,), waiting = tie([start], waiting)
            hidden[layer] = hidden_of(
                k, hidden[layer], states, start, keep, layer_params, rows, frames, width
            )
        hidden[layer], waiting = tie(hidden[layer], waiting)
        return waiting

    for k in range(chunks):
        stats.step()
        (stats.stat,) = next_hidden(0, [k], [stats.stat], True)
    stats.step(len(stats.bits))
    stat_two, mean_one = stats.stat[:2], stats.stat[2:]
    gate, sums_two = gate_two(
        proj_two, delta_local, delta_in, keep, params[1], stat_two, rows, frames, devices
    )
    sums = SumAll(sums_two)
    turned = None
    for k in range(chunks):
        sums.step()
        turned = turn(k, turned, low_one, mean_one)
        turned, (sums.value,) = tie(turned, [sums.value])
    sums.step(len(sums.bits))
    sums_two = sums.value
    slots = padded // devices
    weights = [index_bits(order) for order in orders]
    aligned = slots % 16 == 0
    grad_two, total_two, keeps, sends = deep_term(
        parts, weights if aligned else None, side, gate, proj_two, params[1], stat_two,
        sums_two, turned[0], rows, frames, devices,
    )
    if not aligned:
        keeps = [in_order(keep, order, slots) for keep, order in zip(keeps, weights)]
        sends = [in_order(send, order, slots) for send, order in zip(sends, weights)]
    scatter = Scatter(keeps, sends)
    back = back_one(grad_two, deep_low)
    (back,) = scatter.join(back)
    (back,) = scatter.step(back)
    back_local, back_end = delta_one(back, keep, params[0], rows, frames, width, group)
    second_local, second_end, second_decay = states_two(
        proj_two, delta_local, delta_in, keep, params[1], stat_two, rows, frames, devices
    )
    back_end, second_end = scatter.join(back_end, second_end)
    tall = 2 * rows
    back_end, second_end = scatter.step(back_end, second_end)
    carries = Exchange(
        flags,
        [(back_end, powers[0], True), (second_end, powers[1], False)],
        [total_two.reshape(tall, -1), gram],
    )
    carries.step(3)
    (carries.payload,) = scatter.join(carries.payload)
    while len(scatter.orders[0]) > 1:
        (carries.payload,) = scatter.step(carries.payload)
        carries.step()
        (carries.payload,) = scatter.join(carries.payload)
    (carries.payload,) = scatter.step(carries.payload)
    carries.step(len(carries.bits))
    carries.payload, carries.before = scatter.join(carries.payload, carries.before)
    back_in, second_in = carries.arrived(0), carries.arrived(1)
    sources[1] = (second_local, second_in, params[1])
    total_two = carries.sums()[:, : padded // tall].reshape(1, padded)
    gram = carries.sums()[:, padded // tall :]
    mine = lax.axis_index("tm")
    place = mine // (2 * side_bit()) * side_bit() + mine % side_bit()
    place = (side[0] * (devices // 2) + place) * slots
    mean_own = lax.dynamic_slice_in_dim(mean_one[0], place, slots)[:, None]
    grad_parts = [
        part + mean_own * total_two[:, first : first + lanes]
        for (first, lanes), part in zip(parts, scatter.result())
    ]
    grad_block = jnp.concatenate(grad_parts, axis=1)
    momentum_new = MUON_BETA * momentum_block + grad_block
    start_block = momentum_new.astype(jnp.bfloat16)
    (start_block,), (back_in,) = tie([start_block], [back_in])
    gathered = lax.all_gather(start_block, "tm", axis=0, tiled=True)
    sums_one, input_part, gate_mean = gate_one(
        proj_one, state_local, state_in, back_local, back_in, keep, params[0], stat_one, x,
        shallow_weight, rows, frames, devices,
    )
    decay_two = jnp.sum(second_decay[:rows] + second_decay[rows:] * second_in, axis=0, keepdims=True)
    square = jnp.sum(momentum_new * momentum_new).reshape(1, 1)
    sums_one = (
        sums_one
        + jnp.pad(decay_two, ((feats + 3, SIDE - feats - 4), (0, 0)))
        + jnp.pad(square, ((feats + 4, SIDE - feats - 5), (0, padded - 1)))
    )
    spread = SumSpread(sums_one)
    for k in range(chunks):
        spread.step()
        (spread.value,) = next_hidden(1, [k], [spread.value])
    spread.step(len(spread.steps))
    sums_one = spread.value
    (hidden_one,), (hidden_two,) = hidden
    shallow_grad, shallow_next, shallow_new, shallow_low, input_grad = shallow_step(
        sums_one, gram, params[0], stat_one, shallow_weight, shallow_momentum, x, input_part, gate_mean,
        count * devices, rows, frames,
    )
    (gathered,), (shallow_low,) = tie([gathered], [shallow_low])
    input_grad = input_grad.reshape(rows, frames, feats)
    scale = 1.0 / (jnp.sqrt(sums_one[feats + 4, :1]) + MUON_EPSILON)
    shard = deep_weight.shape[0]
    window, first_row, offset = own_window(shard, width, padded)
    ortho = newton_rows(
        gathered, scale, (first_row // 16).astype(jnp.int32).reshape(1), window
    )
    deep_ortho = lax.dynamic_slice_in_dim(ortho[:, :width].reshape(-1), offset, shard)
    deep_new = MUON_KEEP * deep_weight - MUON_RATE * deep_ortho.astype(jnp.float32)
    deep_grad = from_block(grad_block[:, :width], shard, padded)
    deep_next = MUON_BETA * deep_momentum + deep_grad

    unit_sums = sums_one[feats : feats + 4, :width]
    bias_gain_two = sums_two[:, :width]
    slope = jnp.where(
        1.0 - jnp.exp(-unit_params[:, 0]) > DECAY_FLOOR, jnp.exp(-unit_params[:, 0]), 0.0
    )
    unit_grad = jnp.stack(
        [
            jnp.stack([unit_sums[2] * slope[0], unit_sums[0], unit_sums[1], unit_sums[0]]),
            jnp.stack(
                [unit_sums[3] * slope[1], bias_gain_two[0], bias_gain_two[1], bias_gain_two[0]]
            ),
        ]
    )
    first_fix = 1.0 - FIRST_DECAY**STEP
    second_fix = 1.0 - SECOND_DECAY**STEP
    first_new = FIRST_DECAY * unit_first + (1.0 - FIRST_DECAY) * unit_grad
    second_new = SECOND_DECAY * unit_second + (1.0 - SECOND_DECAY) * unit_grad * unit_grad
    params_new = unit_params - ADAM_RATE * (first_new / first_fix) / (
        jnp.sqrt(second_new / second_fix) + ADAM_EPSILON
    )
    return (
        hidden_one.reshape(rows, frames, width),
        hidden_two.reshape(rows, frames, width),
        input_grad,
        shallow_grad,
        shallow_next,
        shallow_new,
        shallow_low,
        deep_grad,
        deep_next,
        deep_new,
        deep_new.astype(jnp.bfloat16),
        first_new,
        second_new,
        params_new,
    )


def solution(mesh):
    in_specs = (
        P(None, "tm", None),
        P(None, "tm"),
        P(),
        P(),
        P("tm"),
        P("tm"),
        P(),
        P(),
        P(),
        P(None, "tm", None),
    )
    out_specs = (
        P(None, "tm", None),
        P(None, "tm", None),
        P(None, "tm", None),
        P(),
        P(),
        P(),
        P(),
        P("tm"),
        P("tm"),
        P("tm"),
        P("tm"),
        P(),
        P(),
        P(),
    )
    return jax.shard_map(
        per_device, mesh=mesh, in_specs=in_specs, out_specs=out_specs, check_vma=False
    )
```

```python
import copy
import functools

import jax
import jax.numpy as jnp
from jax import lax
from jax.experimental import pallas as pl
from jax.experimental.pallas import tpu as pltpu
from jax.sharding import PartitionSpec as P

NS_STEPS = 2
STEP = 5


NORM_EPSILON = 1e-05
MUON_EPSILON = 1e-07
COEFF_A = 3.4445
COEFF_B = -4.775
COEFF_C = 2.0315
MUON_BETA = 0.5
MUON_RATE = 4.0
MUON_KEEP = 0.999
FIRST_DECAY = 0.9
SECOND_DECAY = 0.95
ADAM_RATE = 0.5
ADAM_EPSILON = 1e-08
DECAY_FLOOR = 0.9
LANE = 128
WIDE = 512
PART = 256
SIDE = 80


def kernel_call(body, grid, in_specs, out_specs, out_shape, scratch=(), flops=0, traffic=0):
    return pl.pallas_call(
        body,
        grid=grid,
        in_specs=in_specs,
        out_specs=out_specs,
        out_shape=out_shape,
        scratch_shapes=list(scratch),
        compiler_params=pltpu.CompilerParams(vmem_limit_bytes=56 * 1024 * 1024),
        cost_estimate=pl.CostEstimate(flops=flops, bytes_accessed=traffic, transcendentals=0),
    )


def shape_of(shape, dtype=jnp.float32):
    return jax.ShapeDtypeStruct(shape, dtype)


def whole(shape):
    return pl.BlockSpec(shape, lambda i: (0,) * len(shape))


def lanes_of(rows, width=WIDE):
    return pl.BlockSpec((rows, width), lambda i: (0, i))


def chunk_call(body, place, in_specs, out_specs, out_shape, arrays, previous, scratch=(), traffic=0):
    count = len(in_specs)
    before = list(previous) if previous is not None else []

    def run(*refs):
        body(*refs[:count], *refs[count + len(before) :])

    return pl.pallas_call(
        run,
        grid=(1,),
        in_specs=list(in_specs) + [pl.BlockSpec(memory_space=pl.ANY)] * len(before),
        out_specs=out_specs,
        out_shape=out_shape,
        scratch_shapes=list(scratch),
        input_output_aliases={count + k: k for k in range(len(before))},
        compiler_params=pltpu.CompilerParams(vmem_limit_bytes=56 * 1024 * 1024),
        cost_estimate=pl.CostEstimate(flops=0, bytes_accessed=traffic, transcendentals=0),
    )(*arrays, *before)


def chunk_at(rows, place):
    return pl.BlockSpec((rows, WIDE), lambda i: (0, place))


def rate_of(params):
    return jnp.maximum(1.0 - jnp.exp(-params[0:1]), DECAY_FLOOR)


def softened(value):
    return jnp.maximum(value, 0.0) + jnp.log(1.0 + jnp.exp(-jnp.abs(value)))


def sigmoid(value):
    return 0.5 * jnp.tanh(0.5 * value) + 0.5


def wide_keep(keep_ref, t, rows):
    keep = keep_ref[pl.ds(pl.multiple_of(t * rows, rows), rows), :]
    return jnp.concatenate([keep] * (WIDE // LANE), axis=1)


def rows_at(ref, t, rows):
    return ref[pl.ds(pl.multiple_of(t * rows, rows), rows), :]


def store_at(ref, t, rows, value):
    ref[pl.ds(pl.multiple_of(t * rows, rows), rows), :] = value


def valid_lanes(shape, total, step):
    return lax.broadcasted_iota(jnp.int32, shape, 1) + step * WIDE < total


def unit_terms(params_ref, stat_ref, total_devices, frames):
    params = params_ref[...]
    stat = stat_ref[...]
    centre = stat[0:1]
    inverse = lax.rsqrt(stat[1:2] / (total_devices * frames) + NORM_EPSILON)
    return centre, inverse, params[2:3], params[3:4] + params[1:2]


def front_body(rows, frames, width, x_ref, w_ref, xt_ref, proj_ref, stat_ref, gram_ref, padded_w):
    step = pl.program_id(0)
    count, feats = x_ref.shape

    @pl.when(step == 0)
    def _():
        i = lax.broadcasted_iota(jnp.int32, (count, count), 0)
        j = lax.broadcasted_iota(jnp.int32, (count, count), 1)
        move = (j == lax.rem(i, rows) * frames + lax.div(i, rows)).astype(jnp.bfloat16)
        moved = jnp.dot(move, x_ref[...], preferred_element_type=jnp.float32).astype(jnp.bfloat16)
        i = lax.broadcasted_iota(jnp.int32, (feats, LANE), 0)
        j = lax.broadcasted_iota(jnp.int32, (feats, LANE), 1)
        wide = jnp.dot(moved, (i == j).astype(jnp.bfloat16), preferred_element_type=jnp.float32)
        lane = lax.broadcasted_iota(jnp.int32, (count, LANE), 1)
        xt = jnp.where(lane == feats, 1.0, wide).astype(jnp.bfloat16)
        xt_ref[...] = xt
        gram = dot_tn(xt, xt)
        high = gram_ref.shape[0]
        for k in range(SIDE // high):
            gram_ref[:, k * LANE : (k + 1) * LANE] = gram[k * high : (k + 1) * high]
        padded_w[...] = jnp.zeros_like(padded_w)

    weight = w_ref[...]
    padded_w[0:feats, :] = jnp.where(valid_lanes(weight.shape, width, step), weight, 0.0)
    proj = jnp.dot(
        xt_ref[...], padded_w[...].astype(jnp.bfloat16), preferred_element_type=jnp.float32
    )
    proj_ref[...] = proj
    mean = jnp.sum(proj, axis=0, keepdims=True) * (1.0 / count)
    off = proj - mean
    stat_ref[0:1, :] = mean
    stat_ref[1:2, :] = jnp.sum(off * off, axis=0, keepdims=True)


def dot_tn(a, b):
    return lax.dot_general(a, b, (((0,), (0,)), ((), ())), preferred_element_type=jnp.float32)


def front(x, weight, rows, frames):
    count, feats = x.shape
    width = weight.shape[1]
    padded = -(-width // WIDE) * WIDE
    return kernel_call(
        functools.partial(front_body, rows, frames, width),
        (padded // WIDE,),
        [whole((count, feats)), lanes_of(feats)],
        [whole((count, LANE)), lanes_of(count), lanes_of(2), whole((2 * rows, SIDE // (2 * rows) * LANE))],
        [
            shape_of((count, LANE), jnp.bfloat16),
            shape_of((count, padded)),
            shape_of((2, padded)),
            shape_of((2 * rows, SIDE // (2 * rows) * LANE)),
        ],
        [pltpu.VMEM((LANE, WIDE), jnp.float32)],
    )(x, weight)


def delta_two_body(rows, frames, width, grad_ref, keep_ref, params_ref, delta_ref, end_ref, held):
    place = pl.program_id(0)
    pieces = WIDE // LANE
    mask = valid_lanes((rows * frames, WIDE), width, place)
    grad = jnp.where(mask, grad_ref[...].astype(jnp.float32), 0.0)
    for g in range(pieces):
        held[g] = grad[:, g * LANE : (g + 1) * LANE]
    rate = rate_of(params_ref[...])

    def body(k, carried):
        t = frames - 1 - k
        own = jnp.concatenate(
            [held[g, pl.ds(t, rows, stride=frames), :] for g in range(pieces)], axis=1
        )
        delta = own + carried
        store_at(delta_ref, t, rows, delta)
        return rate * wide_keep(keep_ref, t, rows) * delta

    end_ref[...] = lax.fori_loop(
        0, frames, body, jnp.zeros((rows, WIDE), jnp.float32), unroll=8
    )


def delta_two(out_grad, keep, params, rows, frames, padded):
    count, width = out_grad.shape
    return kernel_call(
        functools.partial(delta_two_body, rows, frames, width),
        (padded // WIDE,),
        [lanes_of(count), whole((count, LANE)), lanes_of(4)],
        [lanes_of(count), lanes_of(rows)],
        [shape_of((count, padded)), shape_of((rows, padded))],
        [pltpu.VMEM((WIDE // LANE, count, LANE), jnp.float32)],
    )(out_grad, keep, params)


def states_body(
    rows, frames, devices, proj_ref, keep_ref, params_ref, stat_ref, state_ref, end_ref
):
    centre, inverse, gain, offset = unit_terms(params_ref, stat_ref, devices, rows * frames)
    rate = rate_of(params_ref[...])
    share = 1.0 - rate

    def body(t, carried):
        gate = (rows_at(proj_ref, t, rows) - centre) * inverse * gain + offset
        soft = softened(gate)
        carried = rate * wide_keep(keep_ref, t, rows) * carried + share * soft
        store_at(state_ref, t, rows, carried)
        return carried

    end_ref[...] = lax.fori_loop(
        0, frames, body, jnp.zeros((rows, WIDE), jnp.float32), unroll=8
    )


def local_states(proj, keep, params, stat, rows, frames, devices):
    count, padded = proj.shape
    return kernel_call(
        functools.partial(states_body, rows, frames, devices),
        (padded // WIDE,),
        [lanes_of(count), whole((count, LANE)), lanes_of(4), lanes_of(2)],
        [lanes_of(count), lanes_of(rows)],
        [shape_of((count, padded)), shape_of((rows, padded))],
    )(proj, keep, params, stat)


def to_slots(value, group):
    pieces = value.shape[1] // LANE
    lane = lax.broadcasted_iota(jnp.int32, (value.shape[0], LANE), 1)
    parts = [value[:, g * LANE : (g + 1) * LANE] for g in range(pieces)]
    out = []
    for g in range(pieces):
        moved = (LANE - group) * g
        if moved == 0:
            new = parts[g]
        else:
            new = jnp.where(
                lane < moved, pltpu.roll(parts[g - 1], moved, 1), pltpu.roll(parts[g], moved, 1)
            )
        out.append(jnp.where(lane < group, new, 0.0))
    return jnp.concatenate(out, axis=1)


def from_slots(value, group, width):
    pieces = value.shape[1] // LANE
    lane = lax.broadcasted_iota(jnp.int32, (value.shape[0], LANE), 1)
    parts = [value[:, g * LANE : (g + 1) * LANE] for g in range(pieces)]
    out = []
    for j in range(pieces):
        moved = (LANE - group) * j
        new = parts[j] if moved == 0 else pltpu.roll(parts[j], LANE - moved, 1)
        if j + 1 < pieces:
            new = jnp.where(lane < group - moved, new, pltpu.roll(parts[j + 1], group - moved, 1))
        left = width - j * LANE
        out.append(new if left >= LANE else jnp.where(lane < left, new, 0.0))
    return jnp.concatenate(out, axis=1)


def low_one_body(rows, frames, width, group, state_ref, start_ref, keep_ref, params_ref, low_ref, mean_ref):
    pieces = state_ref.shape[1] // LANE
    rate = rate_of(params_ref[...])

    def advance(t, carried):
        keep = rows_at(keep_ref, t, rows)
        carried = rate * jnp.concatenate([keep] * pieces, axis=1) * carried
        return carried, rows_at(state_ref, t, rows) + carried

    def body(k, both):
        carried, total = both
        t = 2 * k
        carried, first = advance(t, carried)
        carried, second = advance(t + 1, carried)
        place = pl.ds(pl.multiple_of(t * rows, 2 * rows), 2 * rows)
        slots = to_slots(jnp.concatenate([first, second], axis=0), group)
        low_ref[place, :] = slots.astype(jnp.bfloat16)
        return carried, total + slots[:rows] + slots[rows:]

    start = start_ref[...]
    _, total = lax.fori_loop(0, frames // 2, body, (start, jnp.zeros_like(start)), unroll=4)
    mean_ref[...] = jnp.sum(total, axis=0, keepdims=True) * (1.0 / (rows * frames))


def low_one_of(states, start, keep, params, rows, frames, width, group):
    count, padded = states.shape
    return kernel_call(
        functools.partial(low_one_body, rows, frames, width, group),
        (1,),
        [whole((count, padded)), whole((rows, padded)), whole((count, LANE)), whole((4, padded))],
        [whole((count, padded)), whole((1, padded))],
        [shape_of((count, padded), jnp.bfloat16), shape_of((1, padded))],
    )(states, start, keep, params)


def hidden_body(rows, frames, state_ref, start_ref, keep_ref, params_ref, hidden_ref, held):
    pieces = WIDE // LANE
    rate = rate_of(params_ref[...])

    def body(t, carry):
        carry = rate * wide_keep(keep_ref, t, rows) * carry
        state = rows_at(state_ref, t, rows) + carry
        for g in range(pieces):
            held[g, pl.ds(pl.multiple_of(t * rows, rows), rows), :] = state[
                :, g * LANE : (g + 1) * LANE
            ]
        return carry

    lax.fori_loop(0, frames, body, start_ref[...], unroll=8)
    for r in range(rows):
        for g in range(pieces):
            hidden_ref[r * frames : (r + 1) * frames, g * LANE : (g + 1) * LANE] = held[
                g, pl.ds(r, frames, stride=rows), :
            ]


def hidden_of(place, previous, states, start, keep, params, rows, frames, width):
    count, _ = states.shape
    return chunk_call(
        functools.partial(hidden_body, rows, frames),
        place,
        [chunk_at(count, place), chunk_at(rows, place), whole((count, LANE)), chunk_at(4, place)],
        [chunk_at(count, place)],
        [shape_of((count, width))],
        (states, start, keep, params),
        previous,
        [pltpu.VMEM((WIDE // LANE, count, LANE), jnp.float32)],
    )


def second_body(low_ref, weight_ref, proj_ref, stat_ref):
    tile = 256
    count = proj_ref.shape[0]
    for j in range(0, WIDE, tile):
        place = slice(j, j + tile)
        for i in range(0, count, tile):
            proj_ref[i : i + tile, place] = jnp.dot(
                low_ref[i : i + tile, :], weight_ref[:, place], preferred_element_type=jnp.float32
            )
        proj = proj_ref[:, place]
        mean = jnp.sum(proj, axis=0, keepdims=True) * (1.0 / count)
        off = proj - mean
        stat_ref[0:1, place] = mean
        stat_ref[1:2, place] = jnp.sum(off * off, axis=0, keepdims=True)


def second_forward(low, weight):
    count, padded = low.shape
    return kernel_call(
        second_body,
        (padded // WIDE,),
        [whole((count, padded)), lanes_of(padded)],
        [lanes_of(count), lanes_of(2)],
        [shape_of((count, padded)), shape_of((2, padded))],
    )(low, weight)


def gate_two_body(
    rows, frames, devices, proj_ref, delta_ref, start_ref, keep_ref, params_ref, stat_ref, gate_ref, sums_ref
):
    centre, inverse, gain, offset = unit_terms(params_ref, stat_ref, devices, rows * frames)
    rate = rate_of(params_ref[...])
    share = 1.0 - rate
    none = jnp.zeros((rows, WIDE), jnp.float32)

    def body(k, carried):
        carry, bias_sum, gain_sum = carried
        t = frames - 1 - k
        delta = rows_at(delta_ref, t, rows) + carry
        normed = (rows_at(proj_ref, t, rows) - centre) * inverse
        gate = share * delta * sigmoid(normed * gain + offset)
        store_at(gate_ref, t, rows, gate)
        carry = rate * wide_keep(keep_ref, t, rows) * carry
        return carry, bias_sum + gate, gain_sum + gate * normed

    _, bias_sum, gain_sum = lax.fori_loop(
        0, frames, body, (start_ref[...], none, none), unroll=8
    )
    sums_ref[0:1, :] = jnp.sum(bias_sum, axis=0, keepdims=True)
    sums_ref[1:2, :] = jnp.sum(gain_sum, axis=0, keepdims=True)


def gate_two(proj, delta, start, keep, params, stat, rows, frames, devices):
    count, padded = proj.shape
    return kernel_call(
        functools.partial(gate_two_body, rows, frames, devices),
        (padded // WIDE,),
        [lanes_of(count), lanes_of(count), lanes_of(rows), whole((count, LANE)), lanes_of(4), lanes_of(2)],
        [lanes_of(count), lanes_of(2)],
        [shape_of((count, padded)), shape_of((2, padded))],
    )(proj, delta, start, keep, params, stat)


def states_two_body(
    rows, frames, devices, proj_ref, delta_ref, start_ref, keep_ref, params_ref, stat_ref,
    state_ref, end_ref, decay_ref, held,
):
    centre, inverse, gain, offset = unit_terms(params_ref, stat_ref, devices, rows * frames)
    rate = rate_of(params_ref[...])
    share = 1.0 - rate
    none = jnp.zeros((rows, WIDE), jnp.float32)

    def backward(k, carry):
        t = frames - 1 - k
        store_at(held, t, rows, rows_at(delta_ref, t, rows) + carry)
        return rate * wide_keep(keep_ref, t, rows) * carry

    lax.fori_loop(0, frames, backward, start_ref[...], unroll=8)

    def forward(t, carried):
        state, reach, decay, factor = carried
        keep = wide_keep(keep_ref, t, rows)
        delta = rows_at(held, t, rows)
        value = (rows_at(proj_ref, t, rows) - centre) * inverse * gain + offset
        soft = softened(value)
        decay = decay + delta * (keep * state - soft)
        factor = factor + delta * keep * reach
        state = rate * keep * state + share * soft
        reach = rate * keep * reach
        store_at(state_ref, t, rows, state)
        return state, reach, decay, factor

    state, _, decay, factor = lax.fori_loop(
        0, frames, forward, (none, jnp.ones_like(none), none, none), unroll=4
    )
    end_ref[...] = state
    decay_ref[0:rows, :] = decay
    decay_ref[rows : 2 * rows, :] = factor


def states_two(proj, delta, start, keep, params, stat, rows, frames, devices):
    count, padded = proj.shape
    return kernel_call(
        functools.partial(states_two_body, rows, frames, devices),
        (padded // WIDE,),
        [
            lanes_of(count),
            lanes_of(count),
            lanes_of(rows),
            whole((count, LANE)),
            lanes_of(4),
            lanes_of(2),
        ],
        [lanes_of(count), lanes_of(rows), lanes_of(2 * rows)],
        [shape_of((count, padded)), shape_of((rows, padded)), shape_of((2 * rows, padded))],
        [pltpu.VMEM((count, WIDE), jnp.float32)],
    )(proj, delta, start, keep, params, stat)


def turn_body(low_ref, mean_ref, turned_ref):
    half = LANE // 2
    turned = (low_ref[...].astype(jnp.float32) - mean_ref[...]).T.astype(jnp.bfloat16)
    for g in range(WIDE // LANE):
        for side in range(2):
            turned_ref[side, g * half : (g + 1) * half, :] = turned[
                g * LANE + side * half : g * LANE + (side + 1) * half
            ]


def turn(place, previous, low, mean):
    count, padded = low.shape
    return chunk_call(
        turn_body,
        place,
        [chunk_at(count, place), chunk_at(1, place)],
        [pl.BlockSpec((2, WIDE // 2, count), lambda i: (0, place, 0))],
        [shape_of((2, padded // 2, count), jnp.bfloat16)],
        (low, mean),
        previous,
    )


def deep_term_body(
    rows, frames, devices, parts, orders, side_ref, gate_ref, proj_ref, params_ref, stat_ref, sums_ref,
    turned_ref, grad_ref, total_ref, *outs,
):
    step = pl.program_id(0)
    total = devices * rows * frames
    centre, inverse, gain, _ = unit_terms(params_ref, stat_ref, devices, rows * frames)
    sums = sums_ref[...] * (1.0 / total)
    normed = (proj_ref[...] - centre) * inverse
    grad = (gain * inverse * (gate_ref[...] - sums[0:1] - normed * sums[1:2])).astype(jnp.bfloat16)
    grad_ref[...] = grad
    total_ref[...] = jnp.sum(grad.astype(jnp.float32), axis=0, keepdims=True)
    side = side_ref[0]
    half = turned_ref.shape[1]
    tile = 256
    for p, (first, lanes) in enumerate(parts):

        @pl.when((step >= first // PART) & (step < (first + lanes) // PART))
        def _():
            for which, out_ref in ((side, outs[p]), (1 - side, outs[len(parts) + p])):
                for k in range(half // tile):
                    part = jnp.dot(
                        turned_ref[which, k * tile : (k + 1) * tile, :],
                        grad_ref[...],
                        preferred_element_type=jnp.float32,
                    ).astype(out_ref.dtype)
                    if orders is None:
                        out_ref[k * tile : (k + 1) * tile, :] = part
                        continue
                    slots = half // 2 ** len(orders[p])
                    for b in range(tile // slots):
                        block = k * (tile // slots) + b
                        place = 0
                        for weight in orders[p]:
                            place = 2 * place + block // weight % 2
                        out_ref[place * slots : (place + 1) * slots, :] = part[
                            b * slots : (b + 1) * slots
                        ]


def deep_term(parts, orders, side, gate, proj, params, stat, sums, turned, rows, frames, devices):
    count, padded = proj.shape
    half = padded // 2

    def some(first, lanes):
        return pl.BlockSpec(
            (half, PART), lambda i: (0, jnp.clip(i - first // PART, 0, lanes // PART - 1))
        )

    found = kernel_call(
        functools.partial(deep_term_body, rows, frames, devices, parts, orders),
        (padded // PART,),
        [
            pl.BlockSpec(memory_space=pltpu.SMEM),
            lanes_of(count, PART),
            lanes_of(count, PART),
            lanes_of(4, PART),
            lanes_of(2, PART),
            lanes_of(2, PART),
            whole((2, half, count)),
        ],
        [lanes_of(count, PART), lanes_of(1, PART)] + [some(*part) for part in parts] * 2,
        [shape_of((count, padded), jnp.bfloat16), shape_of((1, padded))]
        + [shape_of((half, lanes), jnp.bfloat16) for _, lanes in parts] * 2,
    )(side, gate, proj, params, stat, sums, turned)
    return found[0], found[1], found[2 : 2 + len(parts)], found[2 + len(parts) :]


def back_body(grad_ref, weight_ref, back_ref):
    back_ref[...] = dot_nt(grad_ref[...], weight_ref[...])


def back_one(grad, weight):
    count, padded = grad.shape
    return kernel_call(
        back_body,
        (padded // WIDE,),
        [whole((count, padded)), pl.BlockSpec((WIDE, padded), lambda i: (i, 0))],
        lanes_of(count),
        shape_of((count, padded)),
    )(grad, weight)


def delta_one_body(rows, frames, width, group, back_ref, keep_ref, params_ref, delta_ref, end_ref):
    pieces = back_ref.shape[1] // LANE
    rate = rate_of(params_ref[...])

    def body(k, carried):
        t = frames - 1 - k
        delta = from_slots(rows_at(back_ref, t, rows), group, width) + carried
        store_at(delta_ref, t, rows, delta)
        keep = rows_at(keep_ref, t, rows)
        return rate * jnp.concatenate([keep] * pieces, axis=1) * delta

    end_ref[...] = lax.fori_loop(
        0, frames, body, jnp.zeros((rows, back_ref.shape[1]), jnp.float32), unroll=2
    )


def delta_one(back, keep, params, rows, frames, width, group):
    count, padded = back.shape
    return kernel_call(
        functools.partial(delta_one_body, rows, frames, width, group),
        (1,),
        [whole((count, padded)), whole((count, LANE)), whole((4, padded))],
        [whole((count, padded)), whole((rows, padded))],
        [shape_of((count, padded)), shape_of((rows, padded))],
    )(back, keep, params)


def gate_one_body(
    rows,
    frames,
    devices,
    feats,
    width,
    proj_ref,
    state_ref,
    first_ref,
    delta_ref,
    start_ref,
    keep_ref,
    params_ref,
    stat_ref,
    x_ref,
    w_ref,
    sums_ref,
    back_ref,
    mean_ref,
    held,
    gate_ref,
    padded_w,
):
    step = pl.program_id(0)
    centre, inverse, gain, offset = unit_terms(params_ref, stat_ref, devices, rows * frames)
    rate = rate_of(params_ref[...])
    share = 1.0 - rate
    none = jnp.zeros((rows, WIDE), jnp.float32)

    def backward(k, carry):
        t = frames - 1 - k
        store_at(held, t, rows, rows_at(delta_ref, t, rows) + carry)
        return rate * wide_keep(keep_ref, t, rows) * carry

    lax.fori_loop(0, frames, backward, start_ref[...], unroll=8)

    def forward(t, carried):
        carry, before, bias_sum, gain_sum, decay_sum = carried
        keep = wide_keep(keep_ref, t, rows)
        delta = rows_at(held, t, rows)
        normed = (rows_at(proj_ref, t, rows) - centre) * inverse
        value = normed * gain + offset
        soft = softened(value)
        gate = share * delta * sigmoid(value)
        store_at(gate_ref, t, rows, gate)
        decay_sum = decay_sum + delta * (keep * before - soft)
        carry = rate * keep * carry
        before = rows_at(state_ref, t, rows) + carry
        return carry, before, bias_sum + gate, gain_sum + gate * normed, decay_sum

    first = first_ref[...]
    _, _, bias_sum, gain_sum, decay_sum = lax.fori_loop(
        0, frames, forward, (first, first, none, none, none), unroll=4
    )
    bias = jnp.sum(bias_sum, axis=0, keepdims=True)
    mean = bias * (1.0 / (rows * frames))
    x = x_ref[...]
    ones = jnp.ones((rows * frames, LANE), jnp.bfloat16)
    total = jnp.concatenate([dot_tn(x, ones)] * (WIDE // LANE), axis=1)
    centred = gate_ref[...] - mean
    term = dot_tn(x, centred.astype(jnp.bfloat16)) + total * mean
    sums_ref[...] = term[: sums_ref.shape[0]]
    sums_ref[feats : feats + 1, :] = bias
    sums_ref[feats + 1 : feats + 2, :] = jnp.sum(gain_sum, axis=0, keepdims=True)
    sums_ref[feats + 2 : feats + 3, :] = jnp.sum(decay_sum, axis=0, keepdims=True)
    mean_ref[...] = mean
    weight = w_ref[...]
    padded_w[...] = jnp.zeros_like(padded_w)
    padded_w[0:feats, :] = jnp.where(valid_lanes(weight.shape, width, step), weight, 0.0)
    part = dot_nt(
        (gain * inverse * centred).astype(jnp.bfloat16), padded_w[...].astype(jnp.bfloat16)
    )

    @pl.when(step == 0)
    def _():
        back_ref[...] = part

    @pl.when(step > 0)
    def _():
        back_ref[...] += part


def gate_one(proj, states, first, delta, start, keep, params, stat, x, weight, rows, frames, devices):
    count, padded = proj.shape
    feats, width = weight.shape
    return kernel_call(
        functools.partial(gate_one_body, rows, frames, devices, feats, width),
        (padded // WIDE,),
        [
            lanes_of(count),
            lanes_of(count),
            lanes_of(rows),
            lanes_of(count),
            lanes_of(rows),
            whole((count, LANE)),
            lanes_of(4),
            lanes_of(2),
            whole((count, LANE)),
            lanes_of(feats),
        ],
        [lanes_of(SIDE), whole((count, LANE)), lanes_of(1)],
        [shape_of((SIDE, padded)), shape_of((count, LANE)), shape_of((1, padded))],
        [
            pltpu.VMEM((count, WIDE), jnp.float32),
            pltpu.VMEM((count, WIDE), jnp.float32),
            pltpu.VMEM((LANE, WIDE), jnp.float32),
        ],
    )(proj, states, first, delta, start, keep, params, stat, x, weight)


def dot_nt(a, b):
    return lax.dot_general(a, b, (((1,), (1,)), ((), ())), preferred_element_type=jnp.float32)


def shallow_body(
    total, rows, frames, sums_ref, gram_ref, params_ref, stat_ref, w_ref, m_ref, x_ref, back_ref, mean_ref,
    grad_ref, next_ref, new_ref, low_ref, input_ref, held, moved,
):
    feats, width = w_ref.shape
    count = rows * frames
    centre, inverse, gain, _ = unit_terms(params_ref, stat_ref, total // count, count)
    weight = w_ref[...]
    held[...] = jnp.zeros_like(held)
    held[0:feats, 0:width] = weight
    low = held[...].astype(jnp.bfloat16).astype(jnp.float32)
    high = gram_ref.shape[0]
    gram = jnp.concatenate(
        [gram_ref[:, k * LANE : (k + 1) * LANE] for k in range(SIDE // high)], axis=0
    )
    lane = lax.broadcasted_iota(jnp.int32, gram.shape, 1)
    x_sum = jnp.sum(jnp.where(lane == feats, gram, 0.0), axis=1, keepdims=True)
    raw = jnp.dot(
        gram, low, precision=lax.Precision.HIGHEST, preferred_element_type=jnp.float32
    )
    normed = (raw - x_sum * centre) * inverse
    bias = sums_ref[feats : feats + 1, :] * (1.0 / total)
    slope = sums_ref[feats + 1 : feats + 2, :] * (1.0 / total)
    scaled = gain * inverse
    grad = scaled * (sums_ref[...] - x_sum * bias - normed * slope)
    grad = grad[:feats, :width]
    grad_ref[...] = grad

    row = lax.broadcasted_iota(jnp.int32, low.shape, 0)
    turn = slope * inverse
    left = jnp.where(
        row == feats, scaled * (mean_ref[...] - bias + turn * centre), -low * (scaled * turn)
    )
    matrix = lax.dot_general(
        left, low, (((1,), (1,)), ((), ())),
        precision=lax.Precision.HIGHEST, preferred_element_type=jnp.float32,
    )
    moved[...] = back_ref[...] + jnp.dot(
        x_ref[...].astype(jnp.float32), matrix,
        precision=lax.Precision.HIGHEST, preferred_element_type=jnp.float32,
    )
    for r in range(rows):
        input_ref[r * frames : (r + 1) * frames, :] = moved[pl.ds(r, frames, stride=rows), :][:, :feats]

    following = MUON_BETA * m_ref[...] + grad
    next_ref[...] = following
    held[0:feats, 0:width] = following
    m = held[0:SIDE, :]
    current = (m / (jnp.sqrt(jnp.sum(m * m)) + MUON_EPSILON)).astype(jnp.bfloat16)
    for repeat in range(NS_STEPS):
        gram = dot_nt(current, current).astype(jnp.bfloat16)
        square = jnp.dot(gram, gram, preferred_element_type=jnp.float32)
        mixing = (COEFF_B * gram.astype(jnp.float32) + COEFF_C * square).astype(jnp.bfloat16)
        current = (
            COEFF_A * current.astype(jnp.float32)
            + jnp.dot(mixing, current, preferred_element_type=jnp.float32)
        ).astype(jnp.bfloat16)
    new = MUON_KEEP * weight - MUON_RATE * current[:feats, :width].astype(jnp.float32)
    new_ref[...] = new
    low_ref[...] = new.astype(jnp.bfloat16)


def shallow_step(sums, gram, params, stat, weight, momentum, x, back, mean, total, rows, frames):
    padded = sums.shape[1]
    some = shape_of(weight.shape)
    feats = weight.shape[0]
    arrays = (sums, gram, params, stat, weight, momentum, x, back, mean)
    return kernel_call(
        functools.partial(shallow_body, total, rows, frames),
        (1,),
        [whole(value.shape) for value in arrays],
        [whole(weight.shape)] * 4 + [whole((rows * frames, feats))],
        [some, some, some, shape_of(weight.shape, jnp.bfloat16), shape_of((rows * frames, feats))],
        [pltpu.VMEM((LANE, padded), jnp.float32), pltpu.VMEM((rows * frames, LANE), jnp.float32)],
    )(*arrays)


def newton_body(window, tile, first_ref, scale_ref, start_ref, out_ref, m_ref, gram, sems):
    size = m_ref.shape[0]
    blocks = size // tile

    def place(k):
        return slice(k * tile, (k + 1) * tile)

    copies = [
        pltpu.make_async_copy(start_ref.at[place(k), :], m_ref.at[place(k), :], sems.at[k])
        for k in range(blocks)
    ]
    for copy in copies:
        copy.start()
    scale = scale_ref[0]
    square_scale = scale * scale
    for j in range(blocks):
        copies[j].wait()
        for i in range(j + 1):
            part = dot_nt(m_ref[place(i), :], m_ref[place(j), :]) * square_scale
            gram[place(i), place(j)] = part.astype(jnp.bfloat16)
            if i != j:
                gram[place(j), place(i)] = part.T.astype(jnp.bfloat16)
    def taken(ref):
        return ref[pl.ds(pl.multiple_of(first_ref[0] * 16, 16), window), :].astype(jnp.float32)

    def times(value, ref):
        return jnp.dot(value.astype(jnp.bfloat16), ref[...], preferred_element_type=jnp.float32)

    def mixed(once):
        return COEFF_B * once + COEFF_C * times(once, gram)

    def stepped(value):
        return COEFF_A * value + mixed(times(value, gram))

    gram_own = taken(gram)
    mixing_own = mixed(gram_own)
    gram_own = stepped(COEFF_A * gram_own + times(mixing_own, gram))
    square_own = stepped(times(stepped(gram_own), gram))
    second_own = COEFF_B * gram_own + COEFF_C * square_own
    weights = COEFF_A * mixing_own + stepped(second_own)
    result = COEFF_A * COEFF_A * taken(m_ref) + times(weights, m_ref)
    out_ref[...] = (scale * result).astype(jnp.bfloat16)


def newton_rows(start, scale, first, window):
    size = start.shape[0]
    tile = 256
    scalar = pl.BlockSpec(memory_space=pltpu.SMEM)
    return kernel_call(
        functools.partial(newton_body, window, tile),
        (1,),
        [scalar, scalar, pl.BlockSpec(memory_space=pl.ANY)],
        whole((window, size)),
        shape_of((window, size), jnp.bfloat16),
        [pltpu.VMEM((size, size), jnp.bfloat16)] * 2 + [pltpu.SemaphoreType.DMA((size // tile,))],
    )(first, scale, start)


def swap(value, bit):
    size = lax.axis_size("tm")
    return lax.ppermute(value, "tm", [(i, i ^ bit) for i in range(size)])


def steps_of(size):
    bits = []
    bit = 1
    while bit < size:
        bits.append(bit)
        bit *= 2
    return bits


def bit_of(bit):
    return jnp.where((lax.axis_index("tm") & bit) != 0, 1, 0)


class SumSpread:
    def __init__(self, value):
        self.value = value
        self.steps = []
        lanes = value.shape[1]
        cuts = []
        for bit in steps_of(lax.axis_size("tm")):
            if lanes // 2 % WIDE == 0:
                lanes //= 2
                self.steps.append((self.halve, bit))
                cuts.append(bit)
            else:
                self.steps.append((self.pair, bit))
        self.steps += [(self.join, bit) for bit in reversed(cuts)]

    def halve(self, bit):
        lanes = self.value.shape[1] // 2
        mine = lax.dynamic_slice_in_dim(self.value, bit_of(bit) * lanes, lanes, 1)
        away = lax.dynamic_slice_in_dim(self.value, (1 - bit_of(bit)) * lanes, lanes, 1)
        self.value = mine + swap(away, bit)

    def pair(self, bit):
        self.value = self.value + swap(self.value, bit)

    def join(self, bit):
        other = swap(self.value, bit)
        upper = bit_of(bit) == 1
        self.value = jnp.concatenate(
            [jnp.where(upper, other, self.value), jnp.where(upper, self.value, other)], axis=1
        )

    def step(self, times=1):
        for _ in range(times):
            if self.steps:
                action, bit = self.steps.pop(0)
                action(bit)


def tie(first, second):
    return lax.optimization_barrier((list(first), list(second)))


def side_bit():
    return lax.axis_size("tm") // 32


def orders_of(size):
    bits = [bit for bit in steps_of(size) if bit != side_bit()]
    return [bits[k * len(bits) // 3 :] + bits[: k * len(bits) // 3] for k in range(3)]


def index_bits(bits):
    return [bit if bit < side_bit() else bit // 2 for bit in bits]


class Scatter:
    def __init__(self, keeps, sends):
        self.orders = orders_of(lax.axis_size("tm"))
        self.current = list(keeps)
        self.received = [swap(send, side_bit()) for send in sends]

    def step(self, *waiting):
        sends = []
        for p, order in enumerate(self.orders):
            half = self.current[p].shape[0] // 2
            mine, away = [
                lax.dynamic_slice_in_dim(self.current[p], half * index, half).astype(jnp.float32)
                + lax.dynamic_slice_in_dim(self.received[p], half * index, half).astype(jnp.float32)
                for index in (bit_of(order[0]), 1 - bit_of(order[0]))
            ]
            self.current[p] = mine
            sends.append(away.astype(jnp.bfloat16))
        sends, waiting = tie(sends, waiting)
        self.received = [swap(send, order.pop(0)) for send, order in zip(sends, self.orders)]
        return waiting

    def join(self, *done):
        self.received, done = tie(self.received, done)
        return done

    def result(self):
        return [a + b.astype(jnp.float32) for a, b in zip(self.current, self.received)]


class Stats:
    def __init__(self, stat, count):
        self.stat = stat
        self.count = float(count)
        self.bits = steps_of(lax.axis_size("tm"))

    def step(self, times=1):
        for _ in range(min(times, len(self.bits))):
            stat = self.stat
            other = swap(stat, self.bits.pop(0))
            gap = stat[0:1] - other[0:1]
            mean = 0.5 * (stat[0:1] + other[0:1])
            square = (stat[1:2] + other[1:2]) + gap * gap * (0.5 * self.count)
            self.stat = jnp.concatenate([mean, square, 0.5 * (stat[2:] + other[2:])], axis=0)
            self.count *= 2


class Exchange:
    def __init__(self, flags, carries, sums=()):
        self.bits = steps_of(lax.axis_size("tm"))
        high, self.width = carries[0][0].shape
        rows = high * len(carries)
        flags = jnp.broadcast_to(jnp.tile(flags, len(carries))[:, None], (rows, LANE))
        ends = jnp.concatenate([ends for ends, _, _ in carries], axis=0)
        self.payload = jnp.concatenate([ends, flags, *sums], axis=1)
        self.power = jnp.concatenate(
            [jnp.broadcast_to(power, (high, self.width)) for _, power, _ in carries], axis=0
        )
        self.lane = lax.broadcasted_iota(jnp.int32, self.payload.shape, 1)
        self.high = high
        self.reverse = [reverse for _, _, reverse in carries]
        self.before = jnp.zeros_like(ends)
        self.before_keep = jnp.ones_like(ends)

    def step(self, times=1):
        for _ in range(min(times, len(self.bits))):
            self.one()

    def one(self):
        bit = self.bits.pop(0)
        width = self.width
        mine, other = self.payload, swap(self.payload, bit)
        upper = bit_of(bit)
        row = lax.broadcasted_iota(jnp.int32, (len(mine), 1), 0) // self.high
        turned = sum((row == k) * int(reverse) for k, reverse in enumerate(self.reverse))
        following = turned != upper
        other_total = other[:, :width]
        keep_mine, keep_other = mine[:, width : width + 1], other[:, width : width + 1]
        self.before = jnp.where(
            following, self.before_keep * other_total + self.before, self.before
        )
        self.before_keep = jnp.where(
            following, self.before_keep * keep_other * self.power, self.before_keep
        )
        power = jnp.pad(self.power, ((0, 0), (0, mine.shape[1] - width)))
        carried = jnp.where(
            following, keep_mine * power * other + mine, keep_other * power * mine + other
        )
        self.payload = jnp.where(
            self.lane < width,
            carried,
            jnp.where(self.lane < width + LANE, mine * other, mine + other),
        )
        self.power = self.power * self.power

    def parts(self):
        found = []
        for k, reverse in enumerate(self.reverse):
            part = copy.copy(self)
            place = slice(k * self.high, (k + 1) * self.high)
            part.bits = list(self.bits)
            part.payload, part.power, part.lane = [
                value[place] for value in (self.payload, self.power, self.lane)
            ]
            part.before, part.before_keep = self.before[place], self.before_keep[place]
            part.reverse = [reverse]
            found.append(part)
        return found

    def arrived(self, k):
        return self.before[k * self.high : (k + 1) * self.high]

    def sums(self):
        return self.payload[:, self.width + LANE :]


class SumAll:
    def __init__(self, value):
        self.value = value
        self.bits = steps_of(lax.axis_size("tm"))

    def step(self, times=1):
        for _ in range(min(times, len(self.bits))):
            self.value = self.value + swap(self.value, self.bits.pop(0))


def in_order(value, bits, slots):
    count = len(bits)
    axes = [count - bit.bit_length() for bit in bits]
    shape = (2,) * count + (slots, value.shape[1])
    return value.reshape(shape).transpose(axes + [count, count + 1]).reshape(value.shape)


def pad_lanes(value, padded):
    gap = padded - value.shape[-1]
    return jnp.pad(value, [(0, 0)] * (value.ndim - 1) + [(0, gap)])


def flat_places(shard, width, padded):
    size = lax.axis_size("tm")
    members = size * LANE // padded
    slots = LANE // members
    return members, slots, slots * width - shard


def to_block(flat, width, padded):
    size, mine = lax.axis_size("tm"), lax.axis_index("tm")
    members, slots, excess = flat_places(flat.shape[0], width, padded)
    lacking = excess * (members - 1)
    pairs = [(i + 1, i) for i in range(size - 1) if (i + 1) % members]
    extra = lax.ppermute(flat[:lacking], "tm", pairs)
    tail = jnp.zeros((excess,), flat.dtype)
    held = jnp.concatenate([flat, extra, tail])
    return lax.dynamic_slice_in_dim(held, excess * (mine % members), slots * width).reshape(
        slots, width
    )


def from_block(block, shard, padded):
    width = block.shape[1]
    size, mine = lax.axis_size("tm"), lax.axis_index("tm")
    members, slots, excess = flat_places(shard, width, padded)
    lacking = excess * (members - 1)
    pairs = [(i, i + 1) for i in range(size - 1) if (i + 1) % members]
    flat = block.reshape(-1)
    extra = lax.ppermute(flat[slots * width - lacking :], "tm", pairs)
    held = jnp.concatenate([extra, flat])
    return lax.dynamic_slice_in_dim(held, lacking - excess * (mine % members), shard)


def own_window(shard, width, padded):
    mine = lax.axis_index("tm")
    members, _, _ = flat_places(shard, width, padded)
    window = 16
    for k in range(members):
        first = shard * k // width // 16 * 16
        last = -(-shard * (k + 1) // width)
        window = max(window, -(-(last - first) // 16) * 16)
    member = mine % members
    first = jnp.minimum(shard * member // width // 16 * 16, LANE - window)
    return window, LANE * (mine // members) + first, shard * member - first * width


def per_device(
    inputs,
    clip_start,
    shallow_weight,
    shallow_momentum,
    deep_weight,
    deep_momentum,
    unit_params,
    unit_first,
    unit_second,
    out_grad,
):
    devices = lax.axis_size("tm")
    rows, frames, feats = inputs.shape
    width = shallow_weight.shape[1]
    padded = -(-width // WIDE) * WIDE
    group = width // (padded // LANE)
    count = rows * frames
    keep_mask = (1 - clip_start).astype(jnp.float32)
    flags = jnp.min(keep_mask, axis=1)
    keep = jnp.broadcast_to(keep_mask.T.reshape(count, 1), (count, LANE))
    params = pad_lanes(unit_params, padded)
    rates = jnp.maximum(1.0 - jnp.exp(-params[:, 0:1]), DECAY_FLOOR)
    powers = rates
    for _ in range(frames.bit_length() - 1):
        powers = powers * powers

    deep_block = pad_lanes(to_block(deep_weight.astype(jnp.bfloat16), width, padded), padded)
    momentum_block = pad_lanes(to_block(deep_momentum, width, padded), padded)

    shares = [3 * padded // 8, 3 * padded // 8, padded // 4]
    parts = [(sum(shares[:p]), shares[p]) for p in range(3)]
    side = bit_of(side_bit()).astype(jnp.int32).reshape(1)
    chunks = padded // WIDE
    orders = orders_of(devices)
    x, proj_one, stat_one, gram = front(
        inputs.reshape(count, feats), shallow_weight, rows, frames
    )
    (deep_block,), (stat_one,) = tie([deep_block], [stat_one])
    deep_low = lax.all_gather(deep_block, "tm", axis=0, tiled=True)
    stats = Stats(stat_one, count)
    stats.step()
    delta_local, delta_end = delta_two(
        out_grad.reshape(count, width), keep, params[1], rows, frames, padded
    )
    (delta_local, delta_end), (stats.stat,) = tie([delta_local, delta_end], [stats.stat])
    stats.step(len(stats.bits))
    stat_one = stats.stat
    state_local, state_end = local_states(
        proj_one, keep, params[0], stat_one, rows, frames, devices
    )
    carries = Exchange(flags, [(state_end, powers[0], False), (delta_end, powers[1], True)])
    carries.step(len(carries.bits) - 2)
    carries, later = carries.parts()
    carries.step(len(carries.bits))
    (state_in,), (later.payload,) = tie([carries.arrived(0)], [later.payload])
    later.step()
    low_one, mean_one = low_one_of(
        state_local, state_in, keep, params[0], rows, frames, width, group
    )
    (low_one, mean_one), (later.payload, later.before, momentum_block) = tie(
        [low_one, mean_one], [later.payload, later.before, momentum_block]
    )
    later.step(len(later.bits))
    proj_two, stat_two = second_forward(low_one, deep_low)
    (stat_two,), (later.payload, later.before) = tie([stat_two], [later.payload, later.before])
    stats = Stats(jnp.concatenate([stat_two, mean_one], axis=0), count)
    stats.step(len(stats.bits))
    delta_in = later.arrived(0)
    hidden = [None, None]
    sources = [(state_local, state_in, params[0]), None]

    def next_hidden(layer, places, waiting):
        states, start, layer_params = sources[layer]
        for k in places:
            (start,), waiting = tie([start], waiting)
            hidden[layer] = hidden_of(
                k, hidden[layer], states, start, keep, layer_params, rows, frames, width
            )
        hidden[layer], waiting = tie(hidden[layer], waiting)
        return waiting

    stat_two, mean_one = stats.stat[:2], stats.stat[2:]
    gate, sums_two = gate_two(
        proj_two, delta_local, delta_in, keep, params[1], stat_two, rows, frames, devices
    )
    sums = SumAll(sums_two)
    turned = None
    for k in range(chunks):
        sums.step()
        turned = turn(k, turned, low_one, mean_one)
        turned, (sums.value,) = tie(turned, [sums.value])
    sums.step(len(sums.bits))
    sums_two = sums.value
    slots = padded // devices
    weights = [index_bits(order) for order in orders]
    aligned = slots % 16 == 0
    grad_two, total_two, keeps, sends = deep_term(
        parts, weights if aligned else None, side, gate, proj_two, params[1], stat_two,
        sums_two, turned[0], rows, frames, devices,
    )
    if not aligned:
        keeps = [in_order(keep, order, slots) for keep, order in zip(keeps, weights)]
        sends = [in_order(send, order, slots) for send, order in zip(sends, weights)]
    scatter = Scatter(keeps, sends)
    back = back_one(grad_two, deep_low)
    (back,) = scatter.join(back)
    (back,) = scatter.step(back)
    back_local, back_end = delta_one(back, keep, params[0], rows, frames, width, group)
    second_local, second_end, second_decay = states_two(
        proj_two, delta_local, delta_in, keep, params[1], stat_two, rows, frames, devices
    )
    back_end, second_end = scatter.join(back_end, second_end)
    tall = 2 * rows
    back_end, second_end = scatter.step(back_end, second_end)
    carries = Exchange(
        flags,
        [(back_end, powers[0], True), (second_end, powers[1], False)],
        [total_two.reshape(tall, -1), gram],
    )
    carries.step(2)
    (carries.payload,) = next_hidden(0, range(chunks), [carries.payload])
    (carries.payload,) = scatter.join(carries.payload)
    while len(scatter.orders[0]) > 1:
        (carries.payload,) = scatter.step(carries.payload)
        carries.step()
        (carries.payload,) = scatter.join(carries.payload)
    (carries.payload,) = scatter.step(carries.payload)
    carries.step(len(carries.bits))
    carries.payload, carries.before = scatter.join(carries.payload, carries.before)
    back_in, second_in = carries.arrived(0), carries.arrived(1)
    sources[1] = (second_local, second_in, params[1])
    total_two = carries.sums()[:, : padded // tall].reshape(1, padded)
    gram = carries.sums()[:, padded // tall :]
    mine = lax.axis_index("tm")
    place = mine // (2 * side_bit()) * side_bit() + mine % side_bit()
    place = (side[0] * (devices // 2) + place) * slots
    mean_own = lax.dynamic_slice_in_dim(mean_one[0], place, slots)[:, None]
    grad_parts = [
        part + mean_own * total_two[:, first : first + lanes]
        for (first, lanes), part in zip(parts, scatter.result())
    ]
    grad_block = jnp.concatenate(grad_parts, axis=1)
    momentum_new = MUON_BETA * momentum_block + grad_block
    start_block = momentum_new.astype(jnp.bfloat16)
    (start_block,), (back_in,) = tie([start_block], [back_in])
    gathered = lax.all_gather(start_block, "tm", axis=0, tiled=True)
    sums_one, input_part, gate_mean = gate_one(
        proj_one, state_local, state_in, back_local, back_in, keep, params[0], stat_one, x,
        shallow_weight, rows, frames, devices,
    )
    decay_two = jnp.sum(second_decay[:rows] + second_decay[rows:] * second_in, axis=0, keepdims=True)
    square = jnp.sum(momentum_new * momentum_new).reshape(1, 1)
    sums_one = (
        sums_one
        + jnp.pad(decay_two, ((feats + 3, SIDE - feats - 4), (0, 0)))
        + jnp.pad(square, ((feats + 4, SIDE - feats - 5), (0, padded - 1)))
    )
    spread = SumSpread(sums_one)
    for k in range(chunks):
        spread.step()
        (spread.value,) = next_hidden(1, [k], [spread.value])
    spread.step(len(spread.steps))
    sums_one = spread.value
    (hidden_one,), (hidden_two,) = hidden
    shallow_grad, shallow_next, shallow_new, shallow_low, input_grad = shallow_step(
        sums_one, gram, params[0], stat_one, shallow_weight, shallow_momentum, x, input_part, gate_mean,
        count * devices, rows, frames,
    )
    (gathered,), (shallow_low,) = tie([gathered], [shallow_low])
    input_grad = input_grad.reshape(rows, frames, feats)
    scale = 1.0 / (jnp.sqrt(sums_one[feats + 4, :1]) + MUON_EPSILON)
    shard = deep_weight.shape[0]
    window, first_row, offset = own_window(shard, width, padded)
    ortho = newton_rows(
        gathered, scale, (first_row // 16).astype(jnp.int32).reshape(1), window
    )
    deep_ortho = lax.dynamic_slice_in_dim(ortho[:, :width].reshape(-1), offset, shard)
    deep_new = MUON_KEEP * deep_weight - MUON_RATE * deep_ortho.astype(jnp.float32)
    deep_grad = from_block(grad_block[:, :width], shard, padded)
    deep_next = MUON_BETA * deep_momentum + deep_grad

    unit_sums = sums_one[feats : feats + 4, :width]
    bias_gain_two = sums_two[:, :width]
    slope = jnp.where(
        1.0 - jnp.exp(-unit_params[:, 0]) > DECAY_FLOOR, jnp.exp(-unit_params[:, 0]), 0.0
    )
    unit_grad = jnp.stack(
        [
            jnp.stack([unit_sums[2] * slope[0], unit_sums[0], unit_sums[1], unit_sums[0]]),
            jnp.stack(
                [unit_sums[3] * slope[1], bias_gain_two[0], bias_gain_two[1], bias_gain_two[0]]
            ),
        ]
    )
    first_fix = 1.0 - FIRST_DECAY**STEP
    second_fix = 1.0 - SECOND_DECAY**STEP
    first_new = FIRST_DECAY * unit_first + (1.0 - FIRST_DECAY) * unit_grad
    second_new = SECOND_DECAY * unit_second + (1.0 - SECOND_DECAY) * unit_grad * unit_grad
    params_new = unit_params - ADAM_RATE * (first_new / first_fix) / (
        jnp.sqrt(second_new / second_fix) + ADAM_EPSILON
    )
    return (
        hidden_one.reshape(rows, frames, width),
        hidden_two.reshape(rows, frames, width),
        input_grad,
        shallow_grad,
        shallow_next,
        shallow_new,
        shallow_low,
        deep_grad,
        deep_next,
        deep_new,
        deep_new.astype(jnp.bfloat16),
        first_new,
        second_new,
        params_new,
    )


def solution(mesh):
    in_specs = (
        P(None, "tm", None),
        P(None, "tm"),
        P(),
        P(),
        P("tm"),
        P("tm"),
        P(),
        P(),
        P(),
        P(None, "tm", None),
    )
    out_specs = (
        P(None, "tm", None),
        P(None, "tm", None),
        P(None, "tm", None),
        P(),
        P(),
        P(),
        P(),
        P("tm"),
        P("tm"),
        P("tm"),
        P("tm"),
        P(),
        P(),
        P(),
    )
    return jax.shard_map(
        per_device, mesh=mesh, in_specs=in_specs, out_specs=out_specs, check_vma=False
    )
```
